32 devices in a mesh: seq: 4 (over z), batch: 2 (over core), head: 4 (over y, x).
Axes of the slice: x: 2, y: 2, z: 4, core: 2. Of those that a mesh axis runs over, the one named last changes fastest.
Arguments:
- tokens: bfloat16 [4, 2048, 1024], P('batch', 'seq'), may hold values from -6 to 6
- starts: int32 [4], P('batch'), may hold values from 0 to 511
- attn_gain: float32 [1024], P(('seq', 'batch')), may hold values from 0.5 to 1.5
- w_in: float32 [1024, 8, 768], P(('seq', 'batch'), 'head'), may hold values from -0.1875 to 0.1875
- w_rates: float32 [1024, 8, 2], P(('seq', 'batch'), 'head'), may hold values from -0.1875 to 0.1875
- conv_w: float32 [4, 8, 512], P(None, 'head', ('seq', 'batch')), may hold values from -3 to 3
- decay_par: float32 [2, 8], P(None, 'head'), as said below
- o_gain: float32 [256], P(('seq', 'batch')), may hold values from 0.5 to 1.5
- w_out: float32 [8, 256, 1024], P('head', None, ('seq', 'batch')), may hold values from -0.125 to 0.125
- ffn_gain: float32 [1024], P(('seq', 'batch')), may hold values from 0.5 to 1.5
- w_gu: float32 [1024, 2, 2816], P(('seq', 'batch'), None, 'head'), may hold values from -0.1875 to 0.1875
- w_down: float32 [2816, 1024], P('head', ('seq', 'batch')), may hold values from -0.109375 to 0.109375
- cotangent: bfloat16 [4, 2048, 1024], P('batch', 'seq'), may hold values from -6 to 6
Outputs:
- out: bfloat16 [4, 2048, 1024], P('batch', 'seq')
- input_grad: bfloat16 [4, 2048, 1024], P('batch', 'seq')
- grad_attn_gain: float32 [1024], P(('seq', 'batch'))
- grad_w_in: float32 [1024, 8, 768], P(('seq', 'batch'), 'head')
- grad_w_rates: float32 [1024, 8, 2], P(('seq', 'batch'), 'head')
- grad_conv_w: float32 [4, 8, 512], P(None, 'head', ('seq', 'batch'))
- grad_decay_par: float32 [2, 8], P(None, 'head')
- grad_o_gain: float32 [256], P(('seq', 'batch'))
- grad_w_out: float32 [8, 256, 1024], P('head', None, ('seq', 'batch'))
- grad_ffn_gain: float32 [1024], P(('seq', 'batch'))
- grad_w_gu: float32 [1024, 2, 2816], P(('seq', 'batch'), None, 'head')
- grad_w_down: float32 [2816, 1024], P('head', ('seq', 'batch'))
The draws below stay inside these ranges and needn't reach their ends.
Inputs may be any that keep to these rules, and one draw needn't show every extreme that they name: `starts`: a sequence's tokens before its start position are padding; every start lies among the first 512 positions. `decay_par`: row 0 holds logarithms of positive decay rates, row 1 biases added before softplus.
All inputs are finite; a program needn't handle non-finite values.
Results may differ from the reference program's by a relative error of at most 0.025.
Values may be sent and summed in bfloat16 or wider, within the bound.
A program may use at most 320 MiB of HBM per device.

```python
import jax
import jax.numpy as jnp
from jax import lax

D = 1024
H = 8
DK = 128
DV = 256
FF = 2816
CONV = 4
STRETCH = 64
TOK_DEV = 512
QKV = 512
IN_COLS = 768
VALUES = 2048
LEN = 2048
SEQS = 4


def draw_decay_par(key, part):
    first, second = jax.random.split(jax.random.fold_in(key, 11))
    rates = jax.random.uniform(first, (H,), jnp.float32, 1.0, 16.0)
    steps = jnp.exp(jax.random.uniform(second, (H,), jnp.float32, jnp.log(0.001), jnp.log(0.1)))
    return jnp.stack([jnp.log(rates), jnp.log(jnp.expm1(steps))]).astype(jnp.float32)


def place_ends(values, key, low, top_value):
    dims = values.shape
    index_at = [jax.random.randint(jax.random.fold_in(key, axis), (), 0, dims[axis]) for axis in range(len(dims))]
    values = values.at[tuple(index_at)].set(low)
    longest = dims.index(max(dims))
    index_at[longest] = (index_at[longest] + 1) % dims[longest]
    return values.at[tuple(index_at)].set(top_value)


def steps_of(own_key, shape, pieces, low, largest):
    factor_of = 1.0
    for dim, shards_of in pieces:
        draws = jax.random.uniform(jax.random.fold_in(jax.random.fold_in(own_key, 6), dim), (shards_of,), jnp.float32, low / len(pieces), largest / len(pieces))
        factor_of = factor_of * jnp.repeat(jnp.exp(draws), shape[dim] // shards_of).reshape((-1,) + (1,) * (len(shape) - 1 - dim))
    return factor_of


def centred(own_key, dims, width, reach, pieces=(), kind=jnp.bfloat16):
    drawn = width * jax.random.normal(own_key, dims, jnp.float32)
    if pieces:
        drawn = drawn * steps_of(own_key, dims, pieces, -0.22, 0.18)
    return jnp.clip(drawn, -reach, reach).astype(kind)


def setup_inputs(seed: int = 0) -> dict:
    arg_keys = jax.random.split(jax.random.key(seed), 14)
    return {
        "tokens": centred(arg_keys[0], (SEQS, LEN, D), 1.0, 6.0, ((0, 2), (1, 4))),
        "starts": place_ends(jax.random.randint(arg_keys[1], (SEQS,), 0, TOK_DEV), jax.random.fold_in(arg_keys[1], 1), 0, TOK_DEV - 1).astype(jnp.int32),
        "attn_gain": jnp.clip(1.0 + 0.1 * jax.random.normal(arg_keys[2], (D,), jnp.float32), 0.5, 1.5),
        "w_in": centred(arg_keys[3], (D, H, IN_COLS), D ** -0.5, 0.1875, ((0, 8), (1, 4)), jnp.float32),
        "w_rates": centred(arg_keys[4], (D, H, 2), D ** -0.5, 0.1875, ((0, 8), (1, 4)), jnp.float32),
        "conv_w": centred(arg_keys[5], (CONV, H, QKV), CONV ** -0.5, 3.0, ((1, 4), (2, 8)), jnp.float32),
        "decay_par": draw_decay_par(jax.random.fold_in(arg_keys[13], 71), 0),
        "o_gain": jnp.clip(1.0 + 0.1 * jax.random.normal(arg_keys[7], (DV,), jnp.float32), 0.5, 1.5),
        "w_out": centred(arg_keys[8], (H, DV, D), VALUES ** -0.5, 0.125, ((0, 4), (2, 8)), jnp.float32),
        "ffn_gain": jnp.clip(1.0 + 0.1 * jax.random.normal(arg_keys[9], (D,), jnp.float32), 0.5, 1.5),
        "w_gu": centred(arg_keys[10], (D, 2, FF), D ** -0.5, 0.1875, ((0, 8), (2, 4)), jnp.float32),
        "w_down": centred(arg_keys[11], (FF, D), FF ** -0.5, 0.109375, ((0, 4), (1, 8)), jnp.float32),
        "cotangent": centred(arg_keys[12], (SEQS, LEN, D), 1.0, 6.0, ((0, 2), (1, 4))),
    }


top_precision = lax.Precision.HIGHEST
epsilon = 1e-06

@jax.custom_vjp
def low(v):
    return lax.optimization_barrier(v.astype(jnp.bfloat16)).astype(jnp.float32)

@jax.custom_vjp
def low_back(v):
    return v

def low_keep(v):
    return (low(v), None)

def low_pass(kept, grad):
    return (grad,)

def back_keep(v):
    return (v, None)

def back_low(kept, grad):
    return (low(grad),)
low.defvjp(low_keep, low_pass)
low_back.defvjp(back_keep, back_low)

def root_scale(value_rows):
    return lax.rsqrt(lax.optimization_barrier(jnp.mean(value_rows * value_rows, axis=-1, keepdims=True)) + epsilon)

def features(extended, conv_weight):
    tap_count = conv_weight.shape[0]
    span_rows = extended.shape[1] - tap_count + 1
    convolved = extended[:, 0:span_rows] * conv_weight[0]
    for offset in range(1, tap_count):
        convolved = convolved + extended[:, offset:offset + span_rows] * conv_weight[offset]
    active = jax.nn.silu(convolved)
    query_rows = active[..., :DK]
    incoming_keys = active[..., DK:2 * DK]
    value_rows = active[..., 2 * DK:]
    query_rows = query_rows * lax.rsqrt(lax.optimization_barrier(jnp.sum(query_rows * query_rows, axis=-1, keepdims=True)) + epsilon) * DK ** (-0.5)
    incoming_keys = incoming_keys * lax.rsqrt(lax.optimization_barrier(jnp.sum(incoming_keys * incoming_keys, axis=-1, keepdims=True)) + epsilon)
    return (query_rows, incoming_keys, value_rows)

def stretch_rule(memory, segment):

    def token_step(present_value, member):
        query_rows, incoming_keys, value_rows, write_strength, decays = member
        present_value = decays[:, None, None] * present_value
        estimate_value = jnp.einsum('oz,ozq->oq', incoming_keys, present_value, precision=top_precision)
        present_value = present_value + jnp.einsum('yr,yg->yrg', incoming_keys, write_strength[:, None] * (value_rows - estimate_value), precision=top_precision)
        return (present_value, jnp.einsum('oz,ozq->oq', query_rows, present_value, precision=top_precision))
    return lax.scan(token_step, memory, segment)

def delta_rule(query_rows, incoming_keys, value_rows, write_strength, log_gate):
    length = query_rows.shape[0]
    count = length // STRETCH
    shaped = tuple((member.reshape((count, STRETCH) + member.shape[1:]) for member in (query_rows, incoming_keys, value_rows, write_strength, jnp.exp(log_gate))))
    start_state = jnp.zeros((query_rows.shape[1], DK, DV), jnp.float32)
    ending, outputs = lax.scan(jax.checkpoint(stretch_rule), start_state, shaped)
    return outputs.reshape((length,) + outputs.shape[2:])

def forward(inputs, start, weights):
    attn_gain, w_in, w_rates, conv_w, decay_par, o_gain, w_out, ffn_gain, w_gu, w_down = weights
    length = inputs.shape[0]
    qkv_cols = 2 * DK + DV
    normed_in = low(inputs * root_scale(inputs) * low(attn_gain))
    projected = low_back(jnp.einsum('td,dhc->thc', normed_in, low(w_in), precision=top_precision))
    rate_logits = low_back(jnp.einsum('td,dhc->thc', normed_in, low(w_rates), precision=top_precision))
    live_mask = (jnp.arange(length, dtype=jnp.int32) >= start).astype(jnp.float32)
    conv_input = low(projected[:, :, :qkv_cols] * live_mask[:, None, None])
    extended = jnp.concatenate([jnp.zeros((CONV - 1,) + conv_input.shape[1:], jnp.float32), conv_input], axis=0)
    query_rows, incoming_keys, value_rows = features(extended[None], low(conv_w))
    query_rows = low_back(low(query_rows[0]))
    incoming_keys = low_back(low(incoming_keys[0]))
    value_rows = low_back(low(value_rows[0]))
    log_gate = -jnp.exp(decay_par[0]) * jax.nn.softplus(rate_logits[..., 0] + decay_par[1])
    write_strength = jax.nn.sigmoid(rate_logits[..., 1])
    mixed = delta_rule(query_rows, incoming_keys, value_rows, write_strength, log_gate)
    normed = mixed * root_scale(mixed) * low(o_gain) * jax.nn.silu(projected[:, :, qkv_cols:])
    mixer_out = low_back(jnp.einsum('thv,hvd->td', low(normed), low(w_out), precision=top_precision))
    hidden = inputs + mixer_out
    normed_mid = low(hidden * root_scale(hidden) * low(ffn_gain))
    gate_up = low_back(jnp.einsum('td,dgf->tgf', normed_mid, low(w_gu), precision=top_precision))
    activated = low(jax.nn.silu(gate_up[:, 0]) * gate_up[:, 1])
    ffn_out = low_back(jnp.dot(activated, low(w_down), precision=top_precision))
    return hidden + ffn_out

def reference(tokens, starts, attn_gain, w_in, w_rates, conv_w, decay_par, o_gain, w_out, ffn_gain, w_gu, w_down, cotangent):
    weights = (attn_gain, w_in, w_rates, conv_w, decay_par, o_gain, w_out, ffn_gain, w_gu, w_down)

    def per_sequence(totals, member):
        inputs, start, upstream = member
        result, pullback = jax.vjp(lambda data, params: forward(data, start, params), inputs.astype(jnp.float32), weights)
        input_grads, weight_grads = pullback(upstream.astype(jnp.float32))
        totals = jax.tree.map(jnp.add, totals, weight_grads)
        return (totals, (result.astype(jnp.bfloat16), input_grads.astype(jnp.bfloat16)))
    zero_grads = jax.tree.map(jnp.zeros_like, weights)
    grads, (outputs, input_grad) = lax.scan(per_sequence, zero_grads, (tokens, starts, cotangent))
    return (outputs, input_grad, grads[0], grads[1], grads[2], grads[3], grads[4], grads[5], grads[6], grads[7], grads[8], grads[9])
```

```python
import functools

import jax
import jax.numpy as jnp
from jax import lax
from jax.experimental import pallas as pl
from jax.experimental.pallas import tpu as pltpu
from jax.sharding import PartitionSpec as P

DK = 128
DV = 256
CONV = 4
QKV = 2 * DK + DV
CHUNK = 128
HALO = 16
PAD = 128

bf16 = jnp.bfloat16
f32 = jnp.float32
epsilon = 1e-06
NN = ((1,), (0,))
NT = ((1,), (1,))
TN = ((0,), (0,))


def mm(a, b, dims=NN):
    return lax.dot_general(
        a.astype(bf16), b.astype(bf16), (dims, ((), ())), preferred_element_type=f32
    )


def split_mm(a, b):
    a_high, b_high = a.astype(bf16), b.astype(bf16)
    a_low = (a - a_high.astype(f32)).astype(bf16)
    b_low = (b - b_high.astype(f32)).astype(bf16)
    return mm(a_high, b_high) + (mm(a_high, b_low) + mm(a_low, b_high))


def iotas(n):
    return (
        lax.broadcasted_iota(jnp.int32, (n, n), 0),
        lax.broadcasted_iota(jnp.int32, (n, n), 1),
    )


def unit_lower_inverses(mats):
    n = mats[0].shape[0]
    rows, cols = iotas(n)
    eye = (rows == cols).astype(f32)
    pair = ((rows >> 1) == (cols >> 1)) & (rows > cols)
    inverses = [eye - jnp.where(pair, a, 0.0) for a in mats]
    shift = 1
    while (1 << shift) < n:
        corner = ((rows >> (shift + 1)) == (cols >> (shift + 1))) & (
            (rows >> shift) > (cols >> shift)
        )
        firsts = [mm(jnp.where(corner, a, 0.0), x) for a, x in zip(mats, inverses)]
        inverses = [x - mm(x, y) for x, y in zip(inverses, firsts)]
        shift += 1
    residuals = [eye - x - split_mm(a, x) for a, x in zip(mats, inverses)]
    return [x + mm(x, r) for x, r in zip(inverses, residuals)]


def sigmoid(v):
    return 1.0 / (1.0 + jnp.exp(-v))


def softplus(v):
    small = jnp.exp(-jnp.abs(v))
    one_more = 1.0 + small
    gap = one_more - 1.0
    exact = gap == 0.0
    tail = jnp.where(exact, small, jnp.log(one_more) * small / jnp.where(exact, 1.0, gap))
    return jnp.maximum(v, 0.0) + tail


def to_row(column, eye):
    return jnp.sum(jnp.where(eye, column, 0.0), axis=0, keepdims=True)


def pick(block, lane):
    lanes = lax.broadcasted_iota(jnp.int32, block.shape, 1)
    return jnp.sum(jnp.where(lanes == lane, block, 0.0), axis=1, keepdims=True)


def gates(logits, decay_ref, head):
    rate = jnp.exp(jnp.full((1, 1), decay_ref[0, head], f32))
    shifted_logit = pick(logits, 2 * head) + decay_ref[1, head]
    strength = sigmoid(pick(logits, 2 * head + 1))
    log_gate = -rate * softplus(shifted_logit)
    return log_gate, strength, rate, shifted_logit


def decays(log_gate, lower, upper, eye):
    gate_row = to_row(log_gate, eye)
    column = jnp.sum(jnp.where(lower, gate_row, 0.0), axis=1, keepdims=True)
    row = jnp.sum(jnp.where(upper, log_gate, 0.0), axis=0, keepdims=True)
    ratio = jnp.where(lower, jnp.exp(jnp.where(lower, column - row, 0.0)), 0.0)
    total = jnp.sum(log_gate, axis=0, keepdims=True)
    return column, total, ratio


def load_conv_input(main_ref, halo_ref, start_ref, x_scr, seq_place):
    length = main_ref.shape[0]
    s = pl.program_id(1)
    positions = seq_place * length + lax.broadcasted_iota(jnp.int32, (length, 1), 0)
    live = (positions >= start_ref[s]).astype(f32)
    x_scr[pl.ds(0, HALO), :] = halo_ref[0].astype(f32)
    x_scr[pl.ds(HALO, length), :] = (main_ref[...] * live).astype(bf16).astype(f32)


def convolve(x_scr, conv, at):
    total = x_scr[pl.ds(at + HALO - CONV + 1, CHUNK), :] * conv[0:1]
    for j in range(1, CONV):
        total = total + x_scr[pl.ds(at + HALO - CONV + 1 + j, CHUNK), :] * conv[j : j + 1]
    return total


def unit(rows):
    return rows * lax.rsqrt(jnp.sum(rows * rows, axis=1, keepdims=True) + epsilon)


def chunk_kernel(
    place_ref, start_ref, decay_ref, main_ref, halo_ref, rate_ref, conv_ref,
    qkv_ref, inv_ref, n_ref, b_ref, qe_ref, o_ref, tot_ref, map_ref, x_scr,
):
    head = pl.program_id(0)
    load_conv_input(main_ref, halo_ref, start_ref, x_scr, place_ref[0])
    conv = conv_ref[...]
    length = main_ref.shape[0]
    count = length // CHUNK
    rows, cols = iotas(CHUNK)
    lower, upper, eye = rows >= cols, rows <= cols, rows == cols
    parts = []
    for c in range(count):
        at = c * CHUNK
        convolved = convolve(x_scr, conv, at)
        active = convolved * sigmoid(convolved)
        q = (unit(active[:, :DK]) * DK ** (-0.5)).astype(bf16)
        k = unit(active[:, DK : 2 * DK]).astype(bf16)
        v = active[:, 2 * DK :].astype(bf16)
        qkv_ref[pl.ds(at, CHUNK), 0:DK] = q
        qkv_ref[pl.ds(at, CHUNK), DK : 2 * DK] = k
        qkv_ref[pl.ds(at, CHUNK), 2 * DK :] = v
        log_gate, strength, _, _ = gates(rate_ref[pl.ds(at, CHUNK), :], decay_ref, head)
        column, total, ratio = decays(log_gate, lower, upper, eye)
        products = mm(jnp.concatenate([k, q], axis=0), k, NT)
        coupling = jnp.where(rows > cols, strength * ratio * products[:CHUNK], 0.0)
        scores = (ratio * products[CHUNK:]).astype(bf16)
        parts.append((q, k, v, strength, column, total, coupling, scores))
    inverses = unit_lower_inverses([p[6] for p in parts])
    maps = []
    for c in range(count):
        q, k, v, strength, column, total, _, scores = parts[c]
        growth = jnp.exp(column)
        kf, vf, qf = k.astype(f32), v.astype(f32), q.astype(f32)
        inverse = inverses[c].astype(bf16)
        inv_ref[0, 0, c] = inverse
        target = jnp.concatenate([(strength * growth) * kf, strength * vf], axis=1)
        solved = mm(inverse, target).astype(bf16)
        read = mm(scores, solved)
        qe_ref[0, 0, c] = (growth * qf - read[:, :DK]).astype(bf16)
        o_ref[pl.ds(c * CHUNK, CHUNK), :] = read[:, DK:]
        kept = jnp.exp(total - column) * kf
        written = mm(kept, solved, TN)
        low_n = written[:, :DK].astype(bf16)
        n_ref[0, 0, c] = low_n
        b_ref[0, 0, c] = written[:, DK:]
        whole = jnp.exp(total)
        tot_ref[0, 0, pl.ds(c, 1), :] = jnp.broadcast_to(whole, (1, DK))
        maps.append((low_n, written[:, DK:], whole))
    low_n, b, whole = maps[0]
    eye_f = eye.astype(f32)
    trans = whole * eye_f - low_n.astype(f32)
    carried = b
    for low_n, b, whole in maps[1:]:
        both = jnp.concatenate([trans, carried], axis=1)
        moved = whole * both - mm(low_n, both)
        trans = moved[:, :DK]
        carried = moved[:, DK:] + b
    map_ref[0, 0, :, 0:DK] = trans.astype(bf16)
    map_ref[0, 0, :, DK:] = carried.astype(bf16)


def state_kernel(
    place_ref, maps_ref, n_ref, b_ref, qe_ref, o_ref, tot_ref, og_ref, gain_ref,
    s_ref, mixed_ref, normed_ref,
):
    count = n_ref.shape[2]

    def lap(z, state):
        stage = maps_ref[z, 0, 0]
        return mm(stage[:, :DK], state) + stage[:, DK:].astype(f32)

    state = lax.fori_loop(0, place_ref[0], lap, jnp.zeros((DK, DV), f32))
    for c in range(count):
        low_state = state.astype(bf16)
        s_ref[0, 0, c] = low_state
        both = mm(jnp.concatenate([n_ref[0, 0, c], qe_ref[0, 0, c]], axis=0), low_state)
        whole = tot_ref[0, 0, c, 0]
        state = whole * state - both[:DK] + b_ref[0, 0, c]
        at = pl.ds(c * CHUNK, CHUNK)
        mixed = o_ref[at, :] + both[DK:]
        mixed_ref[at, :] = mixed
        og = og_ref[at, :]
        inverse = lax.rsqrt(jnp.mean(mixed * mixed, axis=1, keepdims=True) + epsilon)
        normed_ref[at, :] = (mixed * inverse * gain_ref[0:1] * (og * sigmoid(og))).astype(bf16)


def norm_grad_kernel(
    dn_ref, mixed_ref, og_ref, gain_ref, qe_ref, n_ref, tot_ref,
    do_ref, dog_ref, gg_ref, own_ref,
):
    count = n_ref.shape[2]
    gain = gain_ref[0:1]
    state = jnp.zeros((DK, DV), f32)
    total = jnp.zeros((1, DV), f32)
    for c in reversed(range(count)):
        at = pl.ds(c * CHUNK, CHUNK)
        mixed, og, dn = mixed_ref[at, :], og_ref[at, :], dn_ref[at, :]
        inverse = lax.rsqrt(jnp.mean(mixed * mixed, axis=1, keepdims=True) + epsilon)
        scaled = mixed * inverse
        sig = sigmoid(og)
        silu = og * sig
        through = dn * scaled
        total = total + jnp.sum(through * silu, axis=0, keepdims=True)
        dog_ref[at, :] = (through * gain * sig * (1.0 + og * (1.0 - sig))).astype(bf16)
        weighted = dn * gain * silu
        dmixed = inverse * (
            weighted - scaled * jnp.mean(weighted * scaled, axis=1, keepdims=True)
        )
        dmixed = dmixed.astype(bf16)
        do_ref[at, :] = dmixed
        whole = tot_ref[0, 0, c, 0]
        state = whole * state - mm(n_ref[0, 0, c], state, TN) + mm(qe_ref[0, 0, c], dmixed, TN)
    gg_ref[0, 0] = jnp.broadcast_to(total, (8, DV))
    own_ref[0, 0] = state.astype(bf16)


def rule_grad_kernel(
    place_ref, start_ref, decay_ref, owns_ref, maps_ref, qkv_ref, inv_ref, n_ref, qe_ref,
    tot_ref, s_ref, do_ref, main_ref, halo_ref, rate_ref, conv_ref,
    dci_ref, dhalo_ref, dconv_ref, drate_ref, ddecay_ref, x_scr, g_scr,
):
    head = pl.program_id(0)
    length = main_ref.shape[0]
    count = length // CHUNK
    load_conv_input(main_ref, halo_ref, start_ref, x_scr, place_ref[0])
    conv = conv_ref[...]
    rows, cols = iotas(CHUNK)
    lower, upper, eye = rows >= cols, rows <= cols, rows == cols
    strict = rows > cols
    last = owns_ref.shape[0] - 1

    def lap(i, state):
        z = last - i
        return mm(maps_ref[z, 0, 0][:, :DK], state, TN) + owns_ref[z, 0, 0].astype(f32)

    state = lax.fori_loop(0, last - place_ref[0], lap, jnp.zeros((DK, DV), f32))
    leaving = [None] * count
    for c in reversed(range(count)):
        leaving[c] = state
        at = pl.ds(c * CHUNK, CHUNK)
        state = (
            tot_ref[0, 0, c, 0] * state
            - mm(n_ref[0, 0, c], state, TN)
            + mm(qe_ref[0, 0, c], do_ref[at, :], TN)
        )
    g_scr[pl.ds(0, 8), :] = jnp.zeros((8, QKV), f32)
    g_scr[pl.ds(8 + length, 8), :] = jnp.zeros((8, QKV), f32)
    rate_total = jnp.zeros((1, 1), f32)
    bias_total = jnp.zeros((1, 1), f32)
    conv_total = [jnp.zeros((1, QKV), f32) for _ in range(CONV)]
    lanes = lax.broadcasted_iota(jnp.int32, (CHUNK, PAD), 1)
    for c in range(count):
        at = pl.ds(c * CHUNK, CHUNK)
        q, k, v = qkv_ref[at, 0:DK], qkv_ref[at, DK : 2 * DK], qkv_ref[at, 2 * DK :]
        kf, vf = k.astype(f32), v.astype(f32)
        log_gate, strength, rate, logit = gates(rate_ref[at, :], decay_ref, head)
        column, total, ratio = decays(log_gate, lower, upper, eye)
        growth = jnp.exp(column)
        remain = jnp.exp(total - column)
        whole = jnp.exp(total)
        inverse = inv_ref[0, 0, c]
        s0 = s_ref[0, 0, c]
        do = do_ref[at, :]
        grad_state = leaving[c]
        low_grad_state = grad_state.astype(bf16)
        kq = jnp.concatenate([k, q], axis=0)
        products = mm(kq, k, NT)
        kk, qk = products[:CHUNK], products[CHUNK:]
        reads = mm(kq, s0)
        ks, qs = reads[:CHUNK], reads[CHUNK:]
        fresh = vf - growth * ks
        pseudo = mm(inverse, strength * fresh).astype(bf16)
        scores = (ratio * qk).astype(bf16)
        dpseudo = mm(scores, do, TN) + mm(remain * kf, low_grad_state)
        dtarget = mm(inverse, dpseudo, TN)
        low_dtarget = dtarget.astype(bf16)
        dstrength = jnp.sum(dtarget * fresh, axis=1, keepdims=True)
        dlog = -(strength * growth) * jnp.sum(dtarget * ks, axis=1, keepdims=True)
        dv = strength * dtarget
        outer = mm(jnp.concatenate([low_dtarget, do], axis=0), pseudo, NT)
        dcoupling = jnp.where(strict, -outer[:CHUNK] * ratio, 0.0)
        by_strength = dcoupling * kk
        dstrength = dstrength + jnp.sum(by_strength, axis=1, keepdims=True)
        exponent = strength * by_strength
        dkk = (dcoupling * strength).astype(bf16)
        dqk_f = jnp.where(lower, outer[CHUNK:] * ratio, 0.0)
        exponent = exponent + dqk_f * qk
        dqk = dqk_f.astype(bf16)
        back = mm(jnp.concatenate([low_dtarget, do], axis=0), s0, NT)
        wide = mm(jnp.concatenate([dkk, dqk], axis=0), k)
        dq = growth * back[CHUNK:] + wide[CHUNK:]
        dkept = mm(pseudo, low_grad_state, NT)
        dk = (
            wide[:CHUNK]
            - (strength * growth) * back[:CHUNK]
            + mm(jnp.concatenate([dkk, dqk], axis=0), kq, TN)
            + remain * dkept
        )
        dlog = dlog + growth * jnp.sum(do.astype(f32) * qs, axis=1, keepdims=True)
        from_kept = remain * jnp.sum(kf * dkept, axis=1, keepdims=True)
        dlog = dlog - from_kept + jnp.sum(exponent, axis=1, keepdims=True)
        dlog_row = to_row(dlog, eye) - jnp.sum(exponent, axis=0, keepdims=True)
        tail = jnp.sum(from_kept, axis=0, keepdims=True) + whole * jnp.sum(
            jnp.sum(grad_state * s0.astype(f32), axis=1, keepdims=True), axis=0, keepdims=True
        )
        dgate = jnp.sum(jnp.where(upper, dlog_row, 0.0), axis=1, keepdims=True) + tail
        slope = sigmoid(logit)
        drate0 = -rate * slope * dgate
        drate1 = dstrength * strength * (1.0 - strength)
        rate_total = rate_total + jnp.sum(dgate * log_gate, axis=0, keepdims=True)
        bias_total = bias_total + jnp.sum(drate0, axis=0, keepdims=True)
        drate_ref[at, :] = jnp.where(
            lanes == 2 * head, drate0, jnp.where(lanes == 2 * head + 1, drate1, 0.0)
        )
        convolved = convolve(x_scr, conv, c * CHUNK)
        sig = sigmoid(convolved)
        active = convolved * sig
        slope_conv = sig * (1.0 + convolved * (1.0 - sig))

        def unit_grad(rows_in, grad):
            inv_norm = lax.rsqrt(jnp.sum(rows_in * rows_in, axis=1, keepdims=True) + epsilon)
            y = rows_in * inv_norm
            return inv_norm * (grad - y * jnp.sum(y * grad, axis=1, keepdims=True))

        dq = dq.astype(bf16).astype(f32) * DK ** (-0.5)
        dk = dk.astype(bf16).astype(f32)
        dv = dv.astype(bf16).astype(f32)
        dconv = (
            jnp.concatenate(
                [unit_grad(active[:, :DK], dq), unit_grad(active[:, DK : 2 * DK], dk), dv], axis=1
            )
            * slope_conv
        )
        g_scr[pl.ds(8 + c * CHUNK, CHUNK), :] = dconv
        for j in range(CONV):
            shifted_in = x_scr[pl.ds(c * CHUNK + HALO - CONV + 1 + j, CHUNK), :]
            conv_total[j] = conv_total[j] + jnp.sum(dconv * shifted_in, axis=0, keepdims=True)
    for j in range(CONV):
        dconv_ref[0, 0, pl.ds(j, 1), :] = conv_total[j]
    for c in range(count):
        grad = g_scr[pl.ds(8 + c * CHUNK + CONV - 1, CHUNK), :] * conv[0:1]
        for j in range(1, CONV):
            grad = grad + g_scr[pl.ds(8 + c * CHUNK + CONV - 1 - j, CHUNK), :] * conv[j : j + 1]
        dci_ref[pl.ds(c * CHUNK, CHUNK), :] = grad
    grad = g_scr[pl.ds(CONV - 1, 8), :] * conv[0:1]
    for j in range(1, CONV):
        grad = grad + g_scr[pl.ds(CONV - 1 - j, 8), :] * conv[j : j + 1]
    dhalo_ref[0] = grad
    row8 = lax.broadcasted_iota(jnp.int32, (8, PAD), 0)
    ddecay_ref[0, 0] = jnp.where(row8 == 0, rate_total, jnp.where(row8 == 1, bias_total, 0.0))


def params():
    return pltpu.CompilerParams(
        dimension_semantics=("arbitrary", "arbitrary"), vmem_limit_bytes=48 * 2**20
    )


def smem():
    return pl.BlockSpec(memory_space=pltpu.SMEM)


class Rule:
    def __init__(self, seqs, length, heads, places):
        self.seqs, self.length, self.heads, self.places = seqs, length, heads, places
        self.count = length // CHUNK
        self.grid = (heads, seqs)

    def per_chain(self, *dims):
        zeros = (0,) * len(dims)
        return pl.BlockSpec((1, 1) + dims, lambda h, s: (s, h) + zeros)

    def chain_shape(self, dims, kind):
        return jax.ShapeDtypeStruct((self.seqs, self.heads) + dims, kind)

    def rows(self, width, first):
        return pl.BlockSpec((self.length, width), lambda h, s: (s, first + h))

    def rates(self):
        at = self.heads * (QKV + DV) // PAD
        return pl.BlockSpec((self.length, PAD), lambda h, s: (s, at))

    def og(self):
        return self.rows(DV, self.heads * QKV // DV)

    def halo(self):
        return pl.BlockSpec((1, HALO, QKV), lambda h, s: (s, 0, h))

    def conv(self):
        return pl.BlockSpec((CONV, QKV), lambda h, s: (0, h))

    def gain(self):
        return pl.BlockSpec((1, DV), lambda h, s: (0, 0))

    def everyones(self, width):
        return pl.BlockSpec((self.places, 1, 1, DK, width), lambda h, s: (0, s, h, 0, 0))

    def row_shape(self, width, kind):
        return jax.ShapeDtypeStruct((self.seqs * self.length, self.heads * width), kind)

    def chunks(self, place, starts, decay_par, projected, halo, conv_w):
        c = self.count
        return pl.pallas_call(
            chunk_kernel,
            grid=self.grid,
            in_specs=[
                smem(), smem(), smem(), self.rows(QKV, 0), self.halo(), self.rates(), self.conv(),
            ],
            out_specs=[
                self.rows(QKV, 0), self.per_chain(c, CHUNK, CHUNK), self.per_chain(c, DK, DK),
                self.per_chain(c, DK, DV), self.per_chain(c, CHUNK, DK), self.rows(DV, 0),
                self.per_chain(c, DK), self.per_chain(DK, DK + DV),
            ],
            out_shape=[
                self.row_shape(QKV, bf16), self.chain_shape((c, CHUNK, CHUNK), bf16),
                self.chain_shape((c, DK, DK), bf16), self.chain_shape((c, DK, DV), f32),
                self.chain_shape((c, CHUNK, DK), bf16), self.row_shape(DV, f32),
                self.chain_shape((c, DK), f32), self.chain_shape((DK, DK + DV), bf16),
            ],
            scratch_shapes=[pltpu.VMEM((HALO + self.length, QKV), f32)],
            compiler_params=params(),
            name="chunk_maps",
        )(place, starts, decay_par, projected, halo, projected, conv_w)

    def states(self, place, maps, n, b, qe, o, tot, projected, gain):
        c = self.count
        return pl.pallas_call(
            state_kernel,
            grid=self.grid,
            in_specs=[
                smem(), self.everyones(DK + DV), self.per_chain(c, DK, DK),
                self.per_chain(c, DK, DV), self.per_chain(c, CHUNK, DK), self.rows(DV, 0),
                self.per_chain(c, DK), self.og(), self.gain(),
            ],
            out_specs=[self.per_chain(c, DK, DV), self.rows(DV, 0), self.rows(DV, 0)],
            out_shape=[
                self.chain_shape((c, DK, DV), bf16), self.row_shape(DV, f32),
                self.row_shape(DV, bf16),
            ],
            compiler_params=params(),
            name="states_and_norm",
        )(place, maps, n, b, qe, o, tot, projected, gain)

    def norm_grads(self, dn, mixed, projected, gain, qe, n, tot):
        c = self.count
        return pl.pallas_call(
            norm_grad_kernel,
            grid=self.grid,
            in_specs=[
                self.rows(DV, 0), self.rows(DV, 0), self.og(), self.gain(),
                self.per_chain(c, CHUNK, DK), self.per_chain(c, DK, DK), self.per_chain(c, DK),
            ],
            out_specs=[
                self.rows(DV, 0), self.rows(DV, 0), self.per_chain(8, DV), self.per_chain(DK, DV),
            ],
            out_shape=[
                self.row_shape(DV, bf16), self.row_shape(DV, bf16), self.chain_shape((8, DV), f32),
                self.chain_shape((DK, DV), bf16),
            ],
            compiler_params=params(),
            name="norm_grads",
        )(dn, mixed, projected, gain, qe, n, tot)

    def rule_grads(
        self, place, starts, decay_par, owns, maps, qkv, inv, n, qe, tot, s, do, projected, halo, conv_w
    ):
        c = self.count
        return pl.pallas_call(
            rule_grad_kernel,
            grid=self.grid,
            in_specs=[
                smem(), smem(), smem(), self.everyones(DV), self.everyones(DK + DV),
                self.rows(QKV, 0), self.per_chain(c, CHUNK, CHUNK), self.per_chain(c, DK, DK),
                self.per_chain(c, CHUNK, DK), self.per_chain(c, DK), self.per_chain(c, DK, DV),
                self.rows(DV, 0), self.rows(QKV, 0), self.halo(), self.rates(), self.conv(),
            ],
            out_specs=[
                self.rows(QKV, 0), pl.BlockSpec((1, 8, QKV), lambda h, s: (s, 0, h)),
                self.per_chain(CONV, QKV), self.rows(PAD, 0), self.per_chain(8, PAD),
            ],
            out_shape=[
                self.row_shape(QKV, f32),
                jax.ShapeDtypeStruct((self.seqs, 8, self.heads * QKV), f32),
                self.chain_shape((CONV, QKV), f32), self.row_shape(PAD, f32),
                self.chain_shape((8, PAD), f32),
            ],
            scratch_shapes=[
                pltpu.VMEM((HALO + self.length, QKV), f32),
                pltpu.VMEM((16 + self.length, QKV), f32),
            ],
            compiler_params=params(),
            name="rule_grads",
        )(
            place, starts, decay_par, owns, maps, qkv, inv, n, qe, tot, s, do, projected, halo,
            projected, conv_w,
        )


MESH = pl.DeviceIdType.MESH
SUB = 128


def head_copy(src, dst, send_sem, recv_sem, peer):
    return pltpu.make_async_remote_copy(
        src_ref=src, dst_ref=dst, send_sem=send_sem, recv_sem=recv_sem,
        device_id={"head": peer}, device_id_type=MESH,
    )


def greet_heads(me, peers):
    barrier = pltpu.get_barrier_semaphore()
    for k in range(1, peers):
        pl.semaphore_signal(barrier, inc=1, device_id={"head": me ^ k}, device_id_type=MESH)
    pl.semaphore_wait(barrier, peers - 1)


def part(ref, start, size):
    return ref.at[pl.ds(pl.multiple_of(start, size), size)]


def mixer_ffn_kernel(
    peers, normed_hbm, wout_hbm, ffn_hbm, x_hbm, ct_hbm, gain_ref,
    grads_hbm, ffnp_hbm, ng_hbm, hidden_ref, hgrad_ref, gpart_ref,
    normed_v, wout_v, ffn_v, x_v, ct_v, send1, recv1, nm, act, dgu, send2, recv2, dm, ffnp_v,
    grads_v, ng_v, in_sem, out_sem, ss1, rs1, ss2, rs2, ss3, rs3, ss4, rs4,
):
    me = lax.axis_index("head")
    total, width = ct_hbm.shape
    own_rows = total // peers
    subs = own_rows // SUB
    cells = act.shape[1]
    tile = 256
    loads = [
        pltpu.make_async_copy(normed_hbm, normed_v, in_sem.at[0]),
        pltpu.make_async_copy(wout_hbm, wout_v, in_sem.at[1]),
        pltpu.make_async_copy(part(x_hbm, me * own_rows, own_rows), x_v, in_sem.at[2]),
        pltpu.make_async_copy(ffn_hbm, ffn_v, in_sem.at[3]),
        pltpu.make_async_copy(ct_hbm, ct_v, in_sem.at[4]),
    ]
    for load in loads:
        load.start()
    greet_heads(me, peers)
    loads[0].wait()
    loads[1].wait()

    def sub_copy(k, t):
        rows = pl.ds(pl.multiple_of(t * SUB, SUB), SUB)
        return head_copy(
            send1.at[k, rows], recv1.at[k, rows], ss1.at[k, t], rs1.at[k, t], me ^ k
        )

    def project(i, carry):
        k = peers - 1 - i
        rows = pl.ds(pl.multiple_of((me ^ k) * own_rows, own_rows), own_rows)
        send1[k] = mm(normed_v[rows, :], wout_v[...], NT).astype(bf16)

        @pl.when(k > 0)
        def _():
            for t in range(subs):
                sub_copy(k, t).start()

        return carry

    lax.fori_loop(0, peers, project, 0)
    loads[2].wait()
    gain = gain_ref[...]

    def sub_gather(k, t, owner, buffer, send_sem, recv_sem):
        at = part(buffer, owner * own_rows + t * SUB, SUB)
        return head_copy(at, at, send_sem.at[k, t], recv_sem.at[k, t], me ^ k)

    def normalise(t, carry):
        rows = pl.ds(pl.multiple_of(t * SUB, SUB), SUB)
        hidden = x_v[rows, :].astype(f32) + send1[0, rows, :].astype(f32)
        for k in range(1, peers):
            sub_copy(k, t).wait_recv()
            hidden = hidden + recv1[k, rows, :].astype(f32)
        hidden_ref[rows, :] = hidden
        inverse = lax.rsqrt(jnp.mean(hidden * hidden, axis=1, keepdims=True) + epsilon)
        part(nm, me * own_rows + t * SUB, SUB)[...] = (hidden * inverse * gain).astype(bf16)
        for k in range(peers - 1, 0, -1):
            sub_gather(k, t, me, nm, ss2, rs2).start()
        return carry

    lax.fori_loop(0, subs, normalise, 0)
    loads[3].wait()
    loads[4].wait()

    def mid_copy(k, t):
        rows = pl.ds(pl.multiple_of(t * SUB, SUB), SUB)
        return head_copy(
            send2.at[k, rows], recv2.at[k, rows], ss3.at[k, t], rs3.at[k, t], me ^ k
        )

    def feed_forward(k, carry):
        owner = me ^ k

        @pl.when(k > 0)
        def _():
            for t in range(subs):
                sub_gather(k, t, owner, nm, ss2, rs2).wait_recv()

        rows = pl.ds(pl.multiple_of(owner * own_rows, own_rows), own_rows)

        def cell_tile(j, carry):
            at = pl.ds(pl.multiple_of(j * tile, tile), tile)
            at_up = pl.ds(pl.multiple_of(cells + j * tile, tile), tile)
            at_down = pl.ds(pl.multiple_of(2 * cells + j * tile, tile), tile)
            gate = mm(nm[rows, :], ffn_v[:, at])
            up = mm(nm[rows, :], ffn_v[:, at_up])
            dact = mm(ct_v[rows, :], ffn_v[:, at_down])
            sig = sigmoid(gate)
            silu = gate * sig
            act[rows, at] = (silu * up).astype(bf16)
            dgu[rows, at] = (dact * up * sig * (1.0 + gate * (1.0 - sig))).astype(bf16)
            dgu[rows, at_up] = (dact * silu).astype(bf16)
            return carry

        lax.fori_loop(0, cells // tile, cell_tile, 0)

        def mid_tile(j, carry):
            at = pl.ds(pl.multiple_of(j * tile, tile), tile)
            send2[k, :, at] = mm(dgu[rows, :], ffn_v[at, 0 : 2 * cells], NT).astype(bf16)
            return carry

        lax.fori_loop(0, width // tile, mid_tile, 0)

        @pl.when(k > 0)
        def _():
            for t in range(subs):
                mid_copy(k, t).start()

        return carry

    lax.fori_loop(0, peers, feed_forward, 0)

    def middle_grad(t, carry):
        rows = pl.ds(pl.multiple_of(t * SUB, SUB), SUB)
        dmid = send2[0, rows, :].astype(f32)
        for k in range(1, peers):
            mid_copy(k, t).wait_recv()
            dmid = dmid + recv2[k, rows, :].astype(f32)
        hidden = hidden_ref[rows, :]
        inverse = lax.rsqrt(jnp.mean(hidden * hidden, axis=1, keepdims=True) + epsilon)
        scaled = hidden * inverse
        weighted = dmid * gain
        grad = part(ct_v, me * own_rows + t * SUB, SUB)[...].astype(f32) + inverse * (
            weighted - scaled * jnp.mean(weighted * scaled, axis=1, keepdims=True)
        )
        hgrad_ref[rows, :] = grad
        part(dm, me * own_rows + t * SUB, SUB)[...] = grad.astype(bf16)
        for k in range(peers - 1, 0, -1):
            sub_gather(k, t, me, dm, ss4, rs4).start()
        return carry + jnp.sum(dmid * scaled, axis=0, keepdims=True)

    gain_part = lax.fori_loop(0, subs, middle_grad, jnp.zeros((1, width), f32))
    gpart_ref[...] = jnp.broadcast_to(gain_part, gpart_ref.shape)

    def block_store(i, size, source, target, sem):
        return pltpu.make_async_copy(
            part(source, i * size, size), part(target, i * size, size), sem.at[i]
        )

    def cell_grads(i, carry):
        at = pl.ds(pl.multiple_of(i * tile, tile), tile)
        grads_v[at, 0 : 2 * cells] = mm(nm[:, at], dgu[...], TN).astype(bf16)
        grads_v[at, 2 * cells : 3 * cells] = mm(ct_v[:, at], act[...], TN).astype(bf16)
        return carry

    lax.fori_loop(0, width // tile, cell_grads, 0)

    def ffn_rows(i, carry):
        rows = pl.ds(pl.multiple_of(i * own_rows, own_rows), own_rows)
        ffnp_v[rows, :] = mm(act[rows, :], ffn_v[:, 2 * cells :], NT).astype(bf16)
        block_store(i, own_rows, ffnp_v, ffnp_hbm, out_sem.at[0]).start()
        return carry

    lax.fori_loop(0, peers, ffn_rows, 0)

    def norm_rows(k, carry):
        owner = me ^ k

        @pl.when(k > 0)
        def _():
            for t in range(subs):
                sub_gather(k, t, owner, dm, ss4, rs4).wait_recv()

        rows = pl.ds(pl.multiple_of(owner * own_rows, own_rows), own_rows)
        ng_v[rows, :] = mm(dm[rows, :], wout_v[...])
        block_store(owner, own_rows, ng_v, ng_hbm, out_sem.at[1]).start()
        return carry

    lax.fori_loop(0, peers, norm_rows, 0)

    def out_grads(i, carry):
        at = pl.ds(pl.multiple_of(i * tile, tile), tile)
        grads_v[at, 3 * cells :] = mm(dm[:, at], normed_v[...], TN).astype(bf16)
        block_store(i, tile, grads_v, grads_hbm, out_sem.at[2]).start()
        return carry

    lax.fori_loop(0, width // tile, out_grads, 0)
    for i in range(peers):
        block_store(i, own_rows, ffnp_v, ffnp_hbm, out_sem.at[0]).wait()
        block_store(i, own_rows, ng_v, ng_hbm, out_sem.at[1]).wait()
    for i in range(width // tile):
        block_store(i, tile, grads_v, grads_hbm, out_sem.at[2]).wait()
    for k in range(1, peers):
        for t in range(subs):
            sub_copy(k, t).wait_send()
            sub_gather(k, t, me, nm, ss2, rs2).wait_send()
            mid_copy(k, t).wait_send()
            sub_gather(k, t, me, dm, ss4, rs4).wait_send()


def anywhere():
    return pl.BlockSpec(memory_space=pl.ANY)


def vmem():
    return pl.BlockSpec(memory_space=pltpu.VMEM)


def mixer_ffn(normed, out_full, ffn_full, x, ct, gain):
    peers = lax.axis_size("head")
    total, width = ct.shape
    own_rows = total // peers
    subs = own_rows // SUB
    values = normed.shape[1]
    cells = ffn_full.shape[1] // 3
    sems = pltpu.SemaphoreType.DMA((peers, subs))
    return pl.pallas_call(
        functools.partial(mixer_ffn_kernel, peers),
        in_specs=[anywhere()] * 5 + [vmem()],
        out_specs=[anywhere()] * 3 + [vmem()] * 3,
        out_shape=[
            jax.ShapeDtypeStruct((width, 3 * cells + values), bf16),
            jax.ShapeDtypeStruct((total, width), bf16),
            jax.ShapeDtypeStruct((total, values), f32),
            jax.ShapeDtypeStruct((own_rows, width), f32),
            jax.ShapeDtypeStruct((own_rows, width), f32),
            jax.ShapeDtypeStruct((8, width), f32),
        ],
        scratch_shapes=[
            pltpu.VMEM((total, values), bf16),
            pltpu.VMEM((width, values), bf16),
            pltpu.VMEM((width, 3 * cells), bf16),
            pltpu.VMEM((own_rows, width), bf16),
            pltpu.VMEM((total, width), bf16),
            pltpu.VMEM((peers, own_rows, width), bf16),
            pltpu.VMEM((peers, own_rows, width), bf16),
            pltpu.VMEM((total, width), bf16),
            pltpu.VMEM((total, cells), bf16),
            pltpu.VMEM((total, 2 * cells), bf16),
            pltpu.VMEM((peers, own_rows, width), bf16),
            pltpu.VMEM((peers, own_rows, width), bf16),
            pltpu.VMEM((total, width), bf16),
            pltpu.VMEM((total, width), bf16),
            pltpu.VMEM((width, 3 * cells + values), bf16),
            pltpu.VMEM((total, values), f32),
            pltpu.SemaphoreType.DMA((5,)),
            pltpu.SemaphoreType.DMA((3, max(peers, width // 256))),
        ]
        + [sems] * 8,
        compiler_params=pltpu.CompilerParams(
            collective_id=1, has_side_effects=True, vmem_limit_bytes=56 * 2**20
        ),
        name="mixer_ffn",
    )(normed, out_full, ffn_full, x, ct, gain)


def input_grad_kernel(
    peers, dp_hbm, win_hbm, x_hbm, hgrad_ref, gain_ref,
    out_hbm, gpart_ref,
    dp_v, win_v, x_v, send1, recv1, whole, in_sem, out_sem, ss1, rs1, ss2, rs2,
):
    me = lax.axis_index("head")
    total, width = whole.shape
    own_rows = total // peers
    subs = own_rows // SUB
    loads = [
        pltpu.make_async_copy(dp_hbm, dp_v, in_sem.at[0]),
        pltpu.make_async_copy(win_hbm, win_v, in_sem.at[1]),
        pltpu.make_async_copy(part(x_hbm, me * own_rows, own_rows), x_v, in_sem.at[2]),
    ]
    for load in loads:
        load.start()
    greet_heads(me, peers)
    loads[0].wait()
    loads[1].wait()

    def sub_copy(k, t):
        rows = pl.ds(pl.multiple_of(t * SUB, SUB), SUB)
        return head_copy(
            send1.at[k, rows], recv1.at[k, rows], ss1.at[k, t], rs1.at[k, t], me ^ k
        )

    def project(i, carry):
        k = peers - 1 - i
        rows = pl.ds(pl.multiple_of((me ^ k) * own_rows, own_rows), own_rows)
        send1[k] = mm(dp_v[rows, :], win_v[...], NT).astype(bf16)

        @pl.when(k > 0)
        def _():
            for t in range(subs):
                sub_copy(k, t).start()

        return carry

    lax.fori_loop(0, peers, project, 0)
    loads[2].wait()
    gain = gain_ref[...]

    def sub_gather(k, t, owner):
        at = part(whole, owner * own_rows + t * SUB, SUB)
        return head_copy(at, at, ss2.at[k, t], rs2.at[k, t], me ^ k)

    def input_rows(t, carry):
        rows = pl.ds(pl.multiple_of(t * SUB, SUB), SUB)
        din = send1[0, rows, :].astype(f32)
        for k in range(1, peers):
            sub_copy(k, t).wait_recv()
            din = din + recv1[k, rows, :].astype(f32)
        x = x_v[rows, :].astype(f32)
        inverse = lax.rsqrt(jnp.mean(x * x, axis=1, keepdims=True) + epsilon)
        scaled = x * inverse
        weighted = din * gain
        grad = hgrad_ref[rows, :] + inverse * (
            weighted - scaled * jnp.mean(weighted * scaled, axis=1, keepdims=True)
        )
        part(whole, me * own_rows + t * SUB, SUB)[...] = grad.astype(bf16)
        for k in range(peers - 1, 0, -1):
            sub_gather(k, t, me).start()
        return carry + jnp.sum(din * scaled, axis=0, keepdims=True)

    gain_part = lax.fori_loop(0, subs, input_rows, jnp.zeros((1, width), f32))
    gpart_ref[...] = jnp.broadcast_to(gain_part, gpart_ref.shape)

    def store(i):
        return pltpu.make_async_copy(
            part(whole, i * own_rows, own_rows), part(out_hbm, i * own_rows, own_rows),
            out_sem.at[i],
        )

    store(me).start()
    for k in range(1, peers):
        for t in range(subs):
            sub_gather(k, t, me ^ k).wait_recv()
        store(me ^ k).start()
    for k in range(peers):
        store(me ^ k).wait()
    for k in range(1, peers):
        for t in range(subs):
            sub_copy(k, t).wait_send()
            sub_gather(k, t, me).wait_send()


def input_grads(dp, in_full, x, hgrad, gain):
    peers = lax.axis_size("head")
    total, width = x.shape
    cols = dp.shape[1]
    own_rows = total // peers
    subs = own_rows // SUB
    sems = pltpu.SemaphoreType.DMA((peers, subs))
    return pl.pallas_call(
        functools.partial(input_grad_kernel, peers),
        in_specs=[anywhere()] * 3 + [vmem()] * 2,
        out_specs=[anywhere(), vmem()],
        out_shape=[
            jax.ShapeDtypeStruct((total, width), bf16),
            jax.ShapeDtypeStruct((8, width), f32),
        ],
        scratch_shapes=[
            pltpu.VMEM((total, cols), bf16),
            pltpu.VMEM((width, cols), bf16),
            pltpu.VMEM((own_rows, width), bf16),
            pltpu.VMEM((peers, own_rows, width), bf16),
            pltpu.VMEM((peers, own_rows, width), bf16),
            pltpu.VMEM((total, width), bf16),
            pltpu.SemaphoreType.DMA((3,)),
            pltpu.SemaphoreType.DMA((peers,)),
        ]
        + [sems] * 4,
        compiler_params=pltpu.CompilerParams(
            collective_id=2, has_side_effects=True, vmem_limit_bytes=48 * 2**20
        ),
        name="input_grads",
    )(dp, in_full, x, hgrad, gain)


def shifted(shard, axis, by):
    count = lax.axis_size(axis)
    pairs = [(i, i + by) for i in range(count) if 0 <= i + by < count]
    return lax.ppermute(shard, axis, pairs)


def root_scale(value_rows):
    return lax.rsqrt(jnp.mean(value_rows * value_rows, axis=-1, keepdims=True) + epsilon)


def matmul(a, b, dims=NN):
    return lax.dot_general(a, b, (dims, ((), ())), preferred_element_type=f32)


ALL = ("seq", "batch")


def per_device(
    tokens, starts, attn_gain, w_in, w_rates, conv_w, decay_par, o_gain, w_out, ffn_gain, w_gu,
    w_down, cotangent,
):
    seqs, length, width = tokens.shape
    shard, heads = w_in.shape[:2]
    shards = width // shard
    total = seqs * length
    conv_cols = heads * QKV
    value_cols = heads * DV
    in_cols = conv_cols + value_cols
    units = w_down.shape[0]
    cells = -(-units // 256) * 256
    spare = cells - units

    conv_flat = conv_w.reshape(-1)
    small = jnp.concatenate([attn_gain, ffn_gain, conv_flat, o_gain]).astype(bf16)
    packed_in = jnp.concatenate(
        [
            w_in[:, :, :QKV].reshape(shard, conv_cols),
            w_in[:, :, QKV:].reshape(shard, value_cols),
            w_rates.reshape(shard, 2 * heads),
            jnp.zeros((shard, PAD - 2 * heads), f32),
        ],
        axis=1,
    ).astype(bf16)
    packed_ffn = jnp.pad(
        jnp.stack([w_gu[:, 0], w_gu[:, 1], w_down.T], axis=1).astype(bf16),
        ((0, 0), (0, 0), (0, spare)),
    ).reshape(shard, 3 * cells)
    in_full = lax.all_gather(packed_in, ALL, axis=0, tiled=True)
    small_full = lax.all_gather(small, ALL, axis=0)
    out_full = lax.all_gather(
        w_out.reshape(value_cols, -1).T.astype(bf16), ALL, axis=0, tiled=True
    )
    ffn_full = lax.all_gather(packed_ffn, ALL, axis=0, tiled=True)
    attn_gain_f = small_full[:, :shard].reshape(1, width).astype(f32)
    ffn_gain_f = small_full[:, shard : 2 * shard].reshape(1, width).astype(f32)
    conv_end = 2 * shard + conv_flat.shape[0]
    conv_full = (
        small_full[:, 2 * shard : conv_end]
        .reshape(shards, CONV, heads, -1)
        .transpose(1, 2, 0, 3)
        .reshape(CONV, conv_cols)
        .astype(f32)
    )
    o_gain_full = small_full[:, conv_end:].reshape(1, DV).astype(f32)

    place = lax.axis_index("seq").astype(jnp.int32).reshape(1)
    rule = Rule(seqs, length, heads, lax.axis_size("seq"))

    x = tokens.reshape(total, width)
    ct = cotangent.reshape(total, width)
    inputs = x.astype(f32)
    normed_in = (inputs * root_scale(inputs) * attn_gain_f).astype(bf16)
    projected = matmul(normed_in, in_full)
    ends = projected.reshape(seqs, length, -1)[:, length - CONV + 1 :, :conv_cols]
    end_live = (
        place * length + length - CONV + 1 + jnp.arange(CONV - 1, dtype=jnp.int32)
    )[None, :] >= starts[:, None]
    received = shifted((ends * end_live.astype(f32)[:, :, None]).astype(bf16), "seq", 1)
    halo = jnp.pad(received, ((0, 0), (HALO - CONV + 1, 0), (0, 0)))
    qkv, inv, n, b, qe, o, tot, own_map = rule.chunks(
        place, starts, decay_par, projected, halo, conv_full
    )
    maps = lax.all_gather(own_map, "seq")
    states, mixed, normed = rule.states(place, maps, n, b, qe, o, tot, projected, o_gain_full)

    late_grads, ffn_part, normed_grad, hidden, hidden_grad, ffn_gain_part = mixer_ffn(
        normed, out_full, ffn_full, x, ct, ffn_gain_f
    )
    own_rows = total // lax.axis_size("head")
    ffn_out = lax.psum_scatter(ffn_part, "head", scatter_dimension=0, tiled=True)
    result = lax.all_gather(
        (hidden + ffn_out.astype(f32)).astype(bf16), "head", axis=0, tiled=True
    )
    do, dog, onorm_grads, own = rule.norm_grads(
        normed_grad, mixed, projected, o_gain_full, qe, n, tot
    )
    owns = lax.all_gather(own, "seq")
    dci, dhalo, dconv, drate, ddecay = rule.rule_grads(
        place, starts, decay_par, owns, maps, qkv, inv, n, qe, tot, states, do, projected, halo,
        conv_full,
    )
    returned = shifted(dhalo[:, 8 - CONV + 1 :], "seq", -1)
    positions = place * length + jnp.arange(length, dtype=jnp.int32)
    live = (positions[None, :] >= starts[:, None]).astype(f32)
    dci = (
        dci.reshape(seqs, length, conv_cols)
        + jnp.pad(returned, ((0, 0), (length - CONV + 1, 0), (0, 0)))
    ) * live[:, :, None]
    rate_grad = jnp.sum(drate.reshape(total, heads, PAD), axis=1)
    projected_grad = jnp.concatenate(
        [dci.reshape(total, conv_cols).astype(bf16), dog, rate_grad.astype(bf16)], axis=1
    )
    in_grad = matmul(normed_in, projected_grad, TN)
    input_grad, attn_gain_part = input_grads(
        projected_grad, in_full, x, hidden_grad, attn_gain_f
    )
    onorm_grad = jnp.sum(onorm_grads[:, :, 0], axis=(0, 1))
    decay_part = jnp.sum(ddecay[:, :, :2, 0], axis=0).T
    conv_grad = jnp.sum(dconv, axis=0).transpose(1, 0, 2)

    def scatter(grad, dim=0):
        return lax.psum_scatter(
            grad.astype(bf16), ALL, scatter_dimension=dim, tiled=True
        ).astype(f32)

    late_own = scatter(late_grads)
    in_own = scatter(in_grad)
    gains = lax.psum(
        jnp.concatenate([attn_gain_part[0], ffn_gain_part[0], onorm_grad]), ("head",) + ALL
    )
    at = lax.axis_index(ALL)
    attn_own = lax.dynamic_slice(gains, (at * shard,), (shard,))
    ffn_own = lax.dynamic_slice(gains, (width + at * shard,), (shard,))
    onorm_own = lax.dynamic_slice(gains, (2 * width + at * (DV // shards),), (DV // shards,))
    channels = lax.psum(
        jnp.concatenate([conv_grad.reshape(-1), decay_part.reshape(-1)]), ALL
    )
    conv_own = lax.dynamic_slice(
        channels[: CONV * conv_cols].reshape(CONV, heads, QKV),
        (0, 0, at * (QKV // shards)),
        (CONV, heads, QKV // shards),
    )
    in_main = jnp.concatenate(
        [
            in_own[:, :conv_cols].reshape(shard, heads, QKV),
            in_own[:, conv_cols:in_cols].reshape(shard, heads, DV),
        ],
        axis=2,
    )
    return (
        result.reshape(tokens.shape),
        input_grad.reshape(tokens.shape),
        attn_own,
        in_main,
        in_own[:, in_cols : in_cols + 2 * heads].reshape(shard, heads, 2),
        conv_own,
        channels[CONV * conv_cols :].reshape(2, heads),
        onorm_own,
        late_own[:, 3 * cells :].T.reshape(heads, DV, -1),
        ffn_own,
        late_own[:, : 2 * cells].reshape(shard, 2, cells)[:, :, :units],
        late_own[:, 2 * cells : 2 * cells + units].T,
    )


def solution(mesh):
    weights = P(ALL)
    in_specs = (
        P("batch", "seq", None),
        P("batch"),
        weights,
        P(ALL, "head", None),
        P(ALL, "head", None),
        P(None, "head", ALL),
        P(None, "head"),
        weights,
        P("head", None, ALL),
        weights,
        P(ALL, None, "head"),
        P("head", ALL),
        P("batch", "seq", None),
    )
    out_specs = (
        P("batch", "seq", None),
        P("batch", "seq", None),
        weights,
        P(ALL, "head", None),
        P(ALL, "head", None),
        P(None, "head", ALL),
        P(None, "head"),
        weights,
        P("head", None, ALL),
        weights,
        P(ALL, None, "head"),
        P("head", ALL),
    )
    return jax.shard_map(
        per_device, mesh=mesh, in_specs=in_specs, out_specs=out_specs, check_vma=False
    )
```

```python
import functools

import jax
import jax.numpy as jnp
from jax import lax
from jax.experimental import pallas as pl
from jax.experimental.pallas import tpu as pltpu
from jax.sharding import PartitionSpec as P

DK = 128
DV = 256
CONV = 4
QKV = 2 * DK + DV
CHUNK = 128
HALO = 16
PAD = 128

bf16 = jnp.bfloat16
f32 = jnp.float32
epsilon = 1e-06
NN = ((1,), (0,))
NT = ((1,), (1,))
TN = ((0,), (0,))


def mm(a, b, dims=NN):
    return lax.dot_general(
        a.astype(bf16), b.astype(bf16), (dims, ((), ())), preferred_element_type=f32
    )


def split_mm(a, b):
    a_high, b_high = a.astype(bf16), b.astype(bf16)
    a_low = (a - a_high.astype(f32)).astype(bf16)
    b_low = (b - b_high.astype(f32)).astype(bf16)
    return mm(a_high, b_high) + (mm(a_high, b_low) + mm(a_low, b_high))


def iotas(n):
    return (
        lax.broadcasted_iota(jnp.int32, (n, n), 0),
        lax.broadcasted_iota(jnp.int32, (n, n), 1),
    )


def unit_lower_inverses(mats):
    n = mats[0].shape[0]
    rows, cols = iotas(n)
    eye = (rows == cols).astype(f32)
    pair = ((rows >> 1) == (cols >> 1)) & (rows > cols)
    inverses = [eye - jnp.where(pair, a, 0.0) for a in mats]
    shift = 1
    while (1 << shift) < n:
        corner = ((rows >> (shift + 1)) == (cols >> (shift + 1))) & (
            (rows >> shift) > (cols >> shift)
        )
        firsts = [mm(jnp.where(corner, a, 0.0), x) for a, x in zip(mats, inverses)]
        inverses = [x - mm(x, y) for x, y in zip(inverses, firsts)]
        shift += 1
    residuals = [eye - x - split_mm(a, x) for a, x in zip(mats, inverses)]
    return [x + mm(x, r) for x, r in zip(inverses, residuals)]


def sigmoid(v):
    return 1.0 / (1.0 + jnp.exp(-v))


def softplus(v):
    small = jnp.exp(-jnp.abs(v))
    one_more = 1.0 + small
    gap = one_more - 1.0
    exact = gap == 0.0
    tail = jnp.where(exact, small, jnp.log(one_more) * small / jnp.where(exact, 1.0, gap))
    return jnp.maximum(v, 0.0) + tail


def to_row(column, eye):
    return jnp.sum(jnp.where(eye, column, 0.0), axis=0, keepdims=True)


def pick(block, lane):
    lanes = lax.broadcasted_iota(jnp.int32, block.shape, 1)
    return jnp.sum(jnp.where(lanes == lane, block, 0.0), axis=1, keepdims=True)


def gates(logits, decay_ref, head):
    rate = jnp.exp(jnp.full((1, 1), decay_ref[0, head], f32))
    shifted_logit = pick(logits, 2 * head) + decay_ref[1, head]
    strength = sigmoid(pick(logits, 2 * head + 1))
    log_gate = -rate * softplus(shifted_logit)
    return log_gate, strength, rate, shifted_logit


def decays(log_gate, lower, upper, eye):
    gate_row = to_row(log_gate, eye)
    column = jnp.sum(jnp.where(lower, gate_row, 0.0), axis=1, keepdims=True)
    row = jnp.sum(jnp.where(upper, log_gate, 0.0), axis=0, keepdims=True)
    ratio = jnp.where(lower, jnp.exp(jnp.where(lower, column - row, 0.0)), 0.0)
    total = jnp.sum(log_gate, axis=0, keepdims=True)
    return column, total, ratio


def load_conv_input(main_ref, halo_ref, start, x_scr, first):
    length = main_ref.shape[0]
    positions = first + lax.broadcasted_iota(jnp.int32, (length, 1), 0)
    live = (positions >= start).astype(f32)
    x_scr[pl.ds(0, HALO), :] = halo_ref[0].astype(f32)
    x_scr[pl.ds(HALO, length), :] = (main_ref[...] * live).astype(bf16).astype(f32)


def convolve(x_scr, conv, at):
    total = x_scr[pl.ds(at + HALO - CONV + 1, CHUNK), :] * conv[0:1]
    for j in range(1, CONV):
        total = total + x_scr[pl.ds(at + HALO - CONV + 1 + j, CHUNK), :] * conv[j : j + 1]
    return total


def unit(rows):
    return rows * lax.rsqrt(jnp.sum(rows * rows, axis=1, keepdims=True) + epsilon)


MESH = pl.DeviceIdType.MESH
SUB = 128


def head_copy(src, dst, send_sem, recv_sem, peer):
    return pltpu.make_async_remote_copy(
        src_ref=src, dst_ref=dst, send_sem=send_sem, recv_sem=recv_sem,
        device_id={"head": peer}, device_id_type=MESH,
    )


def greet_heads(me, peers):
    barrier = pltpu.get_barrier_semaphore()
    for k in range(1, peers):
        pl.semaphore_signal(barrier, inc=1, device_id={"head": me ^ k}, device_id_type=MESH)
    pl.semaphore_wait(barrier, peers - 1)


def part(ref, start, size):
    return ref.at[pl.ds(pl.multiple_of(start, size), size)]


def anywhere():
    return pl.BlockSpec(memory_space=pl.ANY)


def vmem():
    return pl.BlockSpec(memory_space=pltpu.VMEM)


def along(axis, source, target, send_sem, recv_sem, to):
    return pltpu.make_async_remote_copy(
        src_ref=source, dst_ref=target, send_sem=send_sem, recv_sem=recv_sem,
        device_id={axis: to}, device_id_type=MESH,
    )


def forward_kernel(
    seqs, places, start_ref, decay_ref, main_ref, halo_ref, rate_ref, conv_ref, og_ref, gain_ref,
    qkv_ref, inv_ref, n_ref, qe_ref, tot_ref, trans_ref, s_ref, mixed_ref, normed_ref,
    x_scr, b_scr, o_scr, carried_scr, send, recv, send_sem, recv_sem,
):
    step = pl.program_id(0)
    chains = n_ref.shape[0]
    count = n_ref.shape[1]
    length = main_ref.shape[0]
    place = lax.axis_index("seq")
    lag = jnp.minimum(place, chains - 1)

    @pl.when(step == 0)
    def _():
        barrier = pltpu.get_barrier_semaphore()

        @pl.when(place > 0)
        def _():
            pl.semaphore_signal(
                barrier, inc=1, device_id={"seq": place - 1}, device_id_type=MESH
            )

        @pl.when(place == 0)
        def _():
            recv[...] = jnp.zeros_like(recv)

        @pl.when(place < places - 1)
        def _():
            pl.semaphore_wait(barrier, 1)

    @pl.when(step < chains)
    def _():
        head = step // seqs
        load_conv_input(
            main_ref, halo_ref, start_ref[step % seqs], x_scr, place * length
        )
        conv = conv_ref[...]
        rows, cols = iotas(CHUNK)
        lower, upper, eye = rows >= cols, rows <= cols, rows == cols
        parts = []
        for c in range(count):
            at = c * CHUNK
            convolved = convolve(x_scr, conv, at)
            active = convolved * sigmoid(convolved)
            q = (unit(active[:, :DK]) * DK ** (-0.5)).astype(bf16)
            k = unit(active[:, DK : 2 * DK]).astype(bf16)
            v = active[:, 2 * DK :].astype(bf16)
            qkv_ref[pl.ds(at, CHUNK), 0:DK] = q
            qkv_ref[pl.ds(at, CHUNK), DK : 2 * DK] = k
            qkv_ref[pl.ds(at, CHUNK), 2 * DK :] = v
            log_gate, strength, _, _ = gates(rate_ref[pl.ds(at, CHUNK), :], decay_ref, head)
            column, total, ratio = decays(log_gate, lower, upper, eye)
            products = mm(jnp.concatenate([k, q], axis=0), k, NT)
            coupling = jnp.where(rows > cols, strength * ratio * products[:CHUNK], 0.0)
            scores = (ratio * products[CHUNK:]).astype(bf16)
            parts.append((q, k, v, strength, column, total, coupling, scores))
        inverses = unit_lower_inverses([p[6] for p in parts])
        maps = []
        for c in range(count):
            q, k, v, strength, column, total, _, scores = parts[c]
            growth = jnp.exp(column)
            kf, vf, qf = k.astype(f32), v.astype(f32), q.astype(f32)
            inverse = inverses[c].astype(bf16)
            inv_ref[0, c] = inverse
            target = jnp.concatenate([(strength * growth) * kf, strength * vf], axis=1)
            solved = mm(inverse, target).astype(bf16)
            read = mm(scores, solved)
            qe_ref[step, c] = (growth * qf - read[:, :DK]).astype(bf16)
            o_scr[step, pl.ds(c * CHUNK, CHUNK), :] = read[:, DK:]
            written = mm(jnp.exp(total - column) * kf, solved, TN)
            low_n = written[:, :DK].astype(bf16)
            n_ref[step, c] = low_n
            b_scr[step, c] = written[:, DK:]
            whole = jnp.exp(total)
            tot_ref[step, pl.ds(c, 1), :] = jnp.broadcast_to(whole, (1, DK))
            maps.append((low_n, written[:, DK:], whole))
        low_n, b, whole = maps[0]
        trans = whole * eye.astype(f32) - low_n.astype(f32)
        carried = b
        for low_n, b, whole in maps[1:]:
            both = jnp.concatenate([trans, carried], axis=1)
            moved = whole * both - mm(low_n, both)
            trans = moved[:, :DK]
            carried = moved[:, DK:] + b
        trans_ref[step] = trans.astype(bf16)
        carried_scr[step] = carried

    @pl.when(step >= chains)
    def _():
        chain = jnp.maximum(step - chains, 0)
        state = recv[chain].astype(f32)
        for c in range(count):
            low_state = state.astype(bf16)
            s_ref[0, c] = low_state
            both = mm(jnp.concatenate([n_ref[chain, c], qe_ref[chain, c]], axis=0), low_state)
            whole = tot_ref[chain, pl.ds(c, 1), 0:1]
            state = whole * state - both[:DK] + b_scr[chain, c]
            at = pl.ds(c * CHUNK, CHUNK)
            mixed = o_scr[chain, at, :] + both[DK:]
            mixed_ref[at, :] = mixed
            og = og_ref[at, :]
            inverse = lax.rsqrt(jnp.mean(mixed * mixed, axis=1, keepdims=True) + epsilon)
            normed_ref[at, :] = (
                mixed * inverse * gain_ref[0:1] * (og * sigmoid(og))
            ).astype(bf16)

    def passed(chain):
        return along(
            "seq", send.at[chain], recv.at[chain], send_sem.at[chain], recv_sem.at[chain],
            jnp.minimum(place + 1, places - 1),
        )

    relayed = step - lag

    @pl.when((relayed >= 0) & (relayed < chains))
    def _():
        chain = jnp.clip(relayed, 0, chains - 1)

        @pl.when(place > 0)
        def _():
            passed(chain).wait_recv()

        @pl.when(place < places - 1)
        def _():
            leaving = mm(trans_ref[chain], recv[chain]) + carried_scr[chain]
            send[chain] = leaving.astype(bf16)
            passed(chain).start()

    @pl.when((step == 2 * chains - 1) & (place < places - 1))
    def _():
        for chain in range(chains):
            passed(chain).wait_send()


def early(chains, make):
    return lambda j: make(jnp.minimum(j, chains - 1))


def late(chains, make):
    return lambda j: make(jnp.maximum(j - chains, 0))


def forward_rule(starts, decay_par, projected, halo, conv_w, gain, seqs, heads):
    places = lax.axis_size("seq")
    chains = seqs * heads
    length = projected.shape[0] // seqs
    count = length // CHUNK
    rates_at = heads * (QKV + DV) // PAD
    og_at = heads * QKV // DV
    row = lambda first: lambda i: (i % seqs, first + i // seqs)
    whole = lambda *dims: pl.BlockSpec(dims, lambda j: (0,) * len(dims))
    shape = jax.ShapeDtypeStruct
    return pl.pallas_call(
        functools.partial(forward_kernel, seqs, places),
        grid=(2 * chains,),
        in_specs=[
            smem(),
            smem(),
            pl.BlockSpec((length, QKV), early(chains, row(0))),
            pl.BlockSpec((1, HALO, QKV), early(chains, lambda i: (i % seqs, 0, i // seqs))),
            pl.BlockSpec((length, PAD), early(chains, lambda i: (i % seqs, rates_at))),
            pl.BlockSpec((CONV, QKV), early(chains, lambda i: (0, i // seqs))),
            pl.BlockSpec((length, DV), late(chains, row(og_at))),
            whole(1, DV),
        ],
        out_specs=[
            pl.BlockSpec((length, QKV), early(chains, row(0))),
            pl.BlockSpec((1, count, CHUNK, CHUNK), early(chains, lambda i: (i, 0, 0, 0))),
            whole(chains, count, DK, DK),
            whole(chains, count, CHUNK, DK),
            whole(chains, count, DK),
            whole(chains, DK, DK),
            pl.BlockSpec((1, count, DK, DV), late(chains, lambda i: (i, 0, 0, 0))),
            pl.BlockSpec((length, DV), late(chains, row(0))),
            pl.BlockSpec((length, DV), late(chains, row(0))),
        ],
        out_shape=[
            shape((seqs * length, heads * QKV), bf16),
            shape((chains, count, CHUNK, CHUNK), bf16),
            shape((chains, count, DK, DK), bf16),
            shape((chains, count, CHUNK, DK), bf16),
            shape((chains, count, DK), f32),
            shape((chains, DK, DK), bf16),
            shape((chains, count, DK, DV), bf16),
            shape((seqs * length, heads * DV), f32),
            shape((seqs * length, heads * DV), bf16),
        ],
        scratch_shapes=[
            pltpu.VMEM((HALO + length, QKV), f32),
            pltpu.VMEM((chains, count, DK, DV), f32),
            pltpu.VMEM((chains, length, DV), f32),
            pltpu.VMEM((chains, DK, DV), f32),
            pltpu.VMEM((chains, DK, DV), bf16),
            pltpu.VMEM((chains, DK, DV), bf16),
            pltpu.SemaphoreType.DMA((chains,)),
            pltpu.SemaphoreType.DMA((chains,)),
        ],
        compiler_params=pltpu.CompilerParams(
            dimension_semantics=("arbitrary",), collective_id=3, has_side_effects=True,
            vmem_limit_bytes=48 * 2**20,
        ),
        name="forward_rule",
    )(starts, decay_par, projected, halo, projected, conv_w, projected, gain)


def backward_kernel(
    seqs, places, peers, start_ref, decay_ref,
    dn_ref, mixed_ref, og_ref, gain_ref, n_ref, qe_ref, tot_ref, trans_ref,
    qkv_ref, inv_ref, s_ref, main_ref, halo_ref, rate_ref, conv_ref, hidden_ref, ffnp_hbm,
    dp_ref, dconv_ref, ddecay_ref, gg_ref, out_hbm,
    x_scr, g_scr, do_scr, own_scr, send, recv, tail_scr, halo_send, halo_recv,
    parts, whole_out, send_sem, recv_sem, halo_send_sem, halo_recv_sem, own_sem, out_sem,
    ss1, rs1, ss2, rs2,
):
    step = pl.program_id(0)
    chains = n_ref.shape[0]
    count = n_ref.shape[1]
    length = main_ref.shape[0]
    heads = chains // seqs
    conv_cols = heads * QKV
    in_cols = conv_cols + heads * DV
    place = lax.axis_index("seq")
    lag = jnp.minimum(places - 1 - place, chains - 1)
    me = lax.axis_index("head")
    own_rows = hidden_ref.shape[0]
    subs = own_rows // SUB

    def ffn_copy(k):
        return head_copy(
            part(ffnp_hbm, (me ^ k) * own_rows, own_rows), parts.at[k], ss1.at[k], rs1.at[k],
            me ^ k,
        )

    def own_copy():
        return pltpu.make_async_copy(
            part(ffnp_hbm, me * own_rows, own_rows), parts.at[0], own_sem.at[0]
        )

    def out_copy(k, owner):
        at = part(whole_out, owner * own_rows, own_rows)
        return head_copy(at, at, ss2.at[k], rs2.at[k], me ^ k)

    def out_store(k):
        owner = me ^ k
        return pltpu.make_async_copy(
            part(whole_out, owner * own_rows, own_rows), part(out_hbm, owner * own_rows, own_rows),
            out_sem.at[k],
        )

    def passed(chain):
        return along(
            "seq", send.at[chain], recv.at[chain], send_sem.at[chain], recv_sem.at[chain],
            jnp.maximum(place - 1, 0),
        )

    def returned(chain):
        return along(
            "seq", halo_send.at[chain], halo_recv.at[chain], halo_send_sem.at[chain],
            halo_recv_sem.at[chain], jnp.maximum(place - 1, 0),
        )

    @pl.when(step == 0)
    def _():
        barrier = pltpu.get_barrier_semaphore()
        for k in range(1, peers):
            pl.semaphore_signal(barrier, inc=1, device_id={"head": me ^ k}, device_id_type=MESH)

        @pl.when(place < places - 1)
        def _():
            pl.semaphore_signal(
                barrier, inc=1, device_id={"seq": place + 1}, device_id_type=MESH
            )

        @pl.when(place == places - 1)
        def _():
            recv[...] = jnp.zeros_like(recv)
            halo_recv[...] = jnp.zeros_like(halo_recv)

        @pl.when(place > 0)
        def _():
            pl.semaphore_wait(barrier, peers)

        @pl.when(place == 0)
        def _():
            pl.semaphore_wait(barrier, peers - 1)

        own_copy().start()
        for k in range(peers - 1, 0, -1):
            ffn_copy(k).start()

    @pl.when(step < chains)
    def _():
        gain = gain_ref[0:1]
        first = (step % seqs) * length
        og_at = pl.ds(pl.multiple_of(conv_cols + (step // seqs) * DV, DV), DV)
        state = jnp.zeros((DK, DV), f32)
        total = jnp.zeros((1, DV), f32)
        for c in reversed(range(count)):
            at = pl.ds(c * CHUNK, CHUNK)
            mixed, og, dn = mixed_ref[at, :], og_ref[at, :], dn_ref[at, :]
            inverse = lax.rsqrt(jnp.mean(mixed * mixed, axis=1, keepdims=True) + epsilon)
            scaled = mixed * inverse
            sig = sigmoid(og)
            silu = og * sig
            through = dn * scaled
            total = total + jnp.sum(through * silu, axis=0, keepdims=True)
            dp_ref[pl.ds(pl.multiple_of(first + c * CHUNK, CHUNK), CHUNK), og_at] = (
                through * gain * sig * (1.0 + og * (1.0 - sig))
            ).astype(bf16)
            weighted = dn * gain * silu
            dmixed = inverse * (
                weighted - scaled * jnp.mean(weighted * scaled, axis=1, keepdims=True)
            )
            dmixed = dmixed.astype(bf16)
            do_scr[step, at, :] = dmixed
            decay = tot_ref[step, pl.ds(c, 1), 0:1]
            state = (
                decay * state - mm(n_ref[step, c], state, TN) + mm(qe_ref[step, c], dmixed, TN)
            )
        gg_ref[0] = jnp.broadcast_to(total, (8, DV))
        own_scr[step] = state

    @pl.when(step >= chains)
    def _():
        chain = jnp.maximum(step - chains, 0)
        head, seq = chain // seqs, chain % seqs
        first = seq * length
        start = start_ref[seq]
        load_conv_input(main_ref, halo_ref, start, x_scr, place * length)
        conv = conv_ref[...]
        rows, cols = iotas(CHUNK)
        lower, upper, eye = rows >= cols, rows <= cols, rows == cols
        strict = rows > cols
        state = recv[chain].astype(f32)
        leaving = [None] * count
        for c in reversed(range(count)):
            leaving[c] = state
            state = (
                tot_ref[chain, pl.ds(c, 1), 0:1] * state
                - mm(n_ref[chain, c], state, TN)
                + mm(qe_ref[chain, c], do_scr[chain, pl.ds(c * CHUNK, CHUNK), :], TN)
            )
        g_scr[pl.ds(0, 8), :] = jnp.zeros((8, QKV), f32)
        g_scr[pl.ds(8 + length, 8), :] = jnp.zeros((8, QKV), f32)
        rate_total = jnp.zeros((1, 1), f32)
        bias_total = jnp.zeros((1, 1), f32)
        conv_total = [jnp.zeros((1, QKV), f32) for _ in range(CONV)]
        lanes = lax.broadcasted_iota(jnp.int32, (CHUNK, PAD), 1)
        for c in range(count):
            at = pl.ds(c * CHUNK, CHUNK)
            q, k, v = qkv_ref[at, 0:DK], qkv_ref[at, DK : 2 * DK], qkv_ref[at, 2 * DK :]
            kf, vf = k.astype(f32), v.astype(f32)
            log_gate, strength, rate, logit = gates(rate_ref[at, :], decay_ref, head)
            column, total, ratio = decays(log_gate, lower, upper, eye)
            growth = jnp.exp(column)
            remain = jnp.exp(total - column)
            whole = jnp.exp(total)
            inverse = inv_ref[0, c]
            s0 = s_ref[0, c]
            do = do_scr[chain, at, :]
            grad_state = leaving[c]
            low_grad_state = grad_state.astype(bf16)
            kq = jnp.concatenate([k, q], axis=0)
            products = mm(kq, k, NT)
            kk, qk = products[:CHUNK], products[CHUNK:]
            reads = mm(kq, s0)
            ks, qs = reads[:CHUNK], reads[CHUNK:]
            fresh = vf - growth * ks
            pseudo = mm(inverse, strength * fresh).astype(bf16)
            scores = (ratio * qk).astype(bf16)
            dpseudo = mm(scores, do, TN) + mm(remain * kf, low_grad_state)
            dtarget = mm(inverse, dpseudo, TN)
            low_dtarget = dtarget.astype(bf16)
            dstrength = jnp.sum(dtarget * fresh, axis=1, keepdims=True)
            dlog = -(strength * growth) * jnp.sum(dtarget * ks, axis=1, keepdims=True)
            dv = strength * dtarget
            both = jnp.concatenate([low_dtarget, do], axis=0)
            outer = mm(both, pseudo, NT)
            dcoupling = jnp.where(strict, -outer[:CHUNK] * ratio, 0.0)
            by_strength = dcoupling * kk
            dstrength = dstrength + jnp.sum(by_strength, axis=1, keepdims=True)
            exponent = strength * by_strength
            dqk_f = jnp.where(lower, outer[CHUNK:] * ratio, 0.0)
            exponent = exponent + dqk_f * qk
            pair = jnp.concatenate([(dcoupling * strength).astype(bf16), dqk_f.astype(bf16)], axis=0)
            back = mm(both, s0, NT)
            wide = mm(pair, k)
            dq = growth * back[CHUNK:] + wide[CHUNK:]
            dkept = mm(pseudo, low_grad_state, NT)
            dk = (
                wide[:CHUNK]
                - (strength * growth) * back[:CHUNK]
                + mm(pair, kq, TN)
                + remain * dkept
            )
            dlog = dlog + growth * jnp.sum(do.astype(f32) * qs, axis=1, keepdims=True)
            from_kept = remain * jnp.sum(kf * dkept, axis=1, keepdims=True)
            dlog = dlog - from_kept + jnp.sum(exponent, axis=1, keepdims=True)
            dlog_row = to_row(dlog, eye) - jnp.sum(exponent, axis=0, keepdims=True)
            tail = jnp.sum(from_kept, axis=0, keepdims=True) + whole * jnp.sum(
                jnp.sum(grad_state * s0.astype(f32), axis=1, keepdims=True), axis=0, keepdims=True
            )
            dgate = jnp.sum(jnp.where(upper, dlog_row, 0.0), axis=1, keepdims=True) + tail
            slope = sigmoid(logit)
            drate0 = -rate * slope * dgate
            drate1 = dstrength * strength * (1.0 - strength)
            rate_total = rate_total + jnp.sum(dgate * log_gate, axis=0, keepdims=True)
            bias_total = bias_total + jnp.sum(drate0, axis=0, keepdims=True)
            here = pl.ds(pl.multiple_of(first + c * CHUNK, CHUNK), CHUNK)
            others = jnp.where(head == 0, 0.0, dp_ref[here, in_cols:].astype(f32))
            dp_ref[here, in_cols:] = jnp.where(
                lanes == 2 * head, drate0, jnp.where(lanes == 2 * head + 1, drate1, others)
            ).astype(bf16)
            convolved = convolve(x_scr, conv, c * CHUNK)
            sig = sigmoid(convolved)
            active = convolved * sig
            slope_conv = sig * (1.0 + convolved * (1.0 - sig))

            def unit_grad(rows_in, grad):
                inv_norm = lax.rsqrt(jnp.sum(rows_in * rows_in, axis=1, keepdims=True) + epsilon)
                y = rows_in * inv_norm
                return inv_norm * (grad - y * jnp.sum(y * grad, axis=1, keepdims=True))

            dq = dq.astype(bf16).astype(f32) * DK ** (-0.5)
            dk = dk.astype(bf16).astype(f32)
            dv = dv.astype(bf16).astype(f32)
            dconv = (
                jnp.concatenate(
                    [unit_grad(active[:, :DK], dq), unit_grad(active[:, DK : 2 * DK], dk), dv],
                    axis=1,
                )
                * slope_conv
            )
            g_scr[pl.ds(8 + c * CHUNK, CHUNK), :] = dconv
            for j in range(CONV):
                shifted_in = x_scr[pl.ds(c * CHUNK + HALO - CONV + 1 + j, CHUNK), :]
                conv_total[j] = conv_total[j] + jnp.sum(dconv * shifted_in, axis=0, keepdims=True)
        for j in range(CONV):
            dconv_ref[0, pl.ds(j, 1), :] = conv_total[j]
        row8 = lax.broadcasted_iota(jnp.int32, (8, PAD), 0)
        ddecay_ref[0] = jnp.where(row8 == 0, rate_total, jnp.where(row8 == 1, bias_total, 0.0))

        def conv_back(at, size):
            grad = g_scr[pl.ds(at + CONV - 1, size), :] * conv[0:1]
            for j in range(1, CONV):
                grad = grad + g_scr[pl.ds(at + CONV - 1 - j, size), :] * conv[j : j + 1]
            return grad

        halo_send[chain] = conv_back(0, 8)

        @pl.when(place > 0)
        def _():
            returned(chain).start()

        conv_at = pl.ds(pl.multiple_of(head * QKV, QKV), QKV)
        for c in range(count):
            grad = conv_back(8 + c * CHUNK, CHUNK)
            positions = place * length + c * CHUNK + lax.broadcasted_iota(
                jnp.int32, (CHUNK, 1), 0
            )
            live = (positions >= start).astype(f32)
            if c == count - 1:
                tail_scr[chain] = grad[CHUNK - HALO :]
            dp_ref[pl.ds(pl.multiple_of(first + c * CHUNK, CHUNK), CHUNK), conv_at] = (
                grad * live
            ).astype(bf16)

    relayed = step - lag

    @pl.when((relayed >= 0) & (relayed < chains))
    def _():
        chain = jnp.clip(relayed, 0, chains - 1)

        @pl.when(place < places - 1)
        def _():
            passed(chain).wait_recv()

        @pl.when(place > 0)
        def _():
            earlier = mm(trans_ref[chain], recv[chain], TN) + own_scr[chain]
            send[chain] = earlier.astype(bf16)
            passed(chain).start()

    @pl.when(step == chains)
    def _():
        own_copy().wait()
        for k in range(1, peers):
            ffn_copy(k).wait_recv()

        def out_rows(t, carry):
            rows = pl.ds(pl.multiple_of(t * SUB, SUB), SUB)
            value = hidden_ref[rows, :]
            for k in range(peers):
                value = value + parts[k, rows, :].astype(f32)
            part(whole_out, me * own_rows + t * SUB, SUB)[...] = value.astype(bf16)
            return carry

        lax.fori_loop(0, subs, out_rows, 0)
        for k in range(peers - 1, 0, -1):
            out_copy(k, me).start()
        out_store(0).start()

    @pl.when(step == 2 * chains - 1)
    def _():
        for chain in range(chains):
            @pl.when(place < places - 1)
            def _():
                returned(chain).wait_recv()

            head, seq = chain // seqs, chain % seqs
            positions = (place + 1) * length - HALO + lax.broadcasted_iota(
                jnp.int32, (HALO, 1), 0
            )
            live = (positions >= start_ref[seq]).astype(f32)
            grad = tail_scr[chain] + jnp.concatenate(
                [jnp.zeros((HALO - 8, QKV), f32), halo_recv[chain]], axis=0
            )
            dp_ref[pl.ds((seq + 1) * length - HALO, HALO), pl.ds(head * QKV, QKV)] = (
                grad * live
            ).astype(bf16)

            @pl.when(place > 0)
            def _():
                returned(chain).wait_send()
                passed(chain).wait_send()

        for k in range(1, peers):
            out_copy(k, me ^ k).wait_recv()
            out_store(k).start()
        for k in range(peers):
            out_store(k).wait()
        for k in range(1, peers):
            ffn_copy(k).wait_send()
            out_copy(k, me).wait_send()


def backward_rule(
    starts, decay_par, dn, mixed, projected, gain, n, qe, tot, trans, qkv, inv, states, halo, conv_w,
    hidden, ffn_part, seqs, heads,
):
    places, peers = lax.axis_size("seq"), lax.axis_size("head")
    chains = seqs * heads
    rows = projected.shape[0]
    length = rows // seqs
    count = length // CHUNK
    width = hidden.shape[1]
    own_rows = hidden.shape[0]
    rates_at = heads * (QKV + DV) // PAD
    og_at = heads * QKV // DV
    row = lambda first: lambda i: (i % seqs, first + i // seqs)
    whole = lambda *dims: pl.BlockSpec(dims, lambda j: (0,) * len(dims))
    chain4 = lambda i: (i, 0, 0, 0)
    chain3 = lambda i: (i, 0, 0)
    shape = jax.ShapeDtypeStruct
    per_chain = pltpu.SemaphoreType.DMA((chains,))
    per_peer = pltpu.SemaphoreType.DMA((peers,))
    return pl.pallas_call(
        functools.partial(backward_kernel, seqs, places, peers),
        grid=(2 * chains,),
        in_specs=[
            smem(),
            smem(),
            pl.BlockSpec((length, DV), early(chains, row(0))),
            pl.BlockSpec((length, DV), early(chains, row(0))),
            pl.BlockSpec((length, DV), early(chains, row(og_at))),
            whole(1, DV),
            whole(chains, count, DK, DK),
            whole(chains, count, CHUNK, DK),
            whole(chains, count, DK),
            whole(chains, DK, DK),
            pl.BlockSpec((length, QKV), late(chains, row(0))),
            pl.BlockSpec((1, count, CHUNK, CHUNK), late(chains, chain4)),
            pl.BlockSpec((1, count, DK, DV), late(chains, chain4)),
            pl.BlockSpec((length, QKV), late(chains, row(0))),
            pl.BlockSpec((1, HALO, QKV), late(chains, lambda i: (i % seqs, 0, i // seqs))),
            pl.BlockSpec((length, PAD), late(chains, lambda i: (i % seqs, rates_at))),
            pl.BlockSpec((CONV, QKV), late(chains, lambda i: (0, i // seqs))),
            whole(own_rows, width),
            anywhere(),
        ],
        out_specs=[
            whole(rows, heads * (QKV + DV) + PAD),
            pl.BlockSpec((1, CONV, QKV), late(chains, chain3)),
            pl.BlockSpec((1, 8, PAD), late(chains, chain3)),
            pl.BlockSpec((1, 8, DV), early(chains, chain3)),
            anywhere(),
        ],
        out_shape=[
            shape((rows, heads * (QKV + DV) + PAD), bf16),
            shape((chains, CONV, QKV), f32),
            shape((chains, 8, PAD), f32),
            shape((chains, 8, DV), f32),
            shape((rows, width), bf16),
        ],
        scratch_shapes=[
            pltpu.VMEM((HALO + length, QKV), f32),
            pltpu.VMEM((16 + length, QKV), f32),
            pltpu.VMEM((chains, length, DV), bf16),
            pltpu.VMEM((chains, DK, DV), f32),
            pltpu.VMEM((chains, DK, DV), bf16),
            pltpu.VMEM((chains, DK, DV), bf16),
            pltpu.VMEM((chains, HALO, QKV), f32),
            pltpu.VMEM((chains, 8, QKV), f32),
            pltpu.VMEM((chains, 8, QKV), f32),
            pltpu.VMEM((peers, own_rows, width), bf16),
            pltpu.VMEM((rows, width), bf16),
            per_chain, per_chain, per_chain, per_chain,
            pltpu.SemaphoreType.DMA((1,)),
            per_peer, per_peer, per_peer, per_peer, per_peer,
        ],
        compiler_params=pltpu.CompilerParams(
            dimension_semantics=("arbitrary",), collective_id=4, has_side_effects=True,
            vmem_limit_bytes=52 * 2**20,
        ),
        name="backward_rule",
    )(
        starts, decay_par, dn, mixed, projected, gain, n, qe, tot, trans, qkv, inv, states, projected,
        halo, projected, conv_w, hidden, ffn_part,
    )


def smem():
    return pl.BlockSpec(memory_space=pltpu.SMEM)


def mixer_ffn_kernel(
    peers, normed_hbm, wout_hbm, ffn_hbm, x_hbm, ct_hbm, gain_ref,
    grads_hbm, ffnp_hbm, ng_hbm, hidden_ref, hgrad_ref, gpart_ref,
    normed_v, wout_v, ffn_v, x_v, ct_v, send1, recv1, nm, act, dgu, send2, recv2, dm, ffnp_v,
    grads_v, ng_v, in_sem, out_sem, ss1, rs1, ss2, rs2, ss3, rs3, ss4, rs4,
):
    me = lax.axis_index("head")
    total, width = ct_hbm.shape
    own_rows = total // peers
    subs = own_rows // SUB
    cells = act.shape[1]
    tile = 256
    loads = [
        pltpu.make_async_copy(normed_hbm, normed_v, in_sem.at[0]),
        pltpu.make_async_copy(wout_hbm, wout_v, in_sem.at[1]),
        pltpu.make_async_copy(part(x_hbm, me * own_rows, own_rows), x_v, in_sem.at[2]),
        pltpu.make_async_copy(ffn_hbm, ffn_v, in_sem.at[3]),
        pltpu.make_async_copy(ct_hbm, ct_v, in_sem.at[4]),
    ]
    for load in loads:
        load.start()
    greet_heads(me, peers)
    loads[0].wait()
    loads[1].wait()

    def sub_copy(k, t):
        rows = pl.ds(pl.multiple_of(t * SUB, SUB), SUB)
        return head_copy(
            send1.at[k, rows], recv1.at[k, rows], ss1.at[k, t], rs1.at[k, t], me ^ k
        )

    def project(i, carry):
        k = peers - 1 - i
        rows = pl.ds(pl.multiple_of((me ^ k) * own_rows, own_rows), own_rows)
        send1[k] = mm(normed_v[rows, :], wout_v[...], NT).astype(bf16)

        @pl.when(k > 0)
        def _():
            for t in range(subs):
                sub_copy(k, t).start()

        return carry

    lax.fori_loop(0, peers, project, 0)
    loads[2].wait()
    gain = gain_ref[...]

    def sub_gather(k, t, owner, buffer, send_sem, recv_sem):
        at = part(buffer, owner * own_rows + t * SUB, SUB)
        return head_copy(at, at, send_sem.at[k, t], recv_sem.at[k, t], me ^ k)

    def normalise(t, carry):
        rows = pl.ds(pl.multiple_of(t * SUB, SUB), SUB)
        hidden = x_v[rows, :].astype(f32) + send1[0, rows, :].astype(f32)
        for k in range(1, peers):
            sub_copy(k, t).wait_recv()
            hidden = hidden + recv1[k, rows, :].astype(f32)
        hidden_ref[rows, :] = hidden
        inverse = lax.rsqrt(jnp.mean(hidden * hidden, axis=1, keepdims=True) + epsilon)
        part(nm, me * own_rows + t * SUB, SUB)[...] = (hidden * inverse * gain).astype(bf16)
        for k in range(peers - 1, 0, -1):
            sub_gather(k, t, me, nm, ss2, rs2).start()
        return carry

    lax.fori_loop(0, subs, normalise, 0)
    loads[3].wait()
    loads[4].wait()

    def mid_copy(k, t):
        rows = pl.ds(pl.multiple_of(t * SUB, SUB), SUB)
        return head_copy(
            send2.at[k, rows], recv2.at[k, rows], ss3.at[k, t], rs3.at[k, t], me ^ k
        )

    def feed_forward(k, carry):
        owner = me ^ k

        @pl.when(k > 0)
        def _():
            for t in range(subs):
                sub_gather(k, t, owner, nm, ss2, rs2).wait_recv()

        rows = pl.ds(pl.multiple_of(owner * own_rows, own_rows), own_rows)

        def cell_tile(j, carry):
            at = pl.ds(pl.multiple_of(j * tile, tile), tile)
            at_up = pl.ds(pl.multiple_of(cells + j * tile, tile), tile)
            at_down = pl.ds(pl.multiple_of(2 * cells + j * tile, tile), tile)
            gate = mm(nm[rows, :], ffn_v[:, at])
            up = mm(nm[rows, :], ffn_v[:, at_up])
            dact = mm(ct_v[rows, :], ffn_v[:, at_down])
            sig = sigmoid(gate)
            silu = gate * sig
            act[rows, at] = (silu * up).astype(bf16)
            dgu[rows, at] = (dact * up * sig * (1.0 + gate * (1.0 - sig))).astype(bf16)
            dgu[rows, at_up] = (dact * silu).astype(bf16)
            return carry

        lax.fori_loop(0, cells // tile, cell_tile, 0)

        def mid_tile(j, carry):
            at = pl.ds(pl.multiple_of(j * tile, tile), tile)
            send2[k, :, at] = mm(dgu[rows, :], ffn_v[at, 0 : 2 * cells], NT).astype(bf16)
            return carry

        lax.fori_loop(0, width // tile, mid_tile, 0)

        @pl.when(k > 0)
        def _():
            for t in range(subs):
                mid_copy(k, t).start()

        return carry

    lax.fori_loop(0, peers, feed_forward, 0)

    def middle_grad(t, carry):
        rows = pl.ds(pl.multiple_of(t * SUB, SUB), SUB)
        dmid = send2[0, rows, :].astype(f32)
        for k in range(1, peers):
            mid_copy(k, t).wait_recv()
            dmid = dmid + recv2[k, rows, :].astype(f32)
        hidden = hidden_ref[rows, :]
        inverse = lax.rsqrt(jnp.mean(hidden * hidden, axis=1, keepdims=True) + epsilon)
        scaled = hidden * inverse
        weighted = dmid * gain
        grad = part(ct_v, me * own_rows + t * SUB, SUB)[...].astype(f32) + inverse * (
            weighted - scaled * jnp.mean(weighted * scaled, axis=1, keepdims=True)
        )
        hgrad_ref[rows, :] = grad
        part(dm, me * own_rows + t * SUB, SUB)[...] = grad.astype(bf16)
        for k in range(peers - 1, 0, -1):
            sub_gather(k, t, me, dm, ss4, rs4).start()
        return carry + jnp.sum(dmid * scaled, axis=0, keepdims=True)

    gain_part = lax.fori_loop(0, subs, middle_grad, jnp.zeros((1, width), f32))
    gpart_ref[...] = jnp.broadcast_to(gain_part, gpart_ref.shape)

    def block_store(i, size, source, target, sem):
        return pltpu.make_async_copy(
            part(source, i * size, size), part(target, i * size, size), sem.at[i]
        )

    def cell_grads(i, carry):
        at = pl.ds(pl.multiple_of(i * tile, tile), tile)
        grads_v[at, 0 : 2 * cells] = mm(nm[:, at], dgu[...], TN).astype(bf16)
        grads_v[at, 2 * cells : 3 * cells] = mm(ct_v[:, at], act[...], TN).astype(bf16)
        return carry

    lax.fori_loop(0, width // tile, cell_grads, 0)

    def ffn_rows(i, carry):
        rows = pl.ds(pl.multiple_of(i * own_rows, own_rows), own_rows)
        ffnp_v[rows, :] = mm(act[rows, :], ffn_v[:, 2 * cells :], NT).astype(bf16)
        block_store(i, own_rows, ffnp_v, ffnp_hbm, out_sem.at[0]).start()
        return carry

    lax.fori_loop(0, peers, ffn_rows, 0)

    def norm_rows(k, carry):
        owner = me ^ k

        @pl.when(k > 0)
        def _():
            for t in range(subs):
                sub_gather(k, t, owner, dm, ss4, rs4).wait_recv()

        rows = pl.ds(pl.multiple_of(owner * own_rows, own_rows), own_rows)
        ng_v[rows, :] = mm(dm[rows, :], wout_v[...])
        block_store(owner, own_rows, ng_v, ng_hbm, out_sem.at[1]).start()
        return carry

    lax.fori_loop(0, peers, norm_rows, 0)

    def out_grads(i, carry):
        at = pl.ds(pl.multiple_of(i * tile, tile), tile)
        grads_v[at, 3 * cells :] = mm(dm[:, at], normed_v[...], TN).astype(bf16)
        block_store(i, tile, grads_v, grads_hbm, out_sem.at[2]).start()
        return carry

    lax.fori_loop(0, width // tile, out_grads, 0)
    for i in range(peers):
        block_store(i, own_rows, ffnp_v, ffnp_hbm, out_sem.at[0]).wait()
        block_store(i, own_rows, ng_v, ng_hbm, out_sem.at[1]).wait()
    for i in range(width // tile):
        block_store(i, tile, grads_v, grads_hbm, out_sem.at[2]).wait()
    for k in range(1, peers):
        for t in range(subs):
            sub_copy(k, t).wait_send()
            sub_gather(k, t, me, nm, ss2, rs2).wait_send()
            mid_copy(k, t).wait_send()
            sub_gather(k, t, me, dm, ss4, rs4).wait_send()


def mixer_ffn(normed, out_full, ffn_full, x, ct, gain):
    peers = lax.axis_size("head")
    total, width = ct.shape
    own_rows = total // peers
    subs = own_rows // SUB
    values = normed.shape[1]
    cells = ffn_full.shape[1] // 3
    sems = pltpu.SemaphoreType.DMA((peers, subs))
    return pl.pallas_call(
        functools.partial(mixer_ffn_kernel, peers),
        in_specs=[anywhere()] * 5 + [vmem()],
        out_specs=[anywhere()] * 3 + [vmem()] * 3,
        out_shape=[
            jax.ShapeDtypeStruct((width, 3 * cells + values), bf16),
            jax.ShapeDtypeStruct((total, width), bf16),
            jax.ShapeDtypeStruct((total, values), f32),
            jax.ShapeDtypeStruct((own_rows, width), f32),
            jax.ShapeDtypeStruct((own_rows, width), f32),
            jax.ShapeDtypeStruct((8, width), f32),
        ],
        scratch_shapes=[
            pltpu.VMEM((total, values), bf16),
            pltpu.VMEM((width, values), bf16),
            pltpu.VMEM((width, 3 * cells), bf16),
            pltpu.VMEM((own_rows, width), bf16),
            pltpu.VMEM((total, width), bf16),
            pltpu.VMEM((peers, own_rows, width), bf16),
            pltpu.VMEM((peers, own_rows, width), bf16),
            pltpu.VMEM((total, width), bf16),
            pltpu.VMEM((total, cells), bf16),
            pltpu.VMEM((total, 2 * cells), bf16),
            pltpu.VMEM((peers, own_rows, width), bf16),
            pltpu.VMEM((peers, own_rows, width), bf16),
            pltpu.VMEM((total, width), bf16),
            pltpu.VMEM((total, width), bf16),
            pltpu.VMEM((width, 3 * cells + values), bf16),
            pltpu.VMEM((total, values), f32),
            pltpu.SemaphoreType.DMA((5,)),
            pltpu.SemaphoreType.DMA((3, max(peers, width // 256))),
        ]
        + [sems] * 8,
        compiler_params=pltpu.CompilerParams(
            collective_id=1, has_side_effects=True, vmem_limit_bytes=56 * 2**20
        ),
        name="mixer_ffn",
    )(normed, out_full, ffn_full, x, ct, gain)


def input_grad_kernel(
    peers, dp_hbm, win_hbm, x_hbm, hgrad_ref, gain_ref,
    out_hbm, gpart_ref,
    dp_v, win_v, x_v, send1, recv1, whole, in_sem, out_sem, ss1, rs1, ss2, rs2,
):
    me = lax.axis_index("head")
    total, width = whole.shape
    own_rows = total // peers
    subs = own_rows // SUB
    loads = [
        pltpu.make_async_copy(dp_hbm, dp_v, in_sem.at[0]),
        pltpu.make_async_copy(win_hbm, win_v, in_sem.at[1]),
        pltpu.make_async_copy(part(x_hbm, me * own_rows, own_rows), x_v, in_sem.at[2]),
    ]
    for load in loads:
        load.start()
    greet_heads(me, peers)
    loads[0].wait()
    loads[1].wait()

    def sub_copy(k, t):
        rows = pl.ds(pl.multiple_of(t * SUB, SUB), SUB)
        return head_copy(
            send1.at[k, rows], recv1.at[k, rows], ss1.at[k, t], rs1.at[k, t], me ^ k
        )

    def project(i, carry):
        k = peers - 1 - i
        rows = pl.ds(pl.multiple_of((me ^ k) * own_rows, own_rows), own_rows)
        send1[k] = mm(dp_v[rows, :], win_v[...], NT).astype(bf16)

        @pl.when(k > 0)
        def _():
            for t in range(subs):
                sub_copy(k, t).start()

        return carry

    lax.fori_loop(0, peers, project, 0)
    loads[2].wait()
    gain = gain_ref[...]

    def sub_gather(k, t, owner):
        at = part(whole, owner * own_rows + t * SUB, SUB)
        return head_copy(at, at, ss2.at[k, t], rs2.at[k, t], me ^ k)

    def input_rows(t, carry):
        rows = pl.ds(pl.multiple_of(t * SUB, SUB), SUB)
        din = send1[0, rows, :].astype(f32)
        for k in range(1, peers):
            sub_copy(k, t).wait_recv()
            din = din + recv1[k, rows, :].astype(f32)
        x = x_v[rows, :].astype(f32)
        inverse = lax.rsqrt(jnp.mean(x * x, axis=1, keepdims=True) + epsilon)
        scaled = x * inverse
        weighted = din * gain
        grad = hgrad_ref[rows, :] + inverse * (
            weighted - scaled * jnp.mean(weighted * scaled, axis=1, keepdims=True)
        )
        part(whole, me * own_rows + t * SUB, SUB)[...] = grad.astype(bf16)
        for k in range(peers - 1, 0, -1):
            sub_gather(k, t, me).start()
        return carry + jnp.sum(din * scaled, axis=0, keepdims=True)

    gain_part = lax.fori_loop(0, subs, input_rows, jnp.zeros((1, width), f32))
    gpart_ref[...] = jnp.broadcast_to(gain_part, gpart_ref.shape)

    def store(i):
        return pltpu.make_async_copy(
            part(whole, i * own_rows, own_rows), part(out_hbm, i * own_rows, own_rows),
            out_sem.at[i],
        )

    store(me).start()
    for k in range(1, peers):
        for t in range(subs):
            sub_gather(k, t, me ^ k).wait_recv()
        store(me ^ k).start()
    for k in range(peers):
        store(me ^ k).wait()
    for k in range(1, peers):
        for t in range(subs):
            sub_copy(k, t).wait_send()
            sub_gather(k, t, me).wait_send()


def input_grads(dp, in_full, x, hgrad, gain):
    peers = lax.axis_size("head")
    total, width = x.shape
    cols = dp.shape[1]
    own_rows = total // peers
    subs = own_rows // SUB
    sems = pltpu.SemaphoreType.DMA((peers, subs))
    return pl.pallas_call(
        functools.partial(input_grad_kernel, peers),
        in_specs=[anywhere()] * 3 + [vmem()] * 2,
        out_specs=[anywhere(), vmem()],
        out_shape=[
            jax.ShapeDtypeStruct((total, width), bf16),
            jax.ShapeDtypeStruct((8, width), f32),
        ],
        scratch_shapes=[
            pltpu.VMEM((total, cols), bf16),
            pltpu.VMEM((width, cols), bf16),
            pltpu.VMEM((own_rows, width), bf16),
            pltpu.VMEM((peers, own_rows, width), bf16),
            pltpu.VMEM((peers, own_rows, width), bf16),
            pltpu.VMEM((total, width), bf16),
            pltpu.SemaphoreType.DMA((3,)),
            pltpu.SemaphoreType.DMA((peers,)),
        ]
        + [sems] * 4,
        compiler_params=pltpu.CompilerParams(
            collective_id=2, has_side_effects=True, vmem_limit_bytes=48 * 2**20
        ),
        name="input_grads",
    )(dp, in_full, x, hgrad, gain)


def shifted(shard, axis, by):
    count = lax.axis_size(axis)
    pairs = [(i, i + by) for i in range(count) if 0 <= i + by < count]
    return lax.ppermute(shard, axis, pairs)


def root_scale(value_rows):
    return lax.rsqrt(jnp.mean(value_rows * value_rows, axis=-1, keepdims=True) + epsilon)


def matmul(a, b, dims=NN):
    return lax.dot_general(a, b, (dims, ((), ())), preferred_element_type=f32)


ALL = ("seq", "batch")


def per_device(
    tokens, starts, attn_gain, w_in, w_rates, conv_w, decay_par, o_gain, w_out, ffn_gain, w_gu,
    w_down, cotangent,
):
    seqs, length, width = tokens.shape
    shard, heads = w_in.shape[:2]
    shards = width // shard
    total = seqs * length
    conv_cols = heads * QKV
    value_cols = heads * DV
    in_cols = conv_cols + value_cols
    units = w_down.shape[0]
    cells = -(-units // 256) * 256
    spare = cells - units

    conv_flat = conv_w.reshape(-1)
    small = jnp.concatenate([attn_gain, ffn_gain, conv_flat, o_gain]).astype(bf16)
    packed_in = jnp.concatenate(
        [
            w_in[:, :, :QKV].reshape(shard, conv_cols),
            w_in[:, :, QKV:].reshape(shard, value_cols),
            w_rates.reshape(shard, 2 * heads),
            jnp.zeros((shard, PAD - 2 * heads), f32),
        ],
        axis=1,
    ).astype(bf16)
    packed_ffn = jnp.pad(
        jnp.stack([w_gu[:, 0], w_gu[:, 1], w_down.T], axis=1).astype(bf16),
        ((0, 0), (0, 0), (0, spare)),
    ).reshape(shard, 3 * cells)
    in_full = lax.all_gather(packed_in, ALL, axis=0, tiled=True)
    small_full = lax.all_gather(small, ALL, axis=0)
    out_full = lax.all_gather(
        w_out.reshape(value_cols, -1).T.astype(bf16), ALL, axis=0, tiled=True
    )
    ffn_full = lax.all_gather(packed_ffn, ALL, axis=0, tiled=True)
    attn_gain_f = small_full[:, :shard].reshape(1, width).astype(f32)
    ffn_gain_f = small_full[:, shard : 2 * shard].reshape(1, width).astype(f32)
    conv_end = 2 * shard + conv_flat.shape[0]
    conv_full = (
        small_full[:, 2 * shard : conv_end]
        .reshape(shards, CONV, heads, -1)
        .transpose(1, 2, 0, 3)
        .reshape(CONV, conv_cols)
        .astype(f32)
    )
    o_gain_full = small_full[:, conv_end:].reshape(1, DV).astype(f32)

    place = lax.axis_index("seq")
    x = tokens.reshape(total, width)
    ct = cotangent.reshape(total, width)
    inputs = x.astype(f32)
    normed_in = (inputs * root_scale(inputs) * attn_gain_f).astype(bf16)
    projected = matmul(normed_in, in_full)
    ends = projected.reshape(seqs, length, -1)[:, length - CONV + 1 :, :conv_cols]
    end_live = (
        place * length + length - CONV + 1 + jnp.arange(CONV - 1, dtype=jnp.int32)
    )[None, :] >= starts[:, None]
    received = shifted((ends * end_live.astype(f32)[:, :, None]).astype(bf16), "seq", 1)
    halo = jnp.pad(received, ((0, 0), (HALO - CONV + 1, 0), (0, 0)))
    qkv, inv, n, qe, tot, trans, states, mixed, normed = forward_rule(
        starts, decay_par, projected, halo, conv_full, o_gain_full, seqs, heads
    )
    late_grads, ffn_part, normed_grad, hidden, hidden_grad, ffn_gain_part = mixer_ffn(
        normed, out_full, ffn_full, x, ct, ffn_gain_f
    )
    projected_grad, dconv, ddecay, onorm_grads, result = backward_rule(
        starts, decay_par, normed_grad, mixed, projected, o_gain_full, n, qe, tot, trans, qkv, inv,
        states, halo, conv_full, hidden, ffn_part, seqs, heads,
    )
    in_grad = matmul(normed_in, projected_grad, TN)
    input_grad, attn_gain_part = input_grads(
        projected_grad, in_full, x, hidden_grad, attn_gain_f
    )
    onorm_grad = jnp.sum(onorm_grads[:, 0], axis=0)
    decay_part = jnp.sum(ddecay[:, :2, 0].reshape(heads, seqs, 2), axis=1).T
    conv_grad = jnp.sum(dconv.reshape(heads, seqs, CONV, QKV), axis=1).transpose(1, 0, 2)

    def scatter(grad, dim=0):
        return lax.psum_scatter(
            grad.astype(bf16), ALL, scatter_dimension=dim, tiled=True
        ).astype(f32)

    late_own = scatter(late_grads)
    in_own = scatter(in_grad)
    gains = lax.psum(
        jnp.concatenate([attn_gain_part[0], ffn_gain_part[0], onorm_grad]), ("head",) + ALL
    )
    at = lax.axis_index(ALL)
    attn_own = lax.dynamic_slice(gains, (at * shard,), (shard,))
    ffn_own = lax.dynamic_slice(gains, (width + at * shard,), (shard,))
    onorm_own = lax.dynamic_slice(gains, (2 * width + at * (DV // shards),), (DV // shards,))
    channels = lax.psum(
        jnp.concatenate([conv_grad.reshape(-1), decay_part.reshape(-1)]), ALL
    )
    conv_own = lax.dynamic_slice(
        channels[: CONV * conv_cols].reshape(CONV, heads, QKV),
        (0, 0, at * (QKV // shards)),
        (CONV, heads, QKV // shards),
    )
    in_main = jnp.concatenate(
        [
            in_own[:, :conv_cols].reshape(shard, heads, QKV),
            in_own[:, conv_cols:in_cols].reshape(shard, heads, DV),
        ],
        axis=2,
    )
    return (
        result.reshape(tokens.shape),
        input_grad.reshape(tokens.shape),
        attn_own,
        in_main,
        in_own[:, in_cols : in_cols + 2 * heads].reshape(shard, heads, 2),
        conv_own,
        channels[CONV * conv_cols :].reshape(2, heads),
        onorm_own,
        late_own[:, 3 * cells :].T.reshape(heads, DV, -1),
        ffn_own,
        late_own[:, : 2 * cells].reshape(shard, 2, cells)[:, :, :units],
        late_own[:, 2 * cells : 2 * cells + units].T,
    )


def solution(mesh):
    weights = P(ALL)
    in_specs = (
        P("batch", "seq", None),
        P("batch"),
        weights,
        P(ALL, "head", None),
        P(ALL, "head", None),
        P(None, "head", ALL),
        P(None, "head"),
        weights,
        P("head", None, ALL),
        weights,
        P(ALL, None, "head"),
        P("head", ALL),
        P("batch", "seq", None),
    )
    out_specs = (
        P("batch", "seq", None),
        P("batch", "seq", None),
        weights,
        P(ALL, "head", None),
        P(ALL, "head", None),
        P(None, "head", ALL),
        P(None, "head"),
        weights,
        P("head", None, ALL),
        weights,
        P(ALL, None, "head"),
        P("head", ALL),
    )
    return jax.shard_map(
        per_device, mesh=mesh, in_specs=in_specs, out_specs=out_specs, check_vma=False
    )
```

```python
import functools

import jax
import jax.numpy as jnp
from jax import lax
from jax.experimental import pallas as pl
from jax.experimental.pallas import tpu as pltpu
from jax.sharding import PartitionSpec as P

DK = 128
DV = 256
CONV = 4
QKV = 2 * DK + DV
CHUNK = 128
HALO = 16
PAD = 128

bf16 = jnp.bfloat16
f32 = jnp.float32
epsilon = 1e-06
NN = ((1,), (0,))
NT = ((1,), (1,))
TN = ((0,), (0,))


def mm(a, b, dims=NN):
    return lax.dot_general(
        a.astype(bf16), b.astype(bf16), (dims, ((), ())), preferred_element_type=f32
    )


def split_mm(a, b):
    a_high, b_high = a.astype(bf16), b.astype(bf16)
    a_low = (a - a_high.astype(f32)).astype(bf16)
    b_low = (b - b_high.astype(f32)).astype(bf16)
    return mm(a_high, b_high) + (mm(a_high, b_low) + mm(a_low, b_high))


def iotas(n):
    return (
        lax.broadcasted_iota(jnp.int32, (n, n), 0),
        lax.broadcasted_iota(jnp.int32, (n, n), 1),
    )


def unit_lower_inverses(mats):
    n = mats[0].shape[0]
    rows, cols = iotas(n)
    eye = (rows == cols).astype(f32)
    pair = ((rows >> 1) == (cols >> 1)) & (rows > cols)
    inverses = [eye - jnp.where(pair, a, 0.0) for a in mats]
    shift = 1
    while (1 << shift) < n:
        corner = ((rows >> (shift + 1)) == (cols >> (shift + 1))) & (
            (rows >> shift) > (cols >> shift)
        )
        firsts = [mm(jnp.where(corner, a, 0.0), x) for a, x in zip(mats, inverses)]
        inverses = [x - mm(x, y) for x, y in zip(inverses, firsts)]
        shift += 1
    residuals = [eye - x - split_mm(a, x) for a, x in zip(mats, inverses)]
    return [x + mm(x, r) for x, r in zip(inverses, residuals)]


def sigmoid(v):
    return 1.0 / (1.0 + jnp.exp(-v))


def softplus(v):
    small = jnp.exp(-jnp.abs(v))
    one_more = 1.0 + small
    gap = one_more - 1.0
    exact = gap == 0.0
    tail = jnp.where(exact, small, jnp.log(one_more) * small / jnp.where(exact, 1.0, gap))
    return jnp.maximum(v, 0.0) + tail


def to_row(column, eye):
    return jnp.sum(jnp.where(eye, column, 0.0), axis=0, keepdims=True)


def pick(block, lane):
    lanes = lax.broadcasted_iota(jnp.int32, block.shape, 1)
    return jnp.sum(jnp.where(lanes == lane, block, 0.0), axis=1, keepdims=True)


def gates(logits, decay_ref, head):
    rate = jnp.exp(jnp.full((1, 1), decay_ref[0, head], f32))
    shifted_logit = pick(logits, 2 * head) + decay_ref[1, head]
    strength = sigmoid(pick(logits, 2 * head + 1))
    log_gate = -rate * softplus(shifted_logit)
    return log_gate, strength, rate, shifted_logit


def decays(log_gate, lower, upper, eye):
    gate_row = to_row(log_gate, eye)
    column = jnp.sum(jnp.where(lower, gate_row, 0.0), axis=1, keepdims=True)
    row = jnp.sum(jnp.where(upper, log_gate, 0.0), axis=0, keepdims=True)
    ratio = jnp.where(lower, jnp.exp(jnp.where(lower, column - row, 0.0)), 0.0)
    total = jnp.sum(log_gate, axis=0, keepdims=True)
    return column, total, ratio


def load_conv_input(main_ref, halo_ref, start, x_scr, first):
    length = main_ref.shape[0]
    positions = first + lax.broadcasted_iota(jnp.int32, (length, 1), 0)
    live = (positions >= start).astype(f32)
    before = first - HALO + lax.broadcasted_iota(jnp.int32, (HALO, 1), 0)
    lived = (before >= start).astype(f32)
    x_scr[pl.ds(0, HALO), :] = (halo_ref[0] * lived).astype(bf16).astype(f32)
    x_scr[pl.ds(HALO, length), :] = (main_ref[...] * live).astype(bf16).astype(f32)


def convolve(x_scr, conv, at):
    total = x_scr[pl.ds(at + HALO - CONV + 1, CHUNK), :] * conv[0:1]
    for j in range(1, CONV):
        total = total + x_scr[pl.ds(at + HALO - CONV + 1 + j, CHUNK), :] * conv[j : j + 1]
    return total


def unit(rows):
    return rows * lax.rsqrt(jnp.sum(rows * rows, axis=1, keepdims=True) + epsilon)


MESH = pl.DeviceIdType.MESH
SUB = 128


def head_copy(src, dst, send_sem, recv_sem, peer):
    return pltpu.make_async_remote_copy(
        src_ref=src, dst_ref=dst, send_sem=send_sem, recv_sem=recv_sem,
        device_id={"head": peer}, device_id_type=MESH,
    )


def greet_heads(me, peers):
    barrier = pltpu.get_barrier_semaphore()
    for k in range(1, peers):
        pl.semaphore_signal(barrier, inc=1, device_id={"head": me ^ k}, device_id_type=MESH)
    pl.semaphore_wait(barrier, peers - 1)


def part(ref, start, size):
    return ref.at[pl.ds(pl.multiple_of(start, size), size)]


class Spread:
    def __init__(self, buffer, size, me, send_sem, recv_sem, piece=None):
        self.buffer, self.size, self.me = buffer, size, me
        self.piece = size if piece is None else piece
        self.send_sem, self.recv_sem = send_sem, recv_sem

    def region(self, owner, t, half):
        rows = pl.ds(pl.multiple_of(owner * self.size + t * self.piece, self.piece), self.piece)
        middle = self.buffer.shape[1] // 2
        if half is None:
            return self.buffer.at[rows]
        return self.buffer.at[rows, pl.ds(half * middle, middle)]

    def copy(self, kind, t, owner):
        at = self.region(owner, t, None if kind < 2 else kind - 2)
        to = self.me ^ (1 if kind in (0, 3) else 2)
        return head_copy(at, at, self.send_sem.at[kind, t], self.recv_sem.at[kind, t], to)

    def start(self, t):
        self.copy(0, t, self.me).start()
        self.copy(1, t, self.me).start()

    def forward(self, t):
        self.copy(0, t, self.me ^ 1).wait_recv()
        self.copy(2, t, self.me ^ 1).start()
        self.copy(1, t, self.me ^ 2).wait_recv()
        self.copy(3, t, self.me ^ 2).start()

    def finish(self, t):
        self.copy(2, t, self.me ^ 3).wait_recv()
        self.copy(3, t, self.me ^ 3).wait_recv()

    def drain(self, t):
        for kind, owner in enumerate((0, 0, 1, 2)):
            self.copy(kind, t, self.me ^ owner).wait_send()


def anywhere():
    return pl.BlockSpec(memory_space=pl.ANY)


def vmem():
    return pl.BlockSpec(memory_space=pltpu.VMEM)


def along(axis, source, target, send_sem, recv_sem, to):
    return pltpu.make_async_remote_copy(
        src_ref=source, dst_ref=target, send_sem=send_sem, recv_sem=recv_sem,
        device_id={axis: to}, device_id_type=MESH,
    )


def forward_kernel(
    seqs, places, start_ref, decay_ref, main_ref, halo_ref, rate_ref, conv_ref,
    qkv_ref, inv_ref, n_ref, qe_ref, tot_ref, trans_ref, s_ref, mixed_ref,
    x_scr, b_scr, o_scr, carried_scr, send, recv, send_sem, recv_sem,
):
    step = pl.program_id(0)
    chains = n_ref.shape[0]
    count = n_ref.shape[1]
    length = main_ref.shape[0]
    place = lax.axis_index("seq")
    lag = jnp.minimum(place, chains - 1)

    @pl.when(step == 0)
    def _():
        barrier = pltpu.get_barrier_semaphore()

        @pl.when(place > 0)
        def _():
            pl.semaphore_signal(
                barrier, inc=1, device_id={"seq": place - 1}, device_id_type=MESH
            )

        @pl.when(place == 0)
        def _():
            recv[...] = jnp.zeros_like(recv)

        @pl.when(place < places - 1)
        def _():
            pl.semaphore_wait(barrier, 1)

    @pl.when(step < chains)
    def _():
        head = step // seqs
        load_conv_input(
            main_ref, halo_ref, start_ref[step % seqs], x_scr, place * length
        )
        conv = conv_ref[...]
        rows, cols = iotas(CHUNK)
        lower, upper, eye = rows >= cols, rows <= cols, rows == cols
        parts = []
        for c in range(count):
            at = c * CHUNK
            convolved = convolve(x_scr, conv, at)
            active = convolved * sigmoid(convolved)
            q = (unit(active[:, :DK]) * DK ** (-0.5)).astype(bf16)
            k = unit(active[:, DK : 2 * DK]).astype(bf16)
            v = active[:, 2 * DK :].astype(bf16)
            qkv_ref[pl.ds(at, CHUNK), 0:DK] = q
            qkv_ref[pl.ds(at, CHUNK), DK : 2 * DK] = k
            qkv_ref[pl.ds(at, CHUNK), 2 * DK :] = v
            log_gate, strength, _, _ = gates(rate_ref[pl.ds(at, CHUNK), :], decay_ref, head)
            column, total, ratio = decays(log_gate, lower, upper, eye)
            products = mm(jnp.concatenate([k, q], axis=0), k, NT)
            coupling = jnp.where(rows > cols, strength * ratio * products[:CHUNK], 0.0)
            scores = (ratio * products[CHUNK:]).astype(bf16)
            parts.append((q, k, v, strength, column, total, coupling, scores))
        inverses = unit_lower_inverses([p[6] for p in parts])
        maps = []
        for c in range(count):
            q, k, v, strength, column, total, _, scores = parts[c]
            growth = jnp.exp(column)
            kf, vf, qf = k.astype(f32), v.astype(f32), q.astype(f32)
            inverse = inverses[c].astype(bf16)
            inv_ref[0, c] = inverse
            target = jnp.concatenate([(strength * growth) * kf, strength * vf], axis=1)
            solved = mm(inverse, target).astype(bf16)
            read = mm(scores, solved)
            qe_ref[step, c] = (growth * qf - read[:, :DK]).astype(bf16)
            o_scr[step, pl.ds(c * CHUNK, CHUNK), :] = read[:, DK:]
            written = mm(jnp.exp(total - column) * kf, solved, TN)
            low_n = written[:, :DK].astype(bf16)
            n_ref[step, c] = low_n
            b_scr[step, c] = written[:, DK:]
            whole = jnp.exp(total)
            tot_ref[step, pl.ds(c, 1), :] = jnp.broadcast_to(whole, (1, DK))
            maps.append((low_n, written[:, DK:], whole))
        low_n, b, whole = maps[0]
        trans = whole * eye.astype(f32) - low_n.astype(f32)
        carried = b
        for low_n, b, whole in maps[1:]:
            both = jnp.concatenate([trans, carried], axis=1)
            moved = whole * both - mm(low_n, both)
            trans = moved[:, :DK]
            carried = moved[:, DK:] + b
        trans_ref[step] = trans.astype(bf16)
        carried_scr[step] = carried

    @pl.when(step >= chains)
    def _():
        chain = jnp.maximum(step - chains, 0)
        state = recv[chain].astype(f32)
        for c in range(count):
            low_state = state.astype(bf16)
            s_ref[0, c] = low_state
            both = mm(jnp.concatenate([n_ref[chain, c], qe_ref[chain, c]], axis=0), low_state)
            whole = tot_ref[chain, pl.ds(c, 1), 0:1]
            state = whole * state - both[:DK] + b_scr[chain, c]
            at = pl.ds(c * CHUNK, CHUNK)
            mixed_ref[at, :] = o_scr[chain, at, :] + both[DK:]

    def passed(chain):
        return along(
            "seq", send.at[chain], recv.at[chain], send_sem.at[chain], recv_sem.at[chain],
            jnp.minimum(place + 1, places - 1),
        )

    relayed = step - lag

    @pl.when((relayed >= 0) & (relayed < chains))
    def _():
        chain = jnp.clip(relayed, 0, chains - 1)

        @pl.when(place > 0)
        def _():
            passed(chain).wait_recv()

        @pl.when(place < places - 1)
        def _():
            leaving = mm(trans_ref[chain], recv[chain]) + carried_scr[chain]
            send[chain] = leaving.astype(bf16)
            passed(chain).start()

    @pl.when((step == 2 * chains - 1) & (place < places - 1))
    def _():
        for chain in range(chains):
            passed(chain).wait_send()


def early(chains, make):
    return lambda j: make(jnp.minimum(j, chains - 1))


def late(chains, make):
    return lambda j: make(jnp.maximum(j - chains, 0))


def forward_rule(starts, decay_par, projected, halo, conv_w, seqs, heads):
    places = lax.axis_size("seq")
    chains = seqs * heads
    length = projected.shape[0] // seqs
    count = length // CHUNK
    rates_at = heads * QKV // PAD
    row = lambda first: lambda i: (i % seqs, first + i // seqs)
    whole = lambda *dims: pl.BlockSpec(dims, lambda j: (0,) * len(dims))
    shape = jax.ShapeDtypeStruct
    return pl.pallas_call(
        functools.partial(forward_kernel, seqs, places),
        grid=(2 * chains,),
        in_specs=[
            smem(),
            smem(),
            pl.BlockSpec((length, QKV), early(chains, row(0))),
            pl.BlockSpec((1, HALO, QKV), early(chains, lambda i: (i % seqs, 0, i // seqs))),
            pl.BlockSpec((length, PAD), early(chains, lambda i: (i % seqs, rates_at))),
            pl.BlockSpec((CONV, QKV), early(chains, lambda i: (0, i // seqs))),
        ],
        out_specs=[
            pl.BlockSpec((length, QKV), early(chains, row(0))),
            pl.BlockSpec((1, count, CHUNK, CHUNK), early(chains, lambda i: (i, 0, 0, 0))),
            whole(chains, count, DK, DK),
            whole(chains, count, CHUNK, DK),
            whole(chains, count, DK),
            whole(chains, DK, DK),
            pl.BlockSpec((1, count, DK, DV), late(chains, lambda i: (i, 0, 0, 0))),
            pl.BlockSpec((length, DV), late(chains, row(0))),
        ],
        out_shape=[
            shape((seqs * length, heads * QKV), bf16),
            shape((chains, count, CHUNK, CHUNK), bf16),
            shape((chains, count, DK, DK), bf16),
            shape((chains, count, CHUNK, DK), bf16),
            shape((chains, count, DK), f32),
            shape((chains, DK, DK), bf16),
            shape((chains, count, DK, DV), bf16),
            shape((seqs * length, heads * DV), f32),
        ],
        scratch_shapes=[
            pltpu.VMEM((HALO + length, QKV), f32),
            pltpu.VMEM((chains, count, DK, DV), f32),
            pltpu.VMEM((chains, length, DV), f32),
            pltpu.VMEM((chains, DK, DV), f32),
            pltpu.VMEM((chains, DK, DV), bf16),
            pltpu.VMEM((chains, DK, DV), bf16),
            pltpu.SemaphoreType.DMA((chains,)),
            pltpu.SemaphoreType.DMA((chains,)),
        ],
        compiler_params=pltpu.CompilerParams(
            dimension_semantics=("arbitrary",), collective_id=3, has_side_effects=True,
            vmem_limit_bytes=48 * 2**20,
        ),
        name="forward_rule",
    )(starts, decay_par, projected, halo, projected, conv_w)


def backward_kernel(
    seqs, places, peers, start_ref, decay_ref,
    dn_ref, mixed_ref, og_ref, gain_ref, n_ref, qe_ref, tot_ref, trans_ref,
    qkv_ref, inv_ref, s_ref, main_ref, halo_ref, rate_ref, conv_ref, hidden_ref, ffnp_hbm,
    dp_ref, dconv_ref, ddecay_ref, gg_ref, out_hbm,
    x_scr, g_scr, do_scr, own_scr, send, recv, tail_scr, halo_send, halo_recv,
    parts, whole_out, send_sem, recv_sem, halo_send_sem, halo_recv_sem, own_sem, out_sem,
    ss1, rs1, gather_send, gather_recv,
):
    step = pl.program_id(0)
    chains = n_ref.shape[0]
    count = n_ref.shape[1]
    length = main_ref.shape[0]
    heads = chains // seqs
    conv_cols = heads * QKV
    in_cols = conv_cols + heads * DV
    place = lax.axis_index("seq")
    lag = jnp.minimum(places - 1 - place, chains - 1)
    me = lax.axis_index("head")
    own_rows = hidden_ref.shape[0]
    subs = own_rows // SUB

    def ffn_copy(k):
        return head_copy(
            part(ffnp_hbm, (me ^ k) * own_rows, own_rows), parts.at[k], ss1.at[k], rs1.at[k],
            me ^ k,
        )

    def own_copy():
        return pltpu.make_async_copy(
            part(ffnp_hbm, me * own_rows, own_rows), parts.at[0], own_sem.at[0]
        )

    ring = Spread(whole_out, own_rows, me, gather_send, gather_recv)

    def out_store(k):
        owner = me ^ k
        return pltpu.make_async_copy(
            part(whole_out, owner * own_rows, own_rows), part(out_hbm, owner * own_rows, own_rows),
            out_sem.at[k],
        )

    def passed(chain):
        return along(
            "seq", send.at[chain], recv.at[chain], send_sem.at[chain], recv_sem.at[chain],
            jnp.maximum(place - 1, 0),
        )

    def returned(chain):
        return along(
            "seq", halo_send.at[chain], halo_recv.at[chain], halo_send_sem.at[chain],
            halo_recv_sem.at[chain], jnp.maximum(place - 1, 0),
        )

    @pl.when(step == 0)
    def _():
        barrier = pltpu.get_barrier_semaphore()
        for k in range(1, peers):
            pl.semaphore_signal(barrier, inc=1, device_id={"head": me ^ k}, device_id_type=MESH)

        @pl.when(place < places - 1)
        def _():
            pl.semaphore_signal(
                barrier, inc=1, device_id={"seq": place + 1}, device_id_type=MESH
            )

        @pl.when(place == places - 1)
        def _():
            recv[...] = jnp.zeros_like(recv)
            halo_recv[...] = jnp.zeros_like(halo_recv)

        @pl.when(place > 0)
        def _():
            pl.semaphore_wait(barrier, peers)

        @pl.when(place == 0)
        def _():
            pl.semaphore_wait(barrier, peers - 1)

        own_copy().start()
        for k in range(peers - 1, 0, -1):
            ffn_copy(k).start()

    @pl.when(step < chains)
    def _():
        gain = gain_ref[0:1]
        first = (step % seqs) * length
        og_at = pl.ds(pl.multiple_of(conv_cols + (step // seqs) * DV, DV), DV)
        state = jnp.zeros((DK, DV), f32)
        total = jnp.zeros((1, DV), f32)
        for c in reversed(range(count)):
            at = pl.ds(c * CHUNK, CHUNK)
            mixed, og, dn = mixed_ref[at, :], og_ref[at, :], dn_ref[at, :]
            inverse = lax.rsqrt(jnp.mean(mixed * mixed, axis=1, keepdims=True) + epsilon)
            scaled = mixed * inverse
            sig = sigmoid(og)
            silu = og * sig
            through = dn * scaled
            total = total + jnp.sum(through * silu, axis=0, keepdims=True)
            dp_ref[pl.ds(pl.multiple_of(first + c * CHUNK, CHUNK), CHUNK), og_at] = (
                through * gain * sig * (1.0 + og * (1.0 - sig))
            ).astype(bf16)
            weighted = dn * gain * silu
            dmixed = inverse * (
                weighted - scaled * jnp.mean(weighted * scaled, axis=1, keepdims=True)
            )
            dmixed = dmixed.astype(bf16)
            do_scr[step, at, :] = dmixed
            decay = tot_ref[step, pl.ds(c, 1), 0:1]
            state = (
                decay * state - mm(n_ref[step, c], state, TN) + mm(qe_ref[step, c], dmixed, TN)
            )
        gg_ref[0] = jnp.broadcast_to(total, (8, DV))
        own_scr[step] = state

    @pl.when(step >= chains)
    def _():
        chain = jnp.maximum(step - chains, 0)
        head, seq = chain // seqs, chain % seqs
        first = seq * length
        start = start_ref[seq]
        load_conv_input(main_ref, halo_ref, start, x_scr, place * length)
        conv = conv_ref[...]
        rows, cols = iotas(CHUNK)
        lower, upper, eye = rows >= cols, rows <= cols, rows == cols
        strict = rows > cols
        state = recv[chain].astype(f32)
        leaving = [None] * count
        for c in reversed(range(count)):
            leaving[c] = state
            state = (
                tot_ref[chain, pl.ds(c, 1), 0:1] * state
                - mm(n_ref[chain, c], state, TN)
                + mm(qe_ref[chain, c], do_scr[chain, pl.ds(c * CHUNK, CHUNK), :], TN)
            )
        g_scr[pl.ds(0, 8), :] = jnp.zeros((8, QKV), f32)
        g_scr[pl.ds(8 + length, 8), :] = jnp.zeros((8, QKV), f32)
        rate_total = jnp.zeros((1, 1), f32)
        bias_total = jnp.zeros((1, 1), f32)
        conv_total = [jnp.zeros((1, QKV), f32) for _ in range(CONV)]
        lanes = lax.broadcasted_iota(jnp.int32, (CHUNK, PAD), 1)
        for c in range(count):
            at = pl.ds(c * CHUNK, CHUNK)
            q, k, v = qkv_ref[at, 0:DK], qkv_ref[at, DK : 2 * DK], qkv_ref[at, 2 * DK :]
            kf, vf = k.astype(f32), v.astype(f32)
            log_gate, strength, rate, logit = gates(rate_ref[at, :], decay_ref, head)
            column, total, ratio = decays(log_gate, lower, upper, eye)
            growth = jnp.exp(column)
            remain = jnp.exp(total - column)
            whole = jnp.exp(total)
            inverse = inv_ref[0, c]
            s0 = s_ref[0, c]
            do = do_scr[chain, at, :]
            grad_state = leaving[c]
            low_grad_state = grad_state.astype(bf16)
            kq = jnp.concatenate([k, q], axis=0)
            products = mm(kq, k, NT)
            kk, qk = products[:CHUNK], products[CHUNK:]
            reads = mm(kq, s0)
            ks, qs = reads[:CHUNK], reads[CHUNK:]
            fresh = vf - growth * ks
            pseudo = mm(inverse, strength * fresh).astype(bf16)
            scores = (ratio * qk).astype(bf16)
            dpseudo = mm(scores, do, TN) + mm(remain * kf, low_grad_state)
            dtarget = mm(inverse, dpseudo, TN)
            low_dtarget = dtarget.astype(bf16)
            dstrength = jnp.sum(dtarget * fresh, axis=1, keepdims=True)
            dlog = -(strength * growth) * jnp.sum(dtarget * ks, axis=1, keepdims=True)
            dv = strength * dtarget
            both = jnp.concatenate([low_dtarget, do], axis=0)
            outer = mm(both, pseudo, NT)
            dcoupling = jnp.where(strict, -outer[:CHUNK] * ratio, 0.0)
            by_strength = dcoupling * kk
            dstrength = dstrength + jnp.sum(by_strength, axis=1, keepdims=True)
            exponent = strength * by_strength
            dqk_f = jnp.where(lower, outer[CHUNK:] * ratio, 0.0)
            exponent = exponent + dqk_f * qk
            pair = jnp.concatenate([(dcoupling * strength).astype(bf16), dqk_f.astype(bf16)], axis=0)
            back = mm(both, s0, NT)
            wide = mm(pair, k)
            dq = growth * back[CHUNK:] + wide[CHUNK:]
            dkept = mm(pseudo, low_grad_state, NT)
            dk = (
                wide[:CHUNK]
                - (strength * growth) * back[:CHUNK]
                + mm(pair, kq, TN)
                + remain * dkept
            )
            dlog = dlog + growth * jnp.sum(do.astype(f32) * qs, axis=1, keepdims=True)
            from_kept = remain * jnp.sum(kf * dkept, axis=1, keepdims=True)
            dlog = dlog - from_kept + jnp.sum(exponent, axis=1, keepdims=True)
            dlog_row = to_row(dlog, eye) - jnp.sum(exponent, axis=0, keepdims=True)
            tail = jnp.sum(from_kept, axis=0, keepdims=True) + whole * jnp.sum(
                jnp.sum(grad_state * s0.astype(f32), axis=1, keepdims=True), axis=0, keepdims=True
            )
            dgate = jnp.sum(jnp.where(upper, dlog_row, 0.0), axis=1, keepdims=True) + tail
            slope = sigmoid(logit)
            drate0 = -rate * slope * dgate
            drate1 = dstrength * strength * (1.0 - strength)
            rate_total = rate_total + jnp.sum(dgate * log_gate, axis=0, keepdims=True)
            bias_total = bias_total + jnp.sum(drate0, axis=0, keepdims=True)
            here = pl.ds(pl.multiple_of(first + c * CHUNK, CHUNK), CHUNK)
            others = jnp.where(head == 0, 0.0, dp_ref[here, in_cols:].astype(f32))
            dp_ref[here, in_cols:] = jnp.where(
                lanes == 2 * head, drate0, jnp.where(lanes == 2 * head + 1, drate1, others)
            ).astype(bf16)
            convolved = convolve(x_scr, conv, c * CHUNK)
            sig = sigmoid(convolved)
            active = convolved * sig
            slope_conv = sig * (1.0 + convolved * (1.0 - sig))

            def unit_grad(rows_in, grad):
                inv_norm = lax.rsqrt(jnp.sum(rows_in * rows_in, axis=1, keepdims=True) + epsilon)
                y = rows_in * inv_norm
                return inv_norm * (grad - y * jnp.sum(y * grad, axis=1, keepdims=True))

            dq = dq.astype(bf16).astype(f32) * DK ** (-0.5)
            dk = dk.astype(bf16).astype(f32)
            dv = dv.astype(bf16).astype(f32)
            dconv = (
                jnp.concatenate(
                    [unit_grad(active[:, :DK], dq), unit_grad(active[:, DK : 2 * DK], dk), dv],
                    axis=1,
                )
                * slope_conv
            )
            g_scr[pl.ds(8 + c * CHUNK, CHUNK), :] = dconv
            for j in range(CONV):
                shifted_in = x_scr[pl.ds(c * CHUNK + HALO - CONV + 1 + j, CHUNK), :]
                conv_total[j] = conv_total[j] + jnp.sum(dconv * shifted_in, axis=0, keepdims=True)
        for j in range(CONV):
            dconv_ref[0, pl.ds(j, 1), :] = conv_total[j]
        row8 = lax.broadcasted_iota(jnp.int32, (8, PAD), 0)
        ddecay_ref[0] = jnp.where(row8 == 0, rate_total, jnp.where(row8 == 1, bias_total, 0.0))

        def conv_back(at, size):
            grad = g_scr[pl.ds(at + CONV - 1, size), :] * conv[0:1]
            for j in range(1, CONV):
                grad = grad + g_scr[pl.ds(at + CONV - 1 - j, size), :] * conv[j : j + 1]
            return grad

        halo_send[chain] = conv_back(0, 8)

        @pl.when(place > 0)
        def _():
            returned(chain).start()

        conv_at = pl.ds(pl.multiple_of(head * QKV, QKV), QKV)
        for c in range(count):
            grad = conv_back(8 + c * CHUNK, CHUNK)
            positions = place * length + c * CHUNK + lax.broadcasted_iota(
                jnp.int32, (CHUNK, 1), 0
            )
            live = (positions >= start).astype(f32)
            if c == count - 1:
                tail_scr[chain] = grad[CHUNK - HALO :]
            dp_ref[pl.ds(pl.multiple_of(first + c * CHUNK, CHUNK), CHUNK), conv_at] = (
                grad * live
            ).astype(bf16)

    relayed = step - lag

    @pl.when((relayed >= 0) & (relayed < chains))
    def _():
        chain = jnp.clip(relayed, 0, chains - 1)

        @pl.when(place < places - 1)
        def _():
            passed(chain).wait_recv()

        @pl.when(place > 0)
        def _():
            earlier = mm(trans_ref[chain], recv[chain], TN) + own_scr[chain]
            send[chain] = earlier.astype(bf16)
            passed(chain).start()

    @pl.when(step == chains)
    def _():
        own_copy().wait()
        for k in range(1, peers):
            ffn_copy(k).wait_recv()

        def out_rows(t, carry):
            rows = pl.ds(pl.multiple_of(t * SUB, SUB), SUB)
            value = hidden_ref[rows, :]
            for k in range(peers):
                value = value + parts[k, rows, :].astype(f32)
            part(whole_out, me * own_rows + t * SUB, SUB)[...] = value.astype(bf16)
            return carry

        lax.fori_loop(0, subs, out_rows, 0)
        ring.start(0)
        out_store(0).start()

    @pl.when(step == chains + 2)
    def _():
        ring.forward(0)

    @pl.when(step == 2 * chains - 1)
    def _():
        for chain in range(chains):
            @pl.when(place < places - 1)
            def _():
                returned(chain).wait_recv()

            head, seq = chain // seqs, chain % seqs
            positions = (place + 1) * length - HALO + lax.broadcasted_iota(
                jnp.int32, (HALO, 1), 0
            )
            live = (positions >= start_ref[seq]).astype(f32)
            grad = tail_scr[chain] + jnp.concatenate(
                [jnp.zeros((HALO - 8, QKV), f32), halo_recv[chain]], axis=0
            )
            dp_ref[pl.ds((seq + 1) * length - HALO, HALO), pl.ds(head * QKV, QKV)] = (
                grad * live
            ).astype(bf16)

            @pl.when(place > 0)
            def _():
                returned(chain).wait_send()
                passed(chain).wait_send()

        ring.finish(0)
        for k in range(1, peers):
            out_store(k).start()
        for k in range(peers):
            out_store(k).wait()
        for k in range(1, peers):
            ffn_copy(k).wait_send()
        ring.drain(0)


def backward_rule(
    starts, decay_par, dn, mixed, og, projected, gain, n, qe, tot, trans, qkv, inv, states, halo, conv_w,
    hidden, ffn_part, seqs, heads,
):
    places, peers = lax.axis_size("seq"), lax.axis_size("head")
    chains = seqs * heads
    rows = projected.shape[0]
    length = rows // seqs
    count = length // CHUNK
    width = hidden.shape[1]
    own_rows = hidden.shape[0]
    rates_at = heads * QKV // PAD
    row = lambda first: lambda i: (i % seqs, first + i // seqs)
    whole = lambda *dims: pl.BlockSpec(dims, lambda j: (0,) * len(dims))
    chain4 = lambda i: (i, 0, 0, 0)
    chain3 = lambda i: (i, 0, 0)
    shape = jax.ShapeDtypeStruct
    per_chain = pltpu.SemaphoreType.DMA((chains,))
    per_peer = pltpu.SemaphoreType.DMA((peers,))
    return pl.pallas_call(
        functools.partial(backward_kernel, seqs, places, peers),
        grid=(2 * chains,),
        in_specs=[
            smem(),
            smem(),
            pl.BlockSpec((length, DV), early(chains, row(0))),
            pl.BlockSpec((length, DV), early(chains, row(0))),
            pl.BlockSpec((length, DV), early(chains, row(0))),
            whole(1, DV),
            whole(chains, count, DK, DK),
            whole(chains, count, CHUNK, DK),
            whole(chains, count, DK),
            whole(chains, DK, DK),
            pl.BlockSpec((length, QKV), late(chains, row(0))),
            pl.BlockSpec((1, count, CHUNK, CHUNK), late(chains, chain4)),
            pl.BlockSpec((1, count, DK, DV), late(chains, chain4)),
            pl.BlockSpec((length, QKV), late(chains, row(0))),
            pl.BlockSpec((1, HALO, QKV), late(chains, lambda i: (i % seqs, 0, i // seqs))),
            pl.BlockSpec((length, PAD), late(chains, lambda i: (i % seqs, rates_at))),
            pl.BlockSpec((CONV, QKV), late(chains, lambda i: (0, i // seqs))),
            whole(own_rows, width),
            anywhere(),
        ],
        out_specs=[
            whole(rows, heads * (QKV + DV) + PAD),
            pl.BlockSpec((1, CONV, QKV), late(chains, chain3)),
            pl.BlockSpec((1, 8, PAD), late(chains, chain3)),
            pl.BlockSpec((1, 8, DV), early(chains, chain3)),
            anywhere(),
        ],
        out_shape=[
            shape((rows, heads * (QKV + DV) + PAD), bf16),
            shape((chains, CONV, QKV), f32),
            shape((chains, 8, PAD), f32),
            shape((chains, 8, DV), f32),
            shape((rows, width), bf16),
        ],
        scratch_shapes=[
            pltpu.VMEM((HALO + length, QKV), f32),
            pltpu.VMEM((16 + length, QKV), f32),
            pltpu.VMEM((chains, length, DV), bf16),
            pltpu.VMEM((chains, DK, DV), f32),
            pltpu.VMEM((chains, DK, DV), bf16),
            pltpu.VMEM((chains, DK, DV), bf16),
            pltpu.VMEM((chains, HALO, QKV), f32),
            pltpu.VMEM((chains, 8, QKV), f32),
            pltpu.VMEM((chains, 8, QKV), f32),
            pltpu.VMEM((peers, own_rows, width), bf16),
            pltpu.VMEM((rows, width), bf16),
            per_chain, per_chain, per_chain, per_chain,
            pltpu.SemaphoreType.DMA((1,)),
            per_peer, per_peer, per_peer,
            pltpu.SemaphoreType.DMA((4, 1)),
            pltpu.SemaphoreType.DMA((4, 1)),
        ],
        compiler_params=pltpu.CompilerParams(
            dimension_semantics=("arbitrary",), collective_id=4, has_side_effects=True,
            vmem_limit_bytes=52 * 2**20,
        ),
        name="backward_rule",
    )(
        starts, decay_par, dn, mixed, og, gain, n, qe, tot, trans, qkv, inv, states, projected,
        halo, projected, conv_w, hidden, ffn_part,
    )


def smem():
    return pl.BlockSpec(memory_space=pltpu.SMEM)


def rows_of(t):
    return pl.ds(pl.multiple_of(t * SUB, SUB), SUB)


class Summed:
    def __init__(self, send, recv, me, send_sem, recv_sem):
        self.send, self.recv, self.me = send, recv, me
        self.send_sem, self.recv_sem = send_sem, recv_sem

    def copy(self, k, t):
        return head_copy(
            self.send.at[k, rows_of(t)], self.recv.at[k, rows_of(t)], self.send_sem.at[k, t],
            self.recv_sem.at[k, t], self.me ^ k,
        )

    def collect(self, t, peers):
        total = self.send[0, rows_of(t), :].astype(f32)
        for k in range(1, peers):
            self.copy(k, t).wait_recv()
            total = total + self.recv[k, rows_of(t), :].astype(f32)
        return total


def block_store(i, size, source, target, sem):
    return pltpu.make_async_copy(
        part(source, i * size, size), part(target, i * size, size), sem.at[i]
    )


def mixer_kernel(
    peers, nin_hbm, mixed_hbm, weights_hbm, x_hbm, gain_ref, o_gain_ref,
    og_hbm, normed_hbm, nm_hbm, hidden_ref,
    nin, mixed, weights, x_v, og_v, normed_v, send1, recv1, nm, in_sem, out_sem,
    ss1, rs1, gather_send, gather_recv,
):
    me = lax.axis_index("head")
    total, width = nm.shape
    values = mixed.shape[1]
    own_rows = total // peers
    subs = own_rows // SUB
    loads = [
        pltpu.make_async_copy(weights_hbm, weights, in_sem.at[0]),
        pltpu.make_async_copy(nin_hbm, nin, in_sem.at[1]),
        pltpu.make_async_copy(mixed_hbm, mixed, in_sem.at[2]),
        pltpu.make_async_copy(part(x_hbm, me * own_rows, own_rows), x_v, in_sem.at[3]),
    ]
    for load in loads:
        load.start()
    greet_heads(me, peers)
    for load in loads[:3]:
        load.wait()
    sums = Summed(send1, recv1, me, ss1, rs1)

    def project(i, carry):
        k = peers - 1 - i
        owner = me ^ k
        rows = pl.ds(pl.multiple_of(owner * own_rows, own_rows), own_rows)
        og = mm(nin[rows, :], weights[:, 0:values])
        og_v[rows, :] = og
        gated = og * sigmoid(og)
        for first in range(0, values, DV):
            at = pl.ds(first, DV)
            own = mixed[rows, at]
            inverse = lax.rsqrt(jnp.mean(own * own, axis=1, keepdims=True) + epsilon)
            normed_v[rows, at] = (
                own * inverse * o_gain_ref[0:1] * gated[:, first : first + DV]
            ).astype(bf16)
        send1[k] = mm(normed_v[rows, :], weights[:, values:], NT).astype(bf16)

        @pl.when(k > 0)
        def _():
            for t in range(subs):
                sums.copy(k, t).start()

        block_store(owner, own_rows, og_v, og_hbm, out_sem.at[0]).start()
        block_store(owner, own_rows, normed_v, normed_hbm, out_sem.at[1]).start()
        return carry

    lax.fori_loop(0, peers, project, 0)
    loads[3].wait()
    gain = gain_ref[...]
    ring = Spread(nm, own_rows, me, gather_send, gather_recv, SUB)
    for t in range(subs):
        rows = rows_of(t)
        hidden = x_v[rows, :].astype(f32) + sums.collect(t, peers)
        hidden_ref[rows, :] = hidden
        inverse = lax.rsqrt(jnp.mean(hidden * hidden, axis=1, keepdims=True) + epsilon)
        part(nm, me * own_rows + t * SUB, SUB)[...] = (hidden * inverse * gain).astype(bf16)
        ring.start(t)
    for t in range(subs):
        ring.forward(t)
    for k in range(peers):
        if k == peers - 1:
            for t in range(subs):
                ring.finish(t)
        block_store(me ^ k, own_rows, nm, nm_hbm, out_sem.at[2]).start()
    for i in range(peers):
        block_store(i, own_rows, og_v, og_hbm, out_sem.at[0]).wait()
        block_store(i, own_rows, normed_v, normed_hbm, out_sem.at[1]).wait()
        block_store(i, own_rows, nm, nm_hbm, out_sem.at[2]).wait()
    for t in range(subs):
        for k in range(1, peers):
            sums.copy(k, t).wait_send()
        ring.drain(t)


def mixer(nin, mixed, weights, x, gain, o_gain):
    peers = lax.axis_size("head")
    total, width = x.shape
    values = mixed.shape[1]
    own_rows = total // peers
    subs = own_rows // SUB
    shape = jax.ShapeDtypeStruct
    sems = pltpu.SemaphoreType.DMA((peers, subs))
    return pl.pallas_call(
        functools.partial(mixer_kernel, peers),
        in_specs=[anywhere()] * 4 + [vmem()] * 2,
        out_specs=[anywhere()] * 3 + [vmem()],
        out_shape=[
            shape((total, values), f32),
            shape((total, values), bf16),
            shape((total, width), bf16),
            shape((own_rows, width), f32),
        ],
        scratch_shapes=[
            pltpu.VMEM((total, width), bf16),
            pltpu.VMEM((total, values), f32),
            pltpu.VMEM((width, 2 * values), bf16),
            pltpu.VMEM((own_rows, width), bf16),
            pltpu.VMEM((total, values), f32),
            pltpu.VMEM((total, values), bf16),
            pltpu.VMEM((peers, own_rows, width), bf16),
            pltpu.VMEM((peers, own_rows, width), bf16),
            pltpu.VMEM((total, width), bf16),
            pltpu.SemaphoreType.DMA((4,)),
            pltpu.SemaphoreType.DMA((3, peers)),
        ]
        + [sems] * 4,
        compiler_params=pltpu.CompilerParams(
            collective_id=1, has_side_effects=True, vmem_limit_bytes=48 * 2**20
        ),
        name="mixer",
    )(nin, mixed, weights, x, gain, o_gain)


def ffn_kernel(
    peers, nm_hbm, ffn_hbm, ct_hbm, normed_hbm, weights_hbm, hidden_ref, gain_ref,
    grads_hbm, ffnp_hbm, ng_hbm, hgrad_ref, gpart_ref,
    nm, ffn_v, ct_v, normed_v, wout_v, act, dgu, send2, recv2, dm, ffnp_v, grads_v, ng_v,
    in_sem, out_sem, ss, rs, gather_send, gather_recv,
):
    me = lax.axis_index("head")
    total, width = nm.shape
    values = normed_v.shape[1]
    own_rows = total // peers
    subs = own_rows // SUB
    cells = act.shape[1]
    tile = 256
    loads = [
        pltpu.make_async_copy(ffn_hbm, ffn_v, in_sem.at[0]),
        pltpu.make_async_copy(nm_hbm, nm, in_sem.at[1]),
        pltpu.make_async_copy(ct_hbm, ct_v, in_sem.at[2]),
        pltpu.make_async_copy(normed_hbm, normed_v, in_sem.at[3]),
        pltpu.make_async_copy(weights_hbm.at[:, pl.ds(values, values)], wout_v, in_sem.at[4]),
    ]
    for load in loads:
        load.start()
    greet_heads(me, peers)
    for load in loads[:3]:
        load.wait()
    gain = gain_ref[...]
    sums = Summed(send2, recv2, me, ss, rs)

    def feed_forward(i, carry):
        k = lax.rem(i + peers - 1, peers)
        rows = pl.ds(pl.multiple_of((me ^ k) * own_rows, own_rows), own_rows)

        def cell_tile(j, carry):
            at = pl.ds(pl.multiple_of(j * tile, tile), tile)
            at_up = pl.ds(pl.multiple_of(cells + j * tile, tile), tile)
            at_down = pl.ds(pl.multiple_of(2 * cells + j * tile, tile), tile)
            gate = mm(nm[rows, :], ffn_v[:, at])
            up = mm(nm[rows, :], ffn_v[:, at_up])
            dact = mm(ct_v[rows, :], ffn_v[:, at_down])
            sig = sigmoid(gate)
            silu = gate * sig
            act[rows, at] = (silu * up).astype(bf16)
            dgu[rows, at] = (dact * up * sig * (1.0 + gate * (1.0 - sig))).astype(bf16)
            dgu[rows, at_up] = (dact * silu).astype(bf16)
            return carry

        lax.fori_loop(0, cells // tile, cell_tile, 0)

        def mid_tile(j, carry):
            at = pl.ds(pl.multiple_of(j * tile, tile), tile)
            send2[k, :, at] = mm(dgu[rows, :], ffn_v[at, 0 : 2 * cells], NT).astype(bf16)
            return carry

        lax.fori_loop(0, width // tile, mid_tile, 0)

        @pl.when(k > 0)
        def _():
            for t in range(subs):
                sums.copy(k, t).start()

        return carry

    lax.fori_loop(0, peers, feed_forward, 0)

    def ffn_rows(i, carry):
        rows = pl.ds(pl.multiple_of(i * own_rows, own_rows), own_rows)
        ffnp_v[rows, :] = mm(act[rows, :], ffn_v[:, 2 * cells :], NT).astype(bf16)
        block_store(i, own_rows, ffnp_v, ffnp_hbm, out_sem.at[0]).start()
        return carry

    lax.fori_loop(0, peers, ffn_rows, 0)
    ring = Spread(dm, own_rows, me, gather_send, gather_recv, SUB)
    gain_part = jnp.zeros((1, width), f32)
    for t in range(subs):
        rows = rows_of(t)
        dmid = sums.collect(t, peers)
        hidden = hidden_ref[rows, :]
        inverse = lax.rsqrt(jnp.mean(hidden * hidden, axis=1, keepdims=True) + epsilon)
        scaled = hidden * inverse
        weighted = dmid * gain
        grad = part(ct_v, me * own_rows + t * SUB, SUB)[...].astype(f32) + inverse * (
            weighted - scaled * jnp.mean(weighted * scaled, axis=1, keepdims=True)
        )
        hgrad_ref[rows, :] = grad
        part(dm, me * own_rows + t * SUB, SUB)[...] = grad.astype(bf16)
        ring.start(t)
        gain_part = gain_part + jnp.sum(dmid * scaled, axis=0, keepdims=True)
    gpart_ref[...] = jnp.broadcast_to(gain_part, gpart_ref.shape)

    def cell_grads(i, carry):
        at = pl.ds(pl.multiple_of(i * tile, tile), tile)
        grads_v[at, 0 : 2 * cells] = mm(nm[:, at], dgu[...], TN).astype(bf16)
        grads_v[at, 2 * cells : 3 * cells] = mm(ct_v[:, at], act[...], TN).astype(bf16)
        return carry

    half = width // tile // 2
    lax.fori_loop(0, half, cell_grads, 0)
    loads[3].wait()
    loads[4].wait()
    for t in range(subs):
        ring.forward(t)
    lax.fori_loop(half, width // tile, cell_grads, 0)

    def norm_rows(k, carry):
        owner = me ^ k

        @pl.when(k == peers - 1)
        def _():
            for t in range(subs):
                ring.finish(t)

        rows = pl.ds(pl.multiple_of(owner * own_rows, own_rows), own_rows)
        ng_v[rows, :] = mm(dm[rows, :], wout_v[...])
        block_store(owner, own_rows, ng_v, ng_hbm, out_sem.at[1]).start()
        return carry

    lax.fori_loop(0, peers, norm_rows, 0)

    def out_grads(i, carry):
        at = pl.ds(pl.multiple_of(i * tile, tile), tile)
        grads_v[at, 3 * cells :] = mm(dm[:, at], normed_v[...], TN).astype(bf16)
        block_store(i, tile, grads_v, grads_hbm, out_sem.at[2]).start()
        return carry

    lax.fori_loop(0, width // tile, out_grads, 0)
    for i in range(peers):
        block_store(i, own_rows, ffnp_v, ffnp_hbm, out_sem.at[0]).wait()
        block_store(i, own_rows, ng_v, ng_hbm, out_sem.at[1]).wait()
    for i in range(width // tile):
        block_store(i, tile, grads_v, grads_hbm, out_sem.at[2]).wait()
    for t in range(subs):
        for k in range(1, peers):
            sums.copy(k, t).wait_send()
        ring.drain(t)


def feed_forward_block(nm, ffn_full, ct, normed, weights, hidden, gain):
    peers = lax.axis_size("head")
    total, width = ct.shape
    own_rows = total // peers
    subs = own_rows // SUB
    values = normed.shape[1]
    cells = ffn_full.shape[1] // 3
    shape = jax.ShapeDtypeStruct
    sems = pltpu.SemaphoreType.DMA((peers, subs))
    return pl.pallas_call(
        functools.partial(ffn_kernel, peers),
        in_specs=[anywhere()] * 5 + [vmem()] * 2,
        out_specs=[anywhere()] * 3 + [vmem()] * 2,
        out_shape=[
            shape((width, 3 * cells + values), bf16),
            shape((total, width), bf16),
            shape((total, values), f32),
            shape((own_rows, width), f32),
            shape((8, width), f32),
        ],
        scratch_shapes=[
            pltpu.VMEM((total, width), bf16),
            pltpu.VMEM((width, 3 * cells), bf16),
            pltpu.VMEM((total, width), bf16),
            pltpu.VMEM((total, values), bf16),
            pltpu.VMEM((width, values), bf16),
            pltpu.VMEM((total, cells), bf16),
            pltpu.VMEM((total, 2 * cells), bf16),
            pltpu.VMEM((peers, own_rows, width), bf16),
            pltpu.VMEM((peers, own_rows, width), bf16),
            pltpu.VMEM((total, width), bf16),
            pltpu.VMEM((total, width), bf16),
            pltpu.VMEM((width, 3 * cells + values), bf16),
            pltpu.VMEM((total, values), f32),
            pltpu.SemaphoreType.DMA((5,)),
            pltpu.SemaphoreType.DMA((3, max(peers, width // 256))),
        ]
        + [sems] * 4,
        compiler_params=pltpu.CompilerParams(
            collective_id=5, has_side_effects=True, vmem_limit_bytes=56 * 2**20
        ),
        name="feed_forward",
    )(nm, ffn_full, ct, normed, weights, hidden, gain)


def input_grad_kernel(
    peers, places, cores, dp_hbm, win_hbm, wog_hbm, x_hbm, hgrad_ref, gain_ref, gains_ref,
    channels_ref,
    out_hbm, gains_out, channels_out,
    dp_v, win_v, wog_v, x_v, send1, recv1, whole, gains_v, gains_recv, gains_sum, gains_all,
    channels_all, in_sem, out_sem, ss1, rs1, gather_send, gather_recv,
    hs, hr, gs, gr, cs, cr,
):
    me = lax.axis_index("head")
    place, core = lax.axis_index("seq"), lax.axis_index("batch")
    total, width = whole.shape
    own_rows = total // peers
    subs = own_rows // SUB
    values = wog_v.shape[1]
    conv_cols = win_v.shape[1] - PAD
    group = places * cores
    flat = place * cores + core
    loads = [
        pltpu.make_async_copy(dp_hbm, dp_v, in_sem.at[0]),
        pltpu.make_async_copy(win_hbm, win_v, in_sem.at[1]),
        pltpu.make_async_copy(wog_hbm.at[:, pl.ds(0, values)], wog_v, in_sem.at[2]),
        pltpu.make_async_copy(part(x_hbm, me * own_rows, own_rows), x_v, in_sem.at[3]),
    ]
    for load in loads:
        load.start()

    def to_group(d, source, target, send_sem, recv_sem):
        to = lax.rem(flat + d, group)
        return pltpu.make_async_remote_copy(
            src_ref=source, dst_ref=target.at[d], send_sem=send_sem.at[d],
            recv_sem=recv_sem.at[d], device_id={"seq": to // cores, "batch": lax.rem(to, cores)},
            device_id_type=MESH,
        )

    barrier = pltpu.get_barrier_semaphore()
    for k in range(1, peers):
        pl.semaphore_signal(barrier, inc=1, device_id={"head": me ^ k}, device_id_type=MESH)
    for d in range(1, group):
        to = lax.rem(flat + d, group)
        pl.semaphore_signal(
            barrier, inc=1, device_id={"seq": to // cores, "batch": lax.rem(to, cores)},
            device_id_type=MESH,
        )
    pl.semaphore_wait(barrier, peers + group - 2)
    for load in loads[:3]:
        load.wait()
    sums = Summed(send1, recv1, me, ss1, rs1)

    def project(i, carry):
        k = peers - 1 - i
        rows = pl.ds(pl.multiple_of((me ^ k) * own_rows, own_rows), own_rows)
        partial = mm(dp_v[rows, 0:conv_cols], win_v[:, 0:conv_cols], NT)
        partial = partial + mm(
            dp_v[rows, conv_cols : conv_cols + values], wog_v[...], NT
        )
        partial = partial + mm(dp_v[rows, conv_cols + values :], win_v[:, conv_cols:], NT)
        send1[k] = partial.astype(bf16)

        @pl.when(k > 0)
        def _():
            for t in range(subs):
                sums.copy(k, t).start()

        return carry

    lax.fori_loop(0, peers, project, 0)
    for d in range(1, group):
        to_group(d, channels_ref, channels_all, cs, cr).start()
    loads[3].wait()
    gain = gain_ref[...]
    ring = Spread(whole, own_rows, me, gather_send, gather_recv, SUB)
    gain_part = jnp.zeros((1, width), f32)
    for t in range(subs):
        rows = rows_of(t)
        din = sums.collect(t, peers)
        x = x_v[rows, :].astype(f32)
        inverse = lax.rsqrt(jnp.mean(x * x, axis=1, keepdims=True) + epsilon)
        scaled = x * inverse
        weighted = din * gain
        grad = hgrad_ref[rows, :] + inverse * (
            weighted - scaled * jnp.mean(weighted * scaled, axis=1, keepdims=True)
        )
        part(whole, me * own_rows + t * SUB, SUB)[...] = grad.astype(bf16)
        ring.start(t)
        gain_part = gain_part + jnp.sum(din * scaled, axis=0, keepdims=True)
    row8 = lax.broadcasted_iota(jnp.int32, (8, width), 0)
    gains_v[...] = jnp.where(row8 == 0, gain_part, gains_ref[...])

    def gains_copy(k):
        return head_copy(gains_v, gains_recv.at[k], hs.at[k], hr.at[k], me ^ k)

    for k in range(1, peers):
        gains_copy(k).start()
    block_store(me, own_rows, whole, out_hbm, out_sem).start()
    gathered = gains_v[...]
    for k in range(1, peers):
        gains_copy(k).wait_recv()
        gathered = gathered + gains_recv[k]
    gains_sum[...] = gathered
    for d in range(1, group):
        to_group(d, gains_sum, gains_all, gs, gr).start()
    for t in range(subs):
        ring.forward(t)
    block_store(me ^ 1, own_rows, whole, out_hbm, out_sem).start()
    block_store(me ^ 2, own_rows, whole, out_hbm, out_sem).start()
    channels = channels_ref[...]
    for d in range(1, group):
        to_group(d, channels_ref, channels_all, cs, cr).wait_recv()
        channels = channels + channels_all[d]
    channels_out[...] = channels
    for d in range(1, group):
        to_group(d, gains_sum, gains_all, gs, gr).wait_recv()
        gathered = gathered + gains_all[d]
    gains_out[...] = gathered
    for t in range(subs):
        ring.finish(t)
    block_store(me ^ 3, own_rows, whole, out_hbm, out_sem).start()
    for k in range(peers):
        block_store(k, own_rows, whole, out_hbm, out_sem).wait()
    for t in range(subs):
        for k in range(1, peers):
            sums.copy(k, t).wait_send()
        ring.drain(t)
    for k in range(1, peers):
        gains_copy(k).wait_send()
    for d in range(1, group):
        to_group(d, channels_ref, channels_all, cs, cr).wait_send()
        to_group(d, gains_sum, gains_all, gs, gr).wait_send()


def input_grads(dp, in_full, gate_full, x, hgrad, gain, gains, channels):
    peers, places, cores = lax.axis_size("head"), lax.axis_size("seq"), lax.axis_size("batch")
    group = places * cores
    total, width = x.shape
    cols = dp.shape[1]
    values = gate_full.shape[1] // 2
    own_rows = total // peers
    subs = own_rows // SUB
    shape = jax.ShapeDtypeStruct
    sems = pltpu.SemaphoreType.DMA((peers, subs))
    per_peer = pltpu.SemaphoreType.DMA((peers,))
    per_member = pltpu.SemaphoreType.DMA((group,))
    return pl.pallas_call(
        functools.partial(input_grad_kernel, peers, places, cores),
        in_specs=[anywhere()] * 4 + [vmem()] * 4,
        out_specs=[anywhere(), vmem(), vmem()],
        out_shape=[
            shape((total, width), bf16), shape(gains.shape, f32), shape(channels.shape, f32),
        ],
        scratch_shapes=[
            pltpu.VMEM((total, cols), bf16),
            pltpu.VMEM((width, cols - values), bf16),
            pltpu.VMEM((width, values), bf16),
            pltpu.VMEM((own_rows, width), bf16),
            pltpu.VMEM((peers, own_rows, width), bf16),
            pltpu.VMEM((peers, own_rows, width), bf16),
            pltpu.VMEM((total, width), bf16),
            pltpu.VMEM(gains.shape, f32),
            pltpu.VMEM((peers,) + gains.shape, f32),
            pltpu.VMEM(gains.shape, f32),
            pltpu.VMEM((group,) + gains.shape, f32),
            pltpu.VMEM((group,) + channels.shape, f32),
            pltpu.SemaphoreType.DMA((4,)),
            pltpu.SemaphoreType.DMA((peers,)),
        ]
        + [sems] * 4
        + [per_peer] * 2
        + [per_member] * 4,
        compiler_params=pltpu.CompilerParams(
            collective_id=2, has_side_effects=True, vmem_limit_bytes=48 * 2**20
        ),
        name="input_grads",
    )(dp, in_full, gate_full, x, hgrad, gain, gains, channels)


def shifted(shard, axis, by):
    count = lax.axis_size(axis)
    pairs = [(i, i + by) for i in range(count) if 0 <= i + by < count]
    return lax.ppermute(shard, axis, pairs)


def root_scale(value_rows):
    return lax.rsqrt(jnp.mean(value_rows * value_rows, axis=-1, keepdims=True) + epsilon)


def matmul(a, b, dims=NN):
    return lax.dot_general(a, b, (dims, ((), ())), preferred_element_type=f32)


ALL = ("seq", "batch")


def per_device(
    tokens, starts, attn_gain, w_in, w_rates, conv_w, decay_par, o_gain, w_out, ffn_gain, w_gu,
    w_down, cotangent,
):
    seqs, length, width = tokens.shape
    shard, heads = w_in.shape[:2]
    shards = width // shard
    total = seqs * length
    conv_cols = heads * QKV
    value_cols = heads * DV
    units = w_down.shape[0]
    cells = -(-units // 256) * 256
    spare = cells - units

    packed_in = jnp.concatenate(
        [
            w_in[:, :, :QKV].reshape(shard, conv_cols),
            w_rates.reshape(shard, 2 * heads),
            jnp.zeros((shard, PAD - 2 * heads), f32),
        ],
        axis=1,
    ).astype(bf16)
    packed_gate = jnp.concatenate(
        [w_in[:, :, QKV:].reshape(shard, value_cols), w_out.reshape(value_cols, -1).T], axis=1
    ).astype(bf16)
    packed_ffn = jnp.pad(
        jnp.stack([w_gu[:, 0], w_gu[:, 1], w_down.T], axis=1).astype(bf16),
        ((0, 0), (0, 0), (0, spare)),
    ).reshape(shard, 3 * cells)
    conv_flat = conv_w.reshape(-1)
    small = jnp.concatenate([attn_gain, ffn_gain, conv_flat, o_gain]).astype(bf16)

    x = tokens.reshape(total, width)
    ct = cotangent.reshape(total, width)
    before = shifted(tokens[:, length - HALO :], "seq", 1).reshape(seqs * HALO, width)
    in_full = lax.all_gather(packed_in, ALL, axis=0, tiled=True)
    small_full = lax.all_gather(small, ALL, axis=0)
    gate_full = lax.all_gather(packed_gate, ALL, axis=0, tiled=True)
    ffn_full = lax.all_gather(packed_ffn, ALL, axis=0, tiled=True)
    attn_gain_f = small_full[:, :shard].reshape(1, width).astype(f32)
    ffn_gain_f = small_full[:, shard : 2 * shard].reshape(1, width).astype(f32)
    conv_end = 2 * shard + conv_flat.shape[0]
    conv_full = (
        small_full[:, 2 * shard : conv_end]
        .reshape(shards, CONV, heads, -1)
        .transpose(1, 2, 0, 3)
        .reshape(CONV, conv_cols)
        .astype(f32)
    )
    o_gain_full = small_full[:, conv_end:].reshape(1, DV).astype(f32)

    def normed_rows(rows):
        rows = rows.astype(f32)
        return (rows * root_scale(rows) * attn_gain_f).astype(bf16)

    normed_in = normed_rows(x)
    projected = matmul(normed_in, in_full)
    halo = matmul(normed_rows(before), in_full[:, :conv_cols]).reshape(seqs, HALO, conv_cols)
    qkv, inv, n, qe, tot, trans, states, mixed = forward_rule(
        starts, decay_par, projected, halo, conv_full, seqs, heads
    )
    og, normed, nm, hidden = mixer(
        normed_in, mixed, gate_full, x, ffn_gain_f, o_gain_full
    )
    late_grads, ffn_part, normed_grad, hidden_grad, ffn_gain_part = feed_forward_block(
        nm, ffn_full, ct, normed, gate_full, hidden, ffn_gain_f
    )
    late_own = lax.psum_scatter(late_grads, ALL, scatter_dimension=0, tiled=True)
    projected_grad, dconv, ddecay, onorm_grads, result = backward_rule(
        starts, decay_par, normed_grad, mixed, og, projected, o_gain_full, n, qe, tot, trans, qkv,
        inv, states, halo, conv_full, hidden, ffn_part, seqs, heads,
    )
    in_grad = matmul(normed_in, projected_grad, TN).astype(bf16)
    in_grad, late_own = lax.optimization_barrier((in_grad, late_own))
    in_own = lax.psum_scatter(in_grad, ALL, scatter_dimension=0, tiled=True)

    onorm_grad = jnp.sum(onorm_grads[:, 0], axis=0)
    decay_part = jnp.sum(ddecay[:, :2, 0].reshape(heads, seqs, 2), axis=1).T
    conv_grad = jnp.sum(dconv.reshape(heads, seqs, CONV, QKV), axis=1).transpose(1, 0, 2)
    gains = jnp.concatenate(
        [
            jnp.zeros((1, width), f32),
            ffn_gain_part[:1],
            jnp.pad(onorm_grad, (0, width - DV))[None],
            jnp.zeros((5, width), f32),
        ]
    )
    taps = CONV * heads
    channels = jnp.concatenate(
        [
            conv_grad.reshape(taps, QKV),
            jnp.pad(decay_part.reshape(1, 2 * heads), ((0, 7), (0, QKV - 2 * heads))),
        ]
    )
    input_grad, gains, channels = input_grads(
        projected_grad, in_full, gate_full, x, hidden_grad, attn_gain_f, gains, channels
    )
    at = lax.axis_index(ALL)
    own_gains = lax.dynamic_slice(gains, (0, at * shard), (2, shard))
    onorm_own = lax.dynamic_slice(gains, (2, at * (DV // shards)), (1, DV // shards))
    conv_own = lax.dynamic_slice(
        channels, (0, at * (QKV // shards)), (taps, QKV // shards)
    ).reshape(CONV, heads, -1)
    in_own = in_own.astype(f32)
    late_own = late_own.astype(f32)
    in_main = jnp.concatenate(
        [
            in_own[:, :conv_cols].reshape(shard, heads, QKV),
            in_own[:, conv_cols : conv_cols + value_cols].reshape(shard, heads, DV),
        ],
        axis=2,
    )
    rates_at = conv_cols + value_cols
    return (
        result.reshape(tokens.shape),
        input_grad.reshape(tokens.shape),
        own_gains[0],
        in_main,
        in_own[:, rates_at : rates_at + 2 * heads].reshape(shard, heads, 2),
        conv_own,
        channels[taps, : 2 * heads].reshape(2, heads),
        onorm_own[0],
        late_own[:, 3 * cells :].T.reshape(heads, DV, -1),
        own_gains[1],
        late_own[:, : 2 * cells].reshape(shard, 2, cells)[:, :, :units],
        late_own[:, 2 * cells : 2 * cells + units].T,
    )


def solution(mesh):
    weights = P(ALL)
    in_specs = (
        P("batch", "seq", None),
        P("batch"),
        weights,
        P(ALL, "head", None),
        P(ALL, "head", None),
        P(None, "head", ALL),
        P(None, "head"),
        weights,
        P("head", None, ALL),
        weights,
        P(ALL, None, "head"),
        P("head", ALL),
        P("batch", "seq", None),
    )
    out_specs = (
        P("batch", "seq", None),
        P("batch", "seq", None),
        weights,
        P(ALL, "head", None),
        P(ALL, "head", None),
        P(None, "head", ALL),
        P(None, "head"),
        weights,
        P("head", None, ALL),
        weights,
        P(ALL, None, "head"),
        P("head", ALL),
    )
    return jax.shard_map(
        per_device, mesh=mesh, in_specs=in_specs, out_specs=out_specs, check_vma=False
    )
```

```python
import functools

import jax
import jax.numpy as jnp
from jax import lax
from jax.experimental import pallas as pl
from jax.experimental.pallas import tpu as pltpu
from jax.sharding import PartitionSpec as P

DK = 128
DV = 256
CONV = 4
QKV = 2 * DK + DV
CHUNK = 128
HALO = 16
PAD = 128

bf16 = jnp.bfloat16
f32 = jnp.float32
epsilon = 1e-06
NN = ((1,), (0,))
NT = ((1,), (1,))
TN = ((0,), (0,))


def mm(a, b, dims=NN):
    return lax.dot_general(
        a.astype(bf16), b.astype(bf16), (dims, ((), ())), preferred_element_type=f32
    )


def split_mm(a, b):
    a_high, b_high = a.astype(bf16), b.astype(bf16)
    a_low = (a - a_high.astype(f32)).astype(bf16)
    b_low = (b - b_high.astype(f32)).astype(bf16)
    return mm(a_high, b_high) + (mm(a_high, b_low) + mm(a_low, b_high))


def iotas(n):
    return (
        lax.broadcasted_iota(jnp.int32, (n, n), 0),
        lax.broadcasted_iota(jnp.int32, (n, n), 1),
    )


def unit_lower_inverses(mats):
    n = mats[0].shape[0]
    rows, cols = iotas(n)
    eye = (rows == cols).astype(f32)
    pair = ((rows >> 1) == (cols >> 1)) & (rows > cols)
    inverses = [eye - jnp.where(pair, a, 0.0) for a in mats]
    shift = 1
    while (1 << shift) < n:
        corner = ((rows >> (shift + 1)) == (cols >> (shift + 1))) & (
            (rows >> shift) > (cols >> shift)
        )
        firsts = [mm(jnp.where(corner, a, 0.0), x) for a, x in zip(mats, inverses)]
        inverses = [x - mm(x, y) for x, y in zip(inverses, firsts)]
        shift += 1
    residuals = [eye - x - split_mm(a, x) for a, x in zip(mats, inverses)]
    return [x + mm(x, r) for x, r in zip(inverses, residuals)]


def sigmoid(v):
    return 1.0 / (1.0 + jnp.exp(-v))


def softplus(v):
    small = jnp.exp(-jnp.abs(v))
    one_more = 1.0 + small
    gap = one_more - 1.0
    exact = gap == 0.0
    tail = jnp.where(exact, small, jnp.log(one_more) * small / jnp.where(exact, 1.0, gap))
    return jnp.maximum(v, 0.0) + tail


def to_row(column, eye):
    return jnp.sum(jnp.where(eye, column, 0.0), axis=0, keepdims=True)


def pick(block, lane):
    lanes = lax.broadcasted_iota(jnp.int32, block.shape, 1)
    return jnp.sum(jnp.where(lanes == lane, block, 0.0), axis=1, keepdims=True)


def gates(logits, decay_ref, head):
    rate = jnp.exp(jnp.full((1, 1), decay_ref[0, head], f32))
    shifted_logit = pick(logits, 2 * head) + decay_ref[1, head]
    strength = sigmoid(pick(logits, 2 * head + 1))
    log_gate = -rate * softplus(shifted_logit)
    return log_gate, strength, rate, shifted_logit


def decays(log_gate, lower, upper, eye):
    gate_row = to_row(log_gate, eye)
    column = jnp.sum(jnp.where(lower, gate_row, 0.0), axis=1, keepdims=True)
    row = jnp.sum(jnp.where(upper, log_gate, 0.0), axis=0, keepdims=True)
    ratio = jnp.where(lower, jnp.exp(jnp.where(lower, column - row, 0.0)), 0.0)
    total = jnp.sum(log_gate, axis=0, keepdims=True)
    return column, total, ratio


def load_conv_input(main_ref, halo_ref, start, x_scr, first):
    length = main_ref.shape[0]
    positions = first + lax.broadcasted_iota(jnp.int32, (length, 1), 0)
    live = (positions >= start).astype(f32)
    before = first - HALO + lax.broadcasted_iota(jnp.int32, (HALO, 1), 0)
    lived = (before >= start).astype(f32)
    x_scr[pl.ds(0, HALO), :] = (halo_ref[0] * lived).astype(bf16).astype(f32)
    x_scr[pl.ds(HALO, length), :] = (main_ref[...] * live).astype(bf16).astype(f32)


def convolve(x_scr, conv, at):
    total = x_scr[pl.ds(at + HALO - CONV + 1, CHUNK), :] * conv[0:1]
    for j in range(1, CONV):
        total = total + x_scr[pl.ds(at + HALO - CONV + 1 + j, CHUNK), :] * conv[j : j + 1]
    return total


def unit(rows):
    return rows * lax.rsqrt(jnp.sum(rows * rows, axis=1, keepdims=True) + epsilon)


MESH = pl.DeviceIdType.MESH
SUB = 128


def head_copy(src, dst, send_sem, recv_sem, peer):
    return pltpu.make_async_remote_copy(
        src_ref=src, dst_ref=dst, send_sem=send_sem, recv_sem=recv_sem,
        device_id={"head": peer}, device_id_type=MESH,
    )


def greet_heads(me, peers):
    barrier = pltpu.get_barrier_semaphore()
    for k in range(1, peers):
        pl.semaphore_signal(barrier, inc=1, device_id={"head": me ^ k}, device_id_type=MESH)
    pl.semaphore_wait(barrier, peers - 1)


def part(ref, start, size):
    return ref.at[pl.ds(pl.multiple_of(start, size), size)]


class Spread:
    def __init__(self, buffer, size, me, send_sem, recv_sem, piece=None):
        self.buffer, self.size, self.me = buffer, size, me
        self.piece = size if piece is None else piece
        self.send_sem, self.recv_sem = send_sem, recv_sem

    def region(self, owner, t, half):
        rows = pl.ds(pl.multiple_of(owner * self.size + t * self.piece, self.piece), self.piece)
        middle = self.buffer.shape[1] // 2
        if half is None:
            return self.buffer.at[rows]
        return self.buffer.at[rows, pl.ds(half * middle, middle)]

    def copy(self, kind, t, owner):
        at = self.region(owner, t, None if kind < 2 else kind - 2)
        to = self.me ^ (1 if kind in (0, 3) else 2)
        return head_copy(at, at, self.send_sem.at[kind, t], self.recv_sem.at[kind, t], to)

    def start(self, t):
        self.copy(0, t, self.me).start()
        self.copy(1, t, self.me).start()

    def forward(self, t):
        self.copy(0, t, self.me ^ 1).wait_recv()
        self.copy(2, t, self.me ^ 1).start()
        self.copy(1, t, self.me ^ 2).wait_recv()
        self.copy(3, t, self.me ^ 2).start()

    def finish(self, t):
        self.copy(2, t, self.me ^ 3).wait_recv()
        self.copy(3, t, self.me ^ 3).wait_recv()

    def drain(self, t):
        for kind, owner in enumerate((0, 0, 1, 2)):
            self.copy(kind, t, self.me ^ owner).wait_send()


class Combine:
    def __init__(self, send, recv, relay, me, send_sem, recv_sem, piece):
        self.send, self.recv, self.relay, self.me = send, recv, relay, me
        self.send_sem, self.recv_sem, self.piece = send_sem, recv_sem, piece
        self.middle = send.shape[2] // 2

    def rows(self, t):
        return pl.ds(pl.multiple_of(t * self.piece, self.piece), self.piece)

    def copy(self, kind, t):
        rows, low, high = self.rows(t), pl.ds(0, self.middle), pl.ds(self.middle, self.middle)
        source, target, to = (
            (self.send.at[3, rows, low], self.relay.at[0, rows], 1),
            (self.send.at[3, rows, high], self.relay.at[1, rows], 2),
            (self.send.at[1, rows, low], self.recv.at[0, rows, low], 1),
            (self.send.at[2, rows, high], self.recv.at[1, rows, high], 2),
            (self.send.at[1, rows, high], self.recv.at[0, rows, high], 1),
            (self.send.at[2, rows, low], self.recv.at[1, rows, low], 2),
        )[kind]
        return head_copy(
            source, target, self.send_sem.at[kind, t], self.recv_sem.at[kind, t], self.me ^ to
        )

    def start(self, k, t):
        if k == 3:
            self.copy(0, t).start()
            self.copy(1, t).start()
        else:
            self.copy(k + 1, t).start()

    def combine(self, t):
        rows = self.rows(t)
        for k, at in ((1, pl.ds(self.middle, self.middle)), (2, pl.ds(0, self.middle))):
            self.copy(2 - k, t).wait_recv()
            both = self.send[k, rows, at].astype(f32) + self.relay[2 - k, rows, :].astype(f32)
            self.send[k, rows, at] = both.astype(bf16)
            self.copy(3 + k, t).start()

    def collect(self, t):
        for kind in range(2, 6):
            self.copy(kind, t).wait_recv()
        return self.total(self.rows(t))

    def total(self, rows):
        return (
            self.send[0, rows, :].astype(f32)
            + self.recv[0, rows, :].astype(f32)
            + self.recv[1, rows, :].astype(f32)
        )

    def drain(self, t):
        for kind in range(6):
            self.copy(kind, t).wait_send()


def sum_buffers(rows, width, pieces):
    return [
        pltpu.VMEM((4, rows, width), bf16),
        pltpu.VMEM((2, rows, width), bf16),
        pltpu.VMEM((2, rows, width // 2), bf16),
        pltpu.SemaphoreType.DMA((6, pieces)),
        pltpu.SemaphoreType.DMA((6, pieces)),
        pltpu.SemaphoreType.DMA((4, pieces)),
        pltpu.SemaphoreType.DMA((4, pieces)),
    ]


class GroupScatter:
    def __init__(self, source, columns, core_recv, seq_send, seq_recv, sems):
        self.source, self.columns = source, columns
        self.core_recv, self.seq_send, self.seq_recv, self.sems = core_recv, seq_send, seq_recv, sems
        self.place, self.core = lax.axis_index("seq"), lax.axis_index("batch")
        self.places, self.shard = core_recv.shape[0], core_recv.shape[1]

    def rows(self, k, core):
        at = ((self.place ^ k) * 2 + core) * self.shard
        return pl.ds(pl.multiple_of(at, self.shard), self.shard)

    def core_copy(self, k):
        return along(
            "batch", self.source.at[self.rows(k, 1 - self.core), self.columns],
            self.core_recv.at[k], self.sems.at[0, k], self.sems.at[1, k], 1 - self.core,
        )

    def seq_copy(self, k):
        return along(
            "seq", self.seq_send.at[k], self.seq_recv.at[k], self.sems.at[2, k],
            self.sems.at[3, k], self.place ^ k,
        )

    def pass_on(self, k):
        self.core_copy(k).wait_recv()
        own = self.source[self.rows(k, self.core), self.columns].astype(f32)
        self.seq_send[k] = (own + self.core_recv[k].astype(f32)).astype(bf16)

        @pl.when(k > 0)
        def _():
            self.seq_copy(k).start()

    def finish(self):
        total = self.seq_send[0].astype(f32)
        for k in range(1, self.places):
            self.seq_copy(k).wait_recv()
            total = total + self.seq_recv[k].astype(f32)
        return total

    def drain(self):
        for k in range(self.places):
            self.core_copy(k).wait_send()
        for k in range(1, self.places):
            self.seq_copy(k).wait_send()


def scatter_buffers(places, shard, columns):
    return [pltpu.VMEM((places, shard, columns), bf16)] * 3 + [
        pltpu.SemaphoreType.DMA((4, places))
    ]


def greet_group(me, peers, places, cores):
    barrier = pltpu.get_barrier_semaphore()
    group = places * cores
    flat = lax.axis_index("seq") * cores + lax.axis_index("batch")
    for k in range(1, peers):
        pl.semaphore_signal(barrier, inc=1, device_id={"head": me ^ k}, device_id_type=MESH)
    for d in range(1, group):
        to = lax.rem(flat + d, group)
        pl.semaphore_signal(
            barrier, inc=1, device_id={"seq": to // cores, "batch": lax.rem(to, cores)},
            device_id_type=MESH,
        )
    pl.semaphore_wait(barrier, peers + group - 2)


def anywhere():
    return pl.BlockSpec(memory_space=pl.ANY)


def vmem():
    return pl.BlockSpec(memory_space=pltpu.VMEM)


def along(axis, source, target, send_sem, recv_sem, to):
    return pltpu.make_async_remote_copy(
        src_ref=source, dst_ref=target, send_sem=send_sem, recv_sem=recv_sem,
        device_id={axis: to}, device_id_type=MESH,
    )


def forward_kernel(
    seqs, places, start_ref, decay_ref, main_ref, halo_ref, rate_ref, conv_ref,
    qkv_ref, inv_ref, n_ref, qe_ref, tot_ref, trans_ref, s_ref, mixed_ref,
    x_scr, b_scr, o_scr, carried_scr, send, recv, send_sem, recv_sem,
):
    step = pl.program_id(0)
    chains = n_ref.shape[0]
    count = n_ref.shape[1]
    length = main_ref.shape[0]
    place = lax.axis_index("seq")
    lag = jnp.minimum(place, chains - 1)

    @pl.when(step == 0)
    def _():
        barrier = pltpu.get_barrier_semaphore()

        @pl.when(place > 0)
        def _():
            pl.semaphore_signal(
                barrier, inc=1, device_id={"seq": place - 1}, device_id_type=MESH
            )

        @pl.when(place == 0)
        def _():
            recv[...] = jnp.zeros_like(recv)

        @pl.when(place < places - 1)
        def _():
            pl.semaphore_wait(barrier, 1)

    @pl.when(step < chains)
    def _():
        head = step // seqs
        load_conv_input(
            main_ref, halo_ref, start_ref[step % seqs], x_scr, place * length
        )
        conv = conv_ref[...]
        rows, cols = iotas(CHUNK)
        lower, upper, eye = rows >= cols, rows <= cols, rows == cols
        parts = []
        for c in range(count):
            at = c * CHUNK
            convolved = convolve(x_scr, conv, at)
            active = convolved * sigmoid(convolved)
            q = (unit(active[:, :DK]) * DK ** (-0.5)).astype(bf16)
            k = unit(active[:, DK : 2 * DK]).astype(bf16)
            v = active[:, 2 * DK :].astype(bf16)
            qkv_ref[pl.ds(at, CHUNK), 0:DK] = q
            qkv_ref[pl.ds(at, CHUNK), DK : 2 * DK] = k
            qkv_ref[pl.ds(at, CHUNK), 2 * DK :] = v
            log_gate, strength, _, _ = gates(rate_ref[pl.ds(at, CHUNK), :], decay_ref, head)
            column, total, ratio = decays(log_gate, lower, upper, eye)
            products = mm(jnp.concatenate([k, q], axis=0), k, NT)
            coupling = jnp.where(rows > cols, strength * ratio * products[:CHUNK], 0.0)
            scores = (ratio * products[CHUNK:]).astype(bf16)
            parts.append((q, k, v, strength, column, total, coupling, scores))
        inverses = unit_lower_inverses([p[6] for p in parts])
        maps = []
        for c in range(count):
            q, k, v, strength, column, total, _, scores = parts[c]
            growth = jnp.exp(column)
            kf, vf, qf = k.astype(f32), v.astype(f32), q.astype(f32)
            inverse = inverses[c].astype(bf16)
            inv_ref[0, c] = inverse
            target = jnp.concatenate([(strength * growth) * kf, strength * vf], axis=1)
            solved = mm(inverse, target).astype(bf16)
            read = mm(scores, solved)
            qe_ref[step, c] = (growth * qf - read[:, :DK]).astype(bf16)
            o_scr[step, pl.ds(c * CHUNK, CHUNK), :] = read[:, DK:]
            written = mm(jnp.exp(total - column) * kf, solved, TN)
            low_n = written[:, :DK].astype(bf16)
            n_ref[step, c] = low_n
            b_scr[step, c] = written[:, DK:]
            whole = jnp.exp(total)
            tot_ref[step, pl.ds(c, 1), :] = jnp.broadcast_to(whole, (1, DK))
            maps.append((low_n, written[:, DK:], whole))
        low_n, b, whole = maps[0]
        trans = whole * eye.astype(f32) - low_n.astype(f32)
        carried = b
        for low_n, b, whole in maps[1:]:
            both = jnp.concatenate([trans, carried], axis=1)
            moved = whole * both - mm(low_n, both)
            trans = moved[:, :DK]
            carried = moved[:, DK:] + b
        trans_ref[step] = trans.astype(bf16)
        carried_scr[step] = carried

    @pl.when(step >= chains)
    def _():
        chain = jnp.maximum(step - chains, 0)
        state = recv[chain].astype(f32)
        for c in range(count):
            low_state = state.astype(bf16)
            s_ref[0, c] = low_state
            both = mm(jnp.concatenate([n_ref[chain, c], qe_ref[chain, c]], axis=0), low_state)
            whole = tot_ref[chain, pl.ds(c, 1), 0:1]
            state = whole * state - both[:DK] + b_scr[chain, c]
            at = pl.ds(c * CHUNK, CHUNK)
            mixed_ref[at, :] = o_scr[chain, at, :] + both[DK:]

    def passed(chain):
        return along(
            "seq", send.at[chain], recv.at[chain], send_sem.at[chain], recv_sem.at[chain],
            jnp.minimum(place + 1, places - 1),
        )

    relayed = step - lag

    @pl.when((relayed >= 0) & (relayed < chains))
    def _():
        chain = jnp.clip(relayed, 0, chains - 1)

        @pl.when(place > 0)
        def _():
            passed(chain).wait_recv()

        @pl.when(place < places - 1)
        def _():
            leaving = mm(trans_ref[chain], recv[chain]) + carried_scr[chain]
            send[chain] = leaving.astype(bf16)
            passed(chain).start()

    @pl.when((step == 2 * chains - 1) & (place < places - 1))
    def _():
        for chain in range(chains):
            passed(chain).wait_send()


def early(chains, make):
    return lambda j: make(jnp.minimum(j, chains - 1))


def late(chains, make):
    return lambda j: make(jnp.maximum(j - chains, 0))


def forward_rule(starts, decay_par, projected, halo, conv_w, seqs, heads):
    places = lax.axis_size("seq")
    chains = seqs * heads
    length = projected.shape[0] // seqs
    count = length // CHUNK
    rates_at = heads * QKV // PAD
    row = lambda first: lambda i: (i % seqs, first + i // seqs)
    whole = lambda *dims: pl.BlockSpec(dims, lambda j: (0,) * len(dims))
    shape = jax.ShapeDtypeStruct
    return pl.pallas_call(
        functools.partial(forward_kernel, seqs, places),
        grid=(2 * chains,),
        in_specs=[
            smem(),
            smem(),
            pl.BlockSpec((length, QKV), early(chains, row(0))),
            pl.BlockSpec((1, HALO, QKV), early(chains, lambda i: (i % seqs, 0, i // seqs))),
            pl.BlockSpec((length, PAD), early(chains, lambda i: (i % seqs, rates_at))),
            pl.BlockSpec((CONV, QKV), early(chains, lambda i: (0, i // seqs))),
        ],
        out_specs=[
            pl.BlockSpec((length, QKV), early(chains, row(0))),
            pl.BlockSpec((1, count, CHUNK, CHUNK), early(chains, lambda i: (i, 0, 0, 0))),
            whole(chains, count, DK, DK),
            whole(chains, count, CHUNK, DK),
            whole(chains, count, DK),
            whole(chains, DK, DK),
            pl.BlockSpec((1, count, DK, DV), late(chains, lambda i: (i, 0, 0, 0))),
            pl.BlockSpec((length, DV), late(chains, row(0))),
        ],
        out_shape=[
            shape((seqs * length, heads * QKV), bf16),
            shape((chains, count, CHUNK, CHUNK), bf16),
            shape((chains, count, DK, DK), bf16),
            shape((chains, count, CHUNK, DK), bf16),
            shape((chains, count, DK), f32),
            shape((chains, DK, DK), bf16),
            shape((chains, count, DK, DV), bf16),
            shape((seqs * length, heads * DV), f32),
        ],
        scratch_shapes=[
            pltpu.VMEM((HALO + length, QKV), f32),
            pltpu.VMEM((chains, count, DK, DV), f32),
            pltpu.VMEM((chains, length, DV), f32),
            pltpu.VMEM((chains, DK, DV), f32),
            pltpu.VMEM((chains, DK, DV), bf16),
            pltpu.VMEM((chains, DK, DV), bf16),
            pltpu.SemaphoreType.DMA((chains,)),
            pltpu.SemaphoreType.DMA((chains,)),
        ],
        compiler_params=pltpu.CompilerParams(
            dimension_semantics=("arbitrary",), collective_id=3, has_side_effects=True,
            vmem_limit_bytes=48 * 2**20,
        ),
        name="forward_rule",
    )(starts, decay_par, projected, halo, projected, conv_w)


def backward_kernel(
    seqs, places, peers, start_ref, decay_ref,
    dn_ref, mixed_ref, og_ref, gain_ref, n_ref, qe_ref, tot_ref, trans_ref,
    qkv_ref, inv_ref, s_ref, main_ref, halo_ref, rate_ref, conv_ref, hidden_ref, ffnp_hbm,
    dp_ref, dconv_ref, ddecay_ref, gg_ref, out_hbm,
    x_scr, g_scr, do_scr, own_scr, send, recv, tail_scr, halo_send, halo_recv,
    whole_out, send_sem, recv_sem, halo_send_sem, halo_recv_sem, load_sem, out_sem,
    sent, got, relay, sum_send, sum_recv, gather_send, gather_recv,
):
    step = pl.program_id(0)
    chains = n_ref.shape[0]
    count = n_ref.shape[1]
    length = main_ref.shape[0]
    heads = chains // seqs
    conv_cols = heads * QKV
    in_cols = conv_cols + heads * DV
    place = lax.axis_index("seq")
    lag = jnp.minimum(places - 1 - place, chains - 1)
    me = lax.axis_index("head")
    own_rows = hidden_ref.shape[0]
    subs = own_rows // SUB

    sums = Combine(sent, got, relay, me, sum_send, sum_recv, own_rows)

    def ffn_load(k):
        return pltpu.make_async_copy(
            part(ffnp_hbm, (me ^ k) * own_rows, own_rows), sent.at[k], load_sem.at[k]
        )

    ring = Spread(whole_out, own_rows, me, gather_send, gather_recv)

    def out_store(k):
        owner = me ^ k
        return pltpu.make_async_copy(
            part(whole_out, owner * own_rows, own_rows), part(out_hbm, owner * own_rows, own_rows),
            out_sem.at[k],
        )

    def passed(chain):
        return along(
            "seq", send.at[chain], recv.at[chain], send_sem.at[chain], recv_sem.at[chain],
            jnp.maximum(place - 1, 0),
        )

    def returned(chain):
        return along(
            "seq", halo_send.at[chain], halo_recv.at[chain], halo_send_sem.at[chain],
            halo_recv_sem.at[chain], jnp.maximum(place - 1, 0),
        )

    @pl.when(step == 0)
    def _():
        for k in range(peers):
            ffn_load(k).start()
        barrier = pltpu.get_barrier_semaphore()
        for k in range(1, peers):
            pl.semaphore_signal(barrier, inc=1, device_id={"head": me ^ k}, device_id_type=MESH)

        @pl.when(place < places - 1)
        def _():
            pl.semaphore_signal(
                barrier, inc=1, device_id={"seq": place + 1}, device_id_type=MESH
            )

        @pl.when(place == places - 1)
        def _():
            recv[...] = jnp.zeros_like(recv)
            halo_recv[...] = jnp.zeros_like(halo_recv)

        @pl.when(place > 0)
        def _():
            pl.semaphore_wait(barrier, peers)

        @pl.when(place == 0)
        def _():
            pl.semaphore_wait(barrier, peers - 1)

        for k in range(peers - 1, 0, -1):
            ffn_load(k).wait()
            sums.start(k, 0)
        ffn_load(0).wait()

    @pl.when(step < chains)
    def _():
        gain = gain_ref[0:1]
        first = (step % seqs) * length
        og_at = pl.ds(pl.multiple_of(conv_cols + (step // seqs) * DV, DV), DV)
        state = jnp.zeros((DK, DV), f32)
        total = jnp.zeros((1, DV), f32)
        for c in reversed(range(count)):
            at = pl.ds(c * CHUNK, CHUNK)
            mixed, og, dn = mixed_ref[at, :], og_ref[at, :], dn_ref[at, :]
            inverse = lax.rsqrt(jnp.mean(mixed * mixed, axis=1, keepdims=True) + epsilon)
            scaled = mixed * inverse
            sig = sigmoid(og)
            silu = og * sig
            through = dn * scaled
            total = total + jnp.sum(through * silu, axis=0, keepdims=True)
            dp_ref[pl.ds(pl.multiple_of(first + c * CHUNK, CHUNK), CHUNK), og_at] = (
                through * gain * sig * (1.0 + og * (1.0 - sig))
            ).astype(bf16)
            weighted = dn * gain * silu
            dmixed = inverse * (
                weighted - scaled * jnp.mean(weighted * scaled, axis=1, keepdims=True)
            )
            dmixed = dmixed.astype(bf16)
            do_scr[step, at, :] = dmixed
            decay = tot_ref[step, pl.ds(c, 1), 0:1]
            state = (
                decay * state - mm(n_ref[step, c], state, TN) + mm(qe_ref[step, c], dmixed, TN)
            )
        gg_ref[0] = jnp.broadcast_to(total, (8, DV))
        own_scr[step] = state

    @pl.when(step >= chains)
    def _():
        chain = jnp.maximum(step - chains, 0)
        head, seq = chain // seqs, chain % seqs
        first = seq * length
        start = start_ref[seq]
        load_conv_input(main_ref, halo_ref, start, x_scr, place * length)
        conv = conv_ref[...]
        rows, cols = iotas(CHUNK)
        lower, upper, eye = rows >= cols, rows <= cols, rows == cols
        strict = rows > cols
        state = recv[chain].astype(f32)
        leaving = [None] * count
        for c in reversed(range(count)):
            leaving[c] = state
            state = (
                tot_ref[chain, pl.ds(c, 1), 0:1] * state
                - mm(n_ref[chain, c], state, TN)
                + mm(qe_ref[chain, c], do_scr[chain, pl.ds(c * CHUNK, CHUNK), :], TN)
            )
        g_scr[pl.ds(0, 8), :] = jnp.zeros((8, QKV), f32)
        g_scr[pl.ds(8 + length, 8), :] = jnp.zeros((8, QKV), f32)
        rate_total = jnp.zeros((1, 1), f32)
        bias_total = jnp.zeros((1, 1), f32)
        conv_total = [jnp.zeros((1, QKV), f32) for _ in range(CONV)]
        lanes = lax.broadcasted_iota(jnp.int32, (CHUNK, PAD), 1)
        for c in range(count):
            at = pl.ds(c * CHUNK, CHUNK)
            q, k, v = qkv_ref[at, 0:DK], qkv_ref[at, DK : 2 * DK], qkv_ref[at, 2 * DK :]
            kf, vf = k.astype(f32), v.astype(f32)
            log_gate, strength, rate, logit = gates(rate_ref[at, :], decay_ref, head)
            column, total, ratio = decays(log_gate, lower, upper, eye)
            growth = jnp.exp(column)
            remain = jnp.exp(total - column)
            whole = jnp.exp(total)
            inverse = inv_ref[0, c]
            s0 = s_ref[0, c]
            do = do_scr[chain, at, :]
            grad_state = leaving[c]
            low_grad_state = grad_state.astype(bf16)
            kq = jnp.concatenate([k, q], axis=0)
            products = mm(kq, k, NT)
            kk, qk = products[:CHUNK], products[CHUNK:]
            reads = mm(kq, s0)
            ks, qs = reads[:CHUNK], reads[CHUNK:]
            fresh = vf - growth * ks
            pseudo = mm(inverse, strength * fresh).astype(bf16)
            scores = (ratio * qk).astype(bf16)
            dpseudo = mm(scores, do, TN) + mm(remain * kf, low_grad_state)
            dtarget = mm(inverse, dpseudo, TN)
            low_dtarget = dtarget.astype(bf16)
            dstrength = jnp.sum(dtarget * fresh, axis=1, keepdims=True)
            dlog = -(strength * growth) * jnp.sum(dtarget * ks, axis=1, keepdims=True)
            dv = strength * dtarget
            both = jnp.concatenate([low_dtarget, do], axis=0)
            outer = mm(both, pseudo, NT)
            dcoupling = jnp.where(strict, -outer[:CHUNK] * ratio, 0.0)
            by_strength = dcoupling * kk
            dstrength = dstrength + jnp.sum(by_strength, axis=1, keepdims=True)
            exponent = strength * by_strength
            dqk_f = jnp.where(lower, outer[CHUNK:] * ratio, 0.0)
            exponent = exponent + dqk_f * qk
            pair = jnp.concatenate([(dcoupling * strength).astype(bf16), dqk_f.astype(bf16)], axis=0)
            back = mm(both, s0, NT)
            wide = mm(pair, k)
            dq = growth * back[CHUNK:] + wide[CHUNK:]
            dkept = mm(pseudo, low_grad_state, NT)
            dk = (
                wide[:CHUNK]
                - (strength * growth) * back[:CHUNK]
                + mm(pair, kq, TN)
                + remain * dkept
            )
            dlog = dlog + growth * jnp.sum(do.astype(f32) * qs, axis=1, keepdims=True)
            from_kept = remain * jnp.sum(kf * dkept, axis=1, keepdims=True)
            dlog = dlog - from_kept + jnp.sum(exponent, axis=1, keepdims=True)
            dlog_row = to_row(dlog, eye) - jnp.sum(exponent, axis=0, keepdims=True)
            tail = jnp.sum(from_kept, axis=0, keepdims=True) + whole * jnp.sum(
                jnp.sum(grad_state * s0.astype(f32), axis=1, keepdims=True), axis=0, keepdims=True
            )
            dgate = jnp.sum(jnp.where(upper, dlog_row, 0.0), axis=1, keepdims=True) + tail
            slope = sigmoid(logit)
            drate0 = -rate * slope * dgate
            drate1 = dstrength * strength * (1.0 - strength)
            rate_total = rate_total + jnp.sum(dgate * log_gate, axis=0, keepdims=True)
            bias_total = bias_total + jnp.sum(drate0, axis=0, keepdims=True)
            here = pl.ds(pl.multiple_of(first + c * CHUNK, CHUNK), CHUNK)
            others = jnp.where(head == 0, 0.0, dp_ref[here, in_cols:].astype(f32))
            dp_ref[here, in_cols:] = jnp.where(
                lanes == 2 * head, drate0, jnp.where(lanes == 2 * head + 1, drate1, others)
            ).astype(bf16)
            convolved = convolve(x_scr, conv, c * CHUNK)
            sig = sigmoid(convolved)
            active = convolved * sig
            slope_conv = sig * (1.0 + convolved * (1.0 - sig))

            def unit_grad(rows_in, grad):
                inv_norm = lax.rsqrt(jnp.sum(rows_in * rows_in, axis=1, keepdims=True) + epsilon)
                y = rows_in * inv_norm
                return inv_norm * (grad - y * jnp.sum(y * grad, axis=1, keepdims=True))

            dq = dq.astype(bf16).astype(f32) * DK ** (-0.5)
            dk = dk.astype(bf16).astype(f32)
            dv = dv.astype(bf16).astype(f32)
            dconv = (
                jnp.concatenate(
                    [unit_grad(active[:, :DK], dq), unit_grad(active[:, DK : 2 * DK], dk), dv],
                    axis=1,
                )
                * slope_conv
            )
            g_scr[pl.ds(8 + c * CHUNK, CHUNK), :] = dconv
            for j in range(CONV):
                shifted_in = x_scr[pl.ds(c * CHUNK + HALO - CONV + 1 + j, CHUNK), :]
                conv_total[j] = conv_total[j] + jnp.sum(dconv * shifted_in, axis=0, keepdims=True)
        for j in range(CONV):
            dconv_ref[0, pl.ds(j, 1), :] = conv_total[j]
        row8 = lax.broadcasted_iota(jnp.int32, (8, PAD), 0)
        ddecay_ref[0] = jnp.where(row8 == 0, rate_total, jnp.where(row8 == 1, bias_total, 0.0))

        def conv_back(at, size):
            grad = g_scr[pl.ds(at + CONV - 1, size), :] * conv[0:1]
            for j in range(1, CONV):
                grad = grad + g_scr[pl.ds(at + CONV - 1 - j, size), :] * conv[j : j + 1]
            return grad

        halo_send[chain] = conv_back(0, 8)

        @pl.when(place > 0)
        def _():
            returned(chain).start()

        conv_at = pl.ds(pl.multiple_of(head * QKV, QKV), QKV)
        for c in range(count):
            grad = conv_back(8 + c * CHUNK, CHUNK)
            positions = place * length + c * CHUNK + lax.broadcasted_iota(
                jnp.int32, (CHUNK, 1), 0
            )
            live = (positions >= start).astype(f32)
            if c == count - 1:
                tail_scr[chain] = grad[CHUNK - HALO :]
            dp_ref[pl.ds(pl.multiple_of(first + c * CHUNK, CHUNK), CHUNK), conv_at] = (
                grad * live
            ).astype(bf16)

    relayed = step - lag

    @pl.when((relayed >= 0) & (relayed < chains))
    def _():
        chain = jnp.clip(relayed, 0, chains - 1)

        @pl.when(place < places - 1)
        def _():
            passed(chain).wait_recv()

        @pl.when(place > 0)
        def _():
            earlier = mm(trans_ref[chain], recv[chain], TN) + own_scr[chain]
            send[chain] = earlier.astype(bf16)
            passed(chain).start()

    @pl.when(step == chains - 1)
    def _():
        sums.combine(0)

    @pl.when(step == chains)
    def _():
        for kind in range(2, 6):
            sums.copy(kind, 0).wait_recv()

        def out_rows(t, carry):
            rows = pl.ds(pl.multiple_of(t * SUB, SUB), SUB)
            part(whole_out, me * own_rows + t * SUB, SUB)[...] = (
                hidden_ref[rows, :] + sums.total(rows)
            ).astype(bf16)
            return carry

        lax.fori_loop(0, subs, out_rows, 0)
        ring.start(0)
        out_store(0).start()

    @pl.when(step == chains + 2)
    def _():
        ring.forward(0)

    @pl.when(step == 2 * chains - 1)
    def _():
        for chain in range(chains):
            @pl.when(place < places - 1)
            def _():
                returned(chain).wait_recv()

            head, seq = chain // seqs, chain % seqs
            positions = (place + 1) * length - HALO + lax.broadcasted_iota(
                jnp.int32, (HALO, 1), 0
            )
            live = (positions >= start_ref[seq]).astype(f32)
            grad = tail_scr[chain] + jnp.concatenate(
                [jnp.zeros((HALO - 8, QKV), f32), halo_recv[chain]], axis=0
            )
            dp_ref[pl.ds((seq + 1) * length - HALO, HALO), pl.ds(head * QKV, QKV)] = (
                grad * live
            ).astype(bf16)

            @pl.when(place > 0)
            def _():
                returned(chain).wait_send()
                passed(chain).wait_send()

        ring.finish(0)
        for k in range(1, peers):
            out_store(k).start()
        for k in range(peers):
            out_store(k).wait()
        sums.drain(0)
        ring.drain(0)


def backward_rule(
    starts, decay_par, dn, mixed, og, projected, gain, n, qe, tot, trans, qkv, inv, states, halo, conv_w,
    hidden, ffn_part, seqs, heads,
):
    places, peers = lax.axis_size("seq"), lax.axis_size("head")
    chains = seqs * heads
    rows = projected.shape[0]
    length = rows // seqs
    count = length // CHUNK
    width = hidden.shape[1]
    own_rows = hidden.shape[0]
    rates_at = heads * QKV // PAD
    row = lambda first: lambda i: (i % seqs, first + i // seqs)
    whole = lambda *dims: pl.BlockSpec(dims, lambda j: (0,) * len(dims))
    chain4 = lambda i: (i, 0, 0, 0)
    chain3 = lambda i: (i, 0, 0)
    shape = jax.ShapeDtypeStruct
    per_chain = pltpu.SemaphoreType.DMA((chains,))
    per_peer = pltpu.SemaphoreType.DMA((peers,))
    return pl.pallas_call(
        functools.partial(backward_kernel, seqs, places, peers),
        grid=(2 * chains,),
        in_specs=[
            smem(),
            smem(),
            pl.BlockSpec((length, DV), early(chains, row(0))),
            pl.BlockSpec((length, DV), early(chains, row(0))),
            pl.BlockSpec((length, DV), early(chains, row(0))),
            whole(1, DV),
            whole(chains, count, DK, DK),
            whole(chains, count, CHUNK, DK),
            whole(chains, count, DK),
            whole(chains, DK, DK),
            pl.BlockSpec((length, QKV), late(chains, row(0))),
            pl.BlockSpec((1, count, CHUNK, CHUNK), late(chains, chain4)),
            pl.BlockSpec((1, count, DK, DV), late(chains, chain4)),
            pl.BlockSpec((length, QKV), late(chains, row(0))),
            pl.BlockSpec((1, HALO, QKV), late(chains, lambda i: (i % seqs, 0, i // seqs))),
            pl.BlockSpec((length, PAD), late(chains, lambda i: (i % seqs, rates_at))),
            pl.BlockSpec((CONV, QKV), late(chains, lambda i: (0, i // seqs))),
            whole(own_rows, width),
            anywhere(),
        ],
        out_specs=[
            whole(rows, heads * (QKV + DV) + PAD),
            pl.BlockSpec((1, CONV, QKV), late(chains, chain3)),
            pl.BlockSpec((1, 8, PAD), late(chains, chain3)),
            pl.BlockSpec((1, 8, DV), early(chains, chain3)),
            anywhere(),
        ],
        out_shape=[
            shape((rows, heads * (QKV + DV) + PAD), bf16),
            shape((chains, CONV, QKV), f32),
            shape((chains, 8, PAD), f32),
            shape((chains, 8, DV), f32),
            shape((rows, width), bf16),
        ],
        scratch_shapes=[
            pltpu.VMEM((HALO + length, QKV), f32),
            pltpu.VMEM((16 + length, QKV), f32),
            pltpu.VMEM((chains, length, DV), bf16),
            pltpu.VMEM((chains, DK, DV), f32),
            pltpu.VMEM((chains, DK, DV), bf16),
            pltpu.VMEM((chains, DK, DV), bf16),
            pltpu.VMEM((chains, HALO, QKV), f32),
            pltpu.VMEM((chains, 8, QKV), f32),
            pltpu.VMEM((chains, 8, QKV), f32),
            pltpu.VMEM((rows, width), bf16),
            per_chain, per_chain, per_chain, per_chain,
            per_peer, per_peer,
        ]
        + sum_buffers(own_rows, width, 1),
        compiler_params=pltpu.CompilerParams(
            dimension_semantics=("arbitrary",), collective_id=4, has_side_effects=True,
            vmem_limit_bytes=52 * 2**20,
        ),
        name="backward_rule",
    )(
        starts, decay_par, dn, mixed, og, gain, n, qe, tot, trans, qkv, inv, states, projected,
        halo, projected, conv_w, hidden, ffn_part,
    )


def smem():
    return pl.BlockSpec(memory_space=pltpu.SMEM)


def rows_of(t):
    return pl.ds(pl.multiple_of(t * SUB, SUB), SUB)


def block_store(i, size, source, target, sem):
    return pltpu.make_async_copy(
        part(source, i * size, size), part(target, i * size, size), sem.at[i]
    )


def mixer_kernel(
    peers, nin_hbm, mixed_hbm, weights_hbm, x_hbm, gain_ref, o_gain_ref,
    og_hbm, normed_hbm, nm_hbm, turned_hbm, hidden_ref,
    nin, turned, mixed, weights, x_v, og_v, normed_v, nm, in_sem, out_sem,
    send, recv, relay, sum_send, sum_recv, gather_send, gather_recv,
):
    me = lax.axis_index("head")
    total, width = nm.shape
    values = mixed.shape[1]
    own_rows = total // peers
    subs = own_rows // SUB
    loads = [
        pltpu.make_async_copy(weights_hbm, weights, in_sem.at[0]),
        pltpu.make_async_copy(nin_hbm, nin, in_sem.at[1]),
        pltpu.make_async_copy(mixed_hbm, mixed, in_sem.at[2]),
        pltpu.make_async_copy(part(x_hbm, me * own_rows, own_rows), x_v, in_sem.at[3]),
    ]
    for load in loads:
        load.start()
    greet_heads(me, peers)
    for load in loads[:3]:
        load.wait()
    sums = Combine(send, recv, relay, me, sum_send, sum_recv, SUB)

    def project(i, carry):
        k = jnp.where(i == 0, peers - 1, lax.rem(i, peers - 1))
        owner = me ^ k
        rows = pl.ds(pl.multiple_of(owner * own_rows, own_rows), own_rows)
        og = mm(nin[rows, :], weights[:, 0:values])
        og_v[rows, :] = og
        gated = og * sigmoid(og)
        for first in range(0, values, DV):
            at = pl.ds(first, DV)
            own = mixed[rows, at]
            inverse = lax.rsqrt(jnp.mean(own * own, axis=1, keepdims=True) + epsilon)
            normed_v[rows, at] = (
                own * inverse * o_gain_ref[0:1] * gated[:, first : first + DV]
            ).astype(bf16)
        send[k] = mm(normed_v[rows, :], weights[:, values:], NT).astype(bf16)

        for kk in range(1, peers):

            @pl.when(k == kk)
            def _():
                for t in range(subs):
                    sums.start(kk, t)

        block_store(owner, own_rows, og_v, og_hbm, out_sem.at[0]).start()
        block_store(owner, own_rows, normed_v, normed_hbm, out_sem.at[1]).start()
        return carry

    lax.fori_loop(0, peers, project, 0)
    tile = 256
    for first in range(0, width, tile):
        turned[first : first + tile, :] = nin[:, first : first + tile].T
    for t in range(subs):
        sums.combine(t)
    turned_store = pltpu.make_async_copy(turned, turned_hbm, in_sem.at[4])
    turned_store.start()
    loads[3].wait()
    gain = gain_ref[...]
    ring = Spread(nm, own_rows, me, gather_send, gather_recv, SUB)
    for t in range(subs):
        rows = rows_of(t)
        hidden = x_v[rows, :].astype(f32) + sums.collect(t)
        hidden_ref[rows, :] = hidden
        inverse = lax.rsqrt(jnp.mean(hidden * hidden, axis=1, keepdims=True) + epsilon)
        part(nm, me * own_rows + t * SUB, SUB)[...] = (hidden * inverse * gain).astype(bf16)
        ring.start(t)
    for t in range(subs):
        ring.forward(t)
    for k in range(peers):
        if k == peers - 1:
            for t in range(subs):
                ring.finish(t)
        block_store(me ^ k, own_rows, nm, nm_hbm, out_sem.at[2]).start()
    turned_store.wait()
    for i in range(peers):
        block_store(i, own_rows, og_v, og_hbm, out_sem.at[0]).wait()
        block_store(i, own_rows, normed_v, normed_hbm, out_sem.at[1]).wait()
        block_store(i, own_rows, nm, nm_hbm, out_sem.at[2]).wait()
    for t in range(subs):
        sums.drain(t)
        ring.drain(t)


def mixer(nin, mixed, weights, x, gain, o_gain):
    peers = lax.axis_size("head")
    total, width = x.shape
    values = mixed.shape[1]
    own_rows = total // peers
    subs = own_rows // SUB
    shape = jax.ShapeDtypeStruct
    return pl.pallas_call(
        functools.partial(mixer_kernel, peers),
        in_specs=[anywhere()] * 4 + [vmem()] * 2,
        out_specs=[anywhere()] * 4 + [vmem()],
        out_shape=[
            shape((total, values), f32),
            shape((total, values), bf16),
            shape((total, width), bf16),
            shape((width, total), bf16),
            shape((own_rows, width), f32),
        ],
        scratch_shapes=[
            pltpu.VMEM((total, width), bf16),
            pltpu.VMEM((width, total), bf16),
            pltpu.VMEM((total, values), f32),
            pltpu.VMEM((width, 2 * values), bf16),
            pltpu.VMEM((own_rows, width), bf16),
            pltpu.VMEM((total, values), f32),
            pltpu.VMEM((total, values), bf16),
            pltpu.VMEM((total, width), bf16),
            pltpu.SemaphoreType.DMA((5,)),
            pltpu.SemaphoreType.DMA((3, peers)),
        ]
        + sum_buffers(own_rows, width, subs),
        compiler_params=pltpu.CompilerParams(
            collective_id=1, has_side_effects=True, vmem_limit_bytes=48 * 2**20
        ),
        name="mixer",
    )(nin, mixed, weights, x, gain, o_gain)


def ffn_kernel(
    peers, places, cores, nm_hbm, ffn_hbm, ct_hbm, normed_hbm, weights_hbm, hidden_ref, gain_ref,
    grads_hbm, ffnp_hbm, ng_hbm, hgrad_ref, gpart_ref, down_ref,
    nm, ffn_v, ct_v, normed_v, wout_v, act, dgu, dm, ffnp_v, grads_v, down_v, ng_v,
    in_sem, out_sem, send, recv, relay, sum_send, sum_recv, gather_send, gather_recv,
    core_recv, seq_send, seq_recv, scatter_sems,
):
    me = lax.axis_index("head")
    total, width = nm.shape
    values = normed_v.shape[1]
    own_rows = total // peers
    subs = own_rows // SUB
    cells = act.shape[1]
    tile = 256
    loads = [
        pltpu.make_async_copy(ffn_hbm, ffn_v, in_sem.at[0]),
        pltpu.make_async_copy(nm_hbm, nm, in_sem.at[1]),
        pltpu.make_async_copy(ct_hbm, ct_v, in_sem.at[2]),
        pltpu.make_async_copy(normed_hbm, normed_v, in_sem.at[3]),
        pltpu.make_async_copy(weights_hbm.at[:, pl.ds(values, values)], wout_v, in_sem.at[4]),
    ]
    for load in loads:
        load.start()
    greet_group(me, peers, places, cores)
    for load in loads[:3]:
        load.wait()
    gain = gain_ref[...]
    sums = Combine(send, recv, relay, me, sum_send, sum_recv, SUB)

    def feed_forward(i, carry):
        k = jnp.where(i == 0, peers - 1, lax.rem(i, peers - 1))
        rows = pl.ds(pl.multiple_of((me ^ k) * own_rows, own_rows), own_rows)

        def cell_tile(j, carry):
            at = pl.ds(pl.multiple_of(j * tile, tile), tile)
            at_up = pl.ds(pl.multiple_of(cells + j * tile, tile), tile)
            at_down = pl.ds(pl.multiple_of(2 * cells + j * tile, tile), tile)
            gate = mm(nm[rows, :], ffn_v[:, at])
            up = mm(nm[rows, :], ffn_v[:, at_up])
            dact = mm(ct_v[rows, :], ffn_v[:, at_down])
            sig = sigmoid(gate)
            silu = gate * sig
            act[rows, at] = (silu * up).astype(bf16)
            dgu[rows, at] = (dact * up * sig * (1.0 + gate * (1.0 - sig))).astype(bf16)
            dgu[rows, at_up] = (dact * silu).astype(bf16)
            return carry

        lax.fori_loop(0, cells // tile, cell_tile, 0)

        def mid_tile(j, carry):
            at = pl.ds(pl.multiple_of(j * tile, tile), tile)
            send[k, :, at] = mm(dgu[rows, :], ffn_v[at, 0 : 2 * cells], NT).astype(bf16)
            return carry

        lax.fori_loop(0, width // tile, mid_tile, 0)

        for kk in range(1, peers):

            @pl.when(k == kk)
            def _():
                for t in range(subs):
                    sums.start(kk, t)

        @pl.when(k == 2)
        def _():
            for t in range(subs):
                sums.combine(t)

        return carry

    lax.fori_loop(0, peers, feed_forward, 0)

    def down_grads(i, carry):
        at = pl.ds(pl.multiple_of(i * tile, tile), tile)
        down_v[at, :] = mm(ct_v[:, at], act[...], TN).astype(bf16)
        return carry

    lax.fori_loop(0, width // tile, down_grads, 0)
    scatter = GroupScatter(down_v, pl.ds(0, cells), core_recv, seq_send, seq_recv, scatter_sems)
    for k in range(places - 1, -1, -1):
        scatter.core_copy(k).start()

    def cell_grads(i, carry):
        at = pl.ds(pl.multiple_of(i * tile, tile), tile)
        grads_v[at, 0 : 2 * cells] = mm(nm[:, at], dgu[...], TN).astype(bf16)
        return carry

    half = width // tile // 2
    lax.fori_loop(0, half, cell_grads, 0)
    for k in range(places - 1, -1, -1):
        scatter.pass_on(k)
    lax.fori_loop(half, width // tile, cell_grads, 0)
    ring = Spread(dm, own_rows, me, gather_send, gather_recv, SUB)
    gain_part = jnp.zeros((1, width), f32)
    for t in range(subs):
        rows = rows_of(t)
        dmid = sums.collect(t)
        hidden = hidden_ref[rows, :]
        inverse = lax.rsqrt(jnp.mean(hidden * hidden, axis=1, keepdims=True) + epsilon)
        scaled = hidden * inverse
        weighted = dmid * gain
        grad = part(ct_v, me * own_rows + t * SUB, SUB)[...].astype(f32) + inverse * (
            weighted - scaled * jnp.mean(weighted * scaled, axis=1, keepdims=True)
        )
        hgrad_ref[rows, :] = grad
        part(dm, me * own_rows + t * SUB, SUB)[...] = grad.astype(bf16)
        ring.start(t)
        gain_part = gain_part + jnp.sum(dmid * scaled, axis=0, keepdims=True)
    gpart_ref[...] = jnp.broadcast_to(gain_part, gpart_ref.shape)

    def ffn_rows(i, carry):
        rows = pl.ds(pl.multiple_of(i * own_rows, own_rows), own_rows)
        ffnp_v[rows, :] = mm(act[rows, :], ffn_v[:, 2 * cells :], NT).astype(bf16)
        block_store(i, own_rows, ffnp_v, ffnp_hbm, out_sem.at[0]).start()
        return carry

    lax.fori_loop(0, peers, ffn_rows, 0)
    loads[3].wait()
    loads[4].wait()
    for t in range(subs):
        ring.forward(t)
    down_ref[...] = scatter.finish()

    def norm_rows(k, carry):
        owner = me ^ k

        @pl.when(k == peers - 1)
        def _():
            for t in range(subs):
                ring.finish(t)

        rows = pl.ds(pl.multiple_of(owner * own_rows, own_rows), own_rows)
        ng_v[rows, :] = mm(dm[rows, :], wout_v[...])
        block_store(owner, own_rows, ng_v, ng_hbm, out_sem.at[1]).start()
        return carry

    lax.fori_loop(0, peers, norm_rows, 0)

    def out_grads(i, carry):
        at = pl.ds(pl.multiple_of(i * tile, tile), tile)
        grads_v[at, 2 * cells :] = mm(dm[:, at], normed_v[...], TN).astype(bf16)
        block_store(i, tile, grads_v, grads_hbm, out_sem.at[2]).start()
        return carry

    lax.fori_loop(0, width // tile, out_grads, 0)
    for i in range(peers):
        block_store(i, own_rows, ffnp_v, ffnp_hbm, out_sem.at[0]).wait()
        block_store(i, own_rows, ng_v, ng_hbm, out_sem.at[1]).wait()
    for i in range(width // tile):
        block_store(i, tile, grads_v, grads_hbm, out_sem.at[2]).wait()
    for t in range(subs):
        sums.drain(t)
        ring.drain(t)
    scatter.drain()


def feed_forward_block(nm, ffn_full, ct, normed, weights, hidden, gain):
    peers, places, cores = lax.axis_size("head"), lax.axis_size("seq"), lax.axis_size("batch")
    total, width = ct.shape
    own_rows = total // peers
    subs = own_rows // SUB
    values = normed.shape[1]
    cells = ffn_full.shape[1] // 3
    shard = width // (places * cores)
    shape = jax.ShapeDtypeStruct
    return pl.pallas_call(
        functools.partial(ffn_kernel, peers, places, cores),
        in_specs=[anywhere()] * 5 + [vmem()] * 2,
        out_specs=[anywhere()] * 3 + [vmem()] * 3,
        out_shape=[
            shape((width, 2 * cells + values), bf16),
            shape((total, width), bf16),
            shape((total, values), f32),
            shape((own_rows, width), f32),
            shape((8, width), f32),
            shape((shard, cells), f32),
        ],
        scratch_shapes=[
            pltpu.VMEM((total, width), bf16),
            pltpu.VMEM((width, 3 * cells), bf16),
            pltpu.VMEM((total, width), bf16),
            pltpu.VMEM((total, values), bf16),
            pltpu.VMEM((width, values), bf16),
            pltpu.VMEM((total, cells), bf16),
            pltpu.VMEM((total, 2 * cells), bf16),
            pltpu.VMEM((total, width), bf16),
            pltpu.VMEM((total, width), bf16),
            pltpu.VMEM((width, 2 * cells + values), bf16),
            pltpu.VMEM((width, cells), bf16),
            pltpu.VMEM((total, values), f32),
            pltpu.SemaphoreType.DMA((5,)),
            pltpu.SemaphoreType.DMA((3, max(peers, width // 256))),
        ]
        + sum_buffers(own_rows, width, subs)
        + scatter_buffers(places, shard, cells),
        compiler_params=pltpu.CompilerParams(
            collective_id=5, has_side_effects=True, vmem_limit_bytes=56 * 2**20
        ),
        name="feed_forward",
    )(nm, ffn_full, ct, normed, weights, hidden, gain)


def input_grad_kernel(
    peers, places, cores, heads, dp_hbm, win_hbm, wog_hbm, nin_hbm, x_hbm, hgrad_ref, gain_ref,
    gains_ref, extras_ref,
    out_hbm, gains_out, grad_out, small_out,
    dp_v, win_v, wog_v, nin_v, x_v, whole, grads_v, gains_v, gains_recv, gains_sum, gains_all,
    in_sem, out_sem,
    send, recv, relay, sum_send, sum_recv, gather_send, gather_recv,
    core_recv, seq_send, seq_recv, scatter_sems, hs, hr, gs, gr,
):
    me = lax.axis_index("head")
    place, core = lax.axis_index("seq"), lax.axis_index("batch")
    total, width = whole.shape
    own_rows = total // peers
    subs = own_rows // SUB
    values = wog_v.shape[1]
    conv_cols = win_v.shape[1] - PAD
    cols = dp_v.shape[1]
    group = places * cores
    pair = cores * (width // group)
    flat = place * cores + core
    loads = [
        pltpu.make_async_copy(dp_hbm, dp_v, in_sem.at[0]),
        pltpu.make_async_copy(win_hbm, win_v, in_sem.at[1]),
        pltpu.make_async_copy(wog_hbm.at[:, pl.ds(0, values)], wog_v, in_sem.at[2]),
        pltpu.make_async_copy(nin_hbm, nin_v, in_sem.at[3]),
        pltpu.make_async_copy(part(x_hbm, me * own_rows, own_rows), x_v, in_sem.at[4]),
    ]
    for load in loads:
        load.start()
    greet_group(me, peers, places, cores)
    for load in loads[:3]:
        load.wait()
    sums = Combine(send, recv, relay, me, sum_send, sum_recv, SUB)

    def project(i, carry):
        k = jnp.where(i == 0, peers - 1, lax.rem(i, peers - 1))
        rows = pl.ds(pl.multiple_of((me ^ k) * own_rows, own_rows), own_rows)
        partial = mm(dp_v[rows, 0:conv_cols], win_v[:, 0:conv_cols], NT)
        partial = partial + mm(
            dp_v[rows, conv_cols : conv_cols + values], wog_v[...], NT
        )
        partial = partial + mm(dp_v[rows, conv_cols + values :], win_v[:, conv_cols:], NT)
        send[k] = partial.astype(bf16)

        for kk in range(1, peers):

            @pl.when(k == kk)
            def _():
                for t in range(subs):
                    sums.start(kk, t)

        return carry

    lax.fori_loop(0, peers - 1, project, 0)
    loads[3].wait()
    scatter = GroupScatter(grads_v, pl.ds(0, cols), core_recv, seq_send, seq_recv, scatter_sems)

    def place_grads(i, carry):
        k = places - 1 - i
        rows = pl.ds(pl.multiple_of((place ^ k) * pair, pair), pair)
        grads = mm(nin_v[rows, :], dp_v[...])
        grads_v[rows, 0 : cols - PAD] = grads[:, : cols - PAD].astype(bf16)
        grads_v[rows, cols - PAD :] = (grads[:, cols - PAD :] + extras_ref[rows, :]).astype(bf16)
        scatter.core_copy(k).start()

        @pl.when(i > 0)
        def _():
            scatter.pass_on(jnp.minimum(k + 1, places - 1))

        return carry

    lax.fori_loop(0, places, place_grads, 0)
    scatter.pass_on(0)
    for t in range(subs):
        sums.combine(t)
    project(peers - 1, 0)
    loads[4].wait()
    gain = gain_ref[...]
    ring = Spread(whole, own_rows, me, gather_send, gather_recv, SUB)
    gain_part = jnp.zeros((1, width), f32)
    for t in range(subs):
        rows = rows_of(t)
        din = sums.collect(t)
        x = x_v[rows, :].astype(f32)
        inverse = lax.rsqrt(jnp.mean(x * x, axis=1, keepdims=True) + epsilon)
        scaled = x * inverse
        weighted = din * gain
        grad = hgrad_ref[rows, :] + inverse * (
            weighted - scaled * jnp.mean(weighted * scaled, axis=1, keepdims=True)
        )
        part(whole, me * own_rows + t * SUB, SUB)[...] = grad.astype(bf16)
        ring.start(t)
        gain_part = gain_part + jnp.sum(din * scaled, axis=0, keepdims=True)
    gains_v[...] = gains_ref[...]
    for r in range(width // 128):
        gains_v[r : r + 1, :] = gain_part[:, r * 128 : (r + 1) * 128]

    def gains_copy(k):
        return head_copy(gains_v, gains_recv.at[k], hs.at[k], hr.at[k], me ^ k)

    def to_group(d):
        to = lax.rem(flat + d, group)
        return pltpu.make_async_remote_copy(
            src_ref=gains_sum, dst_ref=gains_all.at[d], send_sem=gs.at[d], recv_sem=gr.at[d],
            device_id={"seq": to // cores, "batch": lax.rem(to, cores)}, device_id_type=MESH,
        )

    for k in range(1, peers):
        gains_copy(k).start()
    block_store(me, own_rows, whole, out_hbm, out_sem).start()
    gathered = gains_v[...]
    for k in range(1, peers):
        gains_copy(k).wait_recv()
        gathered = gathered + gains_recv[k]
    gains_sum[...] = gathered
    for d in range(1, group):
        to_group(d).start()
    for t in range(subs):
        ring.forward(t)
    block_store(me ^ 1, own_rows, whole, out_hbm, out_sem).start()
    block_store(me ^ 2, own_rows, whole, out_hbm, out_sem).start()
    for d in range(1, group):
        to_group(d).wait_recv()
        gathered = gathered + gains_all[d]
    gains_out[...] = gathered
    for t in range(subs):
        ring.finish(t)
    block_store(me ^ 3, own_rows, whole, out_hbm, out_sem).start()
    grad = scatter.finish()
    for head in range(heads):
        at = head * (QKV + DV)
        grad_out[:, at : at + QKV] = grad[:, head * QKV : (head + 1) * QKV]
        gate_at = conv_cols + head * DV
        grad_out[:, at + QKV : at + QKV + DV] = grad[:, gate_at : gate_at + DV]
    small_out[...] = grad[:, conv_cols + values :]
    for k in range(peers):
        block_store(k, own_rows, whole, out_hbm, out_sem).wait()
    for t in range(subs):
        sums.drain(t)
        ring.drain(t)
    for k in range(1, peers):
        gains_copy(k).wait_send()
    scatter.drain()
    for d in range(1, group):
        to_group(d).wait_send()


def input_grads(dp, in_full, gate_full, nin, x, hgrad, gain, gains, extras, heads):
    peers, places, cores = lax.axis_size("head"), lax.axis_size("seq"), lax.axis_size("batch")
    group = places * cores
    total, width = x.shape
    cols = dp.shape[1]
    values = gate_full.shape[1] // 2
    own_rows = total // peers
    subs = own_rows // SUB
    shard = width // group
    shape = jax.ShapeDtypeStruct
    per_peer = pltpu.SemaphoreType.DMA((peers,))
    per_member = pltpu.SemaphoreType.DMA((group,))
    return pl.pallas_call(
        functools.partial(input_grad_kernel, peers, places, cores, heads),
        in_specs=[anywhere()] * 5 + [vmem()] * 4,
        out_specs=[anywhere()] + [vmem()] * 3,
        out_shape=[
            shape((total, width), bf16), shape(gains.shape, f32),
            shape((shard, cols - PAD), f32), shape((shard, PAD), f32),
        ],
        scratch_shapes=[
            pltpu.VMEM((total, cols), bf16),
            pltpu.VMEM((width, cols - values), bf16),
            pltpu.VMEM((width, values), bf16),
            pltpu.VMEM((width, total), bf16),
            pltpu.VMEM((own_rows, width), bf16),
            pltpu.VMEM((total, width), bf16),
            pltpu.VMEM((width, cols), bf16),
            pltpu.VMEM(gains.shape, f32),
            pltpu.VMEM((peers,) + gains.shape, f32),
            pltpu.VMEM(gains.shape, f32),
            pltpu.VMEM((group,) + gains.shape, f32),
            pltpu.SemaphoreType.DMA((5,)),
            pltpu.SemaphoreType.DMA((peers,)),
        ]
        + sum_buffers(own_rows, width, subs)
        + scatter_buffers(places, shard, cols)
        + [per_peer] * 2
        + [per_member] * 2,
        compiler_params=pltpu.CompilerParams(
            collective_id=2, has_side_effects=True, vmem_limit_bytes=52 * 2**20
        ),
        name="input_grads",
    )(dp, in_full, gate_full, nin, x, hgrad, gain, gains, extras)


def late_kernel(units, cells, late_ref, down_in, gate_ref, up_ref, down_ref, out_ref):
    gate_ref[...] = late_ref[:, 0:units].astype(f32)
    up_ref[...] = late_ref[:, cells : cells + units].astype(f32)
    down_ref[...] = down_in[...].T[0:units]
    out_ref[...] = late_ref[:, 2 * cells :].astype(f32).T


def late_outputs(late, down, units, cells):
    shard = late.shape[0]
    values = late.shape[1] - 2 * cells
    shape = jax.ShapeDtypeStruct
    return pl.pallas_call(
        functools.partial(late_kernel, units, cells),
        in_specs=[vmem()] * 2,
        out_specs=[vmem()] * 4,
        out_shape=[
            shape((shard, units), f32), shape((shard, units), f32), shape((units, shard), f32),
            shape((values, shard), f32),
        ],
        name="late_outputs",
    )(late, down)


def shifted(shard, axis, by):
    count = lax.axis_size(axis)
    pairs = [(i, i + by) for i in range(count) if 0 <= i + by < count]
    return lax.ppermute(shard, axis, pairs)


def root_scale(value_rows):
    return lax.rsqrt(jnp.mean(value_rows * value_rows, axis=-1, keepdims=True) + epsilon)


def matmul(a, b, dims=NN):
    return lax.dot_general(a, b, (dims, ((), ())), preferred_element_type=f32)


ALL = ("seq", "batch")


def per_device(
    tokens, starts, attn_gain, w_in, w_rates, conv_w, decay_par, o_gain, w_out, ffn_gain, w_gu,
    w_down, cotangent,
):
    seqs, length, width = tokens.shape
    shard, heads = w_in.shape[:2]
    shards = width // shard
    total = seqs * length
    conv_cols = heads * QKV
    value_cols = heads * DV
    units = w_down.shape[0]
    cells = -(-units // 256) * 256
    spare = cells - units

    packed_in = jnp.concatenate(
        [
            w_in[:, :, :QKV].reshape(shard, conv_cols),
            w_rates.reshape(shard, 2 * heads),
            jnp.zeros((shard, PAD - 2 * heads), f32),
        ],
        axis=1,
    ).astype(bf16)
    packed_gate = jnp.concatenate(
        [w_in[:, :, QKV:].reshape(shard, value_cols), w_out.reshape(value_cols, -1).T], axis=1
    ).astype(bf16)
    packed_ffn = jnp.pad(
        jnp.stack([w_gu[:, 0], w_gu[:, 1], w_down.T], axis=1).astype(bf16),
        ((0, 0), (0, 0), (0, spare)),
    ).reshape(shard, 3 * cells)
    conv_flat = conv_w.reshape(-1)
    small = jnp.concatenate([attn_gain, ffn_gain, conv_flat, o_gain]).astype(bf16)

    x = tokens.reshape(total, width)
    ct = cotangent.reshape(total, width)
    before = shifted(tokens[:, length - HALO :], "seq", 1).reshape(seqs * HALO, width)
    in_full = lax.all_gather(packed_in, ALL, axis=0, tiled=True)
    small_full = lax.all_gather(small, ALL, axis=0)
    gate_full = lax.all_gather(packed_gate, ALL, axis=0, tiled=True)
    ffn_full = lax.all_gather(packed_ffn, ALL, axis=0, tiled=True)
    attn_gain_f = small_full[:, :shard].reshape(1, width).astype(f32)
    ffn_gain_f = small_full[:, shard : 2 * shard].reshape(1, width).astype(f32)
    conv_end = 2 * shard + conv_flat.shape[0]
    conv_full = (
        small_full[:, 2 * shard : conv_end]
        .reshape(shards, CONV, heads, -1)
        .transpose(1, 2, 0, 3)
        .reshape(CONV, conv_cols)
        .astype(f32)
    )
    o_gain_full = small_full[:, conv_end:].reshape(1, DV).astype(f32)

    def normed_rows(rows):
        rows = rows.astype(f32)
        return (rows * root_scale(rows) * attn_gain_f).astype(bf16)

    normed_in = normed_rows(x)
    projected = matmul(normed_in, in_full)
    halo = matmul(normed_rows(before), in_full[:, :conv_cols]).reshape(seqs, HALO, conv_cols)
    qkv, inv, n, qe, tot, trans, states, mixed = forward_rule(
        starts, decay_par, projected, halo, conv_full, seqs, heads
    )
    og, normed, nm, turned_in, hidden = mixer(
        normed_in, mixed, gate_full, x, ffn_gain_f, o_gain_full
    )
    late_grads, ffn_part, normed_grad, hidden_grad, ffn_gain_part, down_own = feed_forward_block(
        nm, ffn_full, ct, normed, gate_full, hidden, ffn_gain_f
    )
    late_own = lax.psum_scatter(late_grads, ALL, scatter_dimension=0, tiled=True)
    projected_grad, dconv, ddecay, onorm_grads, result = backward_rule(
        starts, decay_par, normed_grad, mixed, og, projected, o_gain_full, n, qe, tot, trans, qkv,
        inv, states, halo, conv_full, hidden, ffn_part, seqs, heads,
    )
    taps = CONV * heads
    per_shard = taps * QKV // shards
    conv_at = 2 * heads
    conv_end = conv_at + per_shard // shard
    onorm_grad = jnp.sum(onorm_grads[:, 0], axis=0)
    decay_part = jnp.sum(ddecay[:, :2, 0].reshape(heads, seqs, 2), axis=1).T.reshape(1, 1, -1)
    conv_grad = jnp.sum(dconv.reshape(heads, seqs, CONV, QKV), axis=1).transpose(1, 0, 2)
    conv_grad = conv_grad.reshape(taps, shards, -1).transpose(1, 0, 2).reshape(shards, -1, shard)
    decay_part = jnp.pad(decay_part, ((0, 0), (0, 0), (0, shard - 2 * heads)))
    extras = jnp.concatenate(
        [
            jnp.zeros((shards, conv_at, shard), f32),
            conv_grad,
            jnp.broadcast_to(decay_part, (shards, 1, shard)),
            jnp.zeros((shards, PAD - conv_end - 1, shard), f32),
        ],
        axis=1,
    ).transpose(0, 2, 1).reshape(width, PAD)
    lane_rows = width // 128
    gains = jnp.concatenate(
        [
            jnp.zeros((lane_rows, 128), f32),
            ffn_gain_part[0].reshape(lane_rows, 128),
            jnp.pad(onorm_grad, (0, width - DV)).reshape(lane_rows, 128),
        ]
    )
    input_grad, gains, in_main, in_small = input_grads(
        projected_grad, in_full, gate_full, turned_in, x, hidden_grad, attn_gain_f, gains, extras,
        heads,
    )
    grad_gate, grad_up, grad_down, grad_out = late_outputs(late_own, down_own, units, cells)
    at = lax.axis_index(ALL)
    gains = gains.reshape(3, width)
    own_gains = lax.dynamic_slice(gains, (0, at * shard), (2, shard))
    onorm_own = lax.dynamic_slice(gains, (2, at * (DV // shards)), (1, DV // shards))
    small_rows = in_small.T
    return (
        result.reshape(tokens.shape),
        input_grad.reshape(tokens.shape),
        own_gains[0],
        in_main.reshape(shard, heads, QKV + DV),
        in_small[:, : 2 * heads].reshape(shard, heads, 2),
        small_rows[conv_at:conv_end].reshape(CONV, heads, -1),
        small_rows[conv_end, : 2 * heads].reshape(2, heads),
        onorm_own[0],
        grad_out.reshape(heads, DV, -1),
        own_gains[1],
        jnp.stack([grad_gate, grad_up], axis=1),
        grad_down,
    )


def solution(mesh):
    weights = P(ALL)
    in_specs = (
        P("batch", "seq", None),
        P("batch"),
        weights,
        P(ALL, "head", None),
        P(ALL, "head", None),
        P(None, "head", ALL),
        P(None, "head"),
        weights,
        P("head", None, ALL),
        weights,
        P(ALL, None, "head"),
        P("head", ALL),
        P("batch", "seq", None),
    )
    out_specs = (
        P("batch", "seq", None),
        P("batch", "seq", None),
        weights,
        P(ALL, "head", None),
        P(ALL, "head", None),
        P(None, "head", ALL),
        P(None, "head"),
        weights,
        P("head", None, ALL),
        weights,
        P(ALL, None, "head"),
        P("head", ALL),
    )
    return jax.shard_map(
        per_device, mesh=mesh, in_specs=in_specs, out_specs=out_specs, check_vma=False
    )
```

```python
import functools

import jax
import jax.numpy as jnp
from jax import lax
from jax.experimental import pallas as pl
from jax.experimental.pallas import tpu as pltpu
from jax.sharding import PartitionSpec as P

DK = 128
DV = 256
CONV = 4
QKV = 2 * DK + DV
CHUNK = 128
HALO = 16
PAD = 128

bf16 = jnp.bfloat16
f32 = jnp.float32
epsilon = 1e-06
NN = ((1,), (0,))
NT = ((1,), (1,))
TN = ((0,), (0,))


def mm(a, b, dims=NN):
    return lax.dot_general(
        a.astype(bf16), b.astype(bf16), (dims, ((), ())), preferred_element_type=f32
    )


def split_mm(a, b):
    a_high, b_high = a.astype(bf16), b.astype(bf16)
    a_low = (a - a_high.astype(f32)).astype(bf16)
    b_low = (b - b_high.astype(f32)).astype(bf16)
    return mm(a_high, b_high) + (mm(a_high, b_low) + mm(a_low, b_high))


def iotas(n):
    return (
        lax.broadcasted_iota(jnp.int32, (n, n), 0),
        lax.broadcasted_iota(jnp.int32, (n, n), 1),
    )


def unit_lower_inverses(mats):
    n = mats[0].shape[0]
    rows, cols = iotas(n)
    eye = (rows == cols).astype(f32)
    pair = ((rows >> 1) == (cols >> 1)) & (rows > cols)
    inverses = [eye - jnp.where(pair, a, 0.0) for a in mats]
    shift = 1
    while (1 << shift) < n:
        corner = ((rows >> (shift + 1)) == (cols >> (shift + 1))) & (
            (rows >> shift) > (cols >> shift)
        )
        firsts = [mm(jnp.where(corner, a, 0.0), x) for a, x in zip(mats, inverses)]
        inverses = [x - mm(x, y) for x, y in zip(inverses, firsts)]
        shift += 1
    residuals = [eye - x - split_mm(a, x) for a, x in zip(mats, inverses)]
    return [x + mm(x, r) for x, r in zip(inverses, residuals)]


def sigmoid(v):
    return 1.0 / (1.0 + jnp.exp(-v))


def softplus(v):
    small = jnp.exp(-jnp.abs(v))
    one_more = 1.0 + small
    gap = one_more - 1.0
    exact = gap == 0.0
    tail = jnp.where(exact, small, jnp.log(one_more) * small / jnp.where(exact, 1.0, gap))
    return jnp.maximum(v, 0.0) + tail


def to_row(column, eye):
    return jnp.sum(jnp.where(eye, column, 0.0), axis=0, keepdims=True)


def pick(block, lane):
    lanes = lax.broadcasted_iota(jnp.int32, block.shape, 1)
    return jnp.sum(jnp.where(lanes == lane, block, 0.0), axis=1, keepdims=True)


def gates(logits, decay_ref, head):
    rate = jnp.exp(jnp.full((1, 1), decay_ref[0, head], f32))
    shifted_logit = pick(logits, 2 * head) + decay_ref[1, head]
    strength = sigmoid(pick(logits, 2 * head + 1))
    log_gate = -rate * softplus(shifted_logit)
    return log_gate, strength, rate, shifted_logit


def decays(log_gate, lower, upper, eye):
    gate_row = to_row(log_gate, eye)
    column = jnp.sum(jnp.where(lower, gate_row, 0.0), axis=1, keepdims=True)
    row = jnp.sum(jnp.where(upper, log_gate, 0.0), axis=0, keepdims=True)
    ratio = jnp.where(lower, jnp.exp(jnp.where(lower, column - row, 0.0)), 0.0)
    total = jnp.sum(log_gate, axis=0, keepdims=True)
    return column, total, ratio


def load_conv_input(main_ref, halo_ref, start, x_scr, first):
    length = main_ref.shape[0]
    positions = first + lax.broadcasted_iota(jnp.int32, (length, 1), 0)
    live = (positions >= start).astype(f32)
    before = first - HALO + lax.broadcasted_iota(jnp.int32, (HALO, 1), 0)
    lived = (before >= start).astype(f32)
    x_scr[pl.ds(0, HALO), :] = (halo_ref[0] * lived).astype(bf16).astype(f32)
    x_scr[pl.ds(HALO, length), :] = (main_ref[...] * live).astype(bf16).astype(f32)


def convolve(x_scr, conv, at):
    total = x_scr[pl.ds(at + HALO - CONV + 1, CHUNK), :] * conv[0:1]
    for j in range(1, CONV):
        total = total + x_scr[pl.ds(at + HALO - CONV + 1 + j, CHUNK), :] * conv[j : j + 1]
    return total


def unit(rows):
    return rows * lax.rsqrt(jnp.sum(rows * rows, axis=1, keepdims=True) + epsilon)


MESH = pl.DeviceIdType.MESH
SUB = 128


def head_copy(src, dst, send_sem, recv_sem, peer):
    return pltpu.make_async_remote_copy(
        src_ref=src, dst_ref=dst, send_sem=send_sem, recv_sem=recv_sem,
        device_id={"head": peer}, device_id_type=MESH,
    )


def greet_heads(me, peers):
    barrier = pltpu.get_barrier_semaphore()
    for k in range(1, peers):
        pl.semaphore_signal(barrier, inc=1, device_id={"head": me ^ k}, device_id_type=MESH)
    pl.semaphore_wait(barrier, peers - 1)


def part(ref, start, size):
    return ref.at[pl.ds(pl.multiple_of(start, size), size)]


def piece_rows(owner, t, total, subs):
    return pl.ds(pl.multiple_of(t * (total // subs) + owner * SUB, SUB), SUB)


def take(ref, owner, subs):
    total = ref.shape[0]
    return jnp.concatenate(
        [ref[piece_rows(owner, t, total, subs), :] for t in range(subs)], axis=0
    )


class Pieces:
    def __init__(self, source, target, total, subs, sems):
        self.source, self.target, self.total, self.subs, self.sems = source, target, total, subs, sems

    def at(self, ref, owner, t):
        rows = piece_rows(owner, t, self.total, self.subs)
        if ref.shape[0] != self.total:
            rows = pl.ds(t * SUB, SUB)
        return ref.at[rows]

    def copies(self, owner):
        return [
            pltpu.make_async_copy(
                self.at(self.source, owner, t), self.at(self.target, owner, t),
                self.sems.at[owner, t],
            )
            for t in range(self.subs)
        ]

    def start(self, owner):
        for copy in self.copies(owner):
            copy.start()

    def wait(self, owner):
        for copy in self.copies(owner):
            copy.wait()


class Spread:
    def __init__(self, buffer, subs, me, send_sem, recv_sem):
        self.buffer, self.subs, self.me = buffer, subs, me
        self.send_sem, self.recv_sem = send_sem, recv_sem

    def region(self, owner, t, half):
        rows = piece_rows(owner, t, self.buffer.shape[0], self.subs)
        middle = self.buffer.shape[1] // 2
        if half is None:
            return self.buffer.at[rows]
        return self.buffer.at[rows, pl.ds(half * middle, middle)]

    def put(self, t, value):
        self.buffer[piece_rows(self.me, t, self.buffer.shape[0], self.subs), :] = value

    def copy(self, kind, t, owner):
        at = self.region(owner, t, None if kind < 2 else kind - 2)
        to = self.me ^ (1 if kind in (0, 3) else 2)
        return head_copy(at, at, self.send_sem.at[kind, t], self.recv_sem.at[kind, t], to)

    def start(self, t):
        self.copy(0, t, self.me).start()
        self.copy(1, t, self.me).start()

    def forward(self, t):
        self.copy(0, t, self.me ^ 1).wait_recv()
        self.copy(2, t, self.me ^ 1).start()
        self.copy(1, t, self.me ^ 2).wait_recv()
        self.copy(3, t, self.me ^ 2).start()

    def finish(self, t):
        self.copy(2, t, self.me ^ 3).wait_recv()
        self.copy(3, t, self.me ^ 3).wait_recv()

    def drain(self, t):
        for kind, owner in enumerate((0, 0, 1, 2)):
            self.copy(kind, t, self.me ^ owner).wait_send()


class Combine:
    def __init__(self, send, recv, relay, me, send_sem, recv_sem, piece):
        self.send, self.recv, self.relay, self.me = send, recv, relay, me
        self.send_sem, self.recv_sem, self.piece = send_sem, recv_sem, piece
        self.middle = send.shape[2] // 2

    def rows(self, t):
        return pl.ds(pl.multiple_of(t * self.piece, self.piece), self.piece)

    def copy(self, kind, t):
        rows, low, high = self.rows(t), pl.ds(0, self.middle), pl.ds(self.middle, self.middle)
        source, target, to = (
            (self.send.at[3, rows, low], self.relay.at[0, rows], 1),
            (self.send.at[3, rows, high], self.relay.at[1, rows], 2),
            (self.send.at[1, rows, low], self.recv.at[0, rows, low], 1),
            (self.send.at[2, rows, high], self.recv.at[1, rows, high], 2),
            (self.send.at[1, rows, high], self.recv.at[0, rows, high], 1),
            (self.send.at[2, rows, low], self.recv.at[1, rows, low], 2),
        )[kind]
        return head_copy(
            source, target, self.send_sem.at[kind, t], self.recv_sem.at[kind, t], self.me ^ to
        )

    def start(self, k, t):
        if k == 3:
            self.copy(0, t).start()
            self.copy(1, t).start()
        else:
            self.copy(k + 1, t).start()

    def combine(self, t):
        rows = self.rows(t)
        for k, at in ((1, pl.ds(self.middle, self.middle)), (2, pl.ds(0, self.middle))):
            self.copy(2 - k, t).wait_recv()
            both = self.send[k, rows, at].astype(f32) + self.relay[2 - k, rows, :].astype(f32)
            self.send[k, rows, at] = both.astype(bf16)
            self.copy(3 + k, t).start()

    def collect(self, t):
        for kind in range(2, 6):
            self.copy(kind, t).wait_recv()
        return self.total(self.rows(t))

    def total(self, rows):
        return (
            self.send[0, rows, :].astype(f32)
            + self.recv[0, rows, :].astype(f32)
            + self.recv[1, rows, :].astype(f32)
        )

    def drain(self, t):
        for kind in range(6):
            self.copy(kind, t).wait_send()


def sum_buffers(rows, width, pieces):
    return [
        pltpu.VMEM((4, rows, width), bf16),
        pltpu.VMEM((2, rows, width), bf16),
        pltpu.VMEM((2, rows, width // 2), bf16),
        pltpu.SemaphoreType.DMA((6, pieces)),
        pltpu.SemaphoreType.DMA((6, pieces)),
        pltpu.SemaphoreType.DMA((4, pieces)),
        pltpu.SemaphoreType.DMA((4, pieces)),
    ]


class GroupScatter:
    def __init__(self, source, columns, core_recv, seq_send, seq_recv, sems):
        self.source, self.columns = source, columns
        self.core_recv, self.seq_send, self.seq_recv, self.sems = core_recv, seq_send, seq_recv, sems
        self.place, self.core = lax.axis_index("seq"), lax.axis_index("batch")
        self.places, self.shard = core_recv.shape[0], core_recv.shape[1]

    def rows(self, k, core):
        at = ((self.place ^ k) * 2 + core) * self.shard
        return pl.ds(pl.multiple_of(at, self.shard), self.shard)

    def core_copy(self, k):
        return along(
            "batch", self.source.at[self.rows(k, 1 - self.core), self.columns],
            self.core_recv.at[k], self.sems.at[0, k], self.sems.at[1, k], 1 - self.core,
        )

    def seq_copy(self, k):
        return along(
            "seq", self.seq_send.at[k], self.seq_recv.at[k], self.sems.at[2, k],
            self.sems.at[3, k], self.place ^ k,
        )

    def pass_on(self, k):
        self.core_copy(k).wait_recv()
        own = self.source[self.rows(k, self.core), self.columns].astype(f32)
        self.seq_send[k] = (own + self.core_recv[k].astype(f32)).astype(bf16)

        @pl.when(k > 0)
        def _():
            self.seq_copy(k).start()

    def finish(self):
        total = self.seq_send[0].astype(f32)
        for k in range(1, self.places):
            self.seq_copy(k).wait_recv()
            total = total + self.seq_recv[k].astype(f32)
        return total

    def drain(self):
        for k in range(self.places):
            self.core_copy(k).wait_send()
        for k in range(1, self.places):
            self.seq_copy(k).wait_send()


class LineScatter:
    def __init__(self, own, core_recv, recv, sems):
        self.own, self.core_recv, self.recv, self.sems = own, core_recv, recv, sems
        self.place, self.core = lax.axis_index("seq"), lax.axis_index("batch")
        self.places = own.shape[0]

    def clear(self):
        @pl.when(self.place == 0)
        def _():
            self.recv[0] = jnp.zeros_like(self.recv[0])

        @pl.when(self.place == self.places - 1)
        def _():
            self.recv[self.places] = jnp.zeros_like(self.recv[0])

    def core_copy(self, d, source):
        return along(
            "batch", source, self.core_recv.at[d], self.sems.at[0, d], self.sems.at[1, d],
            1 - self.core,
        )

    def add_core(self, d, source):
        self.core_copy(d, source).wait_recv()
        self.add(d, self.core_recv[d])

    def add(self, d, other):
        self.own[d] = (self.own[d].astype(f32) + other.astype(f32)).astype(bf16)

    def move(self, d):
        right = d > self.place
        to = jnp.clip(jnp.where(right, self.place + 1, self.place - 1), 0, self.places - 1)
        slot = jnp.where(right | (to != d), d, self.places)
        return along(
            "seq", self.own.at[d], self.recv.at[slot], self.sems.at[2, d], self.sems.at[3, slot], to
        )

    def arrived(self, slot):
        return along(
            "seq", self.own.at[0], self.recv.at[slot], self.sems.at[2, 0], self.sems.at[3, slot],
            jnp.where(self.place > 0, self.place - 1, self.places - 1),
        )

    def advance(self, hop):
        last = self.places - 1

        def towards(d, active, through):
            @pl.when(active)
            def _():
                @pl.when(through)
                def _():
                    self.arrived(d).wait_recv()
                    self.add(d, self.recv[d])

                self.move(d).start()

        turn = hop - self.place
        d = jnp.clip(last - turn, 0, last)
        towards(d, (turn >= 0) & (last - turn > self.place), self.place > 0)
        turn = hop - (last - self.place)
        d = jnp.clip(turn, 0, last)
        towards(d, (turn >= 0) & (turn < self.place), self.place < last)

    def finish(self):
        @pl.when(self.place > 0)
        def _():
            self.arrived(self.place).wait_recv()

        @pl.when(self.place < self.places - 1)
        def _():
            self.arrived(self.places).wait_recv()

        return (
            self.own[self.place].astype(f32)
            + self.recv[self.place].astype(f32)
            + self.recv[self.places].astype(f32)
        )

    def drain(self, source):
        for d in range(self.places):
            self.core_copy(d, source(d)).wait_send()

            @pl.when(self.place != d)
            def _():
                self.move(d).wait_send()


def line_buffers(places, shard, columns):
    return [
        pltpu.VMEM((places, shard, columns), bf16),
        pltpu.VMEM((places, shard, columns), bf16),
        pltpu.VMEM((places + 1, shard, columns), bf16),
        pltpu.SemaphoreType.DMA((4, places + 1)),
    ]


def scatter_buffers(places, shard, columns):
    return [pltpu.VMEM((places, shard, columns), bf16)] * 3 + [
        pltpu.SemaphoreType.DMA((4, places))
    ]


def greet_group(me, peers, places, cores):
    barrier = pltpu.get_barrier_semaphore()
    group = places * cores
    flat = lax.axis_index("seq") * cores + lax.axis_index("batch")
    for k in range(1, peers):
        pl.semaphore_signal(barrier, inc=1, device_id={"head": me ^ k}, device_id_type=MESH)
    for d in range(1, group):
        to = lax.rem(flat + d, group)
        pl.semaphore_signal(
            barrier, inc=1, device_id={"seq": to // cores, "batch": lax.rem(to, cores)},
            device_id_type=MESH,
        )
    pl.semaphore_wait(barrier, peers + group - 2)


def anywhere():
    return pl.BlockSpec(memory_space=pl.ANY)


def vmem():
    return pl.BlockSpec(memory_space=pltpu.VMEM)


def along(axis, source, target, send_sem, recv_sem, to):
    return pltpu.make_async_remote_copy(
        src_ref=source, dst_ref=target, send_sem=send_sem, recv_sem=recv_sem,
        device_id={axis: to}, device_id_type=MESH,
    )


def forward_kernel(
    heads, places, start_ref, decay_ref, main_ref, halo_ref, rate_ref, conv_ref,
    qkv_ref, inv_ref, n_ref, qe_ref, tot_ref, trans_ref, s_ref, mixed_ref,
    x_scr, b_scr, o_scr, carried_scr, send, recv, send_sem, recv_sem,
):
    step = pl.program_id(0)
    chains = n_ref.shape[0]
    count = n_ref.shape[1]
    length = main_ref.shape[0]
    place = lax.axis_index("seq")
    lag = jnp.minimum(place, chains - 1)

    @pl.when(step == 0)
    def _():
        barrier = pltpu.get_barrier_semaphore()

        @pl.when(place > 0)
        def _():
            pl.semaphore_signal(
                barrier, inc=1, device_id={"seq": place - 1}, device_id_type=MESH
            )

        @pl.when(place == 0)
        def _():
            recv[...] = jnp.zeros_like(recv)

        @pl.when(place < places - 1)
        def _():
            pl.semaphore_wait(barrier, 1)

    @pl.when(step < chains)
    def _():
        head = step % heads
        load_conv_input(
            main_ref, halo_ref, start_ref[jnp.minimum(step, chains - 1) // heads], x_scr, place * length
        )
        conv = conv_ref[...]
        rows, cols = iotas(CHUNK)
        lower, upper, eye = rows >= cols, rows <= cols, rows == cols
        parts = []
        for c in range(count):
            at = c * CHUNK
            convolved = convolve(x_scr, conv, at)
            active = convolved * sigmoid(convolved)
            q = (unit(active[:, :DK]) * DK ** (-0.5)).astype(bf16)
            k = unit(active[:, DK : 2 * DK]).astype(bf16)
            v = active[:, 2 * DK :].astype(bf16)
            qkv_ref[pl.ds(at, CHUNK), 0:DK] = q
            qkv_ref[pl.ds(at, CHUNK), DK : 2 * DK] = k
            qkv_ref[pl.ds(at, CHUNK), 2 * DK :] = v
            log_gate, strength, _, _ = gates(rate_ref[pl.ds(at, CHUNK), :], decay_ref, head)
            column, total, ratio = decays(log_gate, lower, upper, eye)
            products = mm(jnp.concatenate([k, q], axis=0), k, NT)
            coupling = jnp.where(rows > cols, strength * ratio * products[:CHUNK], 0.0)
            scores = (ratio * products[CHUNK:]).astype(bf16)
            parts.append((q, k, v, strength, column, total, coupling, scores))
        inverses = unit_lower_inverses([p[6] for p in parts])
        maps = []
        for c in range(count):
            q, k, v, strength, column, total, _, scores = parts[c]
            growth = jnp.exp(column)
            kf, vf, qf = k.astype(f32), v.astype(f32), q.astype(f32)
            inverse = inverses[c].astype(bf16)
            inv_ref[0, c] = inverse
            target = jnp.concatenate([(strength * growth) * kf, strength * vf], axis=1)
            solved = mm(inverse, target).astype(bf16)
            read = mm(scores, solved)
            qe_ref[step, c] = (growth * qf - read[:, :DK]).astype(bf16)
            o_scr[step, pl.ds(c * CHUNK, CHUNK), :] = read[:, DK:]
            written = mm(jnp.exp(total - column) * kf, solved, TN)
            low_n = written[:, :DK].astype(bf16)
            n_ref[step, c] = low_n
            b_scr[step, c] = written[:, DK:]
            whole = jnp.exp(total)
            tot_ref[step, pl.ds(c, 1), :] = jnp.broadcast_to(whole, (1, DK))
            maps.append((low_n, written[:, DK:], whole))
        low_n, b, whole = maps[0]
        trans = whole * eye.astype(f32) - low_n.astype(f32)
        carried = b
        for low_n, b, whole in maps[1:]:
            both = jnp.concatenate([trans, carried], axis=1)
            moved = whole * both - mm(low_n, both)
            trans = moved[:, :DK]
            carried = moved[:, DK:] + b
        trans_ref[step] = trans.astype(bf16)
        carried_scr[step] = carried

    @pl.when(step >= chains)
    def _():
        chain = jnp.maximum(step - chains, 0)
        state = recv[chain].astype(f32)
        for c in range(count):
            low_state = state.astype(bf16)
            s_ref[0, c] = low_state
            both = mm(jnp.concatenate([n_ref[chain, c], qe_ref[chain, c]], axis=0), low_state)
            whole = tot_ref[chain, pl.ds(c, 1), 0:1]
            state = whole * state - both[:DK] + b_scr[chain, c]
            at = pl.ds(c * CHUNK, CHUNK)
            mixed_ref[at, :] = o_scr[chain, at, :] + both[DK:]

    def passed(chain):
        return along(
            "seq", send.at[chain], recv.at[chain], send_sem.at[chain], recv_sem.at[chain],
            jnp.minimum(place + 1, places - 1),
        )

    relayed = step - lag

    @pl.when((relayed >= 0) & (relayed < chains))
    def _():
        chain = jnp.clip(relayed, 0, chains - 1)

        @pl.when(place > 0)
        def _():
            passed(chain).wait_recv()

        @pl.when(place < places - 1)
        def _():
            leaving = mm(trans_ref[chain], recv[chain]) + carried_scr[chain]
            send[chain] = leaving.astype(bf16)
            passed(chain).start()

    @pl.when((step == 2 * chains - 1) & (place < places - 1))
    def _():
        for chain in range(chains):
            passed(chain).wait_send()


def early(chains, make):
    return lambda j: make(jnp.minimum(j, chains - 1))


def late(chains, make):
    return lambda j: make(jnp.maximum(j - chains, 0))


def forward_rule(starts, decay_par, projected, halo, conv_w, seqs, heads):
    places = lax.axis_size("seq")
    chains = seqs * heads
    length = projected.shape[0] // seqs
    count = length // CHUNK
    rates_at = heads * QKV // PAD
    row = lambda first: lambda i: (i // heads, first + i % heads)
    whole = lambda *dims: pl.BlockSpec(dims, lambda j: (0,) * len(dims))
    shape = jax.ShapeDtypeStruct
    return pl.pallas_call(
        functools.partial(forward_kernel, heads, places),
        grid=(2 * chains,),
        in_specs=[
            smem(),
            smem(),
            pl.BlockSpec((length, QKV), early(chains, row(0))),
            pl.BlockSpec((1, HALO, QKV), early(chains, lambda i: (i // heads, 0, i % heads))),
            pl.BlockSpec((length, PAD), early(chains, lambda i: (i // heads, rates_at))),
            pl.BlockSpec((CONV, QKV), early(chains, lambda i: (0, i % heads))),
        ],
        out_specs=[
            pl.BlockSpec((length, QKV), early(chains, row(0))),
            pl.BlockSpec((1, count, CHUNK, CHUNK), early(chains, lambda i: (i, 0, 0, 0))),
            whole(chains, count, DK, DK),
            whole(chains, count, CHUNK, DK),
            whole(chains, count, DK),
            whole(chains, DK, DK),
            pl.BlockSpec((1, count, DK, DV), late(chains, lambda i: (i, 0, 0, 0))),
            pl.BlockSpec((length, DV), late(chains, row(0))),
        ],
        out_shape=[
            shape((seqs * length, heads * QKV), bf16),
            shape((chains, count, CHUNK, CHUNK), bf16),
            shape((chains, count, DK, DK), bf16),
            shape((chains, count, CHUNK, DK), bf16),
            shape((chains, count, DK), f32),
            shape((chains, DK, DK), bf16),
            shape((chains, count, DK, DV), bf16),
            shape((seqs * length, heads * DV), f32),
        ],
        scratch_shapes=[
            pltpu.VMEM((HALO + length, QKV), f32),
            pltpu.VMEM((chains, count, DK, DV), f32),
            pltpu.VMEM((chains, length, DV), f32),
            pltpu.VMEM((chains, DK, DV), f32),
            pltpu.VMEM((chains, DK, DV), bf16),
            pltpu.VMEM((chains, DK, DV), bf16),
            pltpu.SemaphoreType.DMA((chains,)),
            pltpu.SemaphoreType.DMA((chains,)),
        ],
        compiler_params=pltpu.CompilerParams(
            dimension_semantics=("arbitrary",), collective_id=3, has_side_effects=True,
            vmem_limit_bytes=48 * 2**20,
        ),
        name="forward_rule",
    )(starts, decay_par, projected, halo, projected, conv_w)


def backward_kernel(
    heads, places, peers, cores, start_ref, decay_ref,
    dn_ref, mixed_ref, og_ref, o_gain_ref, n_ref, qe_ref, tot_ref, trans_ref,
    qkv_ref, inv_ref, s_ref, main_ref, halo_ref, rate_ref, conv_ref,
    hidden_ref, hgrad_ref, gain_ref, ffn_gain_ref, ffnp_hbm, win_hbm, wog_hbm, nin_hbm, x_hbm,
    late_hbm,
    out_hbm, igrad_hbm, gains_out, grad_out, small_out, late_out,
    dp_ref, x_scr, g_scr, do_scr, own_scr, send, recv, tail_scr, halo_send, halo_recv,
    conv_scr, decay_scr, o_gain_scr, whole_out, whole_in, win_v, wog_v, nin_v, x_v, conv_source,
    gate_source, extras_v, gains_v, gains_recv, gains_sum, gains_all,
    send_sem, recv_sem, halo_send_sem, halo_recv_sem, load_sem, in_sem, late_sem, x_sem, out_sem, hs, hr, gs, gr,
    sent, got, relay, sum_send, sum_recv, gather_send, gather_recv,
    in_sent, in_got, in_relay, in_sum_send, in_sum_recv, in_gather_send, in_gather_recv,
    conv_own, conv_core, conv_recv, conv_sems,
    gate_own, gate_core, gate_recv, gate_sems,
    late_own, late_core, late_recv, late_sems,
):
    step = pl.program_id(0)
    chains = n_ref.shape[0]
    count = n_ref.shape[1]
    length = main_ref.shape[0]
    seqs = chains // heads
    total, width = whole_out.shape
    conv_cols = heads * QKV
    values = heads * DV
    in_cols = conv_cols + values
    place, core = lax.axis_index("seq"), lax.axis_index("batch")
    lag = jnp.minimum(places - 1 - place, chains - 1)
    me = lax.axis_index("head")
    own_rows = hidden_ref.shape[0]
    subs = own_rows // SUB
    group = places * cores
    shard = width // group
    pair = cores * shard
    flat = place * cores + core

    ring = Spread(whole_out, subs, me, gather_send, gather_recv)
    sums = Combine(sent, got, relay, me, sum_send, sum_recv, own_rows)
    in_ring = Spread(whole_in, subs, me, in_gather_send, in_gather_recv)
    in_sums = Combine(in_sent, in_got, in_relay, me, in_sum_send, in_sum_recv, SUB)
    conv_line = LineScatter(conv_own, conv_core, conv_recv, conv_sems)
    gate_line = LineScatter(gate_own, gate_core, gate_recv, gate_sems)
    late_line = LineScatter(late_own, late_core, late_recv, late_sems)

    def late_rows(d, at_core):
        return late_hbm.at[pl.ds(pl.multiple_of((d * cores + at_core) * shard, shard), shard)]

    def late_source(d):
        return late_rows(d, 1 - core)

    def late_load(d):
        return pltpu.make_async_copy(late_rows(d, core), late_own.at[d], late_sem.at[d])

    def hops(third):
        return range(third * (places - 1) // 3, (third + 1) * (places - 1) // 3)

    def far_first(i):
        return jnp.where(i % 2 == 0, places - 1 - i // 2, i // 2)

    def halves(grads):
        top, low = grads[:shard], grads[shard:]
        return jnp.where(core == 0, top, low), jnp.where(core == 0, low, top)
    out_store = Pieces(whole_out, out_hbm, total, subs, out_sem.at[0])
    in_store = Pieces(whole_in, igrad_hbm, total, subs, out_sem.at[1])
    own_x = Pieces(x_hbm, x_v, total, subs, x_sem)
    loads = [
        pltpu.make_async_copy(win_hbm, win_v, in_sem.at[0]),
        pltpu.make_async_copy(wog_hbm.at[:, pl.ds(0, values)], wog_v, in_sem.at[1]),
        pltpu.make_async_copy(nin_hbm, nin_v, in_sem.at[2]),
    ]

    def ffn_loads(k):
        return [
            pltpu.make_async_copy(
                ffnp_hbm.at[piece_rows(me ^ k, t, total, subs)], sent.at[k, pl.ds(t * SUB, SUB)],
                load_sem.at[k, t],
            )
            for t in range(subs)
        ]

    def passed(chain):
        return along(
            "seq", send.at[chain], recv.at[chain], send_sem.at[chain], recv_sem.at[chain],
            jnp.maximum(place - 1, 0),
        )

    def returned(chain):
        return along(
            "seq", halo_send.at[chain], halo_recv.at[chain], halo_send_sem.at[chain],
            halo_recv_sem.at[chain], jnp.maximum(place - 1, 0),
        )

    @pl.when(step == 0)
    def _():
        for k in range(peers - 1, -1, -1):
            for load in ffn_loads(k):
                load.start()

        @pl.when(place == places - 1)
        def _():
            recv[...] = jnp.zeros_like(recv)
            halo_recv[...] = jnp.zeros_like(halo_recv)

        decay_scr[...] = jnp.zeros_like(decay_scr)
        o_gain_scr[...] = jnp.zeros_like(o_gain_scr)
        extras_v[...] = jnp.zeros_like(extras_v)
        for line in (conv_line, gate_line, late_line):
            line.clear()
        for d in range(places):
            late_load(d).start()
        for load in loads:
            load.start()
        own_x.start(me)
        greet_group(me, peers, places, cores)
        for k in range(peers - 1, 0, -1):
            for load in ffn_loads(k):
                load.wait()
            sums.start(k, 0)
        for load in ffn_loads(0):
            load.wait()
        for d in range(places):
            late_line.core_copy(d, late_source(d)).start()

    @pl.when(step < chains)
    def _():
        gain = o_gain_ref[0:1]
        first = (step // heads) * length
        og_at = pl.ds(pl.multiple_of(conv_cols + (step % heads) * DV, DV), DV)
        state = jnp.zeros((DK, DV), f32)
        gain_total = jnp.zeros((1, DV), f32)
        for c in reversed(range(count)):
            at = pl.ds(c * CHUNK, CHUNK)
            mixed, og, dn = mixed_ref[at, :], og_ref[at, :], dn_ref[at, :]
            inverse = lax.rsqrt(jnp.mean(mixed * mixed, axis=1, keepdims=True) + epsilon)
            scaled = mixed * inverse
            sig = sigmoid(og)
            silu = og * sig
            through = dn * scaled
            gain_total = gain_total + jnp.sum(through * silu, axis=0, keepdims=True)
            dp_ref[pl.ds(pl.multiple_of(first + c * CHUNK, CHUNK), CHUNK), og_at] = (
                through * gain * sig * (1.0 + og * (1.0 - sig))
            ).astype(bf16)
            weighted = dn * gain * silu
            dmixed = inverse * (
                weighted - scaled * jnp.mean(weighted * scaled, axis=1, keepdims=True)
            )
            dmixed = dmixed.astype(bf16)
            do_scr[step, at, :] = dmixed
            decay = tot_ref[step, pl.ds(c, 1), 0:1]
            state = (
                decay * state - mm(n_ref[step, c], state, TN) + mm(qe_ref[step, c], dmixed, TN)
            )
        o_gain_scr[0:1, :] = o_gain_scr[0:1, :] + gain_total
        own_scr[step] = state

    @pl.when(step >= chains)
    def _():
        chain = jnp.maximum(step - chains, 0)
        seq, head = chain // heads, chain % heads
        first = seq * length
        start = start_ref[seq]
        load_conv_input(main_ref, halo_ref, start, x_scr, place * length)
        conv = conv_ref[...]
        rows, cols = iotas(CHUNK)
        lower, upper, eye = rows >= cols, rows <= cols, rows == cols
        strict = rows > cols
        state = recv[chain].astype(f32)
        leaving = [None] * count
        for c in reversed(range(count)):
            leaving[c] = state
            state = (
                tot_ref[chain, pl.ds(c, 1), 0:1] * state
                - mm(n_ref[chain, c], state, TN)
                + mm(qe_ref[chain, c], do_scr[chain, pl.ds(c * CHUNK, CHUNK), :], TN)
            )
        g_scr[pl.ds(0, 8), :] = jnp.zeros((8, QKV), f32)
        g_scr[pl.ds(8 + length, 8), :] = jnp.zeros((8, QKV), f32)
        rate_total = jnp.zeros((1, 1), f32)
        bias_total = jnp.zeros((1, 1), f32)
        conv_total = [jnp.zeros((1, QKV), f32) for _ in range(CONV)]
        lanes = lax.broadcasted_iota(jnp.int32, (CHUNK, PAD), 1)
        for c in range(count):
            at = pl.ds(c * CHUNK, CHUNK)
            q, k, v = qkv_ref[at, 0:DK], qkv_ref[at, DK : 2 * DK], qkv_ref[at, 2 * DK :]
            kf, vf = k.astype(f32), v.astype(f32)
            log_gate, strength, rate, logit = gates(rate_ref[at, :], decay_ref, head)
            column, total, ratio = decays(log_gate, lower, upper, eye)
            growth = jnp.exp(column)
            remain = jnp.exp(total - column)
            whole = jnp.exp(total)
            inverse = inv_ref[0, c]
            s0 = s_ref[0, c]
            do = do_scr[chain, at, :]
            grad_state = leaving[c]
            low_grad_state = grad_state.astype(bf16)
            kq = jnp.concatenate([k, q], axis=0)
            products = mm(kq, k, NT)
            kk, qk = products[:CHUNK], products[CHUNK:]
            reads = mm(kq, s0)
            ks, qs = reads[:CHUNK], reads[CHUNK:]
            fresh = vf - growth * ks
            pseudo = mm(inverse, strength * fresh).astype(bf16)
            scores = (ratio * qk).astype(bf16)
            dpseudo = mm(scores, do, TN) + mm(remain * kf, low_grad_state)
            dtarget = mm(inverse, dpseudo, TN)
            low_dtarget = dtarget.astype(bf16)
            dstrength = jnp.sum(dtarget * fresh, axis=1, keepdims=True)
            dlog = -(strength * growth) * jnp.sum(dtarget * ks, axis=1, keepdims=True)
            dv = strength * dtarget
            both = jnp.concatenate([low_dtarget, do], axis=0)
            outer = mm(both, pseudo, NT)
            dcoupling = jnp.where(strict, -outer[:CHUNK] * ratio, 0.0)
            by_strength = dcoupling * kk
            dstrength = dstrength + jnp.sum(by_strength, axis=1, keepdims=True)
            exponent = strength * by_strength
            dqk_f = jnp.where(lower, outer[CHUNK:] * ratio, 0.0)
            exponent = exponent + dqk_f * qk
            pair = jnp.concatenate([(dcoupling * strength).astype(bf16), dqk_f.astype(bf16)], axis=0)
            back = mm(both, s0, NT)
            wide = mm(pair, k)
            dq = growth * back[CHUNK:] + wide[CHUNK:]
            dkept = mm(pseudo, low_grad_state, NT)
            dk = (
                wide[:CHUNK]
                - (strength * growth) * back[:CHUNK]
                + mm(pair, kq, TN)
                + remain * dkept
            )
            dlog = dlog + growth * jnp.sum(do.astype(f32) * qs, axis=1, keepdims=True)
            from_kept = remain * jnp.sum(kf * dkept, axis=1, keepdims=True)
            dlog = dlog - from_kept + jnp.sum(exponent, axis=1, keepdims=True)
            dlog_row = to_row(dlog, eye) - jnp.sum(exponent, axis=0, keepdims=True)
            tail = jnp.sum(from_kept, axis=0, keepdims=True) + whole * jnp.sum(
                jnp.sum(grad_state * s0.astype(f32), axis=1, keepdims=True), axis=0, keepdims=True
            )
            dgate = jnp.sum(jnp.where(upper, dlog_row, 0.0), axis=1, keepdims=True) + tail
            slope = sigmoid(logit)
            drate0 = -rate * slope * dgate
            drate1 = dstrength * strength * (1.0 - strength)
            rate_total = rate_total + jnp.sum(dgate * log_gate, axis=0, keepdims=True)
            bias_total = bias_total + jnp.sum(drate0, axis=0, keepdims=True)
            here = pl.ds(pl.multiple_of(first + c * CHUNK, CHUNK), CHUNK)
            others = jnp.where(head == 0, 0.0, dp_ref[here, in_cols:].astype(f32))
            dp_ref[here, in_cols:] = jnp.where(
                lanes == 2 * head, drate0, jnp.where(lanes == 2 * head + 1, drate1, others)
            ).astype(bf16)
            convolved = convolve(x_scr, conv, c * CHUNK)
            sig = sigmoid(convolved)
            active = convolved * sig
            slope_conv = sig * (1.0 + convolved * (1.0 - sig))

            def unit_grad(rows_in, grad):
                inv_norm = lax.rsqrt(jnp.sum(rows_in * rows_in, axis=1, keepdims=True) + epsilon)
                y = rows_in * inv_norm
                return inv_norm * (grad - y * jnp.sum(y * grad, axis=1, keepdims=True))

            dq = dq.astype(bf16).astype(f32) * DK ** (-0.5)
            dk = dk.astype(bf16).astype(f32)
            dv = dv.astype(bf16).astype(f32)
            dconv = (
                jnp.concatenate(
                    [unit_grad(active[:, :DK], dq), unit_grad(active[:, DK : 2 * DK], dk), dv],
                    axis=1,
                )
                * slope_conv
            )
            g_scr[pl.ds(8 + c * CHUNK, CHUNK), :] = dconv
            for j in range(CONV):
                shifted_in = x_scr[pl.ds(c * CHUNK + HALO - CONV + 1 + j, CHUNK), :]
                conv_total[j] = conv_total[j] + jnp.sum(dconv * shifted_in, axis=0, keepdims=True)
        for j in range(CONV):
            tap = pl.ds(j * heads + head, 1)
            conv_scr[tap, :] = conv_total[j] + jnp.where(seq == 0, 0.0, conv_scr[tap, :])
        spots = lax.broadcasted_iota(jnp.int32, decay_scr.shape, 1)
        top = lax.broadcasted_iota(jnp.int32, decay_scr.shape, 0) == 0
        decay_scr[...] = decay_scr[...] + jnp.where(
            top & (spots == 2 * heads + head), rate_total, 0.0
        ) + jnp.where(top & (spots == 3 * heads + head), bias_total, 0.0)

        def conv_back(at, size):
            grad = g_scr[pl.ds(at + CONV - 1, size), :] * conv[0:1]
            for j in range(1, CONV):
                grad = grad + g_scr[pl.ds(at + CONV - 1 - j, size), :] * conv[j : j + 1]
            return grad

        halo_send[chain] = conv_back(0, 8)

        @pl.when(place > 0)
        def _():
            returned(chain).start()

        conv_at = pl.ds(pl.multiple_of(head * QKV, QKV), QKV)
        for c in range(count):
            grad = conv_back(8 + c * CHUNK, CHUNK)
            positions = place * length + c * CHUNK + lax.broadcasted_iota(
                jnp.int32, (CHUNK, 1), 0
            )
            live = (positions >= start).astype(f32)
            if c == count - 1:
                tail_scr[chain] = grad[CHUNK - HALO :]
            dp_ref[pl.ds(pl.multiple_of(first + c * CHUNK, CHUNK), CHUNK), conv_at] = (
                grad * live
            ).astype(bf16)

    @pl.when(step == chains - 1)
    def _():
        loads[2].wait()

        def gate_grads(i, carry):
            d = far_first(i)
            rows = pl.ds(pl.multiple_of(d * pair, pair), pair)
            mine, others = halves(mm(nin_v[rows, :], dp_ref[:, conv_cols:in_cols]))
            gate_own[d] = mine.astype(bf16)
            gate_source[d] = others.astype(bf16)
            gate_line.core_copy(d, gate_source.at[d]).start()
            return carry

        lax.fori_loop(0, places, gate_grads, 0)
        for d in range(places):
            late_load(d).wait()
            late_line.add_core(d, late_source(d))

    relayed = step - lag

    @pl.when((relayed >= 0) & (relayed < chains))
    def _():
        chain = jnp.clip(relayed, 0, chains - 1)

        @pl.when(place < places - 1)
        def _():
            passed(chain).wait_recv()

        @pl.when(place > 0)
        def _():
            earlier = mm(trans_ref[chain], recv[chain], TN) + own_scr[chain]
            send[chain] = earlier.astype(bf16)
            passed(chain).start()

    @pl.when(step == chains - 1)
    def _():
        sums.combine(0)

    @pl.when(step == chains)
    def _():
        for kind in range(2, 6):
            sums.copy(kind, 0).wait_recv()
        for t in range(subs):
            rows = pl.ds(t * SUB, SUB)
            ring.put(t, (hidden_ref[rows, :] + sums.total(rows)).astype(bf16))
            ring.start(t)
        out_store.start(me)

    @pl.when(step == chains + 2)
    def _():
        for t in range(subs):
            ring.forward(t)

    for third, at_step in enumerate((chains - 1, chains + 1, 2 * chains - 1)):

        @pl.when(step == at_step)
        def _():
            for hop in hops(third):
                late_line.advance(hop)

    for third, at_step in enumerate((chains, chains + 1, chains + 2)):

        @pl.when(step == at_step)
        def _():
            if third == 0:
                for d in range(places):
                    gate_line.add_core(d, gate_source.at[d])
            for hop in hops(third):
                gate_line.advance(hop)

    def mend_ends(seq):
        for head in range(heads):
            chain = seq * heads + head

            @pl.when(place < places - 1)
            def _():
                returned(chain).wait_recv()

            positions = (place + 1) * length - HALO + lax.broadcasted_iota(
                jnp.int32, (HALO, 1), 0
            )
            live = (positions >= start_ref[seq]).astype(f32)
            grad = tail_scr[chain] + jnp.concatenate(
                [jnp.zeros((HALO - 8, QKV), f32), halo_recv[chain]], axis=0
            )
            dp_ref[pl.ds((seq + 1) * length - HALO, HALO), pl.ds(head * QKV, QKV)] = (
                grad * live
            ).astype(bf16)

    def project(t):
        def one(i, carry):
            k = jnp.where(i == 0, peers - 1, lax.rem(i, peers - 1))
            rows = piece_rows(me ^ k, t, total, subs)
            partial = mm(dp_ref[rows, 0:conv_cols], win_v[:, 0:conv_cols], NT)
            partial = partial + mm(dp_ref[rows, conv_cols:in_cols], wog_v[...], NT)
            partial = partial + mm(dp_ref[rows, in_cols:], win_v[:, conv_cols:], NT)
            in_sent[k, pl.ds(t * SUB, SUB), :] = partial.astype(bf16)

            for kk in range(1, peers):

                @pl.when(k == kk)
                def _():
                    in_sums.start(kk, t)

            return carry

        lax.fori_loop(0, peers, one, 0)

    for t in range(seqs - 1):

        @pl.when(step == chains + (t + 1) * heads - 1)
        def _():
            mend_ends(t)
            if t == 0:
                for load in loads[:2]:
                    load.wait()
            project(t)

        @pl.when(step == chains + (t + 1) * heads)
        def _():
            in_sums.combine(t)

    def own_input_grads(t):
        rows = pl.ds(t * SUB, SUB)
        din = in_sums.collect(t)
        x = x_v[rows, :].astype(f32)
        inverse = lax.rsqrt(jnp.mean(x * x, axis=1, keepdims=True) + epsilon)
        scaled = x * inverse
        weighted = din * gain_ref[...]
        grad = hgrad_ref[rows, :] + inverse * (
            weighted - scaled * jnp.mean(weighted * scaled, axis=1, keepdims=True)
        )
        in_ring.put(t, grad.astype(bf16))
        in_ring.start(t)
        return jnp.sum(din * scaled, axis=0, keepdims=True)

    @pl.when(step == 2 * chains - 1)
    def _():
        own_x.wait(me)
        gain_part = jnp.zeros((1, width), f32)
        for t in range(seqs - 1):
            gain_part = gain_part + own_input_grads(t)
        mend_ends(seqs - 1)
        taps = CONV * heads
        per = QKV // group
        lanes = lax.broadcasted_iota(jnp.int32, (taps, PAD), 1)
        for q in range(group):
            at = per * q // PAD * PAD
            shift = (PAD // 2 - per * q) % PAD
            moved = conv_scr[:, at : at + PAD]
            if shift:
                moved = pltpu.roll(moved, shift, 1)
            kept = jnp.where((lanes >= PAD // 2) & (lanes < PAD // 2 + per), moved, 0.0)
            extras_v[q * shard : q * shard + taps, :] = kept + decay_scr[...]
        if seqs == 1:
            for load in loads[:2]:
                load.wait()

        def place_grads(i, carry):
            d = far_first(i)
            rows = pl.ds(pl.multiple_of(d * pair, pair), pair)
            mine, others = halves(mm(nin_v[rows, :], dp_ref[:, 0:conv_cols]))
            conv_own[d, :, 0:conv_cols] = mine.astype(bf16)
            conv_source[d, :, 0:conv_cols] = others.astype(bf16)
            mine, others = halves(mm(nin_v[rows, :], dp_ref[:, in_cols:]) + extras_v[rows, :])
            conv_own[d, :, conv_cols:] = mine.astype(bf16)
            conv_source[d, :, conv_cols:] = others.astype(bf16)
            conv_line.core_copy(d, conv_source.at[d]).start()

            @pl.when(i > 0)
            def _():
                before = far_first(jnp.maximum(i - 1, 0))
                conv_line.add_core(before, conv_source.at[before])

            return carry

        first_places = min(2, places)
        lax.fori_loop(0, first_places, place_grads, 0)
        project(seqs - 1)
        lax.fori_loop(first_places, places, place_grads, 0)
        before = far_first(places - 1)
        conv_line.add_core(before, conv_source.at[before])
        for hop in hops(0):
            conv_line.advance(hop)
        in_sums.combine(seqs - 1)
        gain_part = gain_part + own_input_grads(seqs - 1)
        lane_rows = width // 128
        gains_v[...] = jnp.zeros_like(gains_v)
        for r in range(lane_rows):
            gains_v[r : r + 1, :] = gain_part[:, r * 128 : (r + 1) * 128]
            gains_v[lane_rows + r : lane_rows + r + 1, :] = ffn_gain_ref[
                0:1, r * 128 : (r + 1) * 128
            ]
        for r in range(DV // 128):
            gains_v[2 * lane_rows + r : 2 * lane_rows + r + 1, :] = o_gain_scr[
                0:1, r * 128 : (r + 1) * 128
            ]

        def gains_copy(k):
            return head_copy(gains_v, gains_recv.at[k], hs.at[k], hr.at[k], me ^ k)

        def to_group(d):
            to = lax.rem(flat + d, group)
            return pltpu.make_async_remote_copy(
                src_ref=gains_sum, dst_ref=gains_all.at[d], send_sem=gs.at[d], recv_sem=gr.at[d],
                device_id={"seq": to // cores, "batch": lax.rem(to, cores)}, device_id_type=MESH,
            )

        for k in range(1, peers):
            gains_copy(k).start()
        for hop in hops(1):
            conv_line.advance(hop)
        in_store.start(me)
        for t in range(subs):
            ring.finish(t)
        for k in range(1, peers):
            out_store.start(me ^ k)
        gathered = gains_v[...]
        for k in range(1, peers):
            gains_copy(k).wait_recv()
            gathered = gathered + gains_recv[k]
        gains_sum[...] = gathered
        for d in range(1, group):
            to_group(d).start()
        for t in range(subs):
            in_ring.forward(t)
        for hop in hops(2):
            conv_line.advance(hop)
        in_store.start(me ^ 1)
        in_store.start(me ^ 2)
        for d in range(1, group):
            to_group(d).wait_recv()
            gathered = gathered + gains_all[d]
        gains_out[...] = gathered
        for t in range(subs):
            in_ring.finish(t)
        in_store.start(me ^ 3)
        late_out[...] = late_line.finish()
        grad = gate_line.finish()
        for head in range(heads):
            at = head * (QKV + DV) + QKV
            grad_out[:, at : at + DV] = grad[:, head * DV : (head + 1) * DV]
        grad = conv_line.finish()
        for head in range(heads):
            at = head * (QKV + DV)
            grad_out[:, at : at + QKV] = grad[:, head * QKV : (head + 1) * QKV]
        small_out[...] = grad[:, conv_cols:]
        for k in range(peers):
            out_store.wait(k)
            in_store.wait(k)

        @pl.when(place > 0)
        def _():
            for chain in range(chains):
                returned(chain).wait_send()
                passed(chain).wait_send()

        sums.drain(0)
        for t in range(subs):
            ring.drain(t)
            in_ring.drain(t)
            in_sums.drain(t)
        for k in range(1, peers):
            gains_copy(k).wait_send()
        for d in range(1, group):
            to_group(d).wait_send()
        conv_line.drain(lambda d: conv_source.at[d])
        gate_line.drain(lambda d: gate_source.at[d])
        late_line.drain(late_source)


def backward_rule(
    starts, decay_par, dn, mixed, og, projected, o_gain, n, qe, tot, trans, qkv, inv, states, halo,
    conv_w, hidden, hidden_grad, gain, ffn_gain_part, ffn_part, in_full, gate_full, turned, x, late_grads,
    heads,
):
    places, peers, cores = lax.axis_size("seq"), lax.axis_size("head"), lax.axis_size("batch")
    chains, count = n.shape[:2]
    seqs = chains // heads
    rows = projected.shape[0]
    length = rows // seqs
    width = hidden.shape[1]
    own_rows = hidden.shape[0]
    subs = own_rows // SUB
    rates_at = heads * QKV // PAD
    values = heads * DV
    cols = heads * (QKV + DV) + PAD
    group = places * cores
    shard = width // group
    gain_rows = 3 * width // 128
    row = lambda first: lambda i: (i // heads, first + i % heads)
    whole = lambda *dims: pl.BlockSpec(dims, lambda j: (0,) * len(dims))
    chain4 = lambda i: (i, 0, 0, 0)
    shape = jax.ShapeDtypeStruct
    per_chain = pltpu.SemaphoreType.DMA((chains,))
    per_peer = pltpu.SemaphoreType.DMA((peers,))
    per_member = pltpu.SemaphoreType.DMA((group,))
    pieces = pltpu.SemaphoreType.DMA((peers, subs))
    ffn_sums = sum_buffers(own_rows, width, subs)
    ffn_sums[3:5] = [pltpu.SemaphoreType.DMA((6, 1))] * 2
    return pl.pallas_call(
        functools.partial(backward_kernel, heads, places, peers, cores),
        grid=(2 * chains,),
        in_specs=[
            smem(),
            smem(),
            pl.BlockSpec((length, DV), early(chains, row(0))),
            pl.BlockSpec((length, DV), early(chains, row(0))),
            pl.BlockSpec((length, DV), early(chains, row(0))),
            whole(1, DV),
            whole(chains, count, DK, DK),
            whole(chains, count, CHUNK, DK),
            whole(chains, count, DK),
            whole(chains, DK, DK),
            pl.BlockSpec((length, QKV), late(chains, row(0))),
            pl.BlockSpec((1, count, CHUNK, CHUNK), late(chains, chain4)),
            pl.BlockSpec((1, count, DK, DV), late(chains, chain4)),
            pl.BlockSpec((length, QKV), late(chains, row(0))),
            pl.BlockSpec((1, HALO, QKV), late(chains, lambda i: (i // heads, 0, i % heads))),
            pl.BlockSpec((length, PAD), late(chains, lambda i: (i // heads, rates_at))),
            pl.BlockSpec((CONV, QKV), late(chains, lambda i: (0, i % heads))),
            whole(own_rows, width),
            whole(own_rows, width),
            whole(1, width),
            whole(8, width),
        ]
        + [anywhere()] * 6,
        out_specs=[
            anywhere(),
            anywhere(),
            whole(gain_rows, 128),
            whole(shard, cols - PAD),
            whole(shard, PAD),
            whole(shard, late_grads.shape[1]),
        ],
        out_shape=[
            shape((rows, width), bf16),
            shape((rows, width), bf16),
            shape((gain_rows, 128), f32),
            shape((shard, cols - PAD), f32),
            shape((shard, PAD), f32),
            shape((shard, late_grads.shape[1]), f32),
        ],
        scratch_shapes=[
            pltpu.VMEM((rows, cols), bf16),
            pltpu.VMEM((HALO + length, QKV), f32),
            pltpu.VMEM((16 + length, QKV), f32),
            pltpu.VMEM((chains, length, DV), bf16),
            pltpu.VMEM((chains, DK, DV), f32),
            pltpu.VMEM((chains, DK, DV), bf16),
            pltpu.VMEM((chains, DK, DV), bf16),
            pltpu.VMEM((chains, HALO, QKV), f32),
            pltpu.VMEM((chains, 8, QKV), f32),
            pltpu.VMEM((chains, 8, QKV), f32),
            pltpu.VMEM((CONV * heads, QKV), f32),
            pltpu.VMEM((CONV * heads, PAD), f32),
            pltpu.VMEM((8, DV), f32),
            pltpu.VMEM((rows, width), bf16),
            pltpu.VMEM((rows, width), bf16),
            pltpu.VMEM((width, cols - values), bf16),
            pltpu.VMEM((width, values), bf16),
            pltpu.VMEM((width, rows), bf16),
            pltpu.VMEM((own_rows, width), bf16),
            pltpu.VMEM((places, shard, cols - values), bf16),
            pltpu.VMEM((places, shard, values), bf16),
            pltpu.VMEM((width, PAD), f32),
            pltpu.VMEM((gain_rows, 128), f32),
            pltpu.VMEM((peers, gain_rows, 128), f32),
            pltpu.VMEM((gain_rows, 128), f32),
            pltpu.VMEM((group, gain_rows, 128), f32),
            per_chain, per_chain, per_chain, per_chain,
            pieces,
            pltpu.SemaphoreType.DMA((3,)),
            pltpu.SemaphoreType.DMA((places,)),
            pieces,
            pltpu.SemaphoreType.DMA((2, peers, subs)),
            per_peer, per_peer, per_member, per_member,
        ]
        + ffn_sums
        + sum_buffers(own_rows, width, subs)
        + line_buffers(places, shard, cols - values)
        + line_buffers(places, shard, values)
        + line_buffers(places, shard, late_grads.shape[1]),
        compiler_params=pltpu.CompilerParams(
            dimension_semantics=("arbitrary",), collective_id=4, has_side_effects=True,
            vmem_limit_bytes=62 * 2**20,
        ),
        name="backward_rule",
    )(
        starts, decay_par, dn, mixed, og, o_gain, n, qe, tot, trans, qkv, inv, states, projected,
        halo, projected, conv_w, hidden, hidden_grad, gain, ffn_gain_part, ffn_part, in_full,
        gate_full, turned, x, late_grads,
    )


def smem():
    return pl.BlockSpec(memory_space=pltpu.SMEM)


def rows_of(t):
    return pl.ds(pl.multiple_of(t * SUB, SUB), SUB)


def block_store(i, size, source, target, sem):
    return pltpu.make_async_copy(
        part(source, i * size, size), part(target, i * size, size), sem.at[i]
    )


def mixer_kernel(
    peers, nin_hbm, mixed_hbm, weights_hbm, x_hbm, gain_ref, o_gain_ref,
    og_hbm, normed_hbm, nm_hbm, turned_hbm, hidden_ref,
    nin, turned, mixed, weights, x_v, og_v, normed_v, nm, in_sem, x_sem, out_sem,
    send, recv, relay, sum_send, sum_recv, gather_send, gather_recv,
):
    me = lax.axis_index("head")
    total, width = nm.shape
    values = mixed.shape[1]
    own_rows = total // peers
    subs = own_rows // SUB
    loads = [
        pltpu.make_async_copy(weights_hbm, weights, in_sem.at[0]),
        pltpu.make_async_copy(nin_hbm, nin, in_sem.at[1]),
        pltpu.make_async_copy(mixed_hbm, mixed, in_sem.at[2]),
    ]
    for load in loads:
        load.start()
    own_x = Pieces(x_hbm, x_v, total, subs, x_sem)
    own_x.start(me)
    stores = [
        Pieces(source, target, total, subs, out_sem.at[i])
        for i, (source, target) in enumerate(
            ((og_v, og_hbm), (normed_v, normed_hbm), (nm, nm_hbm))
        )
    ]
    greet_heads(me, peers)
    for load in loads:
        load.wait()
    sums = Combine(send, recv, relay, me, sum_send, sum_recv, SUB)

    def project(i, carry):
        k = jnp.where(i == 0, peers - 1, lax.rem(i, peers - 1))
        owner = me ^ k
        og = mm(take(nin, owner, subs), weights[:, 0:values])
        gated = og * sigmoid(og)
        own = take(mixed, owner, subs)
        normed = []
        for first in range(0, values, DV):
            at = slice(first, first + DV)
            inverse = lax.rsqrt(
                jnp.mean(own[:, at] * own[:, at], axis=1, keepdims=True) + epsilon
            )
            normed.append((own[:, at] * inverse * o_gain_ref[0:1] * gated[:, at]).astype(bf16))
        normed = jnp.concatenate(normed, axis=1)
        send[k] = mm(normed, weights[:, values:], NT).astype(bf16)
        for t in range(subs):
            rows = piece_rows(owner, t, total, subs)
            og_v[rows, :] = og[t * SUB : (t + 1) * SUB]
            normed_v[rows, :] = normed[t * SUB : (t + 1) * SUB]

        for kk in range(1, peers):

            @pl.when(k == kk)
            def _():
                for t in range(subs):
                    sums.start(kk, t)

        stores[0].start(owner)
        stores[1].start(owner)
        return carry

    lax.fori_loop(0, peers, project, 0)
    tile = 256
    for first in range(0, width, tile):
        turned[first : first + tile, :] = nin[:, first : first + tile].T
    for t in range(subs):
        sums.combine(t)
    turned_store = pltpu.make_async_copy(turned, turned_hbm, in_sem.at[3])
    turned_store.start()
    own_x.wait(me)
    gain = gain_ref[...]
    ring = Spread(nm, subs, me, gather_send, gather_recv)
    for t in range(subs):
        rows = rows_of(t)
        hidden = x_v[rows, :].astype(f32) + sums.collect(t)
        hidden_ref[rows, :] = hidden
        inverse = lax.rsqrt(jnp.mean(hidden * hidden, axis=1, keepdims=True) + epsilon)
        ring.put(t, (hidden * inverse * gain).astype(bf16))
        ring.start(t)
    for t in range(subs):
        ring.forward(t)
    for k in range(peers):
        if k == peers - 1:
            for t in range(subs):
                ring.finish(t)
        stores[2].start(me ^ k)
    turned_store.wait()
    for i in range(peers):
        for store in stores:
            store.wait(i)
    for t in range(subs):
        sums.drain(t)
        ring.drain(t)


def mixer(nin, mixed, weights, x, gain, o_gain):
    peers = lax.axis_size("head")
    total, width = x.shape
    values = mixed.shape[1]
    own_rows = total // peers
    subs = own_rows // SUB
    shape = jax.ShapeDtypeStruct
    return pl.pallas_call(
        functools.partial(mixer_kernel, peers),
        in_specs=[anywhere()] * 4 + [vmem()] * 2,
        out_specs=[anywhere()] * 4 + [vmem()],
        out_shape=[
            shape((total, values), f32),
            shape((total, values), bf16),
            shape((total, width), bf16),
            shape((width, total), bf16),
            shape((own_rows, width), f32),
        ],
        scratch_shapes=[
            pltpu.VMEM((total, width), bf16),
            pltpu.VMEM((width, total), bf16),
            pltpu.VMEM((total, values), f32),
            pltpu.VMEM((width, 2 * values), bf16),
            pltpu.VMEM((own_rows, width), bf16),
            pltpu.VMEM((total, values), f32),
            pltpu.VMEM((total, values), bf16),
            pltpu.VMEM((total, width), bf16),
            pltpu.SemaphoreType.DMA((4,)),
            pltpu.SemaphoreType.DMA((peers, subs)),
            pltpu.SemaphoreType.DMA((3, peers, subs)),
        ]
        + sum_buffers(own_rows, width, subs),
        compiler_params=pltpu.CompilerParams(
            collective_id=1, has_side_effects=True, vmem_limit_bytes=48 * 2**20
        ),
        name="mixer",
    )(nin, mixed, weights, x, gain, o_gain)


def ffn_kernel(
    peers, places, cores, nm_hbm, ffn_hbm, ct_hbm, normed_hbm, weights_hbm, hidden_ref, gain_ref,
    grads_hbm, ffnp_hbm, ng_hbm, hgrad_ref, gpart_ref, down_ref,
    nm_b, ct_b, dgu_b, nm, ffn_v, ct_v, normed_v, wout_v, act, dgu, dm, ffnp_v, grads_v, down_v, ng_v,
    in_sem, out_sem, ng_sem, send, recv, relay, sum_send, sum_recv, gather_send, gather_recv,
    core_recv, seq_send, seq_recv, scatter_sems,
):
    me = lax.axis_index("head")
    total, width = nm.shape
    values = normed_v.shape[1]
    own_rows = total // peers
    subs = own_rows // SUB
    cells = act.shape[1]
    tile = 256
    loads = [
        pltpu.make_async_copy(ffn_hbm, ffn_v, in_sem.at[0]),
        pltpu.make_async_copy(nm_hbm, nm, in_sem.at[1]),
        pltpu.make_async_copy(ct_hbm, ct_v, in_sem.at[2]),
        pltpu.make_async_copy(normed_hbm, normed_v, in_sem.at[3]),
        pltpu.make_async_copy(weights_hbm.at[:, pl.ds(values, values)], wout_v, in_sem.at[4]),
    ]
    for load in loads:
        load.start()
    greet_group(me, peers, places, cores)
    for load in loads[:3]:
        load.wait()
    gain = gain_ref[...]
    sums = Combine(send, recv, relay, me, sum_send, sum_recv, SUB)

    def feed_forward(i, carry):
        k = jnp.where(i == 0, peers - 1, lax.rem(i, peers - 1))
        owner = me ^ k
        nm_b[...] = take(nm, owner, subs)
        ct_b[...] = take(ct_v, owner, subs)

        def cell_tile(j, carry):
            at = pl.ds(pl.multiple_of(j * tile, tile), tile)
            at_up = pl.ds(pl.multiple_of(cells + j * tile, tile), tile)
            at_down = pl.ds(pl.multiple_of(2 * cells + j * tile, tile), tile)
            gate = mm(nm_b[...], ffn_v[:, at])
            up = mm(nm_b[...], ffn_v[:, at_up])
            dact = mm(ct_b[...], ffn_v[:, at_down])
            sig = sigmoid(gate)
            silu = gate * sig
            activated = (silu * up).astype(bf16)
            dgu_b[:, at] = (dact * up * sig * (1.0 + gate * (1.0 - sig))).astype(bf16)
            dgu_b[:, at_up] = (dact * silu).astype(bf16)
            for t in range(subs):
                act[piece_rows(owner, t, total, subs), at] = activated[t * SUB : (t + 1) * SUB]
            return carry

        lax.fori_loop(0, cells // tile, cell_tile, 0)

        def mid_tile(j, carry):
            at = pl.ds(pl.multiple_of(j * tile, tile), tile)
            send[k, :, at] = mm(dgu_b[...], ffn_v[at, 0 : 2 * cells], NT).astype(bf16)
            return carry

        lax.fori_loop(0, width // tile, mid_tile, 0)
        for t in range(subs):
            dgu[piece_rows(owner, t, total, subs), :] = dgu_b[rows_of(t), :]

        for kk in range(1, peers):

            @pl.when(k == kk)
            def _():
                for t in range(subs):
                    sums.start(kk, t)

        @pl.when(k == 2)
        def _():
            for t in range(subs):
                sums.combine(t)

        return carry

    lax.fori_loop(0, peers, feed_forward, 0)

    def down_grads(i, carry):
        at = pl.ds(pl.multiple_of(i * tile, tile), tile)
        down_v[at, :] = mm(ct_v[:, at], act[...], TN).astype(bf16)
        return carry

    lax.fori_loop(0, width // tile, down_grads, 0)
    scatter = GroupScatter(down_v, pl.ds(0, cells), core_recv, seq_send, seq_recv, scatter_sems)
    for k in range(places - 1, -1, -1):
        scatter.core_copy(k).start()

    def cell_grads(i, carry):
        at = pl.ds(pl.multiple_of(i * tile, tile), tile)
        grads_v[at, 0 : 2 * cells] = mm(nm[:, at], dgu[...], TN).astype(bf16)
        return carry

    half = width // tile // 2
    lax.fori_loop(0, half, cell_grads, 0)
    for k in range(places - 1, -1, -1):
        scatter.pass_on(k)
    lax.fori_loop(half, width // tile, cell_grads, 0)
    ring = Spread(dm, subs, me, gather_send, gather_recv)
    gain_part = jnp.zeros((1, width), f32)
    for t in range(subs):
        rows = rows_of(t)
        dmid = sums.collect(t)
        hidden = hidden_ref[rows, :]
        inverse = lax.rsqrt(jnp.mean(hidden * hidden, axis=1, keepdims=True) + epsilon)
        scaled = hidden * inverse
        weighted = dmid * gain
        grad = ct_v[piece_rows(me, t, total, subs), :].astype(f32) + inverse * (
            weighted - scaled * jnp.mean(weighted * scaled, axis=1, keepdims=True)
        )
        hgrad_ref[rows, :] = grad
        ring.put(t, grad.astype(bf16))
        ring.start(t)
        gain_part = gain_part + jnp.sum(dmid * scaled, axis=0, keepdims=True)
    gpart_ref[...] = jnp.broadcast_to(gain_part, gpart_ref.shape)

    def ffn_rows(i, carry):
        rows = pl.ds(pl.multiple_of(i * own_rows, own_rows), own_rows)
        ffnp_v[rows, :] = mm(act[rows, :], ffn_v[:, 2 * cells :], NT).astype(bf16)
        block_store(i, own_rows, ffnp_v, ffnp_hbm, out_sem.at[0]).start()
        return carry

    lax.fori_loop(0, peers, ffn_rows, 0)
    loads[3].wait()
    loads[4].wait()
    for t in range(subs):
        ring.forward(t)
    down_ref[...] = scatter.finish()

    ng_store = Pieces(ng_v, ng_hbm, total, subs, ng_sem)

    def norm_rows(k, carry):
        owner = me ^ k

        @pl.when(k == peers - 1)
        def _():
            for t in range(subs):
                ring.finish(t)

        grads = mm(take(dm, owner, subs), wout_v[...])
        for t in range(subs):
            ng_v[piece_rows(owner, t, total, subs), :] = grads[t * SUB : (t + 1) * SUB]
        ng_store.start(owner)
        return carry

    lax.fori_loop(0, peers, norm_rows, 0)

    def out_grads(i, carry):
        at = pl.ds(pl.multiple_of(i * tile, tile), tile)
        grads_v[at, 2 * cells :] = mm(dm[:, at], normed_v[...], TN).astype(bf16)
        block_store(i, tile, grads_v, grads_hbm, out_sem.at[1]).start()
        return carry

    lax.fori_loop(0, width // tile, out_grads, 0)
    for i in range(peers):
        block_store(i, own_rows, ffnp_v, ffnp_hbm, out_sem.at[0]).wait()
        ng_store.wait(i)
    for i in range(width // tile):
        block_store(i, tile, grads_v, grads_hbm, out_sem.at[1]).wait()
    for t in range(subs):
        sums.drain(t)
        ring.drain(t)
    scatter.drain()


def feed_forward_block(nm, ffn_full, ct, normed, weights, hidden, gain):
    peers, places, cores = lax.axis_size("head"), lax.axis_size("seq"), lax.axis_size("batch")
    total, width = ct.shape
    own_rows = total // peers
    subs = own_rows // SUB
    values = normed.shape[1]
    cells = ffn_full.shape[1] // 3
    shard = width // (places * cores)
    shape = jax.ShapeDtypeStruct
    return pl.pallas_call(
        functools.partial(ffn_kernel, peers, places, cores),
        in_specs=[anywhere()] * 5 + [vmem()] * 2,
        out_specs=[anywhere()] * 3 + [vmem()] * 3,
        out_shape=[
            shape((width, 2 * cells + values), bf16),
            shape((total, width), bf16),
            shape((total, values), f32),
            shape((own_rows, width), f32),
            shape((8, width), f32),
            shape((shard, cells), f32),
        ],
        scratch_shapes=[
            pltpu.VMEM((own_rows, width), bf16),
            pltpu.VMEM((own_rows, width), bf16),
            pltpu.VMEM((own_rows, 2 * cells), bf16),
            pltpu.VMEM((total, width), bf16),
            pltpu.VMEM((width, 3 * cells), bf16),
            pltpu.VMEM((total, width), bf16),
            pltpu.VMEM((total, values), bf16),
            pltpu.VMEM((width, values), bf16),
            pltpu.VMEM((total, cells), bf16),
            pltpu.VMEM((total, 2 * cells), bf16),
            pltpu.VMEM((total, width), bf16),
            pltpu.VMEM((total, width), bf16),
            pltpu.VMEM((width, 2 * cells + values), bf16),
            pltpu.VMEM((width, cells), bf16),
            pltpu.VMEM((total, values), f32),
            pltpu.SemaphoreType.DMA((5,)),
            pltpu.SemaphoreType.DMA((2, max(peers, width // 256))),
            pltpu.SemaphoreType.DMA((peers, subs)),
        ]
        + sum_buffers(own_rows, width, subs)
        + scatter_buffers(places, shard, cells),
        compiler_params=pltpu.CompilerParams(
            collective_id=5, has_side_effects=True, vmem_limit_bytes=56 * 2**20
        ),
        name="feed_forward",
    )(nm, ffn_full, ct, normed, weights, hidden, gain)


def late_kernel(units, cells, late_ref, down_in, gate_ref, up_ref, down_ref, out_ref):
    gate_ref[...] = late_ref[:, 0:units].astype(f32)
    up_ref[...] = late_ref[:, cells : cells + units].astype(f32)
    down_ref[...] = down_in[...].T[0:units]
    out_ref[...] = late_ref[:, 2 * cells :].astype(f32).T


def late_outputs(late, down, units, cells):
    shard = late.shape[0]
    values = late.shape[1] - 2 * cells
    shape = jax.ShapeDtypeStruct
    return pl.pallas_call(
        functools.partial(late_kernel, units, cells),
        in_specs=[vmem()] * 2,
        out_specs=[vmem()] * 4,
        out_shape=[
            shape((shard, units), f32), shape((shard, units), f32), shape((units, shard), f32),
            shape((values, shard), f32),
        ],
        name="late_outputs",
    )(late, down)


def shifted(shard, axis, by):
    count = lax.axis_size(axis)
    pairs = [(i, i + by) for i in range(count) if 0 <= i + by < count]
    return lax.ppermute(shard, axis, pairs)


def root_scale(value_rows):
    return lax.rsqrt(jnp.mean(value_rows * value_rows, axis=-1, keepdims=True) + epsilon)


def matmul(a, b, dims=NN):
    return lax.dot_general(a, b, (dims, ((), ())), preferred_element_type=f32)


ALL = ("seq", "batch")


def per_device(
    tokens, starts, attn_gain, w_in, w_rates, conv_w, decay_par, o_gain, w_out, ffn_gain, w_gu,
    w_down, cotangent,
):
    seqs, length, width = tokens.shape
    shard, heads = w_in.shape[:2]
    shards = width // shard
    total = seqs * length
    conv_cols = heads * QKV
    value_cols = heads * DV
    units = w_down.shape[0]
    cells = -(-units // 256) * 256
    spare = cells - units

    packed_in = jnp.concatenate(
        [
            w_in[:, :, :QKV].reshape(shard, conv_cols),
            w_rates.reshape(shard, 2 * heads),
            jnp.zeros((shard, PAD - 2 * heads), f32),
        ],
        axis=1,
    ).astype(bf16)
    packed_gate = jnp.concatenate(
        [w_in[:, :, QKV:].reshape(shard, value_cols), w_out.reshape(value_cols, -1).T], axis=1
    ).astype(bf16)
    packed_ffn = jnp.pad(
        jnp.stack([w_gu[:, 0], w_gu[:, 1], w_down.T], axis=1).astype(bf16),
        ((0, 0), (0, 0), (0, spare)),
    ).reshape(shard, 3 * cells)
    conv_flat = conv_w.reshape(-1)
    small = jnp.concatenate([attn_gain, ffn_gain, conv_flat, o_gain]).astype(bf16)

    x = tokens.reshape(total, width)
    ct = cotangent.reshape(total, width)
    before = shifted(tokens[:, length - HALO :], "seq", 1).reshape(seqs * HALO, width)
    in_full = lax.all_gather(packed_in, ALL, axis=0, tiled=True)
    small_full = lax.all_gather(small, ALL, axis=0)
    gate_full = lax.all_gather(packed_gate, ALL, axis=0, tiled=True)
    ffn_full = lax.all_gather(packed_ffn, ALL, axis=0, tiled=True)
    attn_gain_f = small_full[:, :shard].reshape(1, width).astype(f32)
    ffn_gain_f = small_full[:, shard : 2 * shard].reshape(1, width).astype(f32)
    conv_end = 2 * shard + conv_flat.shape[0]
    conv_full = (
        small_full[:, 2 * shard : conv_end]
        .reshape(shards, CONV, heads, -1)
        .transpose(1, 2, 0, 3)
        .reshape(CONV, conv_cols)
        .astype(f32)
    )
    o_gain_full = small_full[:, conv_end:].reshape(1, DV).astype(f32)

    def normed_rows(rows):
        rows = rows.astype(f32)
        return (rows * root_scale(rows) * attn_gain_f).astype(bf16)

    normed_in = normed_rows(x)
    projected = matmul(normed_in, in_full)
    halo = matmul(normed_rows(before), in_full[:, :conv_cols]).reshape(seqs, HALO, conv_cols)
    qkv, inv, n, qe, tot, trans, states, mixed = forward_rule(
        starts, decay_par, projected, halo, conv_full, seqs, heads
    )
    og, normed, nm, turned_in, hidden = mixer(
        normed_in, mixed, gate_full, x, ffn_gain_f, o_gain_full
    )
    late_grads, ffn_part, normed_grad, hidden_grad, ffn_gain_part, down_own = feed_forward_block(
        nm, ffn_full, ct, normed, gate_full, hidden, ffn_gain_f
    )
    result, input_grad, gains, in_main, in_small, late_own = backward_rule(
        starts, decay_par, normed_grad, mixed, og, projected, o_gain_full, n, qe, tot, trans, qkv,
        inv, states, halo, conv_full, hidden, hidden_grad, attn_gain_f, ffn_gain_part, ffn_part,
        in_full, gate_full, turned_in, x, late_grads, heads,
    )
    taps = CONV * heads
    per = QKV // shards
    grad_gate, grad_up, grad_down, grad_out = late_outputs(late_own, down_own, units, cells)
    at = lax.axis_index(ALL)
    gains = gains.reshape(3, width)
    own_gains = lax.dynamic_slice(gains, (0, at * shard), (2, shard))
    onorm_own = lax.dynamic_slice(gains, (2, at * (DV // shards)), (1, DV // shards))
    return (
        result.reshape(tokens.shape),
        input_grad.reshape(tokens.shape),
        own_gains[0],
        in_main.reshape(shard, heads, QKV + DV),
        in_small[:, : 2 * heads].reshape(shard, heads, 2),
        in_small[:taps, PAD // 2 : PAD // 2 + per].reshape(CONV, heads, per),
        in_small[0, 2 * heads : 4 * heads].reshape(2, heads),
        onorm_own[0],
        grad_out.reshape(heads, DV, -1),
        own_gains[1],
        jnp.stack([grad_gate, grad_up], axis=1),
        grad_down,
    )


def solution(mesh):
    weights = P(ALL)
    in_specs = (
        P("batch", "seq", None),
        P("batch"),
        weights,
        P(ALL, "head", None),
        P(ALL, "head", None),
        P(None, "head", ALL),
        P(None, "head"),
        weights,
        P("head", None, ALL),
        weights,
        P(ALL, None, "head"),
        P("head", ALL),
        P("batch", "seq", None),
    )
    out_specs = (
        P("batch", "seq", None),
        P("batch", "seq", None),
        weights,
        P(ALL, "head", None),
        P(ALL, "head", None),
        P(None, "head", ALL),
        P(None, "head"),
        weights,
        P("head", None, ALL),
        weights,
        P(ALL, None, "head"),
        P("head", ALL),
    )
    return jax.shard_map(
        per_device, mesh=mesh, in_specs=in_specs, out_specs=out_specs, check_vma=False
    )
```

```python
import functools

import jax
import jax.numpy as jnp
from jax import lax
from jax.experimental import pallas as pl
from jax.experimental.pallas import tpu as pltpu
from jax.sharding import PartitionSpec as P

DK = 128
DV = 256
CONV = 4
QKV = 2 * DK + DV
CHUNK = 128
HALO = 16
PAD = 128

bf16 = jnp.bfloat16
f32 = jnp.float32
epsilon = 1e-06
NN = ((1,), (0,))
NT = ((1,), (1,))
TN = ((0,), (0,))


def mm(a, b, dims=NN):
    return lax.dot_general(
        a.astype(bf16), b.astype(bf16), (dims, ((), ())), preferred_element_type=f32
    )


def split_mm(a, b):
    a_high, b_high = a.astype(bf16), b.astype(bf16)
    a_low = (a - a_high.astype(f32)).astype(bf16)
    b_low = (b - b_high.astype(f32)).astype(bf16)
    return mm(a_high, b_high) + (mm(a_high, b_low) + mm(a_low, b_high))


def iotas(n):
    return (
        lax.broadcasted_iota(jnp.int32, (n, n), 0),
        lax.broadcasted_iota(jnp.int32, (n, n), 1),
    )


def unit_lower_inverses(mats):
    n = mats[0].shape[0]
    rows, cols = iotas(n)
    eye = (rows == cols).astype(f32)
    pair = ((rows >> 1) == (cols >> 1)) & (rows > cols)
    inverses = [eye - jnp.where(pair, a, 0.0) for a in mats]
    shift = 1
    while (1 << shift) < n:
        corner = ((rows >> (shift + 1)) == (cols >> (shift + 1))) & (
            (rows >> shift) > (cols >> shift)
        )
        firsts = [mm(jnp.where(corner, a, 0.0), x) for a, x in zip(mats, inverses)]
        inverses = [x - mm(x, y) for x, y in zip(inverses, firsts)]
        shift += 1
    residuals = [eye - x - split_mm(a, x) for a, x in zip(mats, inverses)]
    return [x + mm(x, r) for x, r in zip(inverses, residuals)]


def sigmoid(v):
    return 1.0 / (1.0 + jnp.exp(-v))


def softplus(v):
    small = jnp.exp(-jnp.abs(v))
    one_more = 1.0 + small
    gap = one_more - 1.0
    exact = gap == 0.0
    tail = jnp.where(exact, small, jnp.log(one_more) * small / jnp.where(exact, 1.0, gap))
    return jnp.maximum(v, 0.0) + tail


def to_row(column, eye):
    return jnp.sum(jnp.where(eye, column, 0.0), axis=0, keepdims=True)


def pick(block, lane):
    lanes = lax.broadcasted_iota(jnp.int32, block.shape, 1)
    return jnp.sum(jnp.where(lanes == lane, block, 0.0), axis=1, keepdims=True)


def gates(logits, decay_ref, head):
    rate = jnp.exp(jnp.full((1, 1), decay_ref[0, head], f32))
    shifted_logit = pick(logits, 2 * head) + decay_ref[1, head]
    strength = sigmoid(pick(logits, 2 * head + 1))
    log_gate = -rate * softplus(shifted_logit)
    return log_gate, strength, rate, shifted_logit


def decays(log_gate, lower, upper, eye):
    gate_row = to_row(log_gate, eye)
    column = jnp.sum(jnp.where(lower, gate_row, 0.0), axis=1, keepdims=True)
    row = jnp.sum(jnp.where(upper, log_gate, 0.0), axis=0, keepdims=True)
    ratio = jnp.where(lower, jnp.exp(jnp.where(lower, column - row, 0.0)), 0.0)
    total = jnp.sum(log_gate, axis=0, keepdims=True)
    return column, total, ratio


def load_conv_input(main_ref, halo_ref, start, x_scr, first):
    length = main_ref.shape[0]
    positions = first + lax.broadcasted_iota(jnp.int32, (length, 1), 0)
    live = (positions >= start).astype(f32)
    before = first - HALO + lax.broadcasted_iota(jnp.int32, (HALO, 1), 0)
    lived = (before >= start).astype(f32)
    x_scr[pl.ds(0, HALO), :] = (halo_ref[0] * lived).astype(bf16).astype(f32)
    x_scr[pl.ds(HALO, length), :] = (main_ref[...] * live).astype(bf16).astype(f32)


def convolve(x_scr, conv, at):
    total = x_scr[pl.ds(at + HALO - CONV + 1, CHUNK), :] * conv[0:1]
    for j in range(1, CONV):
        total = total + x_scr[pl.ds(at + HALO - CONV + 1 + j, CHUNK), :] * conv[j : j + 1]
    return total


def unit(rows):
    return rows * lax.rsqrt(jnp.sum(rows * rows, axis=1, keepdims=True) + epsilon)


MESH = pl.DeviceIdType.MESH
SUB = 128


def head_copy(src, dst, send_sem, recv_sem, peer):
    return pltpu.make_async_remote_copy(
        src_ref=src, dst_ref=dst, send_sem=send_sem, recv_sem=recv_sem,
        device_id={"head": peer}, device_id_type=MESH,
    )


def greet_heads(me, peers):
    barrier = pltpu.get_barrier_semaphore()
    for k in range(1, peers):
        pl.semaphore_signal(barrier, inc=1, device_id={"head": me ^ k}, device_id_type=MESH)
    pl.semaphore_wait(barrier, peers - 1)


def part(ref, start, size):
    return ref.at[pl.ds(pl.multiple_of(start, size), size)]


def piece_rows(owner, t, total, subs):
    return pl.ds(pl.multiple_of(t * (total // subs) + owner * SUB, SUB), SUB)


def take(ref, owner, subs):
    total = ref.shape[0]
    return jnp.concatenate(
        [ref[piece_rows(owner, t, total, subs), :] for t in range(subs)], axis=0
    )


class Pieces:
    def __init__(self, source, target, total, subs, sems):
        self.source, self.target, self.total, self.subs, self.sems = source, target, total, subs, sems

    def at(self, ref, owner, t):
        rows = piece_rows(owner, t, self.total, self.subs)
        if ref.shape[0] != self.total:
            rows = pl.ds(t * SUB, SUB)
        return ref.at[rows]

    def copies(self, owner):
        return [
            pltpu.make_async_copy(
                self.at(self.source, owner, t), self.at(self.target, owner, t),
                self.sems.at[owner, t],
            )
            for t in range(self.subs)
        ]

    def start(self, owner):
        for copy in self.copies(owner):
            copy.start()

    def wait(self, owner):
        for copy in self.copies(owner):
            copy.wait()


class Spread:
    def __init__(self, buffer, subs, me, send_sem, recv_sem):
        self.buffer, self.subs, self.me = buffer, subs, me
        self.send_sem, self.recv_sem = send_sem, recv_sem

    def region(self, owner, t, half):
        rows = piece_rows(owner, t, self.buffer.shape[0], self.subs)
        middle = self.buffer.shape[1] // 2
        if half is None:
            return self.buffer.at[rows]
        return self.buffer.at[rows, pl.ds(half * middle, middle)]

    def put(self, t, value):
        self.buffer[piece_rows(self.me, t, self.buffer.shape[0], self.subs), :] = value

    def copy(self, kind, t, owner):
        at = self.region(owner, t, None if kind < 2 else kind - 2)
        to = self.me ^ (1 if kind in (0, 3) else 2)
        return head_copy(at, at, self.send_sem.at[kind, t], self.recv_sem.at[kind, t], to)

    def start(self, t):
        self.copy(0, t, self.me).start()
        self.copy(1, t, self.me).start()

    def forward(self, t):
        self.copy(0, t, self.me ^ 1).wait_recv()
        self.copy(2, t, self.me ^ 1).start()
        self.copy(1, t, self.me ^ 2).wait_recv()
        self.copy(3, t, self.me ^ 2).start()

    def finish(self, t):
        self.copy(2, t, self.me ^ 3).wait_recv()
        self.copy(3, t, self.me ^ 3).wait_recv()

    def drain(self, t):
        for kind, owner in enumerate((0, 0, 1, 2)):
            self.copy(kind, t, self.me ^ owner).wait_send()


class Combine:
    def __init__(self, send, recv, relay, me, send_sem, recv_sem, piece):
        self.send, self.recv, self.relay, self.me = send, recv, relay, me
        self.send_sem, self.recv_sem, self.piece = send_sem, recv_sem, piece
        self.middle = send.shape[2] // 2

    def rows(self, t):
        return pl.ds(pl.multiple_of(t * self.piece, self.piece), self.piece)

    def copy(self, kind, t):
        rows, low, high = self.rows(t), pl.ds(0, self.middle), pl.ds(self.middle, self.middle)
        source, target, to = (
            (self.send.at[3, rows, low], self.relay.at[0, rows], 1),
            (self.send.at[3, rows, high], self.relay.at[1, rows], 2),
            (self.send.at[1, rows, low], self.recv.at[0, rows, low], 1),
            (self.send.at[2, rows, high], self.recv.at[1, rows, high], 2),
            (self.send.at[1, rows, high], self.recv.at[0, rows, high], 1),
            (self.send.at[2, rows, low], self.recv.at[1, rows, low], 2),
        )[kind]
        return head_copy(
            source, target, self.send_sem.at[kind, t], self.recv_sem.at[kind, t], self.me ^ to
        )

    def start(self, k, t):
        if k == 3:
            self.copy(0, t).start()
            self.copy(1, t).start()
        else:
            self.copy(k + 1, t).start()

    def combine(self, t):
        rows = self.rows(t)
        for k, at in ((1, pl.ds(self.middle, self.middle)), (2, pl.ds(0, self.middle))):
            self.copy(2 - k, t).wait_recv()
            both = self.send[k, rows, at].astype(f32) + self.relay[2 - k, rows, :].astype(f32)
            self.send[k, rows, at] = both.astype(bf16)
            self.copy(3 + k, t).start()

    def collect(self, t):
        for kind in range(2, 6):
            self.copy(kind, t).wait_recv()
        return self.total(self.rows(t))

    def total(self, rows):
        return (
            self.send[0, rows, :].astype(f32)
            + self.recv[0, rows, :].astype(f32)
            + self.recv[1, rows, :].astype(f32)
        )

    def drain(self, t):
        for kind in range(6):
            self.copy(kind, t).wait_send()


def sum_buffers(rows, width, pieces):
    return [
        pltpu.VMEM((4, rows, width), bf16),
        pltpu.VMEM((2, rows, width), bf16),
        pltpu.VMEM((2, rows, width // 2), bf16),
        pltpu.SemaphoreType.DMA((6, pieces)),
        pltpu.SemaphoreType.DMA((6, pieces)),
        pltpu.SemaphoreType.DMA((4, pieces)),
        pltpu.SemaphoreType.DMA((4, pieces)),
    ]


class GroupScatter:
    def __init__(self, source, columns, core_recv, seq_send, seq_recv, sems):
        self.source, self.columns = source, columns
        self.core_recv, self.seq_send, self.seq_recv, self.sems = core_recv, seq_send, seq_recv, sems
        self.place, self.core = lax.axis_index("seq"), lax.axis_index("batch")
        self.places, self.shard = core_recv.shape[0], core_recv.shape[1]

    def rows(self, k, core):
        at = ((self.place ^ k) * 2 + core) * self.shard
        return pl.ds(pl.multiple_of(at, self.shard), self.shard)

    def core_copy(self, k):
        return along(
            "batch", self.source.at[self.rows(k, 1 - self.core), self.columns],
            self.core_recv.at[k], self.sems.at[0, k], self.sems.at[1, k], 1 - self.core,
        )

    def seq_copy(self, k):
        return along(
            "seq", self.seq_send.at[k], self.seq_recv.at[k], self.sems.at[2, k],
            self.sems.at[3, k], self.place ^ k,
        )

    def pass_on(self, k):
        self.core_copy(k).wait_recv()
        own = self.source[self.rows(k, self.core), self.columns].astype(f32)
        self.seq_send[k] = (own + self.core_recv[k].astype(f32)).astype(bf16)

        @pl.when(k > 0)
        def _():
            self.seq_copy(k).start()

    def finish(self):
        total = self.seq_send[0].astype(f32)
        for k in range(1, self.places):
            self.seq_copy(k).wait_recv()
            total = total + self.seq_recv[k].astype(f32)
        return total

    def drain(self):
        for k in range(self.places):
            self.core_copy(k).wait_send()
        for k in range(1, self.places):
            self.seq_copy(k).wait_send()


class LineScatter:
    def __init__(self, own, core_recv, recv, sems):
        self.own, self.core_recv, self.recv, self.sems = own, core_recv, recv, sems
        self.place, self.core = lax.axis_index("seq"), lax.axis_index("batch")
        self.places = own.shape[0]

    def clear(self):
        @pl.when(self.place == 0)
        def _():
            self.recv[0] = jnp.zeros_like(self.recv[0])

        @pl.when(self.place == self.places - 1)
        def _():
            self.recv[self.places] = jnp.zeros_like(self.recv[0])

    def core_copy(self, d, source):
        return along(
            "batch", source, self.core_recv.at[d], self.sems.at[0, d], self.sems.at[1, d],
            1 - self.core,
        )

    def add_core(self, d, source):
        self.core_copy(d, source).wait_recv()
        self.add(d, self.core_recv[d])

    def add(self, d, other):
        self.own[d] = (self.own[d].astype(f32) + other.astype(f32)).astype(bf16)

    def move(self, d):
        right = d > self.place
        to = jnp.clip(jnp.where(right, self.place + 1, self.place - 1), 0, self.places - 1)
        slot = jnp.where(right | (to != d), d, self.places)
        return along(
            "seq", self.own.at[d], self.recv.at[slot], self.sems.at[2, d], self.sems.at[3, slot], to
        )

    def arrived(self, slot):
        return along(
            "seq", self.own.at[0], self.recv.at[slot], self.sems.at[2, 0], self.sems.at[3, slot],
            jnp.where(self.place > 0, self.place - 1, self.places - 1),
        )

    def advance(self, hop):
        last = self.places - 1

        def towards(d, active, through):
            @pl.when(active)
            def _():
                @pl.when(through)
                def _():
                    self.arrived(d).wait_recv()
                    self.add(d, self.recv[d])

                self.move(d).start()

        turn = hop - self.place
        d = jnp.clip(last - turn, 0, last)
        towards(d, (turn >= 0) & (last - turn > self.place), self.place > 0)
        turn = hop - (last - self.place)
        d = jnp.clip(turn, 0, last)
        towards(d, (turn >= 0) & (turn < self.place), self.place < last)

    def finish(self):
        @pl.when(self.place > 0)
        def _():
            self.arrived(self.place).wait_recv()

        @pl.when(self.place < self.places - 1)
        def _():
            self.arrived(self.places).wait_recv()

        return (
            self.own[self.place].astype(f32)
            + self.recv[self.place].astype(f32)
            + self.recv[self.places].astype(f32)
        )

    def drain(self, source):
        for d in range(self.places):
            self.core_copy(d, source(d)).wait_send()

            @pl.when(self.place != d)
            def _():
                self.move(d).wait_send()


def line_buffers(places, shard, columns):
    return [
        pltpu.VMEM((places, shard, columns), bf16),
        pltpu.VMEM((places, shard, columns), bf16),
        pltpu.VMEM((places + 1, shard, columns), bf16),
        pltpu.SemaphoreType.DMA((4, places + 1)),
    ]


def scatter_buffers(places, shard, columns):
    return [pltpu.VMEM((places, shard, columns), bf16)] * 3 + [
        pltpu.SemaphoreType.DMA((4, places))
    ]


def greet_group(me, peers, places, cores):
    barrier = pltpu.get_barrier_semaphore()
    group = places * cores
    flat = lax.axis_index("seq") * cores + lax.axis_index("batch")
    for k in range(1, peers):
        pl.semaphore_signal(barrier, inc=1, device_id={"head": me ^ k}, device_id_type=MESH)
    for d in range(1, group):
        to = lax.rem(flat + d, group)
        pl.semaphore_signal(
            barrier, inc=1, device_id={"seq": to // cores, "batch": lax.rem(to, cores)},
            device_id_type=MESH,
        )
    pl.semaphore_wait(barrier, peers + group - 2)


def in_hbm(dims, kind):
    return pltpu.HBM(dims, kind)


def anywhere():
    return pl.BlockSpec(memory_space=pltpu.HBM)


def vmem():
    return pl.BlockSpec(memory_space=pltpu.VMEM)


def along(axis, source, target, send_sem, recv_sem, to):
    return pltpu.make_async_remote_copy(
        src_ref=source, dst_ref=target, send_sem=send_sem, recv_sem=recv_sem,
        device_id={axis: to}, device_id_type=MESH,
    )


def forward_kernel(
    heads, places, start_ref, decay_ref, main_ref, halo_ref, rate_ref, conv_ref,
    qkv_ref, inv_ref, n_ref, qe_ref, tot_ref, trans_ref, s_ref, mixed_ref,
    x_scr, b_scr, o_scr, carried_scr, send, recv, send_sem, recv_sem,
):
    step = pl.program_id(0)
    chains = n_ref.shape[0]
    count = n_ref.shape[1]
    length = main_ref.shape[0]
    place = lax.axis_index("seq")
    lag = jnp.minimum(place, chains - 1)

    @pl.when(step == 0)
    def _():
        barrier = pltpu.get_barrier_semaphore()

        @pl.when(place > 0)
        def _():
            pl.semaphore_signal(
                barrier, inc=1, device_id={"seq": place - 1}, device_id_type=MESH
            )

        @pl.when(place == 0)
        def _():
            recv[...] = jnp.zeros_like(recv)

        @pl.when(place < places - 1)
        def _():
            pl.semaphore_wait(barrier, 1)

    @pl.when(step < chains)
    def _():
        head = step % heads
        load_conv_input(
            main_ref, halo_ref, start_ref[jnp.minimum(step, chains - 1) // heads], x_scr, place * length
        )
        conv = conv_ref[...]
        rows, cols = iotas(CHUNK)
        lower, upper, eye = rows >= cols, rows <= cols, rows == cols
        parts = []
        for c in range(count):
            at = c * CHUNK
            convolved = convolve(x_scr, conv, at)
            active = convolved * sigmoid(convolved)
            q = (unit(active[:, :DK]) * DK ** (-0.5)).astype(bf16)
            k = unit(active[:, DK : 2 * DK]).astype(bf16)
            v = active[:, 2 * DK :].astype(bf16)
            qkv_ref[pl.ds(at, CHUNK), 0:DK] = q
            qkv_ref[pl.ds(at, CHUNK), DK : 2 * DK] = k
            qkv_ref[pl.ds(at, CHUNK), 2 * DK :] = v
            log_gate, strength, _, _ = gates(rate_ref[pl.ds(at, CHUNK), :], decay_ref, head)
            column, total, ratio = decays(log_gate, lower, upper, eye)
            products = mm(jnp.concatenate([k, q], axis=0), k, NT)
            coupling = jnp.where(rows > cols, strength * ratio * products[:CHUNK], 0.0)
            scores = (ratio * products[CHUNK:]).astype(bf16)
            parts.append((q, k, v, strength, column, total, coupling, scores))
        inverses = unit_lower_inverses([p[6] for p in parts])
        maps = []
        for c in range(count):
            q, k, v, strength, column, total, _, scores = parts[c]
            growth = jnp.exp(column)
            kf, vf, qf = k.astype(f32), v.astype(f32), q.astype(f32)
            inverse = inverses[c].astype(bf16)
            inv_ref[0, c] = inverse
            target = jnp.concatenate([(strength * growth) * kf, strength * vf], axis=1)
            solved = mm(inverse, target).astype(bf16)
            read = mm(scores, solved)
            qe_ref[step, c] = (growth * qf - read[:, :DK]).astype(bf16)
            o_scr[step, pl.ds(c * CHUNK, CHUNK), :] = read[:, DK:]
            written = mm(jnp.exp(total - column) * kf, solved, TN)
            low_n = written[:, :DK].astype(bf16)
            n_ref[step, c] = low_n
            b_scr[step, c] = written[:, DK:]
            whole = jnp.exp(total)
            tot_ref[step, pl.ds(c, 1), :] = jnp.broadcast_to(whole, (1, DK))
            maps.append((low_n, written[:, DK:], whole))
        low_n, b, whole = maps[0]
        trans = whole * eye.astype(f32) - low_n.astype(f32)
        carried = b
        for low_n, b, whole in maps[1:]:
            both = jnp.concatenate([trans, carried], axis=1)
            moved = whole * both - mm(low_n, both)
            trans = moved[:, :DK]
            carried = moved[:, DK:] + b
        trans_ref[step] = trans.astype(bf16)
        carried_scr[step] = carried

    @pl.when(step >= chains)
    def _():
        chain = jnp.maximum(step - chains, 0)
        state = recv[chain].astype(f32)
        for c in range(count):
            low_state = state.astype(bf16)
            s_ref[0, c] = low_state
            both = mm(jnp.concatenate([n_ref[chain, c], qe_ref[chain, c]], axis=0), low_state)
            whole = tot_ref[chain, pl.ds(c, 1), 0:1]
            state = whole * state - both[:DK] + b_scr[chain, c]
            at = pl.ds(c * CHUNK, CHUNK)
            mixed_ref[at, :] = o_scr[chain, at, :] + both[DK:]

    half = DV // 2

    def passed(chain, side):
        at = pl.ds(side * half, half)
        return along(
            "seq", send.at[chain, :, at], recv.at[chain, :, at], send_sem.at[chain, side],
            recv_sem.at[chain, side], jnp.minimum(place + 1, places - 1),
        )

    relayed = step - lag

    @pl.when((relayed >= 0) & (relayed < chains))
    def _():
        chain = jnp.clip(relayed, 0, chains - 1)
        for side in range(2):
            at = slice(side * half, (side + 1) * half)

            @pl.when(place > 0)
            def _():
                passed(chain, side).wait_recv()

            @pl.when(place < places - 1)
            def _():
                leaving = mm(trans_ref[chain], recv[chain, :, at]) + carried_scr[chain, :, at]
                send[chain, :, at] = leaving.astype(bf16)
                passed(chain, side).start()

    @pl.when((step == 2 * chains - 1) & (place < places - 1))
    def _():
        for chain in range(chains):
            for side in range(2):
                passed(chain, side).wait_send()


def early(chains, make):
    return lambda j: make(jnp.minimum(j, chains - 1))


def late(chains, make):
    return lambda j: make(jnp.maximum(j - chains, 0))


def forward_rule(starts, decay_par, projected, halo, conv_w, seqs, heads):
    places = lax.axis_size("seq")
    chains = seqs * heads
    length = projected.shape[0] // seqs
    count = length // CHUNK
    rates_at = heads * QKV // PAD
    row = lambda first: lambda i: (i // heads, first + i % heads)
    whole = lambda *dims: pl.BlockSpec(dims, lambda j: (0,) * len(dims))
    shape = in_hbm
    return pl.pallas_call(
        functools.partial(forward_kernel, heads, places),
        grid=(2 * chains,),
        in_specs=[
            smem(),
            smem(),
            pl.BlockSpec((length, QKV), early(chains, row(0))),
            pl.BlockSpec((1, HALO, QKV), early(chains, lambda i: (i // heads, 0, i % heads))),
            pl.BlockSpec((length, PAD), early(chains, lambda i: (i // heads, rates_at))),
            pl.BlockSpec((CONV, QKV), early(chains, lambda i: (0, i % heads))),
        ],
        out_specs=[
            pl.BlockSpec((length, QKV), early(chains, row(0))),
            pl.BlockSpec((1, count, CHUNK, CHUNK), early(chains, lambda i: (i, 0, 0, 0))),
            whole(chains, count, DK, DK),
            whole(chains, count, CHUNK, DK),
            whole(chains, count, DK),
            whole(chains, DK, DK),
            pl.BlockSpec((1, count, DK, DV), late(chains, lambda i: (i, 0, 0, 0))),
            pl.BlockSpec((length, DV), late(chains, row(0))),
        ],
        out_shape=[
            shape((seqs * length, heads * QKV), bf16),
            shape((chains, count, CHUNK, CHUNK), bf16),
            shape((chains, count, DK, DK), bf16),
            shape((chains, count, CHUNK, DK), bf16),
            shape((chains, count, DK), f32),
            shape((chains, DK, DK), bf16),
            shape((chains, count, DK, DV), bf16),
            shape((seqs * length, heads * DV), f32),
        ],
        scratch_shapes=[
            pltpu.VMEM((HALO + length, QKV), f32),
            pltpu.VMEM((chains, count, DK, DV), f32),
            pltpu.VMEM((chains, length, DV), f32),
            pltpu.VMEM((chains, DK, DV), f32),
            pltpu.VMEM((chains, DK, DV), bf16),
            pltpu.VMEM((chains, DK, DV), bf16),
            pltpu.SemaphoreType.DMA((chains, 2)),
            pltpu.SemaphoreType.DMA((chains, 2)),
        ],
        compiler_params=pltpu.CompilerParams(
            dimension_semantics=("arbitrary",), collective_id=3, has_side_effects=True,
            vmem_limit_bytes=48 * 2**20,
        ),
        name="forward_rule",
    )(starts, decay_par, projected, halo, projected, conv_w)


def backward_kernel(
    heads, places, peers, cores, start_ref, decay_ref,
    dn_ref, mixed_ref, og_ref, o_gain_ref, n_ref, qe_ref, tot_ref, trans_ref,
    qkv_ref, inv_ref, s_ref, main_ref, halo_ref, rate_ref, conv_ref,
    hidden_ref, hgrad_ref, gain_ref, ffn_gain_ref, ffnp_hbm, win_hbm, wog_hbm, nin_hbm, x_hbm,
    late_hbm,
    out_hbm, igrad_hbm, gains_out, grad_out, small_out, late_out,
    dp_ref, x_scr, g_scr, do_scr, own_scr, send, recv, tail_scr, halo_send, halo_recv,
    conv_scr, decay_scr, o_gain_scr, whole_out, whole_in, win_v, wog_v, nin_v, x_v, conv_source,
    gate_source, extras_v, gains_v, gains_recv, gains_sum, gains_all,
    send_sem, recv_sem, halo_send_sem, halo_recv_sem, load_sem, in_sem, late_sem, x_sem, out_sem, hs, hr, gs, gr,
    sent, got, relay, sum_send, sum_recv, gather_send, gather_recv,
    in_sent, in_got, in_relay, in_sum_send, in_sum_recv, in_gather_send, in_gather_recv,
    conv_own, conv_core, conv_recv, conv_sems,
    gate_own, gate_core, gate_recv, gate_sems,
    late_own, late_core, late_recv, late_sems,
):
    step = pl.program_id(0)
    chains = n_ref.shape[0]
    count = n_ref.shape[1]
    length = main_ref.shape[0]
    seqs = chains // heads
    total, width = whole_out.shape
    conv_cols = heads * QKV
    values = heads * DV
    in_cols = conv_cols + values
    place, core = lax.axis_index("seq"), lax.axis_index("batch")
    lag = jnp.minimum(places - 1 - place, chains - 1)
    me = lax.axis_index("head")
    own_rows = hidden_ref.shape[0]
    subs = own_rows // SUB
    group = places * cores
    shard = width // group
    pair = cores * shard
    flat = place * cores + core

    ring = Spread(whole_out, subs, me, gather_send, gather_recv)
    sums = Combine(sent, got, relay, me, sum_send, sum_recv, own_rows)
    in_ring = Spread(whole_in, subs, me, in_gather_send, in_gather_recv)
    in_sums = Combine(in_sent, in_got, in_relay, me, in_sum_send, in_sum_recv, SUB)
    conv_line = LineScatter(conv_own, conv_core, conv_recv, conv_sems)
    gate_line = LineScatter(gate_own, gate_core, gate_recv, gate_sems)
    late_line = LineScatter(late_own, late_core, late_recv, late_sems)

    def late_rows(d, at_core):
        return late_hbm.at[pl.ds(pl.multiple_of((d * cores + at_core) * shard, shard), shard)]

    def late_source(d):
        return late_rows(d, 1 - core)

    def late_load(d):
        return pltpu.make_async_copy(late_rows(d, core), late_own.at[d], late_sem.at[d])

    def hops(third):
        return range(third * (places - 1) // 3, (third + 1) * (places - 1) // 3)

    def far_first(i):
        return jnp.where(i % 2 == 0, places - 1 - i // 2, i // 2)

    def halves(grads):
        top, low = grads[:shard], grads[shard:]
        return jnp.where(core == 0, top, low), jnp.where(core == 0, low, top)
    out_store = Pieces(whole_out, out_hbm, total, subs, out_sem.at[0])
    in_store = Pieces(whole_in, igrad_hbm, total, subs, out_sem.at[1])
    own_x = Pieces(x_hbm, x_v, total, subs, x_sem)
    loads = [
        pltpu.make_async_copy(win_hbm, win_v, in_sem.at[0]),
        pltpu.make_async_copy(wog_hbm.at[:, pl.ds(0, values)], wog_v, in_sem.at[1]),
        pltpu.make_async_copy(nin_hbm, nin_v, in_sem.at[2]),
    ]

    def ffn_loads(k):
        return [
            pltpu.make_async_copy(
                ffnp_hbm.at[piece_rows(me ^ k, t, total, subs)], sent.at[k, pl.ds(t * SUB, SUB)],
                load_sem.at[k, t],
            )
            for t in range(subs)
        ]

    half = DV // 2

    def passed(chain, side):
        at = pl.ds(side * half, half)
        return along(
            "seq", send.at[chain, :, at], recv.at[chain, :, at], send_sem.at[chain, side],
            recv_sem.at[chain, side], jnp.maximum(place - 1, 0),
        )

    def returned(chain):
        return along(
            "seq", halo_send.at[chain], halo_recv.at[chain], halo_send_sem.at[chain],
            halo_recv_sem.at[chain], jnp.maximum(place - 1, 0),
        )

    @pl.when(step == 0)
    def _():
        for k in range(peers - 1, -1, -1):
            for load in ffn_loads(k):
                load.start()

        @pl.when(place == places - 1)
        def _():
            recv[...] = jnp.zeros_like(recv)
            halo_recv[...] = jnp.zeros_like(halo_recv)

        decay_scr[...] = jnp.zeros_like(decay_scr)
        o_gain_scr[...] = jnp.zeros_like(o_gain_scr)
        extras_v[...] = jnp.zeros_like(extras_v)
        for line in (conv_line, gate_line, late_line):
            line.clear()
        for d in range(places):
            late_load(d).start()
        for load in loads:
            load.start()
        own_x.start(me)
        greet_group(me, peers, places, cores)
        for k in range(peers - 1, 0, -1):
            for load in ffn_loads(k):
                load.wait()
            sums.start(k, 0)
        for load in ffn_loads(0):
            load.wait()
        for d in range(places):
            late_line.core_copy(d, late_source(d)).start()

    @pl.when(step < chains)
    def _():
        gain = o_gain_ref[0:1]
        first = (step // heads) * length
        og_at = pl.ds(pl.multiple_of(conv_cols + (step % heads) * DV, DV), DV)
        state = jnp.zeros((DK, DV), f32)
        gain_total = jnp.zeros((1, DV), f32)
        for c in reversed(range(count)):
            at = pl.ds(c * CHUNK, CHUNK)
            mixed, og, dn = mixed_ref[at, :], og_ref[at, :], dn_ref[at, :]
            inverse = lax.rsqrt(jnp.mean(mixed * mixed, axis=1, keepdims=True) + epsilon)
            scaled = mixed * inverse
            sig = sigmoid(og)
            silu = og * sig
            through = dn * scaled
            gain_total = gain_total + jnp.sum(through * silu, axis=0, keepdims=True)
            dp_ref[pl.ds(pl.multiple_of(first + c * CHUNK, CHUNK), CHUNK), og_at] = (
                through * gain * sig * (1.0 + og * (1.0 - sig))
            ).astype(bf16)
            weighted = dn * gain * silu
            dmixed = inverse * (
                weighted - scaled * jnp.mean(weighted * scaled, axis=1, keepdims=True)
            )
            dmixed = dmixed.astype(bf16)
            do_scr[step, at, :] = dmixed
            decay = tot_ref[step, pl.ds(c, 1), 0:1]
            state = (
                decay * state - mm(n_ref[step, c], state, TN) + mm(qe_ref[step, c], dmixed, TN)
            )
        o_gain_scr[0:1, :] = o_gain_scr[0:1, :] + gain_total
        own_scr[step] = state

    @pl.when(step >= chains)
    def _():
        chain = jnp.maximum(step - chains, 0)
        seq, head = chain // heads, chain % heads
        first = seq * length
        start = start_ref[seq]
        load_conv_input(main_ref, halo_ref, start, x_scr, place * length)
        conv = conv_ref[...]
        rows, cols = iotas(CHUNK)
        lower, upper, eye = rows >= cols, rows <= cols, rows == cols
        strict = rows > cols
        state = recv[chain].astype(f32)
        leaving = [None] * count
        for c in reversed(range(count)):
            leaving[c] = state
            state = (
                tot_ref[chain, pl.ds(c, 1), 0:1] * state
                - mm(n_ref[chain, c], state, TN)
                + mm(qe_ref[chain, c], do_scr[chain, pl.ds(c * CHUNK, CHUNK), :], TN)
            )
        g_scr[pl.ds(0, 8), :] = jnp.zeros((8, QKV), f32)
        g_scr[pl.ds(8 + length, 8), :] = jnp.zeros((8, QKV), f32)
        rate_total = jnp.zeros((1, 1), f32)
        bias_total = jnp.zeros((1, 1), f32)
        conv_total = [jnp.zeros((1, QKV), f32) for _ in range(CONV)]
        lanes = lax.broadcasted_iota(jnp.int32, (CHUNK, PAD), 1)
        for c in range(count):
            for t in range(seqs - 1):
                if c == count - 1:

                    @pl.when(step == chains + (t + 1) * heads)
                    def _():
                        in_sums.combine(t)

            at = pl.ds(c * CHUNK, CHUNK)
            q, k, v = qkv_ref[at, 0:DK], qkv_ref[at, DK : 2 * DK], qkv_ref[at, 2 * DK :]
            kf, vf = k.astype(f32), v.astype(f32)
            log_gate, strength, rate, logit = gates(rate_ref[at, :], decay_ref, head)
            column, total, ratio = decays(log_gate, lower, upper, eye)
            growth = jnp.exp(column)
            remain = jnp.exp(total - column)
            whole = jnp.exp(total)
            inverse = inv_ref[0, c]
            s0 = s_ref[0, c]
            do = do_scr[chain, at, :]
            grad_state = leaving[c]
            low_grad_state = grad_state.astype(bf16)
            kq = jnp.concatenate([k, q], axis=0)
            products = mm(kq, k, NT)
            kk, qk = products[:CHUNK], products[CHUNK:]
            reads = mm(kq, s0)
            ks, qs = reads[:CHUNK], reads[CHUNK:]
            fresh = vf - growth * ks
            pseudo = mm(inverse, strength * fresh).astype(bf16)
            scores = (ratio * qk).astype(bf16)
            dpseudo = mm(scores, do, TN) + mm(remain * kf, low_grad_state)
            dtarget = mm(inverse, dpseudo, TN)
            low_dtarget = dtarget.astype(bf16)
            dstrength = jnp.sum(dtarget * fresh, axis=1, keepdims=True)
            dlog = -(strength * growth) * jnp.sum(dtarget * ks, axis=1, keepdims=True)
            dv = strength * dtarget
            both = jnp.concatenate([low_dtarget, do], axis=0)
            outer = mm(both, pseudo, NT)
            dcoupling = jnp.where(strict, -outer[:CHUNK] * ratio, 0.0)
            by_strength = dcoupling * kk
            dstrength = dstrength + jnp.sum(by_strength, axis=1, keepdims=True)
            exponent = strength * by_strength
            dqk_f = jnp.where(lower, outer[CHUNK:] * ratio, 0.0)
            exponent = exponent + dqk_f * qk
            pair = jnp.concatenate([(dcoupling * strength).astype(bf16), dqk_f.astype(bf16)], axis=0)
            back = mm(both, s0, NT)
            wide = mm(pair, k)
            dq = growth * back[CHUNK:] + wide[CHUNK:]
            dkept = mm(pseudo, low_grad_state, NT)
            dk = (
                wide[:CHUNK]
                - (strength * growth) * back[:CHUNK]
                + mm(pair, kq, TN)
                + remain * dkept
            )
            dlog = dlog + growth * jnp.sum(do.astype(f32) * qs, axis=1, keepdims=True)
            from_kept = remain * jnp.sum(kf * dkept, axis=1, keepdims=True)
            dlog = dlog - from_kept + jnp.sum(exponent, axis=1, keepdims=True)
            dlog_row = to_row(dlog, eye) - jnp.sum(exponent, axis=0, keepdims=True)
            tail = jnp.sum(from_kept, axis=0, keepdims=True) + whole * jnp.sum(
                jnp.sum(grad_state * s0.astype(f32), axis=1, keepdims=True), axis=0, keepdims=True
            )
            dgate = jnp.sum(jnp.where(upper, dlog_row, 0.0), axis=1, keepdims=True) + tail
            slope = sigmoid(logit)
            drate0 = -rate * slope * dgate
            drate1 = dstrength * strength * (1.0 - strength)
            rate_total = rate_total + jnp.sum(dgate * log_gate, axis=0, keepdims=True)
            bias_total = bias_total + jnp.sum(drate0, axis=0, keepdims=True)
            here = pl.ds(pl.multiple_of(first + c * CHUNK, CHUNK), CHUNK)
            others = jnp.where(head == 0, 0.0, dp_ref[here, in_cols:].astype(f32))
            dp_ref[here, in_cols:] = jnp.where(
                lanes == 2 * head, drate0, jnp.where(lanes == 2 * head + 1, drate1, others)
            ).astype(bf16)
            convolved = convolve(x_scr, conv, c * CHUNK)
            sig = sigmoid(convolved)
            active = convolved * sig
            slope_conv = sig * (1.0 + convolved * (1.0 - sig))

            def unit_grad(rows_in, grad):
                inv_norm = lax.rsqrt(jnp.sum(rows_in * rows_in, axis=1, keepdims=True) + epsilon)
                y = rows_in * inv_norm
                return inv_norm * (grad - y * jnp.sum(y * grad, axis=1, keepdims=True))

            dq = dq.astype(bf16).astype(f32) * DK ** (-0.5)
            dk = dk.astype(bf16).astype(f32)
            dv = dv.astype(bf16).astype(f32)
            dconv = (
                jnp.concatenate(
                    [unit_grad(active[:, :DK], dq), unit_grad(active[:, DK : 2 * DK], dk), dv],
                    axis=1,
                )
                * slope_conv
            )
            g_scr[pl.ds(8 + c * CHUNK, CHUNK), :] = dconv
            for j in range(CONV):
                shifted_in = x_scr[pl.ds(c * CHUNK + HALO - CONV + 1 + j, CHUNK), :]
                conv_total[j] = conv_total[j] + jnp.sum(dconv * shifted_in, axis=0, keepdims=True)
        for j in range(CONV):
            tap = pl.ds(j * heads + head, 1)
            conv_scr[tap, :] = conv_total[j] + jnp.where(seq == 0, 0.0, conv_scr[tap, :])
        spots = lax.broadcasted_iota(jnp.int32, decay_scr.shape, 1)
        top = lax.broadcasted_iota(jnp.int32, decay_scr.shape, 0) == 0
        decay_scr[...] = decay_scr[...] + jnp.where(
            top & (spots == 2 * heads + head), rate_total, 0.0
        ) + jnp.where(top & (spots == 3 * heads + head), bias_total, 0.0)

        def conv_back(at, size):
            grad = g_scr[pl.ds(at + CONV - 1, size), :] * conv[0:1]
            for j in range(1, CONV):
                grad = grad + g_scr[pl.ds(at + CONV - 1 - j, size), :] * conv[j : j + 1]
            return grad

        halo_send[chain] = conv_back(0, 8)

        @pl.when(place > 0)
        def _():
            returned(chain).start()

        conv_at = pl.ds(pl.multiple_of(head * QKV, QKV), QKV)
        for c in range(count):
            grad = conv_back(8 + c * CHUNK, CHUNK)
            positions = place * length + c * CHUNK + lax.broadcasted_iota(
                jnp.int32, (CHUNK, 1), 0
            )
            live = (positions >= start).astype(f32)
            if c == count - 1:
                tail_scr[chain] = grad[CHUNK - HALO :]
            dp_ref[pl.ds(pl.multiple_of(first + c * CHUNK, CHUNK), CHUNK), conv_at] = (
                grad * live
            ).astype(bf16)

    @pl.when(step == chains - 1)
    def _():
        loads[2].wait()

        def gate_grads(i, carry):
            d = far_first(i)
            rows = pl.ds(pl.multiple_of(d * pair, pair), pair)
            mine, others = halves(mm(nin_v[rows, :], dp_ref[:, conv_cols:in_cols]))
            gate_own[d] = mine.astype(bf16)
            gate_source[d] = others.astype(bf16)
            gate_line.core_copy(d, gate_source.at[d]).start()
            return carry

        lax.fori_loop(0, places, gate_grads, 0)
        for d in range(places):
            late_load(d).wait()
            late_line.add_core(d, late_source(d))

    relayed = step - lag

    @pl.when((relayed >= 0) & (relayed < chains))
    def _():
        chain = jnp.clip(relayed, 0, chains - 1)
        for side in range(2):
            at = slice(side * half, (side + 1) * half)

            @pl.when(place < places - 1)
            def _():
                passed(chain, side).wait_recv()

            @pl.when(place > 0)
            def _():
                earlier = mm(trans_ref[chain], recv[chain, :, at], TN) + own_scr[chain, :, at]
                send[chain, :, at] = earlier.astype(bf16)
                passed(chain, side).start()

    @pl.when(step == chains - 1)
    def _():
        sums.combine(0)

    @pl.when(step == chains)
    def _():
        for kind in range(2, 6):
            sums.copy(kind, 0).wait_recv()
        for t in range(subs):
            rows = pl.ds(t * SUB, SUB)
            ring.put(t, (hidden_ref[rows, :] + sums.total(rows)).astype(bf16))
            ring.start(t)
        out_store.start(me)

    @pl.when(step == chains + 2)
    def _():
        for t in range(subs):
            ring.forward(t)

    for third, at_step in enumerate((chains - 1, chains + 1, 2 * chains - 1)):

        @pl.when(step == at_step)
        def _():
            for hop in hops(third):
                late_line.advance(hop)

    for third, at_step in enumerate((chains, chains + 1, chains + 2)):

        @pl.when(step == at_step)
        def _():
            if third == 0:
                for d in range(places):
                    gate_line.add_core(d, gate_source.at[d])
            for hop in hops(third):
                gate_line.advance(hop)

    def mend_ends(seq):
        for head in range(heads):
            chain = seq * heads + head

            @pl.when(place < places - 1)
            def _():
                returned(chain).wait_recv()

            positions = (place + 1) * length - HALO + lax.broadcasted_iota(
                jnp.int32, (HALO, 1), 0
            )
            live = (positions >= start_ref[seq]).astype(f32)
            grad = tail_scr[chain] + jnp.concatenate(
                [jnp.zeros((HALO - 8, QKV), f32), halo_recv[chain]], axis=0
            )
            dp_ref[pl.ds((seq + 1) * length - HALO, HALO), pl.ds(head * QKV, QKV)] = (
                grad * live
            ).astype(bf16)

    def project(t):
        def one(i, carry):
            k = jnp.where(i == 0, peers - 1, lax.rem(i, peers - 1))
            rows = piece_rows(me ^ k, t, total, subs)
            partial = mm(dp_ref[rows, 0:conv_cols], win_v[:, 0:conv_cols], NT)
            partial = partial + mm(dp_ref[rows, conv_cols:in_cols], wog_v[...], NT)
            partial = partial + mm(dp_ref[rows, in_cols:], win_v[:, conv_cols:], NT)
            in_sent[k, pl.ds(t * SUB, SUB), :] = partial.astype(bf16)

            for kk in range(1, peers):

                @pl.when(k == kk)
                def _():
                    in_sums.start(kk, t)

            return carry

        lax.fori_loop(0, peers, one, 0)

    for t in range(seqs - 1):

        @pl.when(step == chains + (t + 1) * heads - 1)
        def _():
            mend_ends(t)
            if t == 0:
                for load in loads[:2]:
                    load.wait()
            project(t)

    def own_input_grads(t):
        rows = pl.ds(t * SUB, SUB)
        din = in_sums.collect(t)
        x = x_v[rows, :].astype(f32)
        inverse = lax.rsqrt(jnp.mean(x * x, axis=1, keepdims=True) + epsilon)
        scaled = x * inverse
        weighted = din * gain_ref[...]
        grad = hgrad_ref[rows, :] + inverse * (
            weighted - scaled * jnp.mean(weighted * scaled, axis=1, keepdims=True)
        )
        in_ring.put(t, grad.astype(bf16))
        in_ring.start(t)
        return jnp.sum(din * scaled, axis=0, keepdims=True)

    @pl.when(step == 2 * chains - 1)
    def _():
        own_x.wait(me)
        gain_part = jnp.zeros((1, width), f32)
        for t in range(seqs - 1):
            gain_part = gain_part + own_input_grads(t)
        mend_ends(seqs - 1)
        taps = CONV * heads
        per = QKV // group
        lanes = lax.broadcasted_iota(jnp.int32, (taps, PAD), 1)
        for q in range(group):
            at = per * q // PAD * PAD
            shift = (PAD // 2 - per * q) % PAD
            moved = conv_scr[:, at : at + PAD]
            if shift:
                moved = pltpu.roll(moved, shift, 1)
            kept = jnp.where((lanes >= PAD // 2) & (lanes < PAD // 2 + per), moved, 0.0)
            extras_v[q * shard : q * shard + taps, :] = kept + decay_scr[...]
        if seqs == 1:
            for load in loads[:2]:
                load.wait()

        def place_grads(i, carry):
            d = far_first(i)
            rows = pl.ds(pl.multiple_of(d * pair, pair), pair)
            mine, others = halves(mm(nin_v[rows, :], dp_ref[:, 0:conv_cols]))
            conv_own[d, :, 0:conv_cols] = mine.astype(bf16)
            conv_source[d, :, 0:conv_cols] = others.astype(bf16)
            mine, others = halves(mm(nin_v[rows, :], dp_ref[:, in_cols:]) + extras_v[rows, :])
            conv_own[d, :, conv_cols:] = mine.astype(bf16)
            conv_source[d, :, conv_cols:] = others.astype(bf16)
            conv_line.core_copy(d, conv_source.at[d]).start()

            @pl.when(i > 0)
            def _():
                before = far_first(jnp.maximum(i - 1, 0))
                conv_line.add_core(before, conv_source.at[before])

            return carry

        first_places = min(2, places)
        lax.fori_loop(0, first_places, place_grads, 0)
        project(seqs - 1)
        lax.fori_loop(first_places, places, place_grads, 0)
        before = far_first(places - 1)
        conv_line.add_core(before, conv_source.at[before])
        for hop in hops(0):
            conv_line.advance(hop)
        in_sums.combine(seqs - 1)
        gain_part = gain_part + own_input_grads(seqs - 1)
        lane_rows = width // 128
        gains_v[...] = jnp.zeros_like(gains_v)
        for r in range(lane_rows):
            gains_v[r : r + 1, :] = gain_part[:, r * 128 : (r + 1) * 128]
            gains_v[lane_rows + r : lane_rows + r + 1, :] = ffn_gain_ref[
                0:1, r * 128 : (r + 1) * 128
            ]
        for r in range(DV // 128):
            gains_v[2 * lane_rows + r : 2 * lane_rows + r + 1, :] = o_gain_scr[
                0:1, r * 128 : (r + 1) * 128
            ]

        def gains_copy(k):
            return head_copy(gains_v, gains_recv.at[k], hs.at[k], hr.at[k], me ^ k)

        def to_group(d):
            to = lax.rem(flat + d, group)
            return pltpu.make_async_remote_copy(
                src_ref=gains_sum, dst_ref=gains_all.at[d], send_sem=gs.at[d], recv_sem=gr.at[d],
                device_id={"seq": to // cores, "batch": lax.rem(to, cores)}, device_id_type=MESH,
            )

        for k in range(1, peers):
            gains_copy(k).start()
        for hop in hops(1):
            conv_line.advance(hop)
        in_store.start(me)
        for t in range(subs):
            ring.finish(t)
        for k in range(1, peers):
            out_store.start(me ^ k)
        gathered = gains_v[...]
        for k in range(1, peers):
            gains_copy(k).wait_recv()
            gathered = gathered + gains_recv[k]
        gains_sum[...] = gathered
        for d in range(1, group):
            to_group(d).start()
        for t in range(subs):
            in_ring.forward(t)
        for hop in hops(2):
            conv_line.advance(hop)
        in_store.start(me ^ 1)
        in_store.start(me ^ 2)
        for d in range(1, group):
            to_group(d).wait_recv()
            gathered = gathered + gains_all[d]
        gains_out[...] = gathered
        for t in range(subs):
            in_ring.finish(t)
        in_store.start(me ^ 3)
        late_out[...] = late_line.finish()
        grad = gate_line.finish()
        for head in range(heads):
            at = head * (QKV + DV) + QKV
            grad_out[:, at : at + DV] = grad[:, head * DV : (head + 1) * DV]
        grad = conv_line.finish()
        for head in range(heads):
            at = head * (QKV + DV)
            grad_out[:, at : at + QKV] = grad[:, head * QKV : (head + 1) * QKV]
        small_out[...] = grad[:, conv_cols:]
        for k in range(peers):
            out_store.wait(k)
            in_store.wait(k)

        @pl.when(place > 0)
        def _():
            for chain in range(chains):
                returned(chain).wait_send()
                for side in range(2):
                    passed(chain, side).wait_send()

        sums.drain(0)
        for t in range(subs):
            ring.drain(t)
            in_ring.drain(t)
            in_sums.drain(t)
        for k in range(1, peers):
            gains_copy(k).wait_send()
        for d in range(1, group):
            to_group(d).wait_send()
        conv_line.drain(lambda d: conv_source.at[d])
        gate_line.drain(lambda d: gate_source.at[d])
        late_line.drain(late_source)


def backward_rule(
    starts, decay_par, dn, mixed, og, projected, o_gain, n, qe, tot, trans, qkv, inv, states, halo,
    conv_w, hidden, hidden_grad, gain, ffn_gain_part, ffn_part, in_full, gate_full, turned, x, late_grads,
    heads,
):
    places, peers, cores = lax.axis_size("seq"), lax.axis_size("head"), lax.axis_size("batch")
    chains, count = n.shape[:2]
    seqs = chains // heads
    rows = projected.shape[0]
    length = rows // seqs
    width = hidden.shape[1]
    own_rows = hidden.shape[0]
    subs = own_rows // SUB
    rates_at = heads * QKV // PAD
    values = heads * DV
    cols = heads * (QKV + DV) + PAD
    group = places * cores
    shard = width // group
    gain_rows = 3 * width // 128
    row = lambda first: lambda i: (i // heads, first + i % heads)
    whole = lambda *dims: pl.BlockSpec(dims, lambda j: (0,) * len(dims))
    chain4 = lambda i: (i, 0, 0, 0)
    shape = jax.ShapeDtypeStruct
    per_chain = pltpu.SemaphoreType.DMA((chains,))
    per_peer = pltpu.SemaphoreType.DMA((peers,))
    per_member = pltpu.SemaphoreType.DMA((group,))
    pieces = pltpu.SemaphoreType.DMA((peers, subs))
    ffn_sums = sum_buffers(own_rows, width, subs)
    ffn_sums[3:5] = [pltpu.SemaphoreType.DMA((6, 1))] * 2
    return pl.pallas_call(
        functools.partial(backward_kernel, heads, places, peers, cores),
        grid=(2 * chains,),
        in_specs=[
            smem(),
            smem(),
            pl.BlockSpec((length, DV), early(chains, row(0))),
            pl.BlockSpec((length, DV), early(chains, row(0))),
            pl.BlockSpec((length, DV), early(chains, row(0))),
            whole(1, DV),
            whole(chains, count, DK, DK),
            whole(chains, count, CHUNK, DK),
            whole(chains, count, DK),
            whole(chains, DK, DK),
            pl.BlockSpec((length, QKV), late(chains, row(0))),
            pl.BlockSpec((1, count, CHUNK, CHUNK), late(chains, chain4)),
            pl.BlockSpec((1, count, DK, DV), late(chains, chain4)),
            pl.BlockSpec((length, QKV), late(chains, row(0))),
            pl.BlockSpec((1, HALO, QKV), late(chains, lambda i: (i // heads, 0, i % heads))),
            pl.BlockSpec((length, PAD), late(chains, lambda i: (i // heads, rates_at))),
            pl.BlockSpec((CONV, QKV), late(chains, lambda i: (0, i % heads))),
            whole(own_rows, width),
            whole(own_rows, width),
            whole(1, width),
            whole(8, width),
        ]
        + [anywhere()] * 6,
        out_specs=[
            anywhere(),
            anywhere(),
            whole(gain_rows, 128),
            whole(shard, cols - PAD),
            whole(shard, PAD),
            whole(shard, late_grads.shape[1]),
        ],
        out_shape=[
            shape((rows, width), bf16),
            shape((rows, width), bf16),
            shape((gain_rows, 128), f32),
            shape((shard, cols - PAD), f32),
            shape((shard, PAD), f32),
            shape((shard, late_grads.shape[1]), f32),
        ],
        scratch_shapes=[
            pltpu.VMEM((rows, cols), bf16),
            pltpu.VMEM((HALO + length, QKV), f32),
            pltpu.VMEM((16 + length, QKV), f32),
            pltpu.VMEM((chains, length, DV), bf16),
            pltpu.VMEM((chains, DK, DV), f32),
            pltpu.VMEM((chains, DK, DV), bf16),
            pltpu.VMEM((chains, DK, DV), bf16),
            pltpu.VMEM((chains, HALO, QKV), f32),
            pltpu.VMEM((chains, 8, QKV), f32),
            pltpu.VMEM((chains, 8, QKV), f32),
            pltpu.VMEM((CONV * heads, QKV), f32),
            pltpu.VMEM((CONV * heads, PAD), f32),
            pltpu.VMEM((8, DV), f32),
            pltpu.VMEM((rows, width), bf16),
            pltpu.VMEM((rows, width), bf16),
            pltpu.VMEM((width, cols - values), bf16),
            pltpu.VMEM((width, values), bf16),
            pltpu.VMEM((width, rows), bf16),
            pltpu.VMEM((own_rows, width), bf16),
            pltpu.VMEM((places, shard, cols - values), bf16),
            pltpu.VMEM((places, shard, values), bf16),
            pltpu.VMEM((width, PAD), f32),
            pltpu.VMEM((gain_rows, 128), f32),
            pltpu.VMEM((peers, gain_rows, 128), f32),
            pltpu.VMEM((gain_rows, 128), f32),
            pltpu.VMEM((group, gain_rows, 128), f32),
            pltpu.SemaphoreType.DMA((chains, 2)),
            pltpu.SemaphoreType.DMA((chains, 2)),
            per_chain, per_chain,
            pieces,
            pltpu.SemaphoreType.DMA((3,)),
            pltpu.SemaphoreType.DMA((places,)),
            pieces,
            pltpu.SemaphoreType.DMA((2, peers, subs)),
            per_peer, per_peer, per_member, per_member,
        ]
        + ffn_sums
        + sum_buffers(own_rows, width, subs)
        + line_buffers(places, shard, cols - values)
        + line_buffers(places, shard, values)
        + line_buffers(places, shard, late_grads.shape[1]),
        compiler_params=pltpu.CompilerParams(
            dimension_semantics=("arbitrary",), collective_id=4, has_side_effects=True,
            vmem_limit_bytes=62 * 2**20,
        ),
        name="backward_rule",
    )(
        starts, decay_par, dn, mixed, og, o_gain, n, qe, tot, trans, qkv, inv, states, projected,
        halo, projected, conv_w, hidden, hidden_grad, gain, ffn_gain_part, ffn_part, in_full,
        gate_full, turned, x, late_grads,
    )


def smem():
    return pl.BlockSpec(memory_space=pltpu.SMEM)


def rows_of(t):
    return pl.ds(pl.multiple_of(t * SUB, SUB), SUB)


def block_store(i, size, source, target, sem):
    return pltpu.make_async_copy(
        part(source, i * size, size), part(target, i * size, size), sem.at[i]
    )


def mixer_kernel(
    peers, nin_hbm, mixed_hbm, weights_hbm, x_hbm, gain_ref, o_gain_ref,
    og_hbm, normed_hbm, nm_hbm, turned_hbm, hidden_ref,
    nin, turned, mixed, weights, x_v, og_v, normed_v, nm, in_sem, x_sem, out_sem,
    send, recv, relay, sum_send, sum_recv, gather_send, gather_recv,
):
    me = lax.axis_index("head")
    total, width = nm.shape
    values = mixed.shape[1]
    own_rows = total // peers
    subs = own_rows // SUB
    loads = [
        pltpu.make_async_copy(weights_hbm, weights, in_sem.at[0]),
        pltpu.make_async_copy(nin_hbm, nin, in_sem.at[1]),
        pltpu.make_async_copy(mixed_hbm, mixed, in_sem.at[2]),
    ]
    for load in loads:
        load.start()
    own_x = Pieces(x_hbm, x_v, total, subs, x_sem)
    own_x.start(me)
    stores = [
        Pieces(source, target, total, subs, out_sem.at[i])
        for i, (source, target) in enumerate(
            ((og_v, og_hbm), (normed_v, normed_hbm), (nm, nm_hbm))
        )
    ]
    greet_heads(me, peers)
    for load in loads:
        load.wait()
    sums = Combine(send, recv, relay, me, sum_send, sum_recv, SUB)

    def project(i, carry):
        k = jnp.where(i == 0, peers - 1, lax.rem(i, peers - 1))
        owner = me ^ k
        og = mm(take(nin, owner, subs), weights[:, 0:values])
        gated = og * sigmoid(og)
        own = take(mixed, owner, subs)
        normed = []
        for first in range(0, values, DV):
            at = slice(first, first + DV)
            inverse = lax.rsqrt(
                jnp.mean(own[:, at] * own[:, at], axis=1, keepdims=True) + epsilon
            )
            normed.append((own[:, at] * inverse * o_gain_ref[0:1] * gated[:, at]).astype(bf16))
        normed = jnp.concatenate(normed, axis=1)
        send[k] = mm(normed, weights[:, values:], NT).astype(bf16)
        for t in range(subs):
            rows = piece_rows(owner, t, total, subs)
            og_v[rows, :] = og[t * SUB : (t + 1) * SUB]
            normed_v[rows, :] = normed[t * SUB : (t + 1) * SUB]

        for kk in range(1, peers):

            @pl.when(k == kk)
            def _():
                for t in range(subs):
                    sums.start(kk, t)

        stores[0].start(owner)
        stores[1].start(owner)
        return carry

    lax.fori_loop(0, peers, project, 0)
    tile = 256
    for first in range(0, width, tile):
        turned[first : first + tile, :] = nin[:, first : first + tile].T
    for t in range(subs):
        sums.combine(t)
    turned_store = pltpu.make_async_copy(turned, turned_hbm, in_sem.at[3])
    turned_store.start()
    own_x.wait(me)
    gain = gain_ref[...]
    ring = Spread(nm, subs, me, gather_send, gather_recv)
    for t in range(subs):
        rows = rows_of(t)
        hidden = x_v[rows, :].astype(f32) + sums.collect(t)
        hidden_ref[rows, :] = hidden
        inverse = lax.rsqrt(jnp.mean(hidden * hidden, axis=1, keepdims=True) + epsilon)
        ring.put(t, (hidden * inverse * gain).astype(bf16))
        ring.start(t)
    for t in range(subs):
        ring.forward(t)
    for k in range(peers):
        if k == peers - 1:
            for t in range(subs):
                ring.finish(t)
        stores[2].start(me ^ k)
    turned_store.wait()
    for i in range(peers):
        for store in stores:
            store.wait(i)
    for t in range(subs):
        sums.drain(t)
        ring.drain(t)


def mixer(nin, mixed, weights, x, gain, o_gain):
    peers = lax.axis_size("head")
    total, width = x.shape
    values = mixed.shape[1]
    own_rows = total // peers
    subs = own_rows // SUB
    shape = in_hbm
    return pl.pallas_call(
        functools.partial(mixer_kernel, peers),
        in_specs=[anywhere()] * 4 + [vmem()] * 2,
        out_specs=[anywhere()] * 4 + [vmem()],
        out_shape=[
            shape((total, values), f32),
            shape((total, values), bf16),
            shape((total, width), bf16),
            shape((width, total), bf16),
            shape((own_rows, width), f32),
        ],
        scratch_shapes=[
            pltpu.VMEM((total, width), bf16),
            pltpu.VMEM((width, total), bf16),
            pltpu.VMEM((total, values), f32),
            pltpu.VMEM((width, 2 * values), bf16),
            pltpu.VMEM((own_rows, width), bf16),
            pltpu.VMEM((total, values), f32),
            pltpu.VMEM((total, values), bf16),
            pltpu.VMEM((total, width), bf16),
            pltpu.SemaphoreType.DMA((4,)),
            pltpu.SemaphoreType.DMA((peers, subs)),
            pltpu.SemaphoreType.DMA((3, peers, subs)),
        ]
        + sum_buffers(own_rows, width, subs),
        compiler_params=pltpu.CompilerParams(
            collective_id=1, has_side_effects=True, vmem_limit_bytes=48 * 2**20
        ),
        name="mixer",
    )(nin, mixed, weights, x, gain, o_gain)


def ffn_kernel(
    peers, places, cores, nm_hbm, ffn_hbm, ct_hbm, normed_hbm, weights_hbm, hidden_ref, gain_ref,
    grads_hbm, ffnp_hbm, ng_hbm, hgrad_ref, gpart_ref, down_ref,
    nm_b, ct_b, dgu_b, nm, ffn_v, ct_v, normed_v, wout_v, act, dgu, dm, ffnp_v, grads_v, down_v, ng_v,
    in_sem, out_sem, ng_sem, send, recv, relay, sum_send, sum_recv, gather_send, gather_recv,
    core_recv, seq_send, seq_recv, scatter_sems,
):
    me = lax.axis_index("head")
    total, width = nm.shape
    values = normed_v.shape[1]
    own_rows = total // peers
    subs = own_rows // SUB
    cells = act.shape[1]
    tile = 256
    loads = [
        pltpu.make_async_copy(ffn_hbm, ffn_v, in_sem.at[0]),
        pltpu.make_async_copy(nm_hbm, nm, in_sem.at[1]),
        pltpu.make_async_copy(ct_hbm, ct_v, in_sem.at[2]),
        pltpu.make_async_copy(normed_hbm, normed_v, in_sem.at[3]),
        pltpu.make_async_copy(weights_hbm.at[:, pl.ds(values, values)], wout_v, in_sem.at[4]),
    ]
    for load in loads:
        load.start()
    greet_group(me, peers, places, cores)
    for load in loads[:3]:
        load.wait()
    gain = gain_ref[...]
    sums = Combine(send, recv, relay, me, sum_send, sum_recv, SUB)

    def feed_forward(i, carry):
        k = jnp.where(i == 0, peers - 1, lax.rem(i, peers - 1))
        owner = me ^ k
        nm_b[...] = take(nm, owner, subs)
        ct_b[...] = take(ct_v, owner, subs)

        def cell_tile(j, carry):
            at = pl.ds(pl.multiple_of(j * tile, tile), tile)
            at_up = pl.ds(pl.multiple_of(cells + j * tile, tile), tile)
            at_down = pl.ds(pl.multiple_of(2 * cells + j * tile, tile), tile)
            gate = mm(nm_b[...], ffn_v[:, at])
            up = mm(nm_b[...], ffn_v[:, at_up])
            dact = mm(ct_b[...], ffn_v[:, at_down])
            sig = sigmoid(gate)
            silu = gate * sig
            activated = (silu * up).astype(bf16)
            dgu_b[:, at] = (dact * up * sig * (1.0 + gate * (1.0 - sig))).astype(bf16)
            dgu_b[:, at_up] = (dact * silu).astype(bf16)
            for t in range(subs):
                act[piece_rows(owner, t, total, subs), at] = activated[t * SUB : (t + 1) * SUB]
            return carry

        lax.fori_loop(0, cells // tile, cell_tile, 0)

        def mid_tile(j, carry):
            at = pl.ds(pl.multiple_of(j * tile, tile), tile)
            send[k, :, at] = mm(dgu_b[...], ffn_v[at, 0 : 2 * cells], NT).astype(bf16)
            return carry

        lax.fori_loop(0, width // tile, mid_tile, 0)
        for t in range(subs):
            dgu[piece_rows(owner, t, total, subs), :] = dgu_b[rows_of(t), :]

        for kk in range(1, peers):

            @pl.when(k == kk)
            def _():
                for t in range(subs):
                    sums.start(kk, t)

        @pl.when(k == 2)
        def _():
            for t in range(subs):
                sums.combine(t)

        return carry

    lax.fori_loop(0, peers, feed_forward, 0)

    def down_grads(i, carry):
        at = pl.ds(pl.multiple_of(i * tile, tile), tile)
        down_v[at, :] = mm(ct_v[:, at], act[...], TN).astype(bf16)
        return carry

    lax.fori_loop(0, width // tile, down_grads, 0)
    scatter = GroupScatter(down_v, pl.ds(0, cells), core_recv, seq_send, seq_recv, scatter_sems)
    for k in range(places - 1, -1, -1):
        scatter.core_copy(k).start()

    def cell_grads(i, carry):
        at = pl.ds(pl.multiple_of(i * tile, tile), tile)
        grads_v[at, 0 : 2 * cells] = mm(nm[:, at], dgu[...], TN).astype(bf16)
        return carry

    half = width // tile // 2
    lax.fori_loop(0, half, cell_grads, 0)
    for k in range(places - 1, -1, -1):
        scatter.pass_on(k)
    lax.fori_loop(half, width // tile, cell_grads, 0)
    ring = Spread(dm, subs, me, gather_send, gather_recv)
    gain_part = jnp.zeros((1, width), f32)
    for t in range(subs):
        rows = rows_of(t)
        dmid = sums.collect(t)
        hidden = hidden_ref[rows, :]
        inverse = lax.rsqrt(jnp.mean(hidden * hidden, axis=1, keepdims=True) + epsilon)
        scaled = hidden * inverse
        weighted = dmid * gain
        grad = ct_v[piece_rows(me, t, total, subs), :].astype(f32) + inverse * (
            weighted - scaled * jnp.mean(weighted * scaled, axis=1, keepdims=True)
        )
        hgrad_ref[rows, :] = grad
        ring.put(t, grad.astype(bf16))
        ring.start(t)
        gain_part = gain_part + jnp.sum(dmid * scaled, axis=0, keepdims=True)
    gpart_ref[...] = jnp.broadcast_to(gain_part, gpart_ref.shape)

    def ffn_rows(i, carry):
        rows = pl.ds(pl.multiple_of(i * own_rows, own_rows), own_rows)
        ffnp_v[rows, :] = mm(act[rows, :], ffn_v[:, 2 * cells :], NT).astype(bf16)
        block_store(i, own_rows, ffnp_v, ffnp_hbm, out_sem.at[0]).start()
        return carry

    lax.fori_loop(0, peers, ffn_rows, 0)
    loads[3].wait()
    loads[4].wait()
    for t in range(subs):
        ring.forward(t)
    down_ref[...] = scatter.finish()

    ng_store = Pieces(ng_v, ng_hbm, total, subs, ng_sem)

    def norm_rows(k, carry):
        owner = me ^ k

        @pl.when(k == peers - 1)
        def _():
            for t in range(subs):
                ring.finish(t)

        grads = mm(take(dm, owner, subs), wout_v[...])
        for t in range(subs):
            ng_v[piece_rows(owner, t, total, subs), :] = grads[t * SUB : (t + 1) * SUB]
        ng_store.start(owner)
        return carry

    lax.fori_loop(0, peers, norm_rows, 0)

    def out_grads(i, carry):
        at = pl.ds(pl.multiple_of(i * tile, tile), tile)
        grads_v[at, 2 * cells :] = mm(dm[:, at], normed_v[...], TN).astype(bf16)
        block_store(i, tile, grads_v, grads_hbm, out_sem.at[1]).start()
        return carry

    lax.fori_loop(0, width // tile, out_grads, 0)
    for i in range(peers):
        block_store(i, own_rows, ffnp_v, ffnp_hbm, out_sem.at[0]).wait()
        ng_store.wait(i)
    for i in range(width // tile):
        block_store(i, tile, grads_v, grads_hbm, out_sem.at[1]).wait()
    for t in range(subs):
        sums.drain(t)
        ring.drain(t)
    scatter.drain()


def feed_forward_block(nm, ffn_full, ct, normed, weights, hidden, gain):
    peers, places, cores = lax.axis_size("head"), lax.axis_size("seq"), lax.axis_size("batch")
    total, width = ct.shape
    own_rows = total // peers
    subs = own_rows // SUB
    values = normed.shape[1]
    cells = ffn_full.shape[1] // 3
    shard = width // (places * cores)
    shape = in_hbm
    return pl.pallas_call(
        functools.partial(ffn_kernel, peers, places, cores),
        in_specs=[anywhere()] * 5 + [vmem()] * 2,
        out_specs=[anywhere()] * 3 + [vmem()] * 3,
        out_shape=[
            shape((width, 2 * cells + values), bf16),
            shape((total, width), bf16),
            shape((total, values), f32),
            shape((own_rows, width), f32),
            shape((8, width), f32),
            shape((shard, cells), f32),
        ],
        scratch_shapes=[
            pltpu.VMEM((own_rows, width), bf16),
            pltpu.VMEM((own_rows, width), bf16),
            pltpu.VMEM((own_rows, 2 * cells), bf16),
            pltpu.VMEM((total, width), bf16),
            pltpu.VMEM((width, 3 * cells), bf16),
            pltpu.VMEM((total, width), bf16),
            pltpu.VMEM((total, values), bf16),
            pltpu.VMEM((width, values), bf16),
            pltpu.VMEM((total, cells), bf16),
            pltpu.VMEM((total, 2 * cells), bf16),
            pltpu.VMEM((total, width), bf16),
            pltpu.VMEM((total, width), bf16),
            pltpu.VMEM((width, 2 * cells + values), bf16),
            pltpu.VMEM((width, cells), bf16),
            pltpu.VMEM((total, values), f32),
            pltpu.SemaphoreType.DMA((5,)),
            pltpu.SemaphoreType.DMA((2, max(peers, width // 256))),
            pltpu.SemaphoreType.DMA((peers, subs)),
        ]
        + sum_buffers(own_rows, width, subs)
        + scatter_buffers(places, shard, cells),
        compiler_params=pltpu.CompilerParams(
            collective_id=5, has_side_effects=True, vmem_limit_bytes=56 * 2**20
        ),
        name="feed_forward",
    )(nm, ffn_full, ct, normed, weights, hidden, gain)


def results_kernel(
    units, cells, late_ref, down_in, main_in, small_in, out_hbm, igrad_hbm,
    cells_ref, down_ref, mixer_ref, main_ref, rates_ref, conv_ref, decay_ref, out_ref, igrad_ref,
    out_v, igrad_v, sems,
):
    loads = [
        pltpu.make_async_copy(out_hbm, out_v, sems.at[0]),
        pltpu.make_async_copy(igrad_hbm, igrad_v, sems.at[1]),
    ]
    copies = [
        pltpu.make_async_copy(out_v, out_ref, sems.at[2]),
        pltpu.make_async_copy(igrad_v, igrad_ref, sems.at[3]),
    ]
    for load in loads:
        load.start()
    taps, heads, per = conv_ref.shape
    for part_at in range(2):
        at = part_at * cells
        cells_ref[part_at] = late_ref[:, at : at + cells].T[0:units]
    down_ref[...] = down_in[...].T[0:units]
    mixer_ref[...] = late_ref[:, 2 * cells :].T
    for load, copy in zip(loads, copies):
        load.wait()
        copy.start()
    wide = main_ref.shape[2]
    for head in range(heads):
        main_ref[:, head, :] = main_in[:, head * wide : (head + 1) * wide]
    small = small_in[...]
    rates_ref[...] = small.T[0 : 2 * heads]
    for tap in range(taps):
        conv_ref[tap] = small[tap * heads : (tap + 1) * heads, PAD // 2 : PAD // 2 + per]
    for row in range(2):
        at = (2 + row) * heads
        decay_ref[row : row + 1, :] = small[0:1, at : at + heads]
    for copy in copies:
        copy.wait()


def results(late, down, main, small, out, igrad, units, cells, heads, per):
    shard = late.shape[0]
    values = late.shape[1] - 2 * cells
    shape = jax.ShapeDtypeStruct
    return pl.pallas_call(
        functools.partial(results_kernel, units, cells),
        in_specs=[vmem()] * 4 + [anywhere()] * 2,
        out_specs=[vmem()] * 7 + [anywhere()] * 2,
        out_shape=[
            shape((2, units, shard), f32),
            shape((units, shard), f32),
            shape((values, shard), f32),
            shape((shard, heads, main.shape[1] // heads), f32),
            shape((2 * heads, shard), f32),
            shape((CONV, heads, per), f32),
            shape((2, heads), f32),
            in_hbm(out.shape, out.dtype),
            in_hbm(igrad.shape, igrad.dtype),
        ],
        scratch_shapes=[
            pltpu.VMEM(out.shape, out.dtype),
            pltpu.VMEM(igrad.shape, igrad.dtype),
            pltpu.SemaphoreType.DMA((4,)),
        ],
        compiler_params=pltpu.CompilerParams(vmem_limit_bytes=32 * 2**20),
        name="results",
    )(late, down, main, small, out, igrad)


def shifted(shard, axis, by):
    count = lax.axis_size(axis)
    pairs = [(i, i + by) for i in range(count) if 0 <= i + by < count]
    return lax.ppermute(shard, axis, pairs)


def root_scale(value_rows):
    return lax.rsqrt(jnp.mean(value_rows * value_rows, axis=-1, keepdims=True) + epsilon)


def matmul(a, b, dims=NN):
    return lax.dot_general(a, b, (dims, ((), ())), preferred_element_type=f32)


ALL = ("seq", "batch")


def per_device(
    tokens, starts, attn_gain, w_in, w_rates, conv_w, decay_par, o_gain, w_out, ffn_gain, w_gu,
    w_down, cotangent,
):
    seqs, length, width = tokens.shape
    shard, heads = w_in.shape[:2]
    shards = width // shard
    total = seqs * length
    conv_cols = heads * QKV
    value_cols = heads * DV
    units = w_down.shape[0]
    cells = -(-units // 256) * 256
    spare = cells - units

    packed_in = jnp.concatenate(
        [
            w_in[:, :, :QKV].reshape(shard, conv_cols),
            w_rates.reshape(shard, 2 * heads),
            jnp.zeros((shard, PAD - 2 * heads), f32),
        ],
        axis=1,
    ).astype(bf16)
    packed_gate = jnp.concatenate(
        [w_in[:, :, QKV:].reshape(shard, value_cols), w_out.reshape(value_cols, -1).T], axis=1
    ).astype(bf16)
    packed_ffn = jnp.pad(
        jnp.stack([w_gu[:, 0], w_gu[:, 1], w_down.T], axis=1).astype(bf16),
        ((0, 0), (0, 0), (0, spare)),
    ).reshape(shard, 3 * cells)
    conv_flat = conv_w.reshape(-1)
    small = jnp.concatenate([attn_gain, ffn_gain, conv_flat, o_gain]).astype(bf16)

    x = tokens.reshape(total, width)
    ct = cotangent.reshape(total, width)
    before = shifted(tokens[:, length - HALO :], "seq", 1).reshape(seqs * HALO, width)
    in_full = lax.all_gather(packed_in, ALL, axis=0, tiled=True)
    small_full = lax.all_gather(small, ALL, axis=0)
    gate_full = lax.all_gather(packed_gate, ALL, axis=0, tiled=True)
    ffn_full = lax.all_gather(packed_ffn, ALL, axis=0, tiled=True)
    attn_gain_f = small_full[:, :shard].reshape(1, width).astype(f32)
    ffn_gain_f = small_full[:, shard : 2 * shard].reshape(1, width).astype(f32)
    conv_end = 2 * shard + conv_flat.shape[0]
    conv_full = (
        small_full[:, 2 * shard : conv_end]
        .reshape(shards, CONV, heads, -1)
        .transpose(1, 2, 0, 3)
        .reshape(CONV, conv_cols)
        .astype(f32)
    )
    o_gain_full = small_full[:, conv_end:].reshape(1, DV).astype(f32)

    def normed_rows(rows):
        rows = rows.astype(f32)
        return (rows * root_scale(rows) * attn_gain_f).astype(bf16)

    normed_in = normed_rows(x)
    projected = pltpu.with_memory_space_constraint(matmul(normed_in, in_full), pltpu.HBM)
    halo = matmul(normed_rows(before), in_full[:, :conv_cols]).reshape(seqs, HALO, conv_cols)
    qkv, inv, n, qe, tot, trans, states, mixed = forward_rule(
        starts, decay_par, projected, halo, conv_full, seqs, heads
    )
    og, normed, nm, turned_in, hidden = mixer(
        normed_in, mixed, gate_full, x, ffn_gain_f, o_gain_full
    )
    late_grads, ffn_part, normed_grad, hidden_grad, ffn_gain_part, down_own = feed_forward_block(
        nm, ffn_full, ct, normed, gate_full, hidden, ffn_gain_f
    )
    result, input_grad, gains, in_main, in_small, late_own = backward_rule(
        starts, decay_par, normed_grad, mixed, og, projected, o_gain_full, n, qe, tot, trans, qkv,
        inv, states, halo, conv_full, hidden, hidden_grad, attn_gain_f, ffn_gain_part, ffn_part,
        in_full, gate_full, turned_in, x, late_grads, heads,
    )
    grad_cells, grad_down, grad_out, grad_in, grad_rates, grad_conv, grad_decay, out, input_grad = (
        results(
            late_own, down_own, in_main, in_small, result, input_grad, units, cells, heads,
            QKV // shards,
        )
    )
    at = lax.axis_index(ALL)
    gains = gains.reshape(3, width)
    own_gains = lax.dynamic_slice(gains, (0, at * shard), (2, shard))
    onorm_own = lax.dynamic_slice(gains, (2, at * (DV // shards)), (1, DV // shards))
    return (
        out.reshape(tokens.shape),
        input_grad.reshape(tokens.shape),
        own_gains[0],
        grad_in,
        grad_rates.reshape(heads, 2, shard).transpose(2, 0, 1),
        grad_conv,
        grad_decay,
        onorm_own[0],
        grad_out.reshape(heads, DV, -1),
        own_gains[1],
        grad_cells.transpose(2, 0, 1),
        grad_down,
    )


def solution(mesh):
    weights = P(ALL)
    in_specs = (
        P("batch", "seq", None),
        P("batch"),
        weights,
        P(ALL, "head", None),
        P(ALL, "head", None),
        P(None, "head", ALL),
        P(None, "head"),
        weights,
        P("head", None, ALL),
        weights,
        P(ALL, None, "head"),
        P("head", ALL),
        P("batch", "seq", None),
    )
    out_specs = (
        P("batch", "seq", None),
        P("batch", "seq", None),
        weights,
        P(ALL, "head", None),
        P(ALL, "head", None),
        P(None, "head", ALL),
        P(None, "head"),
        weights,
        P("head", None, ALL),
        weights,
        P(ALL, None, "head"),
        P("head", ALL),
    )
    return jax.shard_map(
        per_device, mesh=mesh, in_specs=in_specs, out_specs=out_specs, check_vma=False
    )
```

```python
import functools

import jax
import jax.numpy as jnp
from jax import lax
from jax.experimental import pallas as pl
from jax.experimental.pallas import tpu as pltpu
from jax.sharding import PartitionSpec as P

DK = 128
DV = 256
CONV = 4
QKV = 2 * DK + DV
CHUNK = 128
HALO = 16
PAD = 128

bf16 = jnp.bfloat16
f32 = jnp.float32
epsilon = 1e-06
NN = ((1,), (0,))
NT = ((1,), (1,))
TN = ((0,), (0,))


def mm(a, b, dims=NN):
    return lax.dot_general(
        a.astype(bf16), b.astype(bf16), (dims, ((), ())), preferred_element_type=f32
    )


def split_mm(a, b):
    a_high, b_high = a.astype(bf16), b.astype(bf16)
    a_low = (a - a_high.astype(f32)).astype(bf16)
    b_low = (b - b_high.astype(f32)).astype(bf16)
    return mm(a_high, b_high) + (mm(a_high, b_low) + mm(a_low, b_high))


def iotas(n):
    return (
        lax.broadcasted_iota(jnp.int32, (n, n), 0),
        lax.broadcasted_iota(jnp.int32, (n, n), 1),
    )


def unit_lower_inverses(mats):
    n = mats[0].shape[0]
    rows, cols = iotas(n)
    eye = (rows == cols).astype(f32)
    pair = ((rows >> 1) == (cols >> 1)) & (rows > cols)
    inverses = [eye - jnp.where(pair, a, 0.0) for a in mats]
    shift = 1
    while (1 << shift) < n:
        corner = ((rows >> (shift + 1)) == (cols >> (shift + 1))) & (
            (rows >> shift) > (cols >> shift)
        )
        firsts = [mm(jnp.where(corner, a, 0.0), x) for a, x in zip(mats, inverses)]
        inverses = [x - mm(x, y) for x, y in zip(inverses, firsts)]
        shift += 1
    residuals = [eye - x - split_mm(a, x) for a, x in zip(mats, inverses)]
    return [x + mm(x, r) for x, r in zip(inverses, residuals)]


def sigmoid(v):
    return 1.0 / (1.0 + jnp.exp(-v))


def softplus(v):
    small = jnp.exp(-jnp.abs(v))
    one_more = 1.0 + small
    gap = one_more - 1.0
    exact = gap == 0.0
    tail = jnp.where(exact, small, jnp.log(one_more) * small / jnp.where(exact, 1.0, gap))
    return jnp.maximum(v, 0.0) + tail


def to_row(column, eye):
    return jnp.sum(jnp.where(eye, column, 0.0), axis=0, keepdims=True)


def pick(block, lane):
    lanes = lax.broadcasted_iota(jnp.int32, block.shape, 1)
    return jnp.sum(jnp.where(lanes == lane, block, 0.0), axis=1, keepdims=True)


def gates(logits, decay_ref, head):
    rate = jnp.exp(jnp.full((1, 1), decay_ref[0, head], f32))
    shifted_logit = pick(logits, 2 * head) + decay_ref[1, head]
    strength = sigmoid(pick(logits, 2 * head + 1))
    log_gate = -rate * softplus(shifted_logit)
    return log_gate, strength, rate, shifted_logit


def decays(log_gate, lower, upper, eye):
    gate_row = to_row(log_gate, eye)
    column = jnp.sum(jnp.where(lower, gate_row, 0.0), axis=1, keepdims=True)
    row = jnp.sum(jnp.where(upper, log_gate, 0.0), axis=0, keepdims=True)
    ratio = jnp.where(lower, jnp.exp(jnp.where(lower, column - row, 0.0)), 0.0)
    total = jnp.sum(log_gate, axis=0, keepdims=True)
    return column, total, ratio


def load_conv_input(main_ref, halo_ref, start, x_scr, first):
    length = main_ref.shape[0]
    positions = first + lax.broadcasted_iota(jnp.int32, (length, 1), 0)
    live = (positions >= start).astype(f32)
    before = first - HALO + lax.broadcasted_iota(jnp.int32, (HALO, 1), 0)
    lived = (before >= start).astype(f32)
    x_scr[pl.ds(0, HALO), :] = (halo_ref[0] * lived).astype(bf16).astype(f32)
    x_scr[pl.ds(HALO, length), :] = (main_ref[...] * live).astype(bf16).astype(f32)


def convolve(x_scr, conv, at):
    total = x_scr[pl.ds(at + HALO - CONV + 1, CHUNK), :] * conv[0:1]
    for j in range(1, CONV):
        total = total + x_scr[pl.ds(at + HALO - CONV + 1 + j, CHUNK), :] * conv[j : j + 1]
    return total


def unit(rows):
    return rows * lax.rsqrt(jnp.sum(rows * rows, axis=1, keepdims=True) + epsilon)


MESH = pl.DeviceIdType.MESH
SUB = 128


def head_copy(src, dst, send_sem, recv_sem, peer):
    return pltpu.make_async_remote_copy(
        src_ref=src, dst_ref=dst, send_sem=send_sem, recv_sem=recv_sem,
        device_id={"head": peer}, device_id_type=MESH,
    )


def greet_heads(me, peers):
    barrier = pltpu.get_barrier_semaphore()
    for k in range(1, peers):
        pl.semaphore_signal(barrier, inc=1, device_id={"head": me ^ k}, device_id_type=MESH)
    pl.semaphore_wait(barrier, peers - 1)


def part(ref, start, size):
    return ref.at[pl.ds(pl.multiple_of(start, size), size)]


def piece_rows(owner, t, total, subs):
    return pl.ds(pl.multiple_of(t * (total // subs) + owner * SUB, SUB), SUB)


def take(ref, owner, subs):
    total = ref.shape[0]
    return jnp.concatenate(
        [ref[piece_rows(owner, t, total, subs), :] for t in range(subs)], axis=0
    )


class Pieces:
    def __init__(self, source, target, total, subs, sems):
        self.source, self.target, self.total, self.subs, self.sems = source, target, total, subs, sems

    def at(self, ref, owner, t):
        rows = piece_rows(owner, t, self.total, self.subs)
        if ref.shape[0] != self.total:
            rows = pl.ds(t * SUB, SUB)
        return ref.at[rows]

    def copies(self, owner):
        return [
            pltpu.make_async_copy(
                self.at(self.source, owner, t), self.at(self.target, owner, t),
                self.sems.at[owner, t],
            )
            for t in range(self.subs)
        ]

    def start(self, owner):
        for copy in self.copies(owner):
            copy.start()

    def wait(self, owner):
        for copy in self.copies(owner):
            copy.wait()


class Spread:
    def __init__(self, buffer, subs, me, send_sem, recv_sem):
        self.buffer, self.subs, self.me = buffer, subs, me
        self.send_sem, self.recv_sem = send_sem, recv_sem

    def region(self, owner, t, half):
        rows = piece_rows(owner, t, self.buffer.shape[0], self.subs)
        middle = self.buffer.shape[1] // 2
        if half is None:
            return self.buffer.at[rows]
        return self.buffer.at[rows, pl.ds(half * middle, middle)]

    def put(self, t, value):
        self.buffer[piece_rows(self.me, t, self.buffer.shape[0], self.subs), :] = value

    def copy(self, kind, t, owner):
        at = self.region(owner, t, None if kind < 2 else kind - 2)
        to = self.me ^ (1 if kind in (0, 3) else 2)
        return head_copy(at, at, self.send_sem.at[kind, t], self.recv_sem.at[kind, t], to)

    def start(self, t):
        self.copy(0, t, self.me).start()
        self.copy(1, t, self.me).start()

    def forward(self, t):
        self.copy(0, t, self.me ^ 1).wait_recv()
        self.copy(2, t, self.me ^ 1).start()
        self.copy(1, t, self.me ^ 2).wait_recv()
        self.copy(3, t, self.me ^ 2).start()

    def finish(self, t):
        self.copy(2, t, self.me ^ 3).wait_recv()
        self.copy(3, t, self.me ^ 3).wait_recv()

    def drain(self, t):
        for kind, owner in enumerate((0, 0, 1, 2)):
            self.copy(kind, t, self.me ^ owner).wait_send()


class Combine:
    def __init__(self, send, recv, relay, me, send_sem, recv_sem, piece):
        self.send, self.recv, self.relay, self.me = send, recv, relay, me
        self.send_sem, self.recv_sem, self.piece = send_sem, recv_sem, piece
        self.middle = send.shape[2] // 2

    def rows(self, t):
        return pl.ds(pl.multiple_of(t * self.piece, self.piece), self.piece)

    def copy(self, kind, t):
        rows, low, high = self.rows(t), pl.ds(0, self.middle), pl.ds(self.middle, self.middle)
        source, target, to = (
            (self.send.at[3, rows, low], self.relay.at[0, rows], 1),
            (self.send.at[3, rows, high], self.relay.at[1, rows], 2),
            (self.send.at[1, rows, low], self.recv.at[0, rows, low], 1),
            (self.send.at[2, rows, high], self.recv.at[1, rows, high], 2),
            (self.send.at[1, rows, high], self.recv.at[0, rows, high], 1),
            (self.send.at[2, rows, low], self.recv.at[1, rows, low], 2),
        )[kind]
        return head_copy(
            source, target, self.send_sem.at[kind, t], self.recv_sem.at[kind, t], self.me ^ to
        )

    def start(self, k, t):
        if k == 3:
            self.copy(0, t).start()
            self.copy(1, t).start()
        else:
            self.copy(k + 1, t).start()

    def combine(self, t):
        rows = self.rows(t)
        for k, at in ((1, pl.ds(self.middle, self.middle)), (2, pl.ds(0, self.middle))):
            self.copy(2 - k, t).wait_recv()
            both = self.send[k, rows, at].astype(f32) + self.relay[2 - k, rows, :].astype(f32)
            self.send[k, rows, at] = both.astype(bf16)
            self.copy(3 + k, t).start()

    def collect(self, t):
        for kind in range(2, 6):
            self.copy(kind, t).wait_recv()
        return self.total(self.rows(t))

    def total(self, rows):
        return (
            self.send[0, rows, :].astype(f32)
            + self.recv[0, rows, :].astype(f32)
            + self.recv[1, rows, :].astype(f32)
        )

    def drain(self, t):
        for kind in range(6):
            self.copy(kind, t).wait_send()


def sum_buffers(rows, width, pieces):
    return [
        pltpu.VMEM((4, rows, width), bf16),
        pltpu.VMEM((2, rows, width), bf16),
        pltpu.VMEM((2, rows, width // 2), bf16),
        pltpu.SemaphoreType.DMA((6, pieces)),
        pltpu.SemaphoreType.DMA((6, pieces)),
        pltpu.SemaphoreType.DMA((4, pieces)),
        pltpu.SemaphoreType.DMA((4, pieces)),
    ]


class GroupScatter:
    def __init__(self, source, columns, core_recv, seq_send, seq_recv, sems):
        self.source, self.columns = source, columns
        self.core_recv, self.seq_send, self.seq_recv, self.sems = core_recv, seq_send, seq_recv, sems
        self.place, self.core = lax.axis_index("seq"), lax.axis_index("batch")
        self.places, self.shard = core_recv.shape[0], core_recv.shape[1]

    def rows(self, k, core):
        at = ((self.place ^ k) * 2 + core) * self.shard
        return pl.ds(pl.multiple_of(at, self.shard), self.shard)

    def core_copy(self, k):
        return along(
            "batch", self.source.at[self.rows(k, 1 - self.core), self.columns],
            self.core_recv.at[k], self.sems.at[0, k], self.sems.at[1, k], 1 - self.core,
        )

    def seq_copy(self, k):
        return along(
            "seq", self.seq_send.at[k], self.seq_recv.at[k], self.sems.at[2, k],
            self.sems.at[3, k], self.place ^ k,
        )

    def pass_on(self, k):
        self.core_copy(k).wait_recv()
        own = self.source[self.rows(k, self.core), self.columns].astype(f32)
        self.seq_send[k] = (own + self.core_recv[k].astype(f32)).astype(bf16)

        @pl.when(k > 0)
        def _():
            self.seq_copy(k).start()

    def finish(self):
        total = self.seq_send[0].astype(f32)
        for k in range(1, self.places):
            self.seq_copy(k).wait_recv()
            total = total + self.seq_recv[k].astype(f32)
        return total

    def drain(self):
        for k in range(self.places):
            self.core_copy(k).wait_send()
        for k in range(1, self.places):
            self.seq_copy(k).wait_send()


class LineScatter:
    def __init__(self, own, core_recv, recv, sems):
        self.own, self.core_recv, self.recv, self.sems = own, core_recv, recv, sems
        self.place, self.core = lax.axis_index("seq"), lax.axis_index("batch")
        self.places = own.shape[0]

    def clear(self):
        @pl.when(self.place == 0)
        def _():
            self.recv[0] = jnp.zeros_like(self.recv[0])

        @pl.when(self.place == self.places - 1)
        def _():
            self.recv[self.places] = jnp.zeros_like(self.recv[0])

    def core_copy(self, d, source):
        return along(
            "batch", source, self.core_recv.at[d], self.sems.at[0, d], self.sems.at[1, d],
            1 - self.core,
        )

    def add_core(self, d, source):
        self.core_copy(d, source).wait_recv()
        self.add(d, self.core_recv[d])

    def add(self, d, other):
        self.own[d] = (self.own[d].astype(f32) + other.astype(f32)).astype(bf16)

    def move(self, d):
        right = d > self.place
        to = jnp.clip(jnp.where(right, self.place + 1, self.place - 1), 0, self.places - 1)
        slot = jnp.where(right | (to != d), d, self.places)
        return along(
            "seq", self.own.at[d], self.recv.at[slot], self.sems.at[2, d], self.sems.at[3, slot], to
        )

    def arrived(self, slot):
        return along(
            "seq", self.own.at[0], self.recv.at[slot], self.sems.at[2, 0], self.sems.at[3, slot],
            jnp.where(self.place > 0, self.place - 1, self.places - 1),
        )

    def advance(self, hop):
        last = self.places - 1

        def towards(d, active, through):
            @pl.when(active)
            def _():
                @pl.when(through)
                def _():
                    self.arrived(d).wait_recv()
                    self.add(d, self.recv[d])

                self.move(d).start()

        turn = hop - self.place
        d = jnp.clip(last - turn, 0, last)
        towards(d, (turn >= 0) & (last - turn > self.place), self.place > 0)
        turn = hop - (last - self.place)
        d = jnp.clip(turn, 0, last)
        towards(d, (turn >= 0) & (turn < self.place), self.place < last)

    def finish(self):
        @pl.when(self.place > 0)
        def _():
            self.arrived(self.place).wait_recv()

        @pl.when(self.place < self.places - 1)
        def _():
            self.arrived(self.places).wait_recv()

        return (
            self.own[self.place].astype(f32)
            + self.recv[self.place].astype(f32)
            + self.recv[self.places].astype(f32)
        )

    def drain(self, source):
        for d in range(self.places):
            self.core_copy(d, source(d)).wait_send()

            @pl.when(self.place != d)
            def _():
                self.move(d).wait_send()


def line_buffers(places, shard, columns):
    return [
        pltpu.VMEM((places, shard, columns), bf16),
        pltpu.VMEM((places, shard, columns), bf16),
        pltpu.VMEM((places + 1, shard, columns), bf16),
        pltpu.SemaphoreType.DMA((4, places + 1)),
    ]


def scatter_buffers(places, shard, columns):
    return [pltpu.VMEM((places, shard, columns), bf16)] * 3 + [
        pltpu.SemaphoreType.DMA((4, places))
    ]


def call_group(me, peers, places, cores):
    barrier = pltpu.get_barrier_semaphore()
    group = places * cores
    flat = lax.axis_index("seq") * cores + lax.axis_index("batch")
    for k in range(1, peers):
        pl.semaphore_signal(barrier, inc=1, device_id={"head": me ^ k}, device_id_type=MESH)
    for d in range(1, group):
        to = lax.rem(flat + d, group)
        pl.semaphore_signal(
            barrier, inc=1, device_id={"seq": to // cores, "batch": lax.rem(to, cores)},
            device_id_type=MESH,
        )


def meet_group(peers, places, cores):
    pl.semaphore_wait(pltpu.get_barrier_semaphore(), peers + places * cores - 2)


def greet_group(me, peers, places, cores):
    call_group(me, peers, places, cores)
    meet_group(peers, places, cores)


def in_hbm(dims, kind):
    return pltpu.HBM(dims, kind)


def anywhere():
    return pl.BlockSpec(memory_space=pltpu.HBM)


def vmem():
    return pl.BlockSpec(memory_space=pltpu.VMEM)


def along(axis, source, target, send_sem, recv_sem, to):
    return pltpu.make_async_remote_copy(
        src_ref=source, dst_ref=target, send_sem=send_sem, recv_sem=recv_sem,
        device_id={axis: to}, device_id_type=MESH,
    )


def forward_kernel(
    heads, places, start_ref, decay_ref, main_ref, halo_ref, rate_ref, conv_ref,
    qkv_ref, inv_ref, n_ref, qe_ref, tot_ref, trans_ref, s_ref, mixed_ref,
    x_scr, b_scr, o_scr, carried_scr, send, recv, send_sem, recv_sem,
):
    step = pl.program_id(0)
    chains = n_ref.shape[0]
    count = n_ref.shape[1]
    length = main_ref.shape[0]
    place = lax.axis_index("seq")
    lag = jnp.minimum(place, chains - 1)

    @pl.when(step == 0)
    def _():
        barrier = pltpu.get_barrier_semaphore()

        @pl.when(place > 0)
        def _():
            pl.semaphore_signal(
                barrier, inc=1, device_id={"seq": place - 1}, device_id_type=MESH
            )

        @pl.when(place == 0)
        def _():
            recv[...] = jnp.zeros_like(recv)

    @pl.when(step < chains)
    def _():
        head = step % heads
        load_conv_input(
            main_ref, halo_ref, start_ref[jnp.minimum(step, chains - 1) // heads], x_scr, place * length
        )
        conv = conv_ref[...]
        rows, cols = iotas(CHUNK)
        lower, upper, eye = rows >= cols, rows <= cols, rows == cols
        parts = []
        for c in range(count):
            at = c * CHUNK
            convolved = convolve(x_scr, conv, at)
            active = convolved * sigmoid(convolved)
            q = (unit(active[:, :DK]) * DK ** (-0.5)).astype(bf16)
            k = unit(active[:, DK : 2 * DK]).astype(bf16)
            v = active[:, 2 * DK :].astype(bf16)
            qkv_ref[pl.ds(at, CHUNK), 0:DK] = q
            qkv_ref[pl.ds(at, CHUNK), DK : 2 * DK] = k
            qkv_ref[pl.ds(at, CHUNK), 2 * DK :] = v
            log_gate, strength, _, _ = gates(rate_ref[pl.ds(at, CHUNK), :], decay_ref, head)
            column, total, ratio = decays(log_gate, lower, upper, eye)
            products = mm(jnp.concatenate([k, q], axis=0), k, NT)
            coupling = jnp.where(rows > cols, strength * ratio * products[:CHUNK], 0.0)
            scores = (ratio * products[CHUNK:]).astype(bf16)
            parts.append((q, k, v, strength, column, total, coupling, scores))
        inverses = unit_lower_inverses([p[6] for p in parts])
        maps = []
        for c in range(count):
            q, k, v, strength, column, total, _, scores = parts[c]
            growth = jnp.exp(column)
            kf, vf, qf = k.astype(f32), v.astype(f32), q.astype(f32)
            inverse = inverses[c].astype(bf16)
            inv_ref[0, c] = inverse
            target = jnp.concatenate([(strength * growth) * kf, strength * vf], axis=1)
            solved = mm(inverse, target).astype(bf16)
            read = mm(scores, solved)
            qe_ref[step, c] = (growth * qf - read[:, :DK]).astype(bf16)
            o_scr[step, pl.ds(c * CHUNK, CHUNK), :] = read[:, DK:]
            written = mm(jnp.exp(total - column) * kf, solved, TN)
            low_n = written[:, :DK].astype(bf16)
            n_ref[step, c] = low_n
            b_scr[step, c] = written[:, DK:]
            whole = jnp.exp(total)
            tot_ref[step, pl.ds(c, 1), :] = jnp.broadcast_to(whole, (1, DK))
            maps.append((low_n, written[:, DK:], whole))
        low_n, b, whole = maps[0]
        trans = whole * eye.astype(f32) - low_n.astype(f32)
        carried = b
        for low_n, b, whole in maps[1:]:
            both = jnp.concatenate([trans, carried], axis=1)
            moved = whole * both - mm(low_n, both)
            trans = moved[:, :DK]
            carried = moved[:, DK:] + b
        trans_ref[step] = trans.astype(bf16)
        carried_scr[step] = carried

    @pl.when(step >= chains)
    def _():
        chain = jnp.maximum(step - chains, 0)
        state = recv[chain].astype(f32)
        for c in range(count):
            low_state = state.astype(bf16)
            s_ref[0, c] = low_state
            both = mm(jnp.concatenate([n_ref[chain, c], qe_ref[chain, c]], axis=0), low_state)
            whole = tot_ref[chain, pl.ds(c, 1), 0:1]
            state = whole * state - both[:DK] + b_scr[chain, c]
            at = pl.ds(c * CHUNK, CHUNK)
            mixed_ref[at, :] = o_scr[chain, at, :] + both[DK:]

    half = DV // 2

    def passed(chain, side):
        at = pl.ds(side * half, half)
        return along(
            "seq", send.at[chain, :, at], recv.at[chain, :, at], send_sem.at[chain, side],
            recv_sem.at[chain, side], jnp.minimum(place + 1, places - 1),
        )

    @pl.when((step == 0) & (place < places - 1))
    def _():
        pl.semaphore_wait(pltpu.get_barrier_semaphore(), 1)

    relayed = step - lag

    @pl.when((relayed >= 0) & (relayed < chains))
    def _():
        chain = jnp.clip(relayed, 0, chains - 1)
        for side in range(2):
            at = slice(side * half, (side + 1) * half)

            @pl.when(place > 0)
            def _():
                passed(chain, side).wait_recv()

            @pl.when(place < places - 1)
            def _():
                leaving = mm(trans_ref[chain], recv[chain, :, at]) + carried_scr[chain, :, at]
                send[chain, :, at] = leaving.astype(bf16)
                passed(chain, side).start()

    @pl.when((step == 2 * chains - 1) & (place < places - 1))
    def _():
        for chain in range(chains):
            for side in range(2):
                passed(chain, side).wait_send()


def early(chains, make):
    return lambda j: make(jnp.minimum(j, chains - 1))


def late(chains, make):
    return lambda j: make(jnp.maximum(j - chains, 0))


def forward_rule(starts, decay_par, projected, halo, rates, conv_w, seqs, heads):
    places = lax.axis_size("seq")
    chains = seqs * heads
    length = projected.shape[0] // seqs
    count = length // CHUNK
    row = lambda first: lambda i: (i // heads, first + i % heads)
    whole = lambda *dims: pl.BlockSpec(dims, lambda j: (0,) * len(dims))
    shape = in_hbm
    return pl.pallas_call(
        functools.partial(forward_kernel, heads, places),
        grid=(2 * chains,),
        in_specs=[
            smem(),
            smem(),
            pl.BlockSpec((length, QKV), early(chains, row(0))),
            pl.BlockSpec((1, HALO, QKV), early(chains, lambda i: (i // heads, 0, i % heads))),
            pl.BlockSpec((length, PAD), early(chains, lambda i: (i // heads, 0))),
            pl.BlockSpec((CONV, QKV), early(chains, lambda i: (0, i % heads))),
        ],
        out_specs=[
            pl.BlockSpec((length, QKV), early(chains, row(0))),
            pl.BlockSpec((1, count, CHUNK, CHUNK), early(chains, lambda i: (i, 0, 0, 0))),
            whole(chains, count, DK, DK),
            whole(chains, count, CHUNK, DK),
            whole(chains, count, DK),
            whole(chains, DK, DK),
            pl.BlockSpec((1, count, DK, DV), late(chains, lambda i: (i, 0, 0, 0))),
            pl.BlockSpec((length, DV), late(chains, row(0))),
        ],
        out_shape=[
            shape((seqs * length, heads * QKV), bf16),
            shape((chains, count, CHUNK, CHUNK), bf16),
            shape((chains, count, DK, DK), bf16),
            shape((chains, count, CHUNK, DK), bf16),
            shape((chains, count, DK), f32),
            shape((chains, DK, DK), bf16),
            shape((chains, count, DK, DV), bf16),
            shape((seqs * length, heads * DV), f32),
        ],
        scratch_shapes=[
            pltpu.VMEM((HALO + length, QKV), f32),
            pltpu.VMEM((chains, count, DK, DV), f32),
            pltpu.VMEM((chains, length, DV), f32),
            pltpu.VMEM((chains, DK, DV), f32),
            pltpu.VMEM((chains, DK, DV), bf16),
            pltpu.VMEM((chains, DK, DV), bf16),
            pltpu.SemaphoreType.DMA((chains, 2)),
            pltpu.SemaphoreType.DMA((chains, 2)),
        ],
        compiler_params=pltpu.CompilerParams(
            dimension_semantics=("arbitrary",), collective_id=3, has_side_effects=True,
            vmem_limit_bytes=62 * 2**20,
        ),
        name="forward_rule",
    )(starts, decay_par, projected, halo, rates, conv_w)


def backward_kernel(
    heads, places, peers, cores, start_ref, decay_ref,
    dn_ref, mixed_ref, og_ref, o_gain_ref, n_ref, qe_ref, tot_ref, trans_ref,
    qkv_ref, inv_ref, s_ref, main_ref, halo_ref, rate_ref, conv_ref,
    hidden_ref, hgrad_ref, gain_ref, ffn_gain_ref, ffnp_hbm, win_hbm, wog_hbm, wrates_hbm, nin_hbm, x_hbm,
    late_hbm,
    out_hbm, igrad_hbm, gains_out, grad_out, small_out, late_out,
    dp_ref, x_scr, g_scr, do_scr, own_scr, send, recv, tail_scr, halo_send, halo_recv,
    conv_scr, decay_scr, o_gain_scr, whole_out, whole_in, win_v, wog_v, nin_v, x_v, conv_source,
    gate_source, extras_v, gains_v, gains_recv, gains_sum, gains_all,
    send_sem, recv_sem, halo_send_sem, halo_recv_sem, load_sem, in_sem, late_sem, x_sem, out_sem, hs, hr, gs, gr,
    sent, got, relay, sum_send, sum_recv, gather_send, gather_recv,
    in_sent, in_got, in_relay, in_sum_send, in_sum_recv, in_gather_send, in_gather_recv,
    conv_own, conv_core, conv_recv, conv_sems,
    gate_own, gate_core, gate_recv, gate_sems,
    late_own, late_core, late_recv, late_sems,
):
    step = pl.program_id(0)
    chains = n_ref.shape[0]
    count = n_ref.shape[1]
    length = main_ref.shape[0]
    seqs = chains // heads
    total, width = whole_out.shape
    conv_cols = heads * QKV
    values = heads * DV
    in_cols = conv_cols + values
    place, core = lax.axis_index("seq"), lax.axis_index("batch")
    lag = jnp.minimum(places - 1 - place, chains - 1)
    me = lax.axis_index("head")
    own_rows = hidden_ref.shape[0]
    subs = own_rows // SUB
    group = places * cores
    shard = width // group
    pair = cores * shard
    flat = place * cores + core

    ring = Spread(whole_out, subs, me, gather_send, gather_recv)
    sums = Combine(sent, got, relay, me, sum_send, sum_recv, own_rows)
    in_ring = Spread(whole_in, subs, me, in_gather_send, in_gather_recv)
    in_sums = Combine(in_sent, in_got, in_relay, me, in_sum_send, in_sum_recv, SUB)
    conv_line = LineScatter(conv_own, conv_core, conv_recv, conv_sems)
    gate_line = LineScatter(gate_own, gate_core, gate_recv, gate_sems)
    late_line = LineScatter(late_own, late_core, late_recv, late_sems)

    def late_rows(d, at_core):
        return late_hbm.at[pl.ds(pl.multiple_of((d * cores + at_core) * shard, shard), shard)]

    def late_source(d):
        return late_rows(d, 1 - core)

    def late_load(d):
        return pltpu.make_async_copy(late_rows(d, core), late_own.at[d], late_sem.at[d])

    def hops(third):
        return range(third * (places - 1) // 3, (third + 1) * (places - 1) // 3)

    def far_first(i):
        return jnp.where(i % 2 == 0, places - 1 - i // 2, i // 2)

    def halves(grads):
        top, low = grads[:shard], grads[shard:]
        return jnp.where(core == 0, top, low), jnp.where(core == 0, low, top)
    out_store = Pieces(whole_out, out_hbm, total, subs, out_sem.at[0])
    in_store = Pieces(whole_in, igrad_hbm, total, subs, out_sem.at[1])
    own_x = Pieces(x_hbm, x_v, total, subs, x_sem)
    loads = [
        pltpu.make_async_copy(win_hbm, win_v.at[:, pl.ds(0, conv_cols)], in_sem.at[0]),
        pltpu.make_async_copy(wrates_hbm, win_v.at[:, pl.ds(conv_cols, PAD)], in_sem.at[1]),
        pltpu.make_async_copy(wog_hbm.at[:, pl.ds(0, values)], wog_v, in_sem.at[2]),
        pltpu.make_async_copy(nin_hbm, nin_v, in_sem.at[3]),
    ]

    def ffn_loads(k):
        return [
            pltpu.make_async_copy(
                ffnp_hbm.at[piece_rows(me ^ k, t, total, subs)], sent.at[k, pl.ds(t * SUB, SUB)],
                load_sem.at[k, t],
            )
            for t in range(subs)
        ]

    half = DV // 2

    def passed(chain, side):
        at = pl.ds(side * half, half)
        return along(
            "seq", send.at[chain, :, at], recv.at[chain, :, at], send_sem.at[chain, side],
            recv_sem.at[chain, side], jnp.maximum(place - 1, 0),
        )

    def returned(chain):
        return along(
            "seq", halo_send.at[chain], halo_recv.at[chain], halo_send_sem.at[chain],
            halo_recv_sem.at[chain], jnp.maximum(place - 1, 0),
        )

    @pl.when(step == 0)
    def _():
        for k in range(peers - 1, -1, -1):
            for load in ffn_loads(k):
                load.start()

        @pl.when(place == places - 1)
        def _():
            recv[...] = jnp.zeros_like(recv)
            halo_recv[...] = jnp.zeros_like(halo_recv)

        decay_scr[...] = jnp.zeros_like(decay_scr)
        o_gain_scr[...] = jnp.zeros_like(o_gain_scr)
        extras_v[...] = jnp.zeros_like(extras_v)
        for line in (conv_line, gate_line, late_line):
            line.clear()
        for d in range(places):
            late_load(d).start()
        for load in loads:
            load.start()
        own_x.start(me)
        call_group(me, peers, places, cores)

    @pl.when(step < chains)
    def _():
        gain = o_gain_ref[0:1]
        first = (step // heads) * length
        og_at = pl.ds(pl.multiple_of(conv_cols + (step % heads) * DV, DV), DV)
        state = jnp.zeros((DK, DV), f32)
        gain_total = jnp.zeros((1, DV), f32)
        for c in reversed(range(count)):
            at = pl.ds(c * CHUNK, CHUNK)
            mixed, og, dn = mixed_ref[at, :], og_ref[at, :], dn_ref[at, :]
            inverse = lax.rsqrt(jnp.mean(mixed * mixed, axis=1, keepdims=True) + epsilon)
            scaled = mixed * inverse
            sig = sigmoid(og)
            silu = og * sig
            through = dn * scaled
            gain_total = gain_total + jnp.sum(through * silu, axis=0, keepdims=True)
            dp_ref[pl.ds(pl.multiple_of(first + c * CHUNK, CHUNK), CHUNK), og_at] = (
                through * gain * sig * (1.0 + og * (1.0 - sig))
            ).astype(bf16)
            weighted = dn * gain * silu
            dmixed = inverse * (
                weighted - scaled * jnp.mean(weighted * scaled, axis=1, keepdims=True)
            )
            dmixed = dmixed.astype(bf16)
            do_scr[step, at, :] = dmixed
            decay = tot_ref[step, pl.ds(c, 1), 0:1]
            state = (
                decay * state - mm(n_ref[step, c], state, TN) + mm(qe_ref[step, c], dmixed, TN)
            )
        o_gain_scr[0:1, :] = o_gain_scr[0:1, :] + gain_total
        own_scr[step] = state

    @pl.when(step == 0)
    def _():
        meet_group(peers, places, cores)
        for k in range(peers - 1, 0, -1):
            for load in ffn_loads(k):
                load.wait()
            sums.start(k, 0)
        for load in ffn_loads(0):
            load.wait()
        for d in range(places):
            late_line.core_copy(d, late_source(d)).start()

    @pl.when(step >= chains)
    def _():
        chain = jnp.maximum(step - chains, 0)
        seq, head = chain // heads, chain % heads
        first = seq * length
        start = start_ref[seq]
        load_conv_input(main_ref, halo_ref, start, x_scr, place * length)
        conv = conv_ref[...]
        rows, cols = iotas(CHUNK)
        lower, upper, eye = rows >= cols, rows <= cols, rows == cols
        strict = rows > cols
        state = recv[chain].astype(f32)
        leaving = [None] * count
        for c in reversed(range(count)):
            leaving[c] = state
            state = (
                tot_ref[chain, pl.ds(c, 1), 0:1] * state
                - mm(n_ref[chain, c], state, TN)
                + mm(qe_ref[chain, c], do_scr[chain, pl.ds(c * CHUNK, CHUNK), :], TN)
            )
        g_scr[pl.ds(0, 8), :] = jnp.zeros((8, QKV), f32)
        g_scr[pl.ds(8 + length, 8), :] = jnp.zeros((8, QKV), f32)
        rate_total = jnp.zeros((1, 1), f32)
        bias_total = jnp.zeros((1, 1), f32)
        conv_total = [jnp.zeros((1, QKV), f32) for _ in range(CONV)]
        lanes = lax.broadcasted_iota(jnp.int32, (CHUNK, PAD), 1)
        for c in range(count):
            for t in range(seqs - 1):
                if c == count - 1:

                    @pl.when(step == chains + (t + 1) * heads)
                    def _():
                        in_sums.combine(t)

            at = pl.ds(c * CHUNK, CHUNK)
            q, k, v = qkv_ref[at, 0:DK], qkv_ref[at, DK : 2 * DK], qkv_ref[at, 2 * DK :]
            kf, vf = k.astype(f32), v.astype(f32)
            log_gate, strength, rate, logit = gates(rate_ref[at, :], decay_ref, head)
            column, total, ratio = decays(log_gate, lower, upper, eye)
            growth = jnp.exp(column)
            remain = jnp.exp(total - column)
            whole = jnp.exp(total)
            inverse = inv_ref[0, c]
            s0 = s_ref[0, c]
            do = do_scr[chain, at, :]
            grad_state = leaving[c]
            low_grad_state = grad_state.astype(bf16)
            kq = jnp.concatenate([k, q], axis=0)
            products = mm(kq, k, NT)
            kk, qk = products[:CHUNK], products[CHUNK:]
            reads = mm(kq, s0)
            ks, qs = reads[:CHUNK], reads[CHUNK:]
            fresh = vf - growth * ks
            pseudo = mm(inverse, strength * fresh).astype(bf16)
            scores = (ratio * qk).astype(bf16)
            dpseudo = mm(scores, do, TN) + mm(remain * kf, low_grad_state)
            dtarget = mm(inverse, dpseudo, TN)
            low_dtarget = dtarget.astype(bf16)
            dstrength = jnp.sum(dtarget * fresh, axis=1, keepdims=True)
            dlog = -(strength * growth) * jnp.sum(dtarget * ks, axis=1, keepdims=True)
            dv = strength * dtarget
            both = jnp.concatenate([low_dtarget, do], axis=0)
            outer = mm(both, pseudo, NT)
            dcoupling = jnp.where(strict, -outer[:CHUNK] * ratio, 0.0)
            by_strength = dcoupling * kk
            dstrength = dstrength + jnp.sum(by_strength, axis=1, keepdims=True)
            exponent = strength * by_strength
            dqk_f = jnp.where(lower, outer[CHUNK:] * ratio, 0.0)
            exponent = exponent + dqk_f * qk
            pair = jnp.concatenate([(dcoupling * strength).astype(bf16), dqk_f.astype(bf16)], axis=0)
            back = mm(both, s0, NT)
            wide = mm(pair, k)
            dq = growth * back[CHUNK:] + wide[CHUNK:]
            dkept = mm(pseudo, low_grad_state, NT)
            dk = (
                wide[:CHUNK]
                - (strength * growth) * back[:CHUNK]
                + mm(pair, kq, TN)
                + remain * dkept
            )
            dlog = dlog + growth * jnp.sum(do.astype(f32) * qs, axis=1, keepdims=True)
            from_kept = remain * jnp.sum(kf * dkept, axis=1, keepdims=True)
            dlog = dlog - from_kept + jnp.sum(exponent, axis=1, keepdims=True)
            dlog_row = to_row(dlog, eye) - jnp.sum(exponent, axis=0, keepdims=True)
            tail = jnp.sum(from_kept, axis=0, keepdims=True) + whole * jnp.sum(
                jnp.sum(grad_state * s0.astype(f32), axis=1, keepdims=True), axis=0, keepdims=True
            )
            dgate = jnp.sum(jnp.where(upper, dlog_row, 0.0), axis=1, keepdims=True) + tail
            slope = sigmoid(logit)
            drate0 = -rate * slope * dgate
            drate1 = dstrength * strength * (1.0 - strength)
            rate_total = rate_total + jnp.sum(dgate * log_gate, axis=0, keepdims=True)
            bias_total = bias_total + jnp.sum(drate0, axis=0, keepdims=True)
            here = pl.ds(pl.multiple_of(first + c * CHUNK, CHUNK), CHUNK)
            others = jnp.where(head == 0, 0.0, dp_ref[here, in_cols:].astype(f32))
            dp_ref[here, in_cols:] = jnp.where(
                lanes == 2 * head, drate0, jnp.where(lanes == 2 * head + 1, drate1, others)
            ).astype(bf16)
            convolved = convolve(x_scr, conv, c * CHUNK)
            sig = sigmoid(convolved)
            active = convolved * sig
            slope_conv = sig * (1.0 + convolved * (1.0 - sig))

            def unit_grad(rows_in, grad):
                inv_norm = lax.rsqrt(jnp.sum(rows_in * rows_in, axis=1, keepdims=True) + epsilon)
                y = rows_in * inv_norm
                return inv_norm * (grad - y * jnp.sum(y * grad, axis=1, keepdims=True))

            dq = dq.astype(bf16).astype(f32) * DK ** (-0.5)
            dk = dk.astype(bf16).astype(f32)
            dv = dv.astype(bf16).astype(f32)
            dconv = (
                jnp.concatenate(
                    [unit_grad(active[:, :DK], dq), unit_grad(active[:, DK : 2 * DK], dk), dv],
                    axis=1,
                )
                * slope_conv
            )
            g_scr[pl.ds(8 + c * CHUNK, CHUNK), :] = dconv
            for j in range(CONV):
                shifted_in = x_scr[pl.ds(c * CHUNK + HALO - CONV + 1 + j, CHUNK), :]
                conv_total[j] = conv_total[j] + jnp.sum(dconv * shifted_in, axis=0, keepdims=True)
        for j in range(CONV):
            tap = pl.ds(j * heads + head, 1)
            conv_scr[tap, :] = conv_total[j] + jnp.where(seq == 0, 0.0, conv_scr[tap, :])
        spots = lax.broadcasted_iota(jnp.int32, decay_scr.shape, 1)
        top = lax.broadcasted_iota(jnp.int32, decay_scr.shape, 0) == 0
        decay_scr[...] = decay_scr[...] + jnp.where(
            top & (spots == 2 * heads + head), rate_total, 0.0
        ) + jnp.where(top & (spots == 3 * heads + head), bias_total, 0.0)

        def conv_back(at, size):
            grad = g_scr[pl.ds(at + CONV - 1, size), :] * conv[0:1]
            for j in range(1, CONV):
                grad = grad + g_scr[pl.ds(at + CONV - 1 - j, size), :] * conv[j : j + 1]
            return grad

        halo_send[chain] = conv_back(0, 8)

        @pl.when(place > 0)
        def _():
            returned(chain).start()

        conv_at = pl.ds(pl.multiple_of(head * QKV, QKV), QKV)
        for c in range(count):
            grad = conv_back(8 + c * CHUNK, CHUNK)
            positions = place * length + c * CHUNK + lax.broadcasted_iota(
                jnp.int32, (CHUNK, 1), 0
            )
            live = (positions >= start).astype(f32)
            if c == count - 1:
                tail_scr[chain] = grad[CHUNK - HALO :]
            dp_ref[pl.ds(pl.multiple_of(first + c * CHUNK, CHUNK), CHUNK), conv_at] = (
                grad * live
            ).astype(bf16)

    @pl.when(step == chains - 1)
    def _():
        loads[3].wait()

        def gate_grads(i, carry):
            d = far_first(i)
            rows = pl.ds(pl.multiple_of(d * pair, pair), pair)
            mine, others = halves(mm(nin_v[rows, :], dp_ref[:, conv_cols:in_cols]))
            gate_own[d] = mine.astype(bf16)
            gate_source[d] = others.astype(bf16)
            gate_line.core_copy(d, gate_source.at[d]).start()
            return carry

        lax.fori_loop(0, places, gate_grads, 0)
        for d in range(places):
            late_load(d).wait()
            late_line.add_core(d, late_source(d))

    relayed = step - lag

    @pl.when((relayed >= 0) & (relayed < chains))
    def _():
        chain = jnp.clip(relayed, 0, chains - 1)
        for side in range(2):
            at = slice(side * half, (side + 1) * half)

            @pl.when(place < places - 1)
            def _():
                passed(chain, side).wait_recv()

            @pl.when(place > 0)
            def _():
                earlier = mm(trans_ref[chain], recv[chain, :, at], TN) + own_scr[chain, :, at]
                send[chain, :, at] = earlier.astype(bf16)
                passed(chain, side).start()

    @pl.when(step == chains - 1)
    def _():
        sums.combine(0)

    @pl.when(step == chains)
    def _():
        for kind in range(2, 6):
            sums.copy(kind, 0).wait_recv()
        for t in range(subs):
            rows = pl.ds(t * SUB, SUB)
            ring.put(t, (hidden_ref[rows, :] + sums.total(rows)).astype(bf16))
            ring.start(t)
        out_store.start(me)

    @pl.when(step == chains + 2)
    def _():
        for t in range(subs):
            ring.forward(t)

    for third, at_step in enumerate((chains - 1, chains + 1, 2 * chains - 1)):

        @pl.when(step == at_step)
        def _():
            for hop in hops(third):
                late_line.advance(hop)

    for third, at_step in enumerate((chains, chains + 1, chains + 2)):

        @pl.when(step == at_step)
        def _():
            if third == 0:
                for d in range(places):
                    gate_line.add_core(d, gate_source.at[d])
            for hop in hops(third):
                gate_line.advance(hop)

    def mend_ends(seq):
        for head in range(heads):
            chain = seq * heads + head

            @pl.when(place < places - 1)
            def _():
                returned(chain).wait_recv()

            positions = (place + 1) * length - HALO + lax.broadcasted_iota(
                jnp.int32, (HALO, 1), 0
            )
            live = (positions >= start_ref[seq]).astype(f32)
            grad = tail_scr[chain] + jnp.concatenate(
                [jnp.zeros((HALO - 8, QKV), f32), halo_recv[chain]], axis=0
            )
            dp_ref[pl.ds((seq + 1) * length - HALO, HALO), pl.ds(head * QKV, QKV)] = (
                grad * live
            ).astype(bf16)

    def project(t):
        def one(i, carry):
            k = jnp.where(i == 0, peers - 1, lax.rem(i, peers - 1))
            rows = piece_rows(me ^ k, t, total, subs)
            partial = mm(dp_ref[rows, 0:conv_cols], win_v[:, 0:conv_cols], NT)
            partial = partial + mm(dp_ref[rows, conv_cols:in_cols], wog_v[...], NT)
            partial = partial + mm(dp_ref[rows, in_cols:], win_v[:, conv_cols:], NT)
            in_sent[k, pl.ds(t * SUB, SUB), :] = partial.astype(bf16)

            for kk in range(1, peers):

                @pl.when(k == kk)
                def _():
                    in_sums.start(kk, t)

            return carry

        lax.fori_loop(0, peers, one, 0)

    for t in range(seqs - 1):

        @pl.when(step == chains + (t + 1) * heads - 1)
        def _():
            mend_ends(t)
            if t == 0:
                for load in loads[:3]:
                    load.wait()
            project(t)

    def own_input_grads(t):
        rows = pl.ds(t * SUB, SUB)
        din = in_sums.collect(t)
        x = x_v[rows, :].astype(f32)
        inverse = lax.rsqrt(jnp.mean(x * x, axis=1, keepdims=True) + epsilon)
        scaled = x * inverse
        weighted = din * gain_ref[...]
        grad = hgrad_ref[rows, :] + inverse * (
            weighted - scaled * jnp.mean(weighted * scaled, axis=1, keepdims=True)
        )
        in_ring.put(t, grad.astype(bf16))
        in_ring.start(t)
        return jnp.sum(din * scaled, axis=0, keepdims=True)

    @pl.when(step == 2 * chains - 1)
    def _():
        own_x.wait(me)
        gain_part = jnp.zeros((1, width), f32)
        for t in range(seqs - 1):
            gain_part = gain_part + own_input_grads(t)
        mend_ends(seqs - 1)
        taps = CONV * heads
        per = QKV // group
        lanes = lax.broadcasted_iota(jnp.int32, (taps, PAD), 1)
        for q in range(group):
            at = per * q // PAD * PAD
            shift = (PAD // 2 - per * q) % PAD
            moved = conv_scr[:, at : at + PAD]
            if shift:
                moved = pltpu.roll(moved, shift, 1)
            kept = jnp.where((lanes >= PAD // 2) & (lanes < PAD // 2 + per), moved, 0.0)
            extras_v[q * shard : q * shard + taps, :] = kept + decay_scr[...]
        if seqs == 1:
            for load in loads[:3]:
                load.wait()

        def place_grads(i, carry):
            d = far_first(i)
            rows = pl.ds(pl.multiple_of(d * pair, pair), pair)
            mine, others = halves(mm(nin_v[rows, :], dp_ref[:, 0:conv_cols]))
            conv_own[d, :, 0:conv_cols] = mine.astype(bf16)
            conv_source[d, :, 0:conv_cols] = others.astype(bf16)
            mine, others = halves(mm(nin_v[rows, :], dp_ref[:, in_cols:]) + extras_v[rows, :])
            conv_own[d, :, conv_cols:] = mine.astype(bf16)
            conv_source[d, :, conv_cols:] = others.astype(bf16)
            conv_line.core_copy(d, conv_source.at[d]).start()

            @pl.when(i > 0)
            def _():
                before = far_first(jnp.maximum(i - 1, 0))
                conv_line.add_core(before, conv_source.at[before])

            return carry

        first_places = min(2, places)
        lax.fori_loop(0, first_places, place_grads, 0)
        project(seqs - 1)
        lax.fori_loop(first_places, places, place_grads, 0)
        before = far_first(places - 1)
        conv_line.add_core(before, conv_source.at[before])
        for hop in hops(0):
            conv_line.advance(hop)
        in_sums.combine(seqs - 1)
        gain_part = gain_part + own_input_grads(seqs - 1)
        lane_rows = width // 128
        gains_v[...] = jnp.zeros_like(gains_v)
        for r in range(lane_rows):
            gains_v[r : r + 1, :] = gain_part[:, r * 128 : (r + 1) * 128]
            gains_v[lane_rows + r : lane_rows + r + 1, :] = ffn_gain_ref[
                0:1, r * 128 : (r + 1) * 128
            ]
        for r in range(DV // 128):
            gains_v[2 * lane_rows + r : 2 * lane_rows + r + 1, :] = o_gain_scr[
                0:1, r * 128 : (r + 1) * 128
            ]

        def gains_copy(k):
            return head_copy(gains_v, gains_recv.at[k], hs.at[k], hr.at[k], me ^ k)

        def to_group(d):
            to = lax.rem(flat + d, group)
            return pltpu.make_async_remote_copy(
                src_ref=gains_sum, dst_ref=gains_all.at[d], send_sem=gs.at[d], recv_sem=gr.at[d],
                device_id={"seq": to // cores, "batch": lax.rem(to, cores)}, device_id_type=MESH,
            )

        for k in range(1, peers):
            gains_copy(k).start()
        for hop in hops(1):
            conv_line.advance(hop)
        in_store.start(me)
        for t in range(subs):
            ring.finish(t)
        for k in range(1, peers):
            out_store.start(me ^ k)
        gathered = gains_v[...]
        for k in range(1, peers):
            gains_copy(k).wait_recv()
            gathered = gathered + gains_recv[k]
        gains_sum[...] = gathered
        for d in range(1, group):
            to_group(d).start()
        for t in range(subs):
            in_ring.forward(t)
        for hop in hops(2):
            conv_line.advance(hop)
        in_store.start(me ^ 1)
        in_store.start(me ^ 2)
        for d in range(1, group):
            to_group(d).wait_recv()
            gathered = gathered + gains_all[d]
        gains_out[...] = gathered
        for t in range(subs):
            in_ring.finish(t)
        in_store.start(me ^ 3)
        late_out[...] = late_line.finish()
        grad = gate_line.finish()
        for head in range(heads):
            at = head * (QKV + DV) + QKV
            grad_out[:, at : at + DV] = grad[:, head * DV : (head + 1) * DV]
        grad = conv_line.finish()
        for head in range(heads):
            at = head * (QKV + DV)
            grad_out[:, at : at + QKV] = grad[:, head * QKV : (head + 1) * QKV]
        small_out[...] = grad[:, conv_cols:]
        for k in range(peers):
            out_store.wait(k)
            in_store.wait(k)

        @pl.when(place > 0)
        def _():
            for chain in range(chains):
                returned(chain).wait_send()
                for side in range(2):
                    passed(chain, side).wait_send()

        sums.drain(0)
        for t in range(subs):
            ring.drain(t)
            in_ring.drain(t)
            in_sums.drain(t)
        for k in range(1, peers):
            gains_copy(k).wait_send()
        for d in range(1, group):
            to_group(d).wait_send()
        conv_line.drain(lambda d: conv_source.at[d])
        gate_line.drain(lambda d: gate_source.at[d])
        late_line.drain(late_source)


def backward_rule(
    starts, decay_par, dn, mixed, og, projected, rates, o_gain, n, qe, tot, trans, qkv, inv, states, halo,
    conv_w, hidden, hidden_grad, gain, ffn_gain_part, ffn_part, in_full, gate_full,
    rates_full, turned, x, late_grads, heads,
):
    places, peers, cores = lax.axis_size("seq"), lax.axis_size("head"), lax.axis_size("batch")
    chains, count = n.shape[:2]
    seqs = chains // heads
    rows = projected.shape[0]
    length = rows // seqs
    width = hidden.shape[1]
    own_rows = hidden.shape[0]
    subs = own_rows // SUB
    values = heads * DV
    cols = heads * (QKV + DV) + PAD
    group = places * cores
    shard = width // group
    gain_rows = 3 * width // 128
    row = lambda first: lambda i: (i // heads, first + i % heads)
    whole = lambda *dims: pl.BlockSpec(dims, lambda j: (0,) * len(dims))
    chain4 = lambda i: (i, 0, 0, 0)
    shape = jax.ShapeDtypeStruct
    per_chain = pltpu.SemaphoreType.DMA((chains,))
    per_peer = pltpu.SemaphoreType.DMA((peers,))
    per_member = pltpu.SemaphoreType.DMA((group,))
    pieces = pltpu.SemaphoreType.DMA((peers, subs))
    ffn_sums = sum_buffers(own_rows, width, subs)
    ffn_sums[3:5] = [pltpu.SemaphoreType.DMA((6, 1))] * 2
    return pl.pallas_call(
        functools.partial(backward_kernel, heads, places, peers, cores),
        grid=(2 * chains,),
        in_specs=[
            smem(),
            smem(),
            pl.BlockSpec((length, DV), early(chains, row(0))),
            pl.BlockSpec((length, DV), early(chains, row(0))),
            pl.BlockSpec((length, DV), early(chains, row(0))),
            whole(1, DV),
            whole(chains, count, DK, DK),
            whole(chains, count, CHUNK, DK),
            whole(chains, count, DK),
            whole(chains, DK, DK),
            pl.BlockSpec((length, QKV), late(chains, row(0))),
            pl.BlockSpec((1, count, CHUNK, CHUNK), late(chains, chain4)),
            pl.BlockSpec((1, count, DK, DV), late(chains, chain4)),
            pl.BlockSpec((length, QKV), late(chains, row(0))),
            pl.BlockSpec((1, HALO, QKV), late(chains, lambda i: (i // heads, 0, i % heads))),
            pl.BlockSpec((length, PAD), late(chains, lambda i: (i // heads, 0))),
            pl.BlockSpec((CONV, QKV), late(chains, lambda i: (0, i % heads))),
            whole(own_rows, width),
            whole(own_rows, width),
            whole(1, width),
            whole(8, width),
        ]
        + [anywhere()] * 7,
        out_specs=[
            anywhere(),
            anywhere(),
            whole(gain_rows, 128),
            whole(shard, cols - PAD),
            whole(shard, PAD),
            whole(shard, late_grads.shape[1]),
        ],
        out_shape=[
            shape((rows, width), bf16),
            shape((rows, width), bf16),
            shape((gain_rows, 128), f32),
            shape((shard, cols - PAD), f32),
            shape((shard, PAD), f32),
            shape((shard, late_grads.shape[1]), f32),
        ],
        scratch_shapes=[
            pltpu.VMEM((rows, cols), bf16),
            pltpu.VMEM((HALO + length, QKV), f32),
            pltpu.VMEM((16 + length, QKV), f32),
            pltpu.VMEM((chains, length, DV), bf16),
            pltpu.VMEM((chains, DK, DV), f32),
            pltpu.VMEM((chains, DK, DV), bf16),
            pltpu.VMEM((chains, DK, DV), bf16),
            pltpu.VMEM((chains, HALO, QKV), f32),
            pltpu.VMEM((chains, 8, QKV), f32),
            pltpu.VMEM((chains, 8, QKV), f32),
            pltpu.VMEM((CONV * heads, QKV), f32),
            pltpu.VMEM((CONV * heads, PAD), f32),
            pltpu.VMEM((8, DV), f32),
            pltpu.VMEM((rows, width), bf16),
            pltpu.VMEM((rows, width), bf16),
            pltpu.VMEM((width, cols - values), bf16),
            pltpu.VMEM((width, values), bf16),
            pltpu.VMEM((width, rows), bf16),
            pltpu.VMEM((own_rows, width), bf16),
            pltpu.VMEM((places, shard, cols - values), bf16),
            pltpu.VMEM((places, shard, values), bf16),
            pltpu.VMEM((width, PAD), f32),
            pltpu.VMEM((gain_rows, 128), f32),
            pltpu.VMEM((peers, gain_rows, 128), f32),
            pltpu.VMEM((gain_rows, 128), f32),
            pltpu.VMEM((group, gain_rows, 128), f32),
            pltpu.SemaphoreType.DMA((chains, 2)),
            pltpu.SemaphoreType.DMA((chains, 2)),
            per_chain, per_chain,
            pieces,
            pltpu.SemaphoreType.DMA((4,)),
            pltpu.SemaphoreType.DMA((places,)),
            pieces,
            pltpu.SemaphoreType.DMA((2, peers, subs)),
            per_peer, per_peer, per_member, per_member,
        ]
        + ffn_sums
        + sum_buffers(own_rows, width, subs)
        + line_buffers(places, shard, cols - values)
        + line_buffers(places, shard, values)
        + line_buffers(places, shard, late_grads.shape[1]),
        compiler_params=pltpu.CompilerParams(
            dimension_semantics=("arbitrary",), collective_id=4, has_side_effects=True,
            vmem_limit_bytes=62 * 2**20,
        ),
        name="backward_rule",
    )(
        starts, decay_par, dn, mixed, og, o_gain, n, qe, tot, trans, qkv, inv, states, projected,
        halo, rates, conv_w, hidden, hidden_grad, gain, ffn_gain_part, ffn_part, in_full,
        gate_full, rates_full, turned, x, late_grads,
    )


def smem():
    return pl.BlockSpec(memory_space=pltpu.SMEM)


def rows_of(t):
    return pl.ds(pl.multiple_of(t * SUB, SUB), SUB)


def block_store(i, size, source, target, sem):
    return pltpu.make_async_copy(
        part(source, i * size, size), part(target, i * size, size), sem.at[i]
    )


def mixer_kernel(
    peers, nin_hbm, mixed_hbm, weights_hbm, x_hbm, gain_ref, o_gain_ref,
    og_hbm, normed_hbm, nm_hbm, turned_hbm, hidden_ref,
    nin, turned, mixed, weights, x_v, og_v, normed_v, nm, in_sem, x_sem, out_sem,
    send, recv, relay, sum_send, sum_recv, gather_send, gather_recv,
):
    me = lax.axis_index("head")
    total, width = nm.shape
    values = mixed.shape[1]
    own_rows = total // peers
    subs = own_rows // SUB
    loads = [
        pltpu.make_async_copy(weights_hbm, weights, in_sem.at[0]),
        pltpu.make_async_copy(nin_hbm, nin, in_sem.at[1]),
        pltpu.make_async_copy(mixed_hbm, mixed, in_sem.at[2]),
    ]
    for load in loads:
        load.start()
    own_x = Pieces(x_hbm, x_v, total, subs, x_sem)
    own_x.start(me)
    stores = [
        Pieces(source, target, total, subs, out_sem.at[i])
        for i, (source, target) in enumerate(
            ((og_v, og_hbm), (normed_v, normed_hbm), (nm, nm_hbm))
        )
    ]
    greet_heads(me, peers)
    for load in loads:
        load.wait()
    sums = Combine(send, recv, relay, me, sum_send, sum_recv, SUB)

    def project(i, carry):
        k = jnp.where(i == 0, peers - 1, lax.rem(i, peers - 1))
        owner = me ^ k
        og = mm(take(nin, owner, subs), weights[:, 0:values])
        gated = og * sigmoid(og)
        own = take(mixed, owner, subs)
        normed = []
        for first in range(0, values, DV):
            at = slice(first, first + DV)
            inverse = lax.rsqrt(
                jnp.mean(own[:, at] * own[:, at], axis=1, keepdims=True) + epsilon
            )
            normed.append((own[:, at] * inverse * o_gain_ref[0:1] * gated[:, at]).astype(bf16))
        normed = jnp.concatenate(normed, axis=1)
        send[k] = mm(normed, weights[:, values:], NT).astype(bf16)
        for t in range(subs):
            rows = piece_rows(owner, t, total, subs)
            og_v[rows, :] = og[t * SUB : (t + 1) * SUB]
            normed_v[rows, :] = normed[t * SUB : (t + 1) * SUB]

        for kk in range(1, peers):

            @pl.when(k == kk)
            def _():
                for t in range(subs):
                    sums.start(kk, t)

        stores[0].start(owner)
        stores[1].start(owner)
        return carry

    lax.fori_loop(0, peers, project, 0)
    tile = 256
    for first in range(0, width, tile):
        turned[first : first + tile, :] = nin[:, first : first + tile].T
    for t in range(subs):
        sums.combine(t)
    turned_store = pltpu.make_async_copy(turned, turned_hbm, in_sem.at[3])
    turned_store.start()
    own_x.wait(me)
    gain = gain_ref[...]
    ring = Spread(nm, subs, me, gather_send, gather_recv)
    for t in range(subs):
        rows = rows_of(t)
        hidden = x_v[rows, :].astype(f32) + sums.collect(t)
        hidden_ref[rows, :] = hidden
        inverse = lax.rsqrt(jnp.mean(hidden * hidden, axis=1, keepdims=True) + epsilon)
        ring.put(t, (hidden * inverse * gain).astype(bf16))
        ring.start(t)
    for t in range(subs):
        ring.forward(t)
    for k in range(peers):
        if k == peers - 1:
            for t in range(subs):
                ring.finish(t)
        stores[2].start(me ^ k)
    turned_store.wait()
    for i in range(peers):
        for store in stores:
            store.wait(i)
    for t in range(subs):
        sums.drain(t)
        ring.drain(t)


def mixer(nin, mixed, weights, x, gain, o_gain):
    peers = lax.axis_size("head")
    total, width = x.shape
    values = mixed.shape[1]
    own_rows = total // peers
    subs = own_rows // SUB
    shape = in_hbm
    return pl.pallas_call(
        functools.partial(mixer_kernel, peers),
        in_specs=[anywhere()] * 4 + [vmem()] * 2,
        out_specs=[anywhere()] * 4 + [vmem()],
        out_shape=[
            shape((total, values), f32),
            shape((total, values), bf16),
            shape((total, width), bf16),
            shape((width, total), bf16),
            shape((own_rows, width), f32),
        ],
        scratch_shapes=[
            pltpu.VMEM((total, width), bf16),
            pltpu.VMEM((width, total), bf16),
            pltpu.VMEM((total, values), f32),
            pltpu.VMEM((width, 2 * values), bf16),
            pltpu.VMEM((own_rows, width), bf16),
            pltpu.VMEM((total, values), f32),
            pltpu.VMEM((total, values), bf16),
            pltpu.VMEM((total, width), bf16),
            pltpu.SemaphoreType.DMA((4,)),
            pltpu.SemaphoreType.DMA((peers, subs)),
            pltpu.SemaphoreType.DMA((3, peers, subs)),
        ]
        + sum_buffers(own_rows, width, subs),
        compiler_params=pltpu.CompilerParams(
            collective_id=1, has_side_effects=True, vmem_limit_bytes=62 * 2**20
        ),
        name="mixer",
    )(nin, mixed, weights, x, gain, o_gain)


def ffn_kernel(
    peers, places, cores, nm_hbm, ffn_hbm, ct_hbm, normed_hbm, weights_hbm, hidden_ref, gain_ref,
    grads_hbm, ffnp_hbm, ng_hbm, hgrad_ref, gpart_ref, down_ref,
    nm_b, ct_b, dgu_b, nm, ffn_v, ends_v, ct_v, normed_v, wout_v, act, dgu, dm, ffnp_v, grads_v, down_v, ng_v,
    in_sem, out_sem, ng_sem, send, recv, relay, sum_send, sum_recv, gather_send, gather_recv,
    core_recv, seq_send, seq_recv, scatter_sems,
):
    me = lax.axis_index("head")
    total, width = nm.shape
    values = normed_v.shape[1]
    own_rows = total // peers
    subs = own_rows // SUB
    cells = act.shape[1]
    tile = 256
    whole_cells = cells - PAD
    loads = [
        pltpu.make_async_copy(
            ffn_hbm.at[:, pl.ds(p * whole_cells, whole_cells)],
            ffn_v.at[:, pl.ds(p * cells, whole_cells)], in_sem.at[5 + p],
        )
        for p in range(3)
    ] + [
        pltpu.make_async_copy(
            ffn_hbm.at[:, pl.ds(3 * whole_cells, PAD)], ends_v, in_sem.at[0]
        ),
        pltpu.make_async_copy(
            ffn_hbm.at[:, pl.ds(3 * whole_cells + PAD, PAD)],
            ffn_v.at[:, pl.ds(3 * cells - PAD, PAD)], in_sem.at[8],
        ),
        pltpu.make_async_copy(nm_hbm, nm, in_sem.at[1]),
        pltpu.make_async_copy(ct_hbm, ct_v, in_sem.at[2]),
        pltpu.make_async_copy(normed_hbm, normed_v, in_sem.at[3]),
        pltpu.make_async_copy(weights_hbm.at[:, pl.ds(values, values)], wout_v, in_sem.at[4]),
    ]
    for load in loads:
        load.start()
    greet_group(me, peers, places, cores)
    for load in loads[:7]:
        load.wait()
    low = lax.broadcasted_iota(jnp.int32, ends_v.shape, 1) < PAD // 2
    ends = ends_v[...].astype(f32)
    ffn_v[:, whole_cells:cells] = jnp.where(low, ends, 0.0).astype(bf16)
    ffn_v[:, cells + whole_cells : 2 * cells] = jnp.where(
        low, pltpu.roll(ends, PAD // 2, 1), 0.0
    ).astype(bf16)
    gain = gain_ref[...]
    sums = Combine(send, recv, relay, me, sum_send, sum_recv, SUB)

    def feed_forward(i, carry):
        k = jnp.where(i == 0, peers - 1, lax.rem(i, peers - 1))
        owner = me ^ k
        nm_b[...] = take(nm, owner, subs)
        ct_b[...] = take(ct_v, owner, subs)

        def cell_tile(j, carry):
            at = pl.ds(pl.multiple_of(j * tile, tile), tile)
            at_up = pl.ds(pl.multiple_of(cells + j * tile, tile), tile)
            at_down = pl.ds(pl.multiple_of(2 * cells + j * tile, tile), tile)
            gate = mm(nm_b[...], ffn_v[:, at])
            up = mm(nm_b[...], ffn_v[:, at_up])
            dact = mm(ct_b[...], ffn_v[:, at_down])
            sig = sigmoid(gate)
            silu = gate * sig
            activated = (silu * up).astype(bf16)
            dgu_b[:, at] = (dact * up * sig * (1.0 + gate * (1.0 - sig))).astype(bf16)
            dgu_b[:, at_up] = (dact * silu).astype(bf16)
            for t in range(subs):
                act[piece_rows(owner, t, total, subs), at] = activated[t * SUB : (t + 1) * SUB]
            return carry

        lax.fori_loop(0, cells // tile, cell_tile, 0)

        def mid_tile(j, carry):
            at = pl.ds(pl.multiple_of(j * tile, tile), tile)
            send[k, :, at] = mm(dgu_b[...], ffn_v[at, 0 : 2 * cells], NT).astype(bf16)
            return carry

        lax.fori_loop(0, width // tile, mid_tile, 0)
        for t in range(subs):
            dgu[piece_rows(owner, t, total, subs), :] = dgu_b[rows_of(t), :]

        for kk in range(1, peers):

            @pl.when(k == kk)
            def _():
                for t in range(subs):
                    sums.start(kk, t)

        @pl.when(k == 2)
        def _():
            for t in range(subs):
                sums.combine(t)

        return carry

    lax.fori_loop(0, peers, feed_forward, 0)

    def down_grads(i, carry):
        at = pl.ds(pl.multiple_of(i * tile, tile), tile)
        down_v[at, :] = mm(ct_v[:, at], act[...], TN).astype(bf16)
        return carry

    lax.fori_loop(0, width // tile, down_grads, 0)
    scatter = GroupScatter(down_v, pl.ds(0, cells), core_recv, seq_send, seq_recv, scatter_sems)
    for k in range(places - 1, -1, -1):
        scatter.core_copy(k).start()

    def cell_grads(i, carry):
        at = pl.ds(pl.multiple_of(i * tile, tile), tile)
        grads_v[at, 0 : 2 * cells] = mm(nm[:, at], dgu[...], TN).astype(bf16)
        return carry

    half = width // tile // 2
    lax.fori_loop(0, half, cell_grads, 0)
    for k in range(places - 1, -1, -1):
        scatter.pass_on(k)
    lax.fori_loop(half, width // tile, cell_grads, 0)
    ring = Spread(dm, subs, me, gather_send, gather_recv)
    gain_part = jnp.zeros((1, width), f32)
    for t in range(subs):
        rows = rows_of(t)
        dmid = sums.collect(t)
        hidden = hidden_ref[rows, :]
        inverse = lax.rsqrt(jnp.mean(hidden * hidden, axis=1, keepdims=True) + epsilon)
        scaled = hidden * inverse
        weighted = dmid * gain
        grad = ct_v[piece_rows(me, t, total, subs), :].astype(f32) + inverse * (
            weighted - scaled * jnp.mean(weighted * scaled, axis=1, keepdims=True)
        )
        hgrad_ref[rows, :] = grad
        ring.put(t, grad.astype(bf16))
        ring.start(t)
        gain_part = gain_part + jnp.sum(dmid * scaled, axis=0, keepdims=True)
    gpart_ref[...] = jnp.broadcast_to(gain_part, gpart_ref.shape)

    def ffn_rows(i, carry):
        rows = pl.ds(pl.multiple_of(i * own_rows, own_rows), own_rows)
        ffnp_v[rows, :] = mm(act[rows, :], ffn_v[:, 2 * cells :], NT).astype(bf16)
        block_store(i, own_rows, ffnp_v, ffnp_hbm, out_sem.at[0]).start()
        return carry

    lax.fori_loop(0, peers, ffn_rows, 0)
    loads[7].wait()
    loads[8].wait()
    for t in range(subs):
        ring.forward(t)
    down_ref[...] = scatter.finish()

    ng_store = Pieces(ng_v, ng_hbm, total, subs, ng_sem)

    def norm_rows(k, carry):
        owner = me ^ k

        @pl.when(k == peers - 1)
        def _():
            for t in range(subs):
                ring.finish(t)

        grads = mm(take(dm, owner, subs), wout_v[...])
        for t in range(subs):
            ng_v[piece_rows(owner, t, total, subs), :] = grads[t * SUB : (t + 1) * SUB]
        ng_store.start(owner)
        return carry

    lax.fori_loop(0, peers, norm_rows, 0)

    def out_grads(i, carry):
        at = pl.ds(pl.multiple_of(i * tile, tile), tile)
        grads_v[at, 2 * cells :] = mm(dm[:, at], normed_v[...], TN).astype(bf16)
        block_store(i, tile, grads_v, grads_hbm, out_sem.at[1]).start()
        return carry

    lax.fori_loop(0, width // tile, out_grads, 0)
    for i in range(peers):
        block_store(i, own_rows, ffnp_v, ffnp_hbm, out_sem.at[0]).wait()
        ng_store.wait(i)
    for i in range(width // tile):
        block_store(i, tile, grads_v, grads_hbm, out_sem.at[1]).wait()
    for t in range(subs):
        sums.drain(t)
        ring.drain(t)
    scatter.drain()


def feed_forward_block(nm, ffn_full, ct, normed, weights, hidden, gain, cells):
    peers, places, cores = lax.axis_size("head"), lax.axis_size("seq"), lax.axis_size("batch")
    total, width = ct.shape
    own_rows = total // peers
    subs = own_rows // SUB
    values = normed.shape[1]
    shard = width // (places * cores)
    shape = in_hbm
    return pl.pallas_call(
        functools.partial(ffn_kernel, peers, places, cores),
        in_specs=[anywhere()] * 5 + [vmem()] * 2,
        out_specs=[anywhere()] * 3 + [vmem()] * 3,
        out_shape=[
            shape((width, 2 * cells + values), bf16),
            shape((total, width), bf16),
            shape((total, values), f32),
            shape((own_rows, width), f32),
            shape((8, width), f32),
            shape((shard, cells), f32),
        ],
        scratch_shapes=[
            pltpu.VMEM((own_rows, width), bf16),
            pltpu.VMEM((own_rows, width), bf16),
            pltpu.VMEM((own_rows, 2 * cells), bf16),
            pltpu.VMEM((total, width), bf16),
            pltpu.VMEM((width, 3 * cells), bf16),
            pltpu.VMEM((width, PAD), bf16),
            pltpu.VMEM((total, width), bf16),
            pltpu.VMEM((total, values), bf16),
            pltpu.VMEM((width, values), bf16),
            pltpu.VMEM((total, cells), bf16),
            pltpu.VMEM((total, 2 * cells), bf16),
            pltpu.VMEM((total, width), bf16),
            pltpu.VMEM((total, width), bf16),
            pltpu.VMEM((width, 2 * cells + values), bf16),
            pltpu.VMEM((width, cells), bf16),
            pltpu.VMEM((total, values), f32),
            pltpu.SemaphoreType.DMA((9,)),
            pltpu.SemaphoreType.DMA((2, max(peers, width // 256))),
            pltpu.SemaphoreType.DMA((peers, subs)),
        ]
        + sum_buffers(own_rows, width, subs)
        + scatter_buffers(places, shard, cells),
        compiler_params=pltpu.CompilerParams(
            collective_id=5, has_side_effects=True, vmem_limit_bytes=62 * 2**20
        ),
        name="feed_forward",
    )(nm, ffn_full, ct, normed, weights, hidden, gain)


def results_kernel(
    units, cells, late_hbm, down_hbm, main_hbm, small_hbm, out_hbm, igrad_hbm,
    cells_ref, down_ref, mixer_ref, main_ref, rates_ref, conv_ref, decay_ref, out_ref, igrad_ref,
    late_ref, down_in, main_in, small_in, out_v, igrad_v, sems,
):
    loads = [
        pltpu.make_async_copy(out_hbm, out_v, sems.at[0]),
        pltpu.make_async_copy(igrad_hbm, igrad_v, sems.at[1]),
    ]
    copies = [
        pltpu.make_async_copy(out_v, out_ref, sems.at[2]),
        pltpu.make_async_copy(igrad_v, igrad_ref, sems.at[3]),
    ]
    firsts = [
        pltpu.make_async_copy(late_hbm, late_ref, sems.at[4]),
        pltpu.make_async_copy(down_hbm, down_in, sems.at[5]),
        pltpu.make_async_copy(main_hbm, main_in, sems.at[6]),
        pltpu.make_async_copy(small_hbm, small_in, sems.at[7]),
    ]
    for load in firsts + loads:
        load.start()
    firsts[0].wait()
    taps, heads, per = conv_ref.shape
    for part_at in range(2):
        at = part_at * cells
        cells_ref[part_at] = late_ref[:, at : at + cells].T[0:units]
    firsts[1].wait()
    down_ref[...] = down_in[...].T[0:units]
    mixer_ref[...] = late_ref[:, 2 * cells :].T
    for load, copy in zip(loads, copies):
        load.wait()
        copy.start()
    firsts[2].wait()
    firsts[3].wait()
    wide = main_ref.shape[2]
    for head in range(heads):
        main_ref[:, head, :] = main_in[:, head * wide : (head + 1) * wide]
    small = small_in[...]
    rates_ref[...] = small.T[0 : 2 * heads]
    for tap in range(taps):
        conv_ref[tap] = small[tap * heads : (tap + 1) * heads, PAD // 2 : PAD // 2 + per]
    for row in range(2):
        at = (2 + row) * heads
        decay_ref[row : row + 1, :] = small[0:1, at : at + heads]
    for copy in copies:
        copy.wait()


def results(late, down, main, small, out, igrad, units, cells, heads, per):
    shard = late.shape[0]
    values = late.shape[1] - 2 * cells
    shape = jax.ShapeDtypeStruct
    return pl.pallas_call(
        functools.partial(results_kernel, units, cells),
        in_specs=[anywhere()] * 6,
        out_specs=[vmem()] * 7 + [anywhere()] * 2,
        out_shape=[
            shape((2, units, shard), f32),
            shape((units, shard), f32),
            shape((values, shard), f32),
            shape((shard, heads, main.shape[1] // heads), f32),
            shape((2 * heads, shard), f32),
            shape((CONV, heads, per), f32),
            shape((2, heads), f32),
            in_hbm(out.shape, out.dtype),
            in_hbm(igrad.shape, igrad.dtype),
        ],
        scratch_shapes=[
            pltpu.VMEM(late.shape, f32),
            pltpu.VMEM(down.shape, f32),
            pltpu.VMEM(main.shape, f32),
            pltpu.VMEM(small.shape, f32),
            pltpu.VMEM(out.shape, out.dtype),
            pltpu.VMEM(igrad.shape, igrad.dtype),
            pltpu.SemaphoreType.DMA((8,)),
        ],
        compiler_params=pltpu.CompilerParams(vmem_limit_bytes=62 * 2**20),
        name="results",
    )(late, down, main, small, out, igrad)


def shifted(shard, axis, by):
    count = lax.axis_size(axis)
    pairs = [(i, i + by) for i in range(count) if 0 <= i + by < count]
    return lax.ppermute(shard, axis, pairs)


def root_scale(value_rows):
    return lax.rsqrt(jnp.mean(value_rows * value_rows, axis=-1, keepdims=True) + epsilon)


def matmul(a, b, dims=NN):
    return lax.dot_general(a, b, (dims, ((), ())), preferred_element_type=f32)


ALL = ("seq", "batch")


def per_device(
    tokens, starts, attn_gain, w_in, w_rates, conv_w, decay_par, o_gain, w_out, ffn_gain, w_gu,
    w_down, cotangent,
):
    seqs, length, width = tokens.shape
    shard, heads = w_in.shape[:2]
    shards = width // shard
    total = seqs * length
    conv_cols = heads * QKV
    value_cols = heads * DV
    units = w_down.shape[0]
    cells = -(-units // 256) * 256

    packed_in = w_in[:, :, :QKV].reshape(shard, conv_cols).astype(bf16)
    packed_gate = jnp.concatenate(
        [w_in[:, :, QKV:].reshape(shard, value_cols), w_out.reshape(value_cols, -1).T], axis=1
    ).astype(bf16)
    whole_cells = cells - PAD
    gate, up, down = w_gu[:, 0], w_gu[:, 1], w_down.T
    ends = jnp.zeros((shard, PAD // 2 - (units - whole_cells)), f32)
    packed_ffn = jnp.concatenate(
        [part[:, :whole_cells] for part in (gate, up, down)]
        + [
            piece
            for part in (gate, up, down)
            for piece in (part[:, whole_cells:], ends)
        ]
        + [jnp.zeros((shard, PAD // 2), f32)],
        axis=1,
    ).astype(bf16)
    conv_flat = conv_w.reshape(-1)
    small = jnp.concatenate(
        [attn_gain, ffn_gain, conv_flat, o_gain, w_rates.reshape(-1)]
    ).astype(bf16)

    x = tokens.reshape(total, width)
    ct = cotangent.reshape(total, width)
    before = shifted(tokens[:, length - HALO :], "seq", 1).reshape(seqs * HALO, width)
    in_full = lax.all_gather(packed_in, ALL, axis=0, tiled=True)
    small_full = lax.all_gather(small, ALL, axis=0)
    gate_full = lax.all_gather(packed_gate, ALL, axis=0, tiled=True)
    ffn_full = lax.all_gather(packed_ffn, ALL, axis=0, tiled=True)
    attn_gain_f = small_full[:, :shard].reshape(1, width).astype(f32)
    ffn_gain_f = small_full[:, shard : 2 * shard].reshape(1, width).astype(f32)
    conv_end = 2 * shard + conv_flat.shape[0]
    conv_full = (
        small_full[:, 2 * shard : conv_end]
        .reshape(shards, CONV, heads, -1)
        .transpose(1, 2, 0, 3)
        .reshape(CONV, conv_cols)
        .astype(f32)
    )
    rates_at = conv_end + o_gain.shape[0]
    o_gain_full = small_full[:, conv_end:rates_at].reshape(1, DV).astype(f32)
    rates_full = jnp.pad(
        small_full[:, rates_at:].reshape(width, 2 * heads), ((0, 0), (0, PAD - 2 * heads))
    )

    def normed_rows(rows):
        rows = rows.astype(f32)
        return (rows * root_scale(rows) * attn_gain_f).astype(bf16)

    normed_in = normed_rows(x)
    rates = matmul(normed_in, rates_full)
    projected = pltpu.with_memory_space_constraint(matmul(normed_in, in_full), pltpu.HBM)
    halo = matmul(normed_rows(before), in_full).reshape(seqs, HALO, conv_cols)
    qkv, inv, n, qe, tot, trans, states, mixed = forward_rule(
        starts, decay_par, projected, halo, rates, conv_full, seqs, heads
    )
    og, normed, nm, turned_in, hidden = mixer(
        normed_in, mixed, gate_full, x, ffn_gain_f, o_gain_full
    )
    late_grads, ffn_part, normed_grad, hidden_grad, ffn_gain_part, down_own = feed_forward_block(
        nm, ffn_full, ct, normed, gate_full, hidden, ffn_gain_f, cells
    )
    result, input_grad, gains, in_main, in_small, late_own = backward_rule(
        starts, decay_par, normed_grad, mixed, og, projected, rates, o_gain_full, n, qe, tot, trans, qkv,
        inv, states, halo, conv_full, hidden, hidden_grad, attn_gain_f, ffn_gain_part, ffn_part,
        in_full, gate_full, rates_full, turned_in, x, late_grads, heads,
    )
    grad_cells, grad_down, grad_out, grad_in, grad_rates, grad_conv, grad_decay, out, input_grad = (
        results(
            late_own, down_own, in_main, in_small, result, input_grad, units, cells, heads,
            QKV // shards,
        )
    )
    at = lax.axis_index(ALL)
    gains = gains.reshape(3, width)
    own_gains = lax.dynamic_slice(gains, (0, at * shard), (2, shard))
    onorm_own = lax.dynamic_slice(gains, (2, at * (DV // shards)), (1, DV // shards))
    return (
        out.reshape(tokens.shape),
        input_grad.reshape(tokens.shape),
        own_gains[0],
        grad_in,
        grad_rates.reshape(heads, 2, shard).transpose(2, 0, 1),
        grad_conv,
        grad_decay,
        onorm_own[0],
        grad_out.reshape(heads, DV, -1),
        own_gains[1],
        grad_cells.transpose(2, 0, 1),
        grad_down,
    )


def solution(mesh):
    weights = P(ALL)
    in_specs = (
        P("batch", "seq", None),
        P("batch"),
        weights,
        P(ALL, "head", None),
        P(ALL, "head", None),
        P(None, "head", ALL),
        P(None, "head"),
        weights,
        P("head", None, ALL),
        weights,
        P(ALL, None, "head"),
        P("head", ALL),
        P("batch", "seq", None),
    )
    out_specs = (
        P("batch", "seq", None),
        P("batch", "seq", None),
        weights,
        P(ALL, "head", None),
        P(ALL, "head", None),
        P(None, "head", ALL),
        P(None, "head"),
        weights,
        P("head", None, ALL),
        weights,
        P(ALL, None, "head"),
        P("head", ALL),
    )
    return jax.shard_map(
        per_device, mesh=mesh, in_specs=in_specs, out_specs=out_specs, check_vma=False
    )
```

```python
import functools

import jax
import jax.numpy as jnp
from jax import lax
from jax.experimental import pallas as pl
from jax.experimental.pallas import tpu as pltpu
from jax.sharding import PartitionSpec as P

DK = 128
DV = 256
CONV = 4
QKV = 2 * DK + DV
CHUNK = 128
HALO = 16
PAD = 128

bf16 = jnp.bfloat16
f32 = jnp.float32
epsilon = 1e-06
NN = ((1,), (0,))
NT = ((1,), (1,))
TN = ((0,), (0,))


def mm(a, b, dims=NN):
    return lax.dot_general(
        a.astype(bf16), b.astype(bf16), (dims, ((), ())), preferred_element_type=f32
    )


def split_mm(a, b):
    a_high, b_high = a.astype(bf16), b.astype(bf16)
    a_low = (a - a_high.astype(f32)).astype(bf16)
    b_low = (b - b_high.astype(f32)).astype(bf16)
    return mm(a_high, b_high) + (mm(a_high, b_low) + mm(a_low, b_high))


def iotas(n):
    return (
        lax.broadcasted_iota(jnp.int32, (n, n), 0),
        lax.broadcasted_iota(jnp.int32, (n, n), 1),
    )


def unit_lower_inverses(mats):
    n = mats[0].shape[0]
    rows, cols = iotas(n)
    eye = (rows == cols).astype(f32)
    pair = ((rows >> 1) == (cols >> 1)) & (rows > cols)
    inverses = [eye - jnp.where(pair, a, 0.0) for a in mats]
    shift = 1
    while (1 << shift) < n:
        corner = ((rows >> (shift + 1)) == (cols >> (shift + 1))) & (
            (rows >> shift) > (cols >> shift)
        )
        firsts = [mm(jnp.where(corner, a, 0.0), x) for a, x in zip(mats, inverses)]
        inverses = [x - mm(x, y) for x, y in zip(inverses, firsts)]
        shift += 1
    residuals = [eye - x - split_mm(a, x) for a, x in zip(mats, inverses)]
    return [x + mm(x, r) for x, r in zip(inverses, residuals)]


def sigmoid(v):
    return 1.0 / (1.0 + jnp.exp(-v))


def softplus(v):
    small = jnp.exp(-jnp.abs(v))
    one_more = 1.0 + small
    gap = one_more - 1.0
    exact = gap == 0.0
    tail = jnp.where(exact, small, jnp.log(one_more) * small / jnp.where(exact, 1.0, gap))
    return jnp.maximum(v, 0.0) + tail


def to_row(column, eye):
    return jnp.sum(jnp.where(eye, column, 0.0), axis=0, keepdims=True)


def pick(block, lane):
    lanes = lax.broadcasted_iota(jnp.int32, block.shape, 1)
    return jnp.sum(jnp.where(lanes == lane, block, 0.0), axis=1, keepdims=True)


def gates(logits, decay_ref, head):
    rate = jnp.exp(jnp.full((1, 1), decay_ref[0, head], f32))
    shifted_logit = pick(logits, 2 * head) + decay_ref[1, head]
    strength = sigmoid(pick(logits, 2 * head + 1))
    log_gate = -rate * softplus(shifted_logit)
    return log_gate, strength, rate, shifted_logit


def decays(log_gate, lower, upper, eye):
    gate_row = to_row(log_gate, eye)
    column = jnp.sum(jnp.where(lower, gate_row, 0.0), axis=1, keepdims=True)
    row = jnp.sum(jnp.where(upper, log_gate, 0.0), axis=0, keepdims=True)
    ratio = jnp.where(lower, jnp.exp(jnp.where(lower, column - row, 0.0)), 0.0)
    total = jnp.sum(log_gate, axis=0, keepdims=True)
    return column, total, ratio


def load_conv_input(main_ref, halo_ref, start, x_scr, first):
    length = main_ref.shape[0]
    positions = first + lax.broadcasted_iota(jnp.int32, (length, 1), 0)
    live = (positions >= start).astype(f32)
    before = first - HALO + lax.broadcasted_iota(jnp.int32, (HALO, 1), 0)
    lived = (before >= start).astype(f32)
    x_scr[pl.ds(0, HALO), :] = (halo_ref[0] * lived).astype(bf16).astype(f32)
    x_scr[pl.ds(HALO, length), :] = (main_ref[...] * live).astype(bf16).astype(f32)


def convolve(x_scr, conv, at):
    total = x_scr[pl.ds(at + HALO - CONV + 1, CHUNK), :] * conv[0:1]
    for j in range(1, CONV):
        total = total + x_scr[pl.ds(at + HALO - CONV + 1 + j, CHUNK), :] * conv[j : j + 1]
    return total


def unit(rows):
    return rows * lax.rsqrt(jnp.sum(rows * rows, axis=1, keepdims=True) + epsilon)


MESH = pl.DeviceIdType.MESH
SUB = 128


def head_copy(src, dst, send_sem, recv_sem, peer):
    return pltpu.make_async_remote_copy(
        src_ref=src, dst_ref=dst, send_sem=send_sem, recv_sem=recv_sem,
        device_id={"head": peer}, device_id_type=MESH,
    )


def greet_heads(me, peers):
    barrier = pltpu.get_barrier_semaphore()
    for k in range(1, peers):
        pl.semaphore_signal(barrier, inc=1, device_id={"head": me ^ k}, device_id_type=MESH)
    pl.semaphore_wait(barrier, peers - 1)


def part(ref, start, size):
    return ref.at[pl.ds(pl.multiple_of(start, size), size)]


def piece_rows(owner, t, total, subs):
    return pl.ds(pl.multiple_of(t * (total // subs) + owner * SUB, SUB), SUB)


def take(ref, owner, subs):
    total = ref.shape[0]
    return jnp.concatenate(
        [ref[piece_rows(owner, t, total, subs), :] for t in range(subs)], axis=0
    )


class Pieces:
    def __init__(self, source, target, total, subs, sems):
        self.source, self.target, self.total, self.subs, self.sems = source, target, total, subs, sems

    def at(self, ref, owner, t):
        rows = piece_rows(owner, t, self.total, self.subs)
        if ref.shape[0] != self.total:
            rows = pl.ds(t * SUB, SUB)
        return ref.at[rows]

    def copies(self, owner):
        return [
            pltpu.make_async_copy(
                self.at(self.source, owner, t), self.at(self.target, owner, t),
                self.sems.at[owner, t],
            )
            for t in range(self.subs)
        ]

    def start(self, owner):
        for copy in self.copies(owner):
            copy.start()

    def wait(self, owner):
        for copy in self.copies(owner):
            copy.wait()


class Spread:
    def __init__(self, buffer, subs, me, send_sem, recv_sem):
        self.buffer, self.subs, self.me = buffer, subs, me
        self.send_sem, self.recv_sem = send_sem, recv_sem

    def region(self, owner, t, half):
        rows = piece_rows(owner, t, self.buffer.shape[0], self.subs)
        middle = self.buffer.shape[1] // 2
        if half is None:
            return self.buffer.at[rows]
        return self.buffer.at[rows, pl.ds(half * middle, middle)]

    def put(self, t, value):
        self.buffer[piece_rows(self.me, t, self.buffer.shape[0], self.subs), :] = value

    def copy(self, kind, t, owner):
        at = self.region(owner, t, None if kind < 2 else kind - 2)
        to = self.me ^ (1 if kind in (0, 3) else 2)
        return head_copy(at, at, self.send_sem.at[kind, t], self.recv_sem.at[kind, t], to)

    def start(self, t):
        self.copy(0, t, self.me).start()
        self.copy(1, t, self.me).start()

    def forward(self, t):
        self.copy(0, t, self.me ^ 1).wait_recv()
        self.copy(2, t, self.me ^ 1).start()
        self.copy(1, t, self.me ^ 2).wait_recv()
        self.copy(3, t, self.me ^ 2).start()

    def finish(self, t):
        self.copy(2, t, self.me ^ 3).wait_recv()
        self.copy(3, t, self.me ^ 3).wait_recv()

    def drain(self, t):
        for kind, owner in enumerate((0, 0, 1, 2)):
            self.copy(kind, t, self.me ^ owner).wait_send()


class Combine:
    def __init__(self, send, recv, relay, me, send_sem, recv_sem, piece):
        self.send, self.recv, self.relay, self.me = send, recv, relay, me
        self.send_sem, self.recv_sem, self.piece = send_sem, recv_sem, piece
        self.middle = send.shape[2] // 2

    def rows(self, t):
        return pl.ds(pl.multiple_of(t * self.piece, self.piece), self.piece)

    def copy(self, kind, t):
        rows, low, high = self.rows(t), pl.ds(0, self.middle), pl.ds(self.middle, self.middle)
        source, target, to = (
            (self.send.at[3, rows, low], self.relay.at[0, rows], 1),
            (self.send.at[3, rows, high], self.relay.at[1, rows], 2),
            (self.send.at[1, rows, low], self.recv.at[0, rows, low], 1),
            (self.send.at[2, rows, high], self.recv.at[1, rows, high], 2),
            (self.send.at[1, rows, high], self.recv.at[0, rows, high], 1),
            (self.send.at[2, rows, low], self.recv.at[1, rows, low], 2),
        )[kind]
        return head_copy(
            source, target, self.send_sem.at[kind, t], self.recv_sem.at[kind, t], self.me ^ to
        )

    def start(self, k, t):
        if k == 3:
            self.copy(0, t).start()
            self.copy(1, t).start()
        else:
            self.copy(k + 1, t).start()

    def combine(self, t):
        rows = self.rows(t)
        for k, at in ((1, pl.ds(self.middle, self.middle)), (2, pl.ds(0, self.middle))):
            self.copy(2 - k, t).wait_recv()
            both = self.send[k, rows, at].astype(f32) + self.relay[2 - k, rows, :].astype(f32)
            self.send[k, rows, at] = both.astype(bf16)
            self.copy(3 + k, t).start()

    def collect(self, t):
        for kind in range(2, 6):
            self.copy(kind, t).wait_recv()
        return self.total(self.rows(t))

    def total(self, rows):
        return (
            self.send[0, rows, :].astype(f32)
            + self.recv[0, rows, :].astype(f32)
            + self.recv[1, rows, :].astype(f32)
        )

    def drain(self, t):
        for kind in range(6):
            self.copy(kind, t).wait_send()


def sum_buffers(rows, width, pieces):
    return [
        pltpu.VMEM((4, rows, width), bf16),
        pltpu.VMEM((2, rows, width), bf16),
        pltpu.VMEM((2, rows, width // 2), bf16),
        pltpu.SemaphoreType.DMA((6, pieces)),
        pltpu.SemaphoreType.DMA((6, pieces)),
        pltpu.SemaphoreType.DMA((4, pieces)),
        pltpu.SemaphoreType.DMA((4, pieces)),
    ]


class GroupScatter:
    def __init__(self, source, columns, core_recv, seq_send, seq_recv, sems):
        self.source, self.columns = source, columns
        self.core_recv, self.seq_send, self.seq_recv, self.sems = core_recv, seq_send, seq_recv, sems
        self.place, self.core = lax.axis_index("seq"), lax.axis_index("batch")
        self.places, self.shard = core_recv.shape[0], core_recv.shape[1]

    def rows(self, k, core):
        at = ((self.place ^ k) * 2 + core) * self.shard
        return pl.ds(pl.multiple_of(at, self.shard), self.shard)

    def core_copy(self, k):
        return along(
            "batch", self.source.at[self.rows(k, 1 - self.core), self.columns],
            self.core_recv.at[k], self.sems.at[0, k], self.sems.at[1, k], 1 - self.core,
        )

    def seq_copy(self, k):
        return along(
            "seq", self.seq_send.at[k], self.seq_recv.at[k], self.sems.at[2, k],
            self.sems.at[3, k], self.place ^ k,
        )

    def pass_on(self, k):
        self.core_copy(k).wait_recv()
        own = self.source[self.rows(k, self.core), self.columns].astype(f32)
        self.seq_send[k] = (own + self.core_recv[k].astype(f32)).astype(bf16)

        @pl.when(k > 0)
        def _():
            self.seq_copy(k).start()

    def finish(self):
        total = self.seq_send[0].astype(f32)
        for k in range(1, self.places):
            self.seq_copy(k).wait_recv()
            total = total + self.seq_recv[k].astype(f32)
        return total

    def drain(self):
        for k in range(self.places):
            self.core_copy(k).wait_send()
        for k in range(1, self.places):
            self.seq_copy(k).wait_send()


class LineScatter:
    def __init__(self, own, core_recv, recv, sems):
        self.own, self.core_recv, self.recv, self.sems = own, core_recv, recv, sems
        self.place, self.core = lax.axis_index("seq"), lax.axis_index("batch")
        self.places = own.shape[0]

    def clear(self):
        @pl.when(self.place == 0)
        def _():
            self.recv[0] = jnp.zeros_like(self.recv[0])

        @pl.when(self.place == self.places - 1)
        def _():
            self.recv[self.places] = jnp.zeros_like(self.recv[0])

    def core_copy(self, d, source):
        return along(
            "batch", source, self.core_recv.at[d], self.sems.at[0, d], self.sems.at[1, d],
            1 - self.core,
        )

    def add_core(self, d, source):
        self.core_copy(d, source).wait_recv()
        self.add(d, self.core_recv[d])

    def add(self, d, other):
        self.own[d] = (self.own[d].astype(f32) + other.astype(f32)).astype(bf16)

    def move(self, d):
        right = d > self.place
        to = jnp.clip(jnp.where(right, self.place + 1, self.place - 1), 0, self.places - 1)
        slot = jnp.where(right | (to != d), d, self.places)
        return along(
            "seq", self.own.at[d], self.recv.at[slot], self.sems.at[2, d], self.sems.at[3, slot], to
        )

    def arrived(self, slot):
        return along(
            "seq", self.own.at[0], self.recv.at[slot], self.sems.at[2, 0], self.sems.at[3, slot],
            jnp.where(self.place > 0, self.place - 1, self.places - 1),
        )

    def advance(self, hop):
        last = self.places - 1

        def towards(d, active, through):
            @pl.when(active)
            def _():
                @pl.when(through)
                def _():
                    self.arrived(d).wait_recv()
                    self.add(d, self.recv[d])

                self.move(d).start()

        turn = hop - self.place
        d = jnp.clip(last - turn, 0, last)
        towards(d, (turn >= 0) & (last - turn > self.place), self.place > 0)
        turn = hop - (last - self.place)
        d = jnp.clip(turn, 0, last)
        towards(d, (turn >= 0) & (turn < self.place), self.place < last)

    def finish(self):
        @pl.when(self.place > 0)
        def _():
            self.arrived(self.place).wait_recv()

        @pl.when(self.place < self.places - 1)
        def _():
            self.arrived(self.places).wait_recv()

        return (
            self.own[self.place].astype(f32)
            + self.recv[self.place].astype(f32)
            + self.recv[self.places].astype(f32)
        )

    def drain(self, source):
        for d in range(self.places):
            self.core_copy(d, source(d)).wait_send()

            @pl.when(self.place != d)
            def _():
                self.move(d).wait_send()


def line_buffers(places, shard, columns):
    return [
        pltpu.VMEM((places, shard, columns), bf16),
        pltpu.VMEM((places, shard, columns), bf16),
        pltpu.VMEM((places + 1, shard, columns), bf16),
        pltpu.SemaphoreType.DMA((4, places + 1)),
    ]


def scatter_buffers(places, shard, columns):
    return [pltpu.VMEM((places, shard, columns), bf16)] * 3 + [
        pltpu.SemaphoreType.DMA((4, places))
    ]


def call_group(me, peers, places, cores):
    barrier = pltpu.get_barrier_semaphore()
    group = places * cores
    flat = lax.axis_index("seq") * cores + lax.axis_index("batch")
    for k in range(1, peers):
        pl.semaphore_signal(barrier, inc=1, device_id={"head": me ^ k}, device_id_type=MESH)
    for d in range(1, group):
        to = lax.rem(flat + d, group)
        pl.semaphore_signal(
            barrier, inc=1, device_id={"seq": to // cores, "batch": lax.rem(to, cores)},
            device_id_type=MESH,
        )


def meet_group(peers, places, cores):
    pl.semaphore_wait(pltpu.get_barrier_semaphore(), peers + places * cores - 2)


def greet_group(me, peers, places, cores):
    call_group(me, peers, places, cores)
    meet_group(peers, places, cores)


def in_hbm(dims, kind):
    return pltpu.HBM(dims, kind)


def anywhere():
    return pl.BlockSpec(memory_space=pltpu.HBM)


def vmem():
    return pl.BlockSpec(memory_space=pltpu.VMEM)


def along(axis, source, target, send_sem, recv_sem, to):
    return pltpu.make_async_remote_copy(
        src_ref=source, dst_ref=target, send_sem=send_sem, recv_sem=recv_sem,
        device_id={axis: to}, device_id_type=MESH,
    )


def forward_kernel(
    heads, places, start_ref, decay_ref, main_ref, halo_ref, rate_ref, conv_ref,
    qkv_ref, inv_ref, n_ref, qe_ref, tot_ref, trans_ref, s_ref, mixed_ref,
    x_scr, b_scr, o_scr, carried_scr, send, recv, send_sem, recv_sem,
):
    step = pl.program_id(0)
    chains = n_ref.shape[0]
    count = n_ref.shape[1]
    length = main_ref.shape[0]
    place = lax.axis_index("seq")
    lag = jnp.minimum(place, chains - 1)

    @pl.when(step == 0)
    def _():
        barrier = pltpu.get_barrier_semaphore()

        @pl.when(place > 0)
        def _():
            pl.semaphore_signal(
                barrier, inc=1, device_id={"seq": place - 1}, device_id_type=MESH
            )

        @pl.when(place == 0)
        def _():
            recv[...] = jnp.zeros_like(recv)

    @pl.when(step < chains)
    def _():
        head = step % heads
        load_conv_input(
            main_ref, halo_ref, start_ref[jnp.minimum(step, chains - 1) // heads], x_scr, place * length
        )
        conv = conv_ref[...]
        rows, cols = iotas(CHUNK)
        lower, upper, eye = rows >= cols, rows <= cols, rows == cols
        parts = []
        for c in range(count):
            at = c * CHUNK
            convolved = convolve(x_scr, conv, at)
            active = convolved * sigmoid(convolved)
            q = (unit(active[:, :DK]) * DK ** (-0.5)).astype(bf16)
            k = unit(active[:, DK : 2 * DK]).astype(bf16)
            v = active[:, 2 * DK :].astype(bf16)
            qkv_ref[pl.ds(at, CHUNK), 0:DK] = q
            qkv_ref[pl.ds(at, CHUNK), DK : 2 * DK] = k
            qkv_ref[pl.ds(at, CHUNK), 2 * DK :] = v
            log_gate, strength, _, _ = gates(rate_ref[pl.ds(at, CHUNK), :], decay_ref, head)
            column, total, ratio = decays(log_gate, lower, upper, eye)
            products = mm(jnp.concatenate([k, q], axis=0), k, NT)
            coupling = jnp.where(rows > cols, strength * ratio * products[:CHUNK], 0.0)
            scores = (ratio * products[CHUNK:]).astype(bf16)
            parts.append((q, k, v, strength, column, total, coupling, scores))
        inverses = unit_lower_inverses([p[6] for p in parts])
        maps = []
        for c in range(count):
            q, k, v, strength, column, total, _, scores = parts[c]
            growth = jnp.exp(column)
            kf, vf, qf = k.astype(f32), v.astype(f32), q.astype(f32)
            inverse = inverses[c].astype(bf16)
            inv_ref[0, c] = inverse
            target = jnp.concatenate([(strength * growth) * kf, strength * vf], axis=1)
            solved = mm(inverse, target).astype(bf16)
            read = mm(scores, solved)
            qe_ref[step, c] = (growth * qf - read[:, :DK]).astype(bf16)
            o_scr[step, pl.ds(c * CHUNK, CHUNK), :] = read[:, DK:]
            written = mm(jnp.exp(total - column) * kf, solved, TN)
            low_n = written[:, :DK].astype(bf16)
            n_ref[step, c] = low_n
            b_scr[step, c] = written[:, DK:]
            whole = jnp.exp(total)
            tot_ref[step, pl.ds(c, 1), :] = jnp.broadcast_to(whole, (1, DK))
            maps.append((low_n, written[:, DK:], whole))
        low_n, b, whole = maps[0]
        trans = whole * eye.astype(f32) - low_n.astype(f32)
        carried = b
        for low_n, b, whole in maps[1:]:
            both = jnp.concatenate([trans, carried], axis=1)
            moved = whole * both - mm(low_n, both)
            trans = moved[:, :DK]
            carried = moved[:, DK:] + b
        trans_ref[step] = trans.astype(bf16)
        carried_scr[step] = carried

    @pl.when(step >= chains)
    def _():
        chain = jnp.maximum(step - chains, 0)
        state = recv[chain].astype(f32)
        for c in range(count):
            low_state = state.astype(bf16)
            s_ref[0, c] = low_state
            both = mm(jnp.concatenate([n_ref[chain, c], qe_ref[chain, c]], axis=0), low_state)
            whole = tot_ref[chain, pl.ds(c, 1), 0:1]
            state = whole * state - both[:DK] + b_scr[chain, c]
            at = pl.ds(c * CHUNK, CHUNK)
            mixed_ref[at, :] = o_scr[chain, at, :] + both[DK:]

    half = DV // 2

    def passed(chain, side):
        at = pl.ds(side * half, half)
        return along(
            "seq", send.at[chain, :, at], recv.at[chain, :, at], send_sem.at[chain, side],
            recv_sem.at[chain, side], jnp.minimum(place + 1, places - 1),
        )

    @pl.when((step == 0) & (place < places - 1))
    def _():
        pl.semaphore_wait(pltpu.get_barrier_semaphore(), 1)

    relayed = step - lag

    @pl.when((relayed >= 0) & (relayed < chains))
    def _():
        chain = jnp.clip(relayed, 0, chains - 1)
        for side in range(2):
            at = slice(side * half, (side + 1) * half)

            @pl.when(place > 0)
            def _():
                passed(chain, side).wait_recv()

            @pl.when(place < places - 1)
            def _():
                leaving = mm(trans_ref[chain], recv[chain, :, at]) + carried_scr[chain, :, at]
                send[chain, :, at] = leaving.astype(bf16)
                passed(chain, side).start()

    @pl.when((step == 2 * chains - 1) & (place < places - 1))
    def _():
        for chain in range(chains):
            for side in range(2):
                passed(chain, side).wait_send()


def early(chains, make):
    return lambda j: make(jnp.minimum(j, chains - 1))


def late(chains, make):
    return lambda j: make(jnp.maximum(j - chains, 0))


def forward_rule(starts, decay_par, projected, halo, rates, conv_w, seqs, heads):
    places = lax.axis_size("seq")
    chains = seqs * heads
    length = projected.shape[0] // seqs
    count = length // CHUNK
    row = lambda first: lambda i: (i // heads, first + i % heads)
    whole = lambda *dims: pl.BlockSpec(dims, lambda j: (0,) * len(dims))
    shape = in_hbm
    return pl.pallas_call(
        functools.partial(forward_kernel, heads, places),
        grid=(2 * chains,),
        in_specs=[
            smem(),
            smem(),
            pl.BlockSpec((length, QKV), early(chains, row(0))),
            pl.BlockSpec((1, HALO, QKV), early(chains, lambda i: (i // heads, 0, i % heads))),
            pl.BlockSpec((length, PAD), early(chains, lambda i: (i // heads, 0))),
            pl.BlockSpec((CONV, QKV), early(chains, lambda i: (0, i % heads))),
        ],
        out_specs=[
            pl.BlockSpec((length, QKV), early(chains, row(0))),
            pl.BlockSpec((1, count, CHUNK, CHUNK), early(chains, lambda i: (i, 0, 0, 0))),
            whole(chains, count, DK, DK),
            whole(chains, count, CHUNK, DK),
            whole(chains, count, DK),
            whole(chains, DK, DK),
            pl.BlockSpec((1, count, DK, DV), late(chains, lambda i: (i, 0, 0, 0))),
            pl.BlockSpec((length, DV), late(chains, row(0))),
        ],
        out_shape=[
            shape((seqs * length, heads * QKV), bf16),
            shape((chains, count, CHUNK, CHUNK), bf16),
            shape((chains, count, DK, DK), bf16),
            shape((chains, count, CHUNK, DK), bf16),
            shape((chains, count, DK), f32),
            shape((chains, DK, DK), bf16),
            shape((chains, count, DK, DV), bf16),
            shape((seqs * length, heads * DV), f32),
        ],
        scratch_shapes=[
            pltpu.VMEM((HALO + length, QKV), f32),
            pltpu.VMEM((chains, count, DK, DV), f32),
            pltpu.VMEM((chains, length, DV), f32),
            pltpu.VMEM((chains, DK, DV), f32),
            pltpu.VMEM((chains, DK, DV), bf16),
            pltpu.VMEM((chains, DK, DV), bf16),
            pltpu.SemaphoreType.DMA((chains, 2)),
            pltpu.SemaphoreType.DMA((chains, 2)),
        ],
        compiler_params=pltpu.CompilerParams(
            dimension_semantics=("arbitrary",), collective_id=3, has_side_effects=True,
            vmem_limit_bytes=48 * 2**20,
        ),
        name="forward_rule",
    )(starts, decay_par, projected, halo, rates, conv_w)


def backward_kernel(
    heads, places, peers, cores, start_ref, decay_ref,
    dn_ref, mixed_ref, og_ref, o_gain_ref, n_ref, qe_ref, tot_ref, trans_ref,
    qkv_ref, inv_ref, s_ref, main_ref, halo_ref, rate_ref, conv_ref,
    hidden_ref, hgrad_ref, gain_ref, ffn_gain_ref, ffnp_hbm, win_hbm, wog_hbm, wrates_hbm, nin_hbm, x_hbm,
    late_hbm,
    out_hbm, igrad_hbm, gains_out, grad_out, small_out, late_out,
    dp_ref, x_scr, g_scr, do_scr, own_scr, send, recv, tail_scr, halo_send, halo_recv,
    conv_scr, decay_scr, o_gain_scr, whole_out, whole_in, win_v, wog_v, nin_v, x_v, conv_source,
    gate_source, extras_v, gains_v, gains_recv, gains_sum, gains_all,
    send_sem, recv_sem, halo_send_sem, halo_recv_sem, load_sem, in_sem, late_sem, x_sem, out_sem, hs, hr, gs, gr,
    sent, got, relay, sum_send, sum_recv, gather_send, gather_recv,
    in_sent, in_got, in_relay, in_sum_send, in_sum_recv, in_gather_send, in_gather_recv,
    conv_own, conv_core, conv_recv, conv_sems,
    gate_own, gate_core, gate_recv, gate_sems,
    late_own, late_core, late_recv, late_sems,
):
    step = pl.program_id(0)
    chains = n_ref.shape[0]
    count = n_ref.shape[1]
    length = main_ref.shape[0]
    seqs = chains // heads
    total, width = whole_out.shape
    conv_cols = heads * QKV
    values = heads * DV
    in_cols = conv_cols + values
    place, core = lax.axis_index("seq"), lax.axis_index("batch")
    lag = jnp.minimum(places - 1 - place, chains - 1)
    me = lax.axis_index("head")
    own_rows = hidden_ref.shape[0]
    subs = own_rows // SUB
    group = places * cores
    shard = width // group
    pair = cores * shard
    flat = place * cores + core

    ring = Spread(whole_out, subs, me, gather_send, gather_recv)
    sums = Combine(sent, got, relay, me, sum_send, sum_recv, own_rows)
    in_ring = Spread(whole_in, subs, me, in_gather_send, in_gather_recv)
    in_sums = Combine(in_sent, in_got, in_relay, me, in_sum_send, in_sum_recv, SUB)
    conv_line = LineScatter(conv_own, conv_core, conv_recv, conv_sems)
    gate_line = LineScatter(gate_own, gate_core, gate_recv, gate_sems)
    late_line = LineScatter(late_own, late_core, late_recv, late_sems)

    def late_rows(d, at_core):
        return late_hbm.at[pl.ds(pl.multiple_of((d * cores + at_core) * shard, shard), shard)]

    def late_source(d):
        return late_rows(d, 1 - core)

    def late_load(d):
        return pltpu.make_async_copy(late_rows(d, core), late_own.at[d], late_sem.at[d])

    def hops(third):
        return range(third * (places - 1) // 3, (third + 1) * (places - 1) // 3)

    def far_first(i):
        return jnp.where(i % 2 == 0, places - 1 - i // 2, i // 2)

    def halves(grads):
        top, low = grads[:shard], grads[shard:]
        return jnp.where(core == 0, top, low), jnp.where(core == 0, low, top)
    out_store = Pieces(whole_out, out_hbm, total, subs, out_sem.at[0])
    in_store = Pieces(whole_in, igrad_hbm, total, subs, out_sem.at[1])
    own_x = Pieces(x_hbm, x_v, total, subs, x_sem)
    loads = [
        pltpu.make_async_copy(win_hbm, win_v.at[:, pl.ds(0, conv_cols)], in_sem.at[0]),
        pltpu.make_async_copy(wrates_hbm, win_v.at[:, pl.ds(conv_cols, PAD)], in_sem.at[1]),
        pltpu.make_async_copy(wog_hbm.at[:, pl.ds(0, values)], wog_v, in_sem.at[2]),
        pltpu.make_async_copy(nin_hbm, nin_v, in_sem.at[3]),
    ]

    def ffn_loads(k):
        return [
            pltpu.make_async_copy(
                ffnp_hbm.at[piece_rows(me ^ k, t, total, subs)], sent.at[k, pl.ds(t * SUB, SUB)],
                load_sem.at[k, t],
            )
            for t in range(subs)
        ]

    half = DV // 2

    def passed(chain, side):
        at = pl.ds(side * half, half)
        return along(
            "seq", send.at[chain, :, at], recv.at[chain, :, at], send_sem.at[chain, side],
            recv_sem.at[chain, side], jnp.maximum(place - 1, 0),
        )

    def returned(chain):
        return along(
            "seq", halo_send.at[chain], halo_recv.at[chain], halo_send_sem.at[chain],
            halo_recv_sem.at[chain], jnp.maximum(place - 1, 0),
        )

    @pl.when(step == 0)
    def _():
        for k in range(peers - 1, -1, -1):
            for load in ffn_loads(k):
                load.start()

        @pl.when(place == places - 1)
        def _():
            recv[...] = jnp.zeros_like(recv)
            halo_recv[...] = jnp.zeros_like(halo_recv)

        decay_scr[...] = jnp.zeros_like(decay_scr)
        o_gain_scr[...] = jnp.zeros_like(o_gain_scr)
        extras_v[...] = jnp.zeros_like(extras_v)
        for line in (conv_line, gate_line, late_line):
            line.clear()
        for d in range(places):
            late_load(d).start()
        for load in loads:
            load.start()
        own_x.start(me)
        call_group(me, peers, places, cores)

    @pl.when(step < chains)
    def _():
        gain = o_gain_ref[0:1]
        first = (step // heads) * length
        og_at = pl.ds(pl.multiple_of(conv_cols + (step % heads) * DV, DV), DV)
        state = jnp.zeros((DK, DV), f32)
        gain_total = jnp.zeros((1, DV), f32)
        for c in reversed(range(count)):
            at = pl.ds(c * CHUNK, CHUNK)
            mixed, og, dn = mixed_ref[at, :], og_ref[at, :], dn_ref[at, :]
            inverse = lax.rsqrt(jnp.mean(mixed * mixed, axis=1, keepdims=True) + epsilon)
            scaled = mixed * inverse
            sig = sigmoid(og)
            silu = og * sig
            through = dn * scaled
            gain_total = gain_total + jnp.sum(through * silu, axis=0, keepdims=True)
            dp_ref[pl.ds(pl.multiple_of(first + c * CHUNK, CHUNK), CHUNK), og_at] = (
                through * gain * sig * (1.0 + og * (1.0 - sig))
            ).astype(bf16)
            weighted = dn * gain * silu
            dmixed = inverse * (
                weighted - scaled * jnp.mean(weighted * scaled, axis=1, keepdims=True)
            )
            dmixed = dmixed.astype(bf16)
            do_scr[step, at, :] = dmixed
            decay = tot_ref[step, pl.ds(c, 1), 0:1]
            state = (
                decay * state - mm(n_ref[step, c], state, TN) + mm(qe_ref[step, c], dmixed, TN)
            )
        o_gain_scr[0:1, :] = o_gain_scr[0:1, :] + gain_total
        own_scr[step] = state

    @pl.when(step == 0)
    def _():
        meet_group(peers, places, cores)
        for k in range(peers - 1, 0, -1):
            for load in ffn_loads(k):
                load.wait()
            sums.start(k, 0)
        for load in ffn_loads(0):
            load.wait()
        for d in range(places):
            late_line.core_copy(d, late_source(d)).start()

    @pl.when(step >= chains)
    def _():
        chain = jnp.maximum(step - chains, 0)
        seq, head = chain // heads, chain % heads
        first = seq * length
        start = start_ref[seq]
        load_conv_input(main_ref, halo_ref, start, x_scr, place * length)
        conv = conv_ref[...]
        rows, cols = iotas(CHUNK)
        lower, upper, eye = rows >= cols, rows <= cols, rows == cols
        strict = rows > cols
        state = recv[chain].astype(f32)
        leaving = [None] * count
        for c in reversed(range(count)):
            leaving[c] = state
            state = (
                tot_ref[chain, pl.ds(c, 1), 0:1] * state
                - mm(n_ref[chain, c], state, TN)
                + mm(qe_ref[chain, c], do_scr[chain, pl.ds(c * CHUNK, CHUNK), :], TN)
            )
        g_scr[pl.ds(0, 8), :] = jnp.zeros((8, QKV), f32)
        g_scr[pl.ds(8 + length, 8), :] = jnp.zeros((8, QKV), f32)
        rate_total = jnp.zeros((1, 1), f32)
        bias_total = jnp.zeros((1, 1), f32)
        conv_total = [jnp.zeros((1, QKV), f32) for _ in range(CONV)]
        lanes = lax.broadcasted_iota(jnp.int32, (CHUNK, PAD), 1)
        for c in range(count):
            for t in range(seqs - 1):
                if c == count - 1:

                    @pl.when(step == chains + (t + 1) * heads)
                    def _():
                        in_sums.combine(t)

            at = pl.ds(c * CHUNK, CHUNK)
            q, k, v = qkv_ref[at, 0:DK], qkv_ref[at, DK : 2 * DK], qkv_ref[at, 2 * DK :]
            kf, vf = k.astype(f32), v.astype(f32)
            log_gate, strength, rate, logit = gates(rate_ref[at, :], decay_ref, head)
            column, total, ratio = decays(log_gate, lower, upper, eye)
            growth = jnp.exp(column)
            remain = jnp.exp(total - column)
            whole = jnp.exp(total)
            inverse = inv_ref[0, c]
            s0 = s_ref[0, c]
            do = do_scr[chain, at, :]
            grad_state = leaving[c]
            low_grad_state = grad_state.astype(bf16)
            kq = jnp.concatenate([k, q], axis=0)
            products = mm(kq, k, NT)
            kk, qk = products[:CHUNK], products[CHUNK:]
            reads = mm(kq, s0)
            ks, qs = reads[:CHUNK], reads[CHUNK:]
            fresh = vf - growth * ks
            pseudo = mm(inverse, strength * fresh).astype(bf16)
            scores = (ratio * qk).astype(bf16)
            dpseudo = mm(scores, do, TN) + mm(remain * kf, low_grad_state)
            dtarget = mm(inverse, dpseudo, TN)
            low_dtarget = dtarget.astype(bf16)
            dstrength = jnp.sum(dtarget * fresh, axis=1, keepdims=True)
            dlog = -(strength * growth) * jnp.sum(dtarget * ks, axis=1, keepdims=True)
            dv = strength * dtarget
            both = jnp.concatenate([low_dtarget, do], axis=0)
            outer = mm(both, pseudo, NT)
            dcoupling = jnp.where(strict, -outer[:CHUNK] * ratio, 0.0)
            by_strength = dcoupling * kk
            dstrength = dstrength + jnp.sum(by_strength, axis=1, keepdims=True)
            exponent = strength * by_strength
            dqk_f = jnp.where(lower, outer[CHUNK:] * ratio, 0.0)
            exponent = exponent + dqk_f * qk
            pair = jnp.concatenate([(dcoupling * strength).astype(bf16), dqk_f.astype(bf16)], axis=0)
            back = mm(both, s0, NT)
            wide = mm(pair, k)
            dq = growth * back[CHUNK:] + wide[CHUNK:]
            dkept = mm(pseudo, low_grad_state, NT)
            dk = (
                wide[:CHUNK]
                - (strength * growth) * back[:CHUNK]
                + mm(pair, kq, TN)
                + remain * dkept
            )
            dlog = dlog + growth * jnp.sum(do.astype(f32) * qs, axis=1, keepdims=True)
            from_kept = remain * jnp.sum(kf * dkept, axis=1, keepdims=True)
            dlog = dlog - from_kept + jnp.sum(exponent, axis=1, keepdims=True)
            dlog_row = to_row(dlog, eye) - jnp.sum(exponent, axis=0, keepdims=True)
            tail = jnp.sum(from_kept, axis=0, keepdims=True) + whole * jnp.sum(
                jnp.sum(grad_state * s0.astype(f32), axis=1, keepdims=True), axis=0, keepdims=True
            )
            dgate = jnp.sum(jnp.where(upper, dlog_row, 0.0), axis=1, keepdims=True) + tail
            slope = sigmoid(logit)
            drate0 = -rate * slope * dgate
            drate1 = dstrength * strength * (1.0 - strength)
            rate_total = rate_total + jnp.sum(dgate * log_gate, axis=0, keepdims=True)
            bias_total = bias_total + jnp.sum(drate0, axis=0, keepdims=True)
            here = pl.ds(pl.multiple_of(first + c * CHUNK, CHUNK), CHUNK)
            others = jnp.where(head == 0, 0.0, dp_ref[here, in_cols:].astype(f32))
            dp_ref[here, in_cols:] = jnp.where(
                lanes == 2 * head, drate0, jnp.where(lanes == 2 * head + 1, drate1, others)
            ).astype(bf16)
            convolved = convolve(x_scr, conv, c * CHUNK)
            sig = sigmoid(convolved)
            active = convolved * sig
            slope_conv = sig * (1.0 + convolved * (1.0 - sig))

            def unit_grad(rows_in, grad):
                inv_norm = lax.rsqrt(jnp.sum(rows_in * rows_in, axis=1, keepdims=True) + epsilon)
                y = rows_in * inv_norm
                return inv_norm * (grad - y * jnp.sum(y * grad, axis=1, keepdims=True))

            dq = dq.astype(bf16).astype(f32) * DK ** (-0.5)
            dk = dk.astype(bf16).astype(f32)
            dv = dv.astype(bf16).astype(f32)
            dconv = (
                jnp.concatenate(
                    [unit_grad(active[:, :DK], dq), unit_grad(active[:, DK : 2 * DK], dk), dv],
                    axis=1,
                )
                * slope_conv
            )
            g_scr[pl.ds(8 + c * CHUNK, CHUNK), :] = dconv
            for j in range(CONV):
                shifted_in = x_scr[pl.ds(c * CHUNK + HALO - CONV + 1 + j, CHUNK), :]
                conv_total[j] = conv_total[j] + jnp.sum(dconv * shifted_in, axis=0, keepdims=True)
        for j in range(CONV):
            tap = pl.ds(j * heads + head, 1)
            conv_scr[tap, :] = conv_total[j] + jnp.where(seq == 0, 0.0, conv_scr[tap, :])
        spots = lax.broadcasted_iota(jnp.int32, decay_scr.shape, 1)
        top = lax.broadcasted_iota(jnp.int32, decay_scr.shape, 0) == 0
        decay_scr[...] = decay_scr[...] + jnp.where(
            top & (spots == 2 * heads + head), rate_total, 0.0
        ) + jnp.where(top & (spots == 3 * heads + head), bias_total, 0.0)

        def conv_back(at, size):
            grad = g_scr[pl.ds(at + CONV - 1, size), :] * conv[0:1]
            for j in range(1, CONV):
                grad = grad + g_scr[pl.ds(at + CONV - 1 - j, size), :] * conv[j : j + 1]
            return grad

        halo_send[chain] = conv_back(0, 8)

        @pl.when(place > 0)
        def _():
            returned(chain).start()

        conv_at = pl.ds(pl.multiple_of(head * QKV, QKV), QKV)
        for c in range(count):
            grad = conv_back(8 + c * CHUNK, CHUNK)
            positions = place * length + c * CHUNK + lax.broadcasted_iota(
                jnp.int32, (CHUNK, 1), 0
            )
            live = (positions >= start).astype(f32)
            if c == count - 1:
                tail_scr[chain] = grad[CHUNK - HALO :]
            dp_ref[pl.ds(pl.multiple_of(first + c * CHUNK, CHUNK), CHUNK), conv_at] = (
                grad * live
            ).astype(bf16)

    @pl.when(step == chains - 1)
    def _():
        loads[3].wait()

        def gate_grads(i, carry):
            d = far_first(i)
            rows = pl.ds(pl.multiple_of(d * pair, pair), pair)
            mine, others = halves(mm(nin_v[rows, :], dp_ref[:, conv_cols:in_cols]))
            gate_own[d] = mine.astype(bf16)
            gate_source[d] = others.astype(bf16)
            gate_line.core_copy(d, gate_source.at[d]).start()
            return carry

        lax.fori_loop(0, places, gate_grads, 0)
        for d in range(places):
            late_load(d).wait()
            late_line.add_core(d, late_source(d))

    relayed = step - lag

    @pl.when((relayed >= 0) & (relayed < chains))
    def _():
        chain = jnp.clip(relayed, 0, chains - 1)
        for side in range(2):
            at = slice(side * half, (side + 1) * half)

            @pl.when(place < places - 1)
            def _():
                passed(chain, side).wait_recv()

            @pl.when(place > 0)
            def _():
                earlier = mm(trans_ref[chain], recv[chain, :, at], TN) + own_scr[chain, :, at]
                send[chain, :, at] = earlier.astype(bf16)
                passed(chain, side).start()

    @pl.when(step == chains - 1)
    def _():
        sums.combine(0)

    @pl.when(step == chains)
    def _():
        for kind in range(2, 6):
            sums.copy(kind, 0).wait_recv()
        for t in range(subs):
            rows = pl.ds(t * SUB, SUB)
            ring.put(t, (hidden_ref[rows, :] + sums.total(rows)).astype(bf16))
            ring.start(t)
        out_store.start(me)

    @pl.when(step == chains + 2)
    def _():
        for t in range(subs):
            ring.forward(t)

    for third, at_step in enumerate((chains - 1, chains + 1, 2 * chains - 1)):

        @pl.when(step == at_step)
        def _():
            for hop in hops(third):
                late_line.advance(hop)

    for third, at_step in enumerate((chains, chains + 1, chains + 2)):

        @pl.when(step == at_step)
        def _():
            if third == 0:
                for d in range(places):
                    gate_line.add_core(d, gate_source.at[d])
            for hop in hops(third):
                gate_line.advance(hop)

    def mend_ends(seq):
        for head in range(heads):
            chain = seq * heads + head

            @pl.when(place < places - 1)
            def _():
                returned(chain).wait_recv()

            positions = (place + 1) * length - HALO + lax.broadcasted_iota(
                jnp.int32, (HALO, 1), 0
            )
            live = (positions >= start_ref[seq]).astype(f32)
            grad = tail_scr[chain] + jnp.concatenate(
                [jnp.zeros((HALO - 8, QKV), f32), halo_recv[chain]], axis=0
            )
            dp_ref[pl.ds((seq + 1) * length - HALO, HALO), pl.ds(head * QKV, QKV)] = (
                grad * live
            ).astype(bf16)

    def project(t):
        def one(i, carry):
            k = jnp.where(i == 0, peers - 1, lax.rem(i, peers - 1))
            rows = piece_rows(me ^ k, t, total, subs)
            partial = mm(dp_ref[rows, 0:conv_cols], win_v[:, 0:conv_cols], NT)
            partial = partial + mm(dp_ref[rows, conv_cols:in_cols], wog_v[...], NT)
            partial = partial + mm(dp_ref[rows, in_cols:], win_v[:, conv_cols:], NT)
            in_sent[k, pl.ds(t * SUB, SUB), :] = partial.astype(bf16)

            for kk in range(1, peers):

                @pl.when(k == kk)
                def _():
                    in_sums.start(kk, t)

            return carry

        lax.fori_loop(0, peers, one, 0)

    for t in range(seqs - 1):

        @pl.when(step == chains + (t + 1) * heads - 1)
        def _():
            mend_ends(t)
            if t == 0:
                for load in loads[:3]:
                    load.wait()
            project(t)

    def own_input_grads(t):
        rows = pl.ds(t * SUB, SUB)
        din = in_sums.collect(t)
        x = x_v[rows, :].astype(f32)
        inverse = lax.rsqrt(jnp.mean(x * x, axis=1, keepdims=True) + epsilon)
        scaled = x * inverse
        weighted = din * gain_ref[...]
        grad = hgrad_ref[rows, :] + inverse * (
            weighted - scaled * jnp.mean(weighted * scaled, axis=1, keepdims=True)
        )
        in_ring.put(t, grad.astype(bf16))
        in_ring.start(t)
        return jnp.sum(din * scaled, axis=0, keepdims=True)

    @pl.when(step == 2 * chains - 1)
    def _():
        own_x.wait(me)
        gain_part = jnp.zeros((1, width), f32)
        for t in range(seqs - 1):
            gain_part = gain_part + own_input_grads(t)
        mend_ends(seqs - 1)
        taps = CONV * heads
        per = QKV // group
        lanes = lax.broadcasted_iota(jnp.int32, (taps, PAD), 1)
        for q in range(group):
            at = per * q // PAD * PAD
            shift = (PAD // 2 - per * q) % PAD
            moved = conv_scr[:, at : at + PAD]
            if shift:
                moved = pltpu.roll(moved, shift, 1)
            kept = jnp.where((lanes >= PAD // 2) & (lanes < PAD // 2 + per), moved, 0.0)
            extras_v[q * shard : q * shard + taps, :] = kept + decay_scr[...]
        if seqs == 1:
            for load in loads[:3]:
                load.wait()

        def place_grads(i, carry):
            d = far_first(i)
            rows = pl.ds(pl.multiple_of(d * pair, pair), pair)
            mine, others = halves(mm(nin_v[rows, :], dp_ref[:, 0:conv_cols]))
            conv_own[d, :, 0:conv_cols] = mine.astype(bf16)
            conv_source[d, :, 0:conv_cols] = others.astype(bf16)
            mine, others = halves(mm(nin_v[rows, :], dp_ref[:, in_cols:]) + extras_v[rows, :])
            conv_own[d, :, conv_cols:] = mine.astype(bf16)
            conv_source[d, :, conv_cols:] = others.astype(bf16)
            conv_line.core_copy(d, conv_source.at[d]).start()

            @pl.when(i > 0)
            def _():
                before = far_first(jnp.maximum(i - 1, 0))
                conv_line.add_core(before, conv_source.at[before])

            return carry

        first_places = min(2, places)
        lax.fori_loop(0, first_places, place_grads, 0)
        project(seqs - 1)
        lax.fori_loop(first_places, places, place_grads, 0)
        before = far_first(places - 1)
        conv_line.add_core(before, conv_source.at[before])
        for hop in hops(0):
            conv_line.advance(hop)
        in_sums.combine(seqs - 1)
        gain_part = gain_part + own_input_grads(seqs - 1)
        lane_rows = width // 128
        gains_v[...] = jnp.zeros_like(gains_v)
        for r in range(lane_rows):
            gains_v[r : r + 1, :] = gain_part[:, r * 128 : (r + 1) * 128]
            gains_v[lane_rows + r : lane_rows + r + 1, :] = ffn_gain_ref[
                0:1, r * 128 : (r + 1) * 128
            ]
        for r in range(DV // 128):
            gains_v[2 * lane_rows + r : 2 * lane_rows + r + 1, :] = o_gain_scr[
                0:1, r * 128 : (r + 1) * 128
            ]

        def gains_copy(k):
            return head_copy(gains_v, gains_recv.at[k], hs.at[k], hr.at[k], me ^ k)

        def to_group(d):
            to = lax.rem(flat + d, group)
            return pltpu.make_async_remote_copy(
                src_ref=gains_sum, dst_ref=gains_all.at[d], send_sem=gs.at[d], recv_sem=gr.at[d],
                device_id={"seq": to // cores, "batch": lax.rem(to, cores)}, device_id_type=MESH,
            )

        for k in range(1, peers):
            gains_copy(k).start()
        for hop in hops(1):
            conv_line.advance(hop)
        in_store.start(me)
        for t in range(subs):
            ring.finish(t)
        for k in range(1, peers):
            out_store.start(me ^ k)
        gathered = gains_v[...]
        for k in range(1, peers):
            gains_copy(k).wait_recv()
            gathered = gathered + gains_recv[k]
        gains_sum[...] = gathered
        for d in range(1, group):
            to_group(d).start()
        for t in range(subs):
            in_ring.forward(t)
        for hop in hops(2):
            conv_line.advance(hop)
        in_store.start(me ^ 1)
        in_store.start(me ^ 2)
        for d in range(1, group):
            to_group(d).wait_recv()
            gathered = gathered + gains_all[d]
        gains_out[...] = gathered
        for t in range(subs):
            in_ring.finish(t)
        in_store.start(me ^ 3)
        late_out[...] = late_line.finish()
        grad = gate_line.finish()
        for head in range(heads):
            at = head * (QKV + DV) + QKV
            grad_out[:, at : at + DV] = grad[:, head * DV : (head + 1) * DV]
        grad = conv_line.finish()
        for head in range(heads):
            at = head * (QKV + DV)
            grad_out[:, at : at + QKV] = grad[:, head * QKV : (head + 1) * QKV]
        small_out[...] = grad[:, conv_cols:]
        for k in range(peers):
            out_store.wait(k)
            in_store.wait(k)

        @pl.when(place > 0)
        def _():
            for chain in range(chains):
                returned(chain).wait_send()
                for side in range(2):
                    passed(chain, side).wait_send()

        sums.drain(0)
        for t in range(subs):
            ring.drain(t)
            in_ring.drain(t)
            in_sums.drain(t)
        for k in range(1, peers):
            gains_copy(k).wait_send()
        for d in range(1, group):
            to_group(d).wait_send()
        conv_line.drain(lambda d: conv_source.at[d])
        gate_line.drain(lambda d: gate_source.at[d])
        late_line.drain(late_source)


def backward_rule(
    starts, decay_par, dn, mixed, og, projected, rates, o_gain, n, qe, tot, trans, qkv, inv, states, halo,
    conv_w, hidden, hidden_grad, gain, ffn_gain_part, ffn_part, in_full, gate_full,
    rates_full, turned, x, late_grads, heads,
):
    places, peers, cores = lax.axis_size("seq"), lax.axis_size("head"), lax.axis_size("batch")
    chains, count = n.shape[:2]
    seqs = chains // heads
    rows = projected.shape[0]
    length = rows // seqs
    width = hidden.shape[1]
    own_rows = hidden.shape[0]
    subs = own_rows // SUB
    values = heads * DV
    cols = heads * (QKV + DV) + PAD
    group = places * cores
    shard = width // group
    gain_rows = 3 * width // 128
    row = lambda first: lambda i: (i // heads, first + i % heads)
    whole = lambda *dims: pl.BlockSpec(dims, lambda j: (0,) * len(dims))
    chain4 = lambda i: (i, 0, 0, 0)
    shape = jax.ShapeDtypeStruct
    per_chain = pltpu.SemaphoreType.DMA((chains,))
    per_peer = pltpu.SemaphoreType.DMA((peers,))
    per_member = pltpu.SemaphoreType.DMA((group,))
    pieces = pltpu.SemaphoreType.DMA((peers, subs))
    ffn_sums = sum_buffers(own_rows, width, subs)
    ffn_sums[3:5] = [pltpu.SemaphoreType.DMA((6, 1))] * 2
    return pl.pallas_call(
        functools.partial(backward_kernel, heads, places, peers, cores),
        grid=(2 * chains,),
        in_specs=[
            smem(),
            smem(),
            pl.BlockSpec((length, DV), early(chains, row(0))),
            pl.BlockSpec((length, DV), early(chains, row(0))),
            pl.BlockSpec((length, DV), early(chains, row(0))),
            whole(1, DV),
            whole(chains, count, DK, DK),
            whole(chains, count, CHUNK, DK),
            whole(chains, count, DK),
            whole(chains, DK, DK),
            pl.BlockSpec((length, QKV), late(chains, row(0))),
            pl.BlockSpec((1, count, CHUNK, CHUNK), late(chains, chain4)),
            pl.BlockSpec((1, count, DK, DV), late(chains, chain4)),
            pl.BlockSpec((length, QKV), late(chains, row(0))),
            pl.BlockSpec((1, HALO, QKV), late(chains, lambda i: (i // heads, 0, i % heads))),
            pl.BlockSpec((length, PAD), late(chains, lambda i: (i // heads, 0))),
            pl.BlockSpec((CONV, QKV), late(chains, lambda i: (0, i % heads))),
            whole(own_rows, width),
            whole(own_rows, width),
            whole(1, width),
            whole(8, width),
        ]
        + [anywhere()] * 7,
        out_specs=[
            anywhere(),
            anywhere(),
            whole(gain_rows, 128),
            whole(shard, cols - PAD),
            whole(shard, PAD),
            whole(shard, late_grads.shape[1]),
        ],
        out_shape=[
            shape((rows, width), bf16),
            shape((rows, width), bf16),
            shape((gain_rows, 128), f32),
            shape((shard, cols - PAD), f32),
            shape((shard, PAD), f32),
            shape((shard, late_grads.shape[1]), f32),
        ],
        scratch_shapes=[
            pltpu.VMEM((rows, cols), bf16),
            pltpu.VMEM((HALO + length, QKV), f32),
            pltpu.VMEM((16 + length, QKV), f32),
            pltpu.VMEM((chains, length, DV), bf16),
            pltpu.VMEM((chains, DK, DV), f32),
            pltpu.VMEM((chains, DK, DV), bf16),
            pltpu.VMEM((chains, DK, DV), bf16),
            pltpu.VMEM((chains, HALO, QKV), f32),
            pltpu.VMEM((chains, 8, QKV), f32),
            pltpu.VMEM((chains, 8, QKV), f32),
            pltpu.VMEM((CONV * heads, QKV), f32),
            pltpu.VMEM((CONV * heads, PAD), f32),
            pltpu.VMEM((8, DV), f32),
            pltpu.VMEM((rows, width), bf16),
            pltpu.VMEM((rows, width), bf16),
            pltpu.VMEM((width, cols - values), bf16),
            pltpu.VMEM((width, values), bf16),
            pltpu.VMEM((width, rows), bf16),
            pltpu.VMEM((own_rows, width), bf16),
            pltpu.VMEM((places, shard, cols - values), bf16),
            pltpu.VMEM((places, shard, values), bf16),
            pltpu.VMEM((width, PAD), f32),
            pltpu.VMEM((gain_rows, 128), f32),
            pltpu.VMEM((peers, gain_rows, 128), f32),
            pltpu.VMEM((gain_rows, 128), f32),
            pltpu.VMEM((group, gain_rows, 128), f32),
            pltpu.SemaphoreType.DMA((chains, 2)),
            pltpu.SemaphoreType.DMA((chains, 2)),
            per_chain, per_chain,
            pieces,
            pltpu.SemaphoreType.DMA((4,)),
            pltpu.SemaphoreType.DMA((places,)),
            pieces,
            pltpu.SemaphoreType.DMA((2, peers, subs)),
            per_peer, per_peer, per_member, per_member,
        ]
        + ffn_sums
        + sum_buffers(own_rows, width, subs)
        + line_buffers(places, shard, cols - values)
        + line_buffers(places, shard, values)
        + line_buffers(places, shard, late_grads.shape[1]),
        compiler_params=pltpu.CompilerParams(
            dimension_semantics=("arbitrary",), collective_id=4, has_side_effects=True,
            vmem_limit_bytes=62 * 2**20,
        ),
        name="backward_rule",
    )(
        starts, decay_par, dn, mixed, og, o_gain, n, qe, tot, trans, qkv, inv, states, projected,
        halo, rates, conv_w, hidden, hidden_grad, gain, ffn_gain_part, ffn_part, in_full,
        gate_full, rates_full, turned, x, late_grads,
    )


def smem():
    return pl.BlockSpec(memory_space=pltpu.SMEM)


def rows_of(t):
    return pl.ds(pl.multiple_of(t * SUB, SUB), SUB)


def block_store(i, size, source, target, sem):
    return pltpu.make_async_copy(
        part(source, i * size, size), part(target, i * size, size), sem.at[i]
    )


def mixer_kernel(
    peers, nin_hbm, mixed_hbm, weights_hbm, x_hbm, gain_ref, o_gain_ref,
    og_hbm, normed_hbm, nm_hbm, turned_hbm, hidden_ref,
    nin, turned, mixed, weights, x_v, og_v, normed_v, nm, in_sem, x_sem, out_sem,
    send, recv, relay, sum_send, sum_recv, gather_send, gather_recv,
):
    me = lax.axis_index("head")
    total, width = nm.shape
    values = mixed.shape[1]
    own_rows = total // peers
    subs = own_rows // SUB
    loads = [
        pltpu.make_async_copy(weights_hbm, weights, in_sem.at[0]),
        pltpu.make_async_copy(nin_hbm, nin, in_sem.at[1]),
        pltpu.make_async_copy(mixed_hbm, mixed, in_sem.at[2]),
    ]
    for load in loads:
        load.start()
    own_x = Pieces(x_hbm, x_v, total, subs, x_sem)
    own_x.start(me)
    stores = [
        Pieces(source, target, total, subs, out_sem.at[i])
        for i, (source, target) in enumerate(
            ((og_v, og_hbm), (normed_v, normed_hbm), (nm, nm_hbm))
        )
    ]
    greet_heads(me, peers)
    for load in loads:
        load.wait()
    sums = Combine(send, recv, relay, me, sum_send, sum_recv, SUB)

    def project(i, carry):
        k = jnp.where(i == 0, peers - 1, lax.rem(i, peers - 1))
        owner = me ^ k
        og = mm(take(nin, owner, subs), weights[:, 0:values])
        gated = og * sigmoid(og)
        own = take(mixed, owner, subs)
        normed = []
        for first in range(0, values, DV):
            at = slice(first, first + DV)
            inverse = lax.rsqrt(
                jnp.mean(own[:, at] * own[:, at], axis=1, keepdims=True) + epsilon
            )
            normed.append((own[:, at] * inverse * o_gain_ref[0:1] * gated[:, at]).astype(bf16))
        normed = jnp.concatenate(normed, axis=1)
        send[k] = mm(normed, weights[:, values:], NT).astype(bf16)
        for t in range(subs):
            rows = piece_rows(owner, t, total, subs)
            og_v[rows, :] = og[t * SUB : (t + 1) * SUB]
            normed_v[rows, :] = normed[t * SUB : (t + 1) * SUB]

        for kk in range(1, peers):

            @pl.when(k == kk)
            def _():
                for t in range(subs):
                    sums.start(kk, t)

        stores[0].start(owner)
        stores[1].start(owner)
        return carry

    lax.fori_loop(0, peers, project, 0)
    tile = 256
    for first in range(0, width, tile):
        turned[first : first + tile, :] = nin[:, first : first + tile].T
    for t in range(subs):
        sums.combine(t)
    turned_store = pltpu.make_async_copy(turned, turned_hbm, in_sem.at[3])
    turned_store.start()
    own_x.wait(me)
    gain = gain_ref[...]
    ring = Spread(nm, subs, me, gather_send, gather_recv)
    for t in range(subs):
        rows = rows_of(t)
        hidden = x_v[rows, :].astype(f32) + sums.collect(t)
        hidden_ref[rows, :] = hidden
        inverse = lax.rsqrt(jnp.mean(hidden * hidden, axis=1, keepdims=True) + epsilon)
        ring.put(t, (hidden * inverse * gain).astype(bf16))
        ring.start(t)
    for t in range(subs):
        ring.forward(t)
    for k in range(peers):
        if k == peers - 1:
            for t in range(subs):
                ring.finish(t)
        stores[2].start(me ^ k)
    turned_store.wait()
    for i in range(peers):
        for store in stores:
            store.wait(i)
    for t in range(subs):
        sums.drain(t)
        ring.drain(t)


def mixer(nin, mixed, weights, x, gain, o_gain):
    peers = lax.axis_size("head")
    total, width = x.shape
    values = mixed.shape[1]
    own_rows = total // peers
    subs = own_rows // SUB
    shape = in_hbm
    return pl.pallas_call(
        functools.partial(mixer_kernel, peers),
        in_specs=[anywhere()] * 4 + [vmem()] * 2,
        out_specs=[anywhere()] * 4 + [vmem()],
        out_shape=[
            shape((total, values), f32),
            shape((total, values), bf16),
            shape((total, width), bf16),
            shape((width, total), bf16),
            shape((own_rows, width), f32),
        ],
        scratch_shapes=[
            pltpu.VMEM((total, width), bf16),
            pltpu.VMEM((width, total), bf16),
            pltpu.VMEM((total, values), f32),
            pltpu.VMEM((width, 2 * values), bf16),
            pltpu.VMEM((own_rows, width), bf16),
            pltpu.VMEM((total, values), f32),
            pltpu.VMEM((total, values), bf16),
            pltpu.VMEM((total, width), bf16),
            pltpu.SemaphoreType.DMA((4,)),
            pltpu.SemaphoreType.DMA((peers, subs)),
            pltpu.SemaphoreType.DMA((3, peers, subs)),
        ]
        + sum_buffers(own_rows, width, subs),
        compiler_params=pltpu.CompilerParams(
            collective_id=1, has_side_effects=True, vmem_limit_bytes=62 * 2**20
        ),
        name="mixer",
    )(nin, mixed, weights, x, gain, o_gain)


def ffn_kernel(
    peers, places, cores, nm_hbm, ffn_hbm, ct_hbm, normed_hbm, weights_hbm, hidden_ref, gain_ref,
    grads_hbm, ffnp_hbm, ng_hbm, hgrad_ref, gpart_ref, down_ref,
    nm_b, ct_b, dgu_b, nm, ffn_v, ends_v, ct_v, normed_v, wout_v, act, dgu, dm, ffnp_v, grads_v, down_v, ng_v, out_acc,
    in_sem, out_sem, ng_sem, send, recv, relay, sum_send, sum_recv, gather_send, gather_recv,
    core_recv, seq_send, seq_recv, scatter_sems,
):
    me = lax.axis_index("head")
    total, width = nm.shape
    values = normed_v.shape[1]
    own_rows = total // peers
    subs = own_rows // SUB
    cells = act.shape[1]
    tile = 256
    whole_cells = cells - PAD
    loads = [
        pltpu.make_async_copy(
            ffn_hbm.at[:, pl.ds(p * whole_cells, whole_cells)],
            ffn_v.at[:, pl.ds(p * cells, whole_cells)], in_sem.at[5 + p],
        )
        for p in range(3)
    ] + [
        pltpu.make_async_copy(
            ffn_hbm.at[:, pl.ds(3 * whole_cells, PAD)], ends_v, in_sem.at[0]
        ),
        pltpu.make_async_copy(
            ffn_hbm.at[:, pl.ds(3 * whole_cells + PAD, PAD)],
            ffn_v.at[:, pl.ds(3 * cells - PAD, PAD)], in_sem.at[8],
        ),
        pltpu.make_async_copy(nm_hbm, nm, in_sem.at[1]),
        pltpu.make_async_copy(ct_hbm, ct_v, in_sem.at[2]),
        pltpu.make_async_copy(normed_hbm, normed_v, in_sem.at[3]),
        pltpu.make_async_copy(weights_hbm.at[:, pl.ds(values, values)], wout_v, in_sem.at[4]),
    ]
    for load in loads:
        load.start()
    greet_group(me, peers, places, cores)
    for load in loads[:7]:
        load.wait()
    low = lax.broadcasted_iota(jnp.int32, ends_v.shape, 1) < PAD // 2
    ends = ends_v[...].astype(f32)
    ffn_v[:, whole_cells:cells] = jnp.where(low, ends, 0.0).astype(bf16)
    ffn_v[:, cells + whole_cells : 2 * cells] = jnp.where(
        low, pltpu.roll(ends, PAD // 2, 1), 0.0
    ).astype(bf16)
    gain = gain_ref[...]
    sums = Combine(send, recv, relay, me, sum_send, sum_recv, SUB)

    def feed_forward(i, carry):
        k = jnp.where(i == 0, peers - 1, lax.rem(i, peers - 1))
        owner = me ^ k
        nm_b[...] = take(nm, owner, subs)
        ct_b[...] = take(ct_v, owner, subs)

        def cell_tile(j, carry):
            at = pl.ds(pl.multiple_of(j * tile, tile), tile)
            at_up = pl.ds(pl.multiple_of(cells + j * tile, tile), tile)
            at_down = pl.ds(pl.multiple_of(2 * cells + j * tile, tile), tile)
            gate = mm(nm_b[...], ffn_v[:, at])
            up = mm(nm_b[...], ffn_v[:, at_up])
            dact = mm(ct_b[...], ffn_v[:, at_down])
            sig = sigmoid(gate)
            silu = gate * sig
            activated = (silu * up).astype(bf16)
            dgu_b[:, at] = (dact * up * sig * (1.0 + gate * (1.0 - sig))).astype(bf16)
            dgu_b[:, at_up] = (dact * silu).astype(bf16)
            for t in range(subs):
                act[piece_rows(owner, t, total, subs), at] = activated[t * SUB : (t + 1) * SUB]
            return carry

        lax.fori_loop(0, cells // tile, cell_tile, 0)

        def mid_tile(j, carry):
            at = pl.ds(pl.multiple_of(j * tile, tile), tile)
            send[k, :, at] = mm(dgu_b[...], ffn_v[at, 0 : 2 * cells], NT).astype(bf16)
            return carry

        lax.fori_loop(0, width // tile, mid_tile, 0)
        for t in range(subs):
            dgu[piece_rows(owner, t, total, subs), :] = dgu_b[rows_of(t), :]

        for kk in range(1, peers):

            @pl.when(k == kk)
            def _():
                for t in range(subs):
                    sums.start(kk, t)

        @pl.when(k == 2)
        def _():
            for t in range(subs):
                sums.combine(t)

        return carry

    lax.fori_loop(0, peers, feed_forward, 0)

    def down_grads(i, carry):
        at = pl.ds(pl.multiple_of(i * tile, tile), tile)
        down_v[at, 0:cells] = mm(ct_v[:, at], act[...], TN).astype(bf16)
        down_v[at, cells:] = mm(nm[:, at], dgu[:, 0:tile], TN).astype(bf16)
        return carry

    lax.fori_loop(0, width // tile, down_grads, 0)
    scatter = GroupScatter(down_v, pl.ds(0, cells + tile), core_recv, seq_send, seq_recv, scatter_sems)
    for k in range(places - 1, -1, -1):
        scatter.core_copy(k).start()

    def cell_grads(i, carry):
        at = pl.ds(pl.multiple_of(i * tile, tile), tile)
        grads_v[at, 0 : 2 * cells - tile] = mm(nm[:, at], dgu[:, tile:], TN).astype(bf16)
        return carry

    half = width // tile // 2
    lax.fori_loop(0, half, cell_grads, 0)
    for k in range(places - 1, -1, -1):
        scatter.pass_on(k)
    lax.fori_loop(half, width // tile, cell_grads, 0)
    ring = Spread(dm, subs, me, gather_send, gather_recv)
    gain_part = jnp.zeros((1, width), f32)
    for t in range(subs):
        rows = rows_of(t)
        dmid = sums.collect(t)
        hidden = hidden_ref[rows, :]
        inverse = lax.rsqrt(jnp.mean(hidden * hidden, axis=1, keepdims=True) + epsilon)
        scaled = hidden * inverse
        weighted = dmid * gain
        grad = ct_v[piece_rows(me, t, total, subs), :].astype(f32) + inverse * (
            weighted - scaled * jnp.mean(weighted * scaled, axis=1, keepdims=True)
        )
        hgrad_ref[rows, :] = grad
        ring.put(t, grad.astype(bf16))
        ring.start(t)
        gain_part = gain_part + jnp.sum(dmid * scaled, axis=0, keepdims=True)
    gpart_ref[...] = jnp.broadcast_to(gain_part, gpart_ref.shape)

    def ffn_rows(i, carry):
        rows = pl.ds(pl.multiple_of(i * own_rows, own_rows), own_rows)
        ffnp_v[rows, :] = mm(act[rows, :], ffn_v[:, 2 * cells :], NT).astype(bf16)
        block_store(i, own_rows, ffnp_v, ffnp_hbm, out_sem.at[0]).start()
        return carry

    lax.fori_loop(0, peers, ffn_rows, 0)
    loads[7].wait()
    loads[8].wait()
    for t in range(subs):
        ring.forward(t)

    ng_store = Pieces(ng_v, ng_hbm, total, subs, ng_sem)

    def norm_rows(k, carry):
        owner = me ^ k

        @pl.when(k == peers - 1)
        def _():
            for t in range(subs):
                ring.finish(t)

        block = take(dm, owner, subs)
        grads = mm(block, wout_v[...])
        for t in range(subs):
            ng_v[piece_rows(owner, t, total, subs), :] = grads[t * SUB : (t + 1) * SUB]
        ng_store.start(owner)
        rows = take(normed_v, owner, subs)
        for first in range(0, width, tile):
            at = slice(first, first + tile)
            before = jnp.where(k == 0, 0.0, out_acc[at, :])
            out_acc[at, :] = before + mm(block[:, at], rows, TN)
        return carry

    lax.fori_loop(0, peers, norm_rows, 0)

    def out_grads(i, carry):
        at = pl.ds(pl.multiple_of(i * tile, tile), tile)
        grads_v[at, 2 * cells - tile :] = out_acc[at, :].astype(bf16)
        block_store(i, tile, grads_v, grads_hbm, out_sem.at[1]).start()
        return carry

    lax.fori_loop(0, width // tile, out_grads, 0)
    down_ref[...] = scatter.finish()
    for i in range(peers):
        block_store(i, own_rows, ffnp_v, ffnp_hbm, out_sem.at[0]).wait()
        ng_store.wait(i)
    for i in range(width // tile):
        block_store(i, tile, grads_v, grads_hbm, out_sem.at[1]).wait()
    for t in range(subs):
        sums.drain(t)
        ring.drain(t)
    scatter.drain()


def feed_forward_block(nm, ffn_full, ct, normed, weights, hidden, gain, cells):
    peers, places, cores = lax.axis_size("head"), lax.axis_size("seq"), lax.axis_size("batch")
    total, width = ct.shape
    own_rows = total // peers
    subs = own_rows // SUB
    values = normed.shape[1]
    shard = width // (places * cores)
    shape = in_hbm
    return pl.pallas_call(
        functools.partial(ffn_kernel, peers, places, cores),
        in_specs=[anywhere()] * 5 + [vmem()] * 2,
        out_specs=[anywhere()] * 3 + [vmem()] * 3,
        out_shape=[
            shape((width, 2 * cells - 256 + values), bf16),
            shape((total, width), bf16),
            shape((total, values), f32),
            shape((own_rows, width), f32),
            shape((8, width), f32),
            shape((shard, cells + 256), f32),
        ],
        scratch_shapes=[
            pltpu.VMEM((own_rows, width), bf16),
            pltpu.VMEM((own_rows, width), bf16),
            pltpu.VMEM((own_rows, 2 * cells), bf16),
            pltpu.VMEM((total, width), bf16),
            pltpu.VMEM((width, 3 * cells), bf16),
            pltpu.VMEM((width, PAD), bf16),
            pltpu.VMEM((total, width), bf16),
            pltpu.VMEM((total, values), bf16),
            pltpu.VMEM((width, values), bf16),
            pltpu.VMEM((total, cells), bf16),
            pltpu.VMEM((total, 2 * cells), bf16),
            pltpu.VMEM((total, width), bf16),
            pltpu.VMEM((total, width), bf16),
            pltpu.VMEM((width, 2 * cells - 256 + values), bf16),
            pltpu.VMEM((width, cells + 256), bf16),
            pltpu.VMEM((total, values), f32),
            pltpu.VMEM((width, values), f32),
            pltpu.SemaphoreType.DMA((9,)),
            pltpu.SemaphoreType.DMA((2, max(peers, width // 256))),
            pltpu.SemaphoreType.DMA((peers, subs)),
        ]
        + sum_buffers(own_rows, width, subs)
        + scatter_buffers(places, shard, cells + 256),
        compiler_params=pltpu.CompilerParams(
            collective_id=5, has_side_effects=True, vmem_limit_bytes=62 * 2**20
        ),
        name="feed_forward",
    )(nm, ffn_full, ct, normed, weights, hidden, gain)


def results_kernel(
    units, cells, late_hbm, down_hbm, main_hbm, small_hbm, out_hbm, igrad_hbm,
    cells_ref, down_ref, mixer_ref, main_ref, rates_ref, conv_ref, decay_ref, out_ref, igrad_ref,
    late_ref, down_in, main_in, small_in, out_v, igrad_v, sems,
):
    loads = [
        pltpu.make_async_copy(out_hbm, out_v, sems.at[0]),
        pltpu.make_async_copy(igrad_hbm, igrad_v, sems.at[1]),
    ]
    copies = [
        pltpu.make_async_copy(out_v, out_ref, sems.at[2]),
        pltpu.make_async_copy(igrad_v, igrad_ref, sems.at[3]),
    ]
    firsts = [
        pltpu.make_async_copy(late_hbm, late_ref, sems.at[4]),
        pltpu.make_async_copy(down_hbm, down_in, sems.at[5]),
        pltpu.make_async_copy(main_hbm, main_in, sems.at[6]),
        pltpu.make_async_copy(small_hbm, small_in, sems.at[7]),
    ]
    for load in loads + firsts:
        load.start()
    for load, copy in zip(loads, copies):
        load.wait()
        copy.start()
    firsts[0].wait()
    taps, heads, per = conv_ref.shape
    firsts[1].wait()
    early = down_in.shape[1] - cells
    up_at = cells - early
    cells_ref[0, 0:early] = down_in[:, cells:].T
    cells_ref[0, early:units] = late_ref[:, 0:up_at].T[0 : units - early]
    cells_ref[1] = late_ref[:, up_at : up_at + cells].T[0:units]
    down_ref[...] = down_in[:, 0:cells].T[0:units]
    mixer_ref[...] = late_ref[:, up_at + cells :].T
    firsts[2].wait()
    firsts[3].wait()
    wide = main_ref.shape[2]
    for head in range(heads):
        main_ref[:, head, :] = main_in[:, head * wide : (head + 1) * wide]
    small = small_in[...]
    rates_ref[...] = small.T[0 : 2 * heads]
    for tap in range(taps):
        conv_ref[tap] = small[tap * heads : (tap + 1) * heads, PAD // 2 : PAD // 2 + per]
    for row in range(2):
        at = (2 + row) * heads
        decay_ref[row : row + 1, :] = small[0:1, at : at + heads]
    for copy in copies:
        copy.wait()


def results(late, down, main, small, out, igrad, units, cells, heads, per):
    shard = late.shape[0]
    values = late.shape[1] + down.shape[1] - 3 * cells
    shape = jax.ShapeDtypeStruct
    return pl.pallas_call(
        functools.partial(results_kernel, units, cells),
        in_specs=[anywhere()] * 6,
        out_specs=[vmem()] * 7 + [anywhere()] * 2,
        out_shape=[
            shape((2, units, shard), f32),
            shape((units, shard), f32),
            shape((values, shard), f32),
            shape((shard, heads, main.shape[1] // heads), f32),
            shape((2 * heads, shard), f32),
            shape((CONV, heads, per), f32),
            shape((2, heads), f32),
            in_hbm(out.shape, out.dtype),
            in_hbm(igrad.shape, igrad.dtype),
        ],
        scratch_shapes=[
            pltpu.VMEM(late.shape, f32),
            pltpu.VMEM(down.shape, f32),
            pltpu.VMEM(main.shape, f32),
            pltpu.VMEM(small.shape, f32),
            pltpu.VMEM(out.shape, out.dtype),
            pltpu.VMEM(igrad.shape, igrad.dtype),
            pltpu.SemaphoreType.DMA((8,)),
        ],
        compiler_params=pltpu.CompilerParams(vmem_limit_bytes=62 * 2**20),
        name="results",
    )(late, down, main, small, out, igrad)


def shifted(shard, axis, by):
    count = lax.axis_size(axis)
    pairs = [(i, i + by) for i in range(count) if 0 <= i + by < count]
    return lax.ppermute(shard, axis, pairs)


def root_scale(value_rows):
    return lax.rsqrt(jnp.mean(value_rows * value_rows, axis=-1, keepdims=True) + epsilon)


def matmul(a, b, dims=NN):
    return lax.dot_general(a, b, (dims, ((), ())), preferred_element_type=f32)


ALL = ("seq", "batch")


def per_device(
    tokens, starts, attn_gain, w_in, w_rates, conv_w, decay_par, o_gain, w_out, ffn_gain, w_gu,
    w_down, cotangent,
):
    seqs, length, width = tokens.shape
    shard, heads = w_in.shape[:2]
    shards = width // shard
    total = seqs * length
    conv_cols = heads * QKV
    value_cols = heads * DV
    units = w_down.shape[0]
    cells = -(-units // 256) * 256

    packed_in = w_in[:, :, :QKV].reshape(shard, conv_cols).astype(bf16)
    packed_gate = jnp.concatenate(
        [w_in[:, :, QKV:].reshape(shard, value_cols), w_out.reshape(value_cols, -1).T], axis=1
    ).astype(bf16)
    whole_cells = cells - PAD
    gate, up, down = w_gu[:, 0], w_gu[:, 1], w_down.T
    ends = jnp.zeros((shard, PAD // 2 - (units - whole_cells)), f32)
    packed_ffn = jnp.concatenate(
        [part[:, :whole_cells] for part in (gate, up, down)]
        + [
            piece
            for part in (gate, up, down)
            for piece in (part[:, whole_cells:], ends)
        ]
        + [jnp.zeros((shard, PAD // 2), f32)],
        axis=1,
    ).astype(bf16)
    conv_flat = conv_w.reshape(-1)
    small = jnp.concatenate(
        [attn_gain, ffn_gain, conv_flat, o_gain, w_rates.reshape(-1)]
    ).astype(bf16)

    x = tokens.reshape(total, width)
    ct = cotangent.reshape(total, width)
    before = shifted(tokens[:, length - HALO :], "seq", 1).reshape(seqs * HALO, width)
    in_full = lax.all_gather(packed_in, ALL, axis=0, tiled=True)
    small_full = lax.all_gather(small, ALL, axis=0)
    gate_full = lax.all_gather(packed_gate, ALL, axis=0, tiled=True)
    ffn_full = lax.all_gather(packed_ffn, ALL, axis=0, tiled=True)
    attn_gain_f = small_full[:, :shard].reshape(1, width).astype(f32)
    ffn_gain_f = small_full[:, shard : 2 * shard].reshape(1, width).astype(f32)
    conv_end = 2 * shard + conv_flat.shape[0]
    conv_full = (
        small_full[:, 2 * shard : conv_end]
        .reshape(shards, CONV, heads, -1)
        .transpose(1, 2, 0, 3)
        .reshape(CONV, conv_cols)
        .astype(f32)
    )
    rates_at = conv_end + o_gain.shape[0]
    o_gain_full = small_full[:, conv_end:rates_at].reshape(1, DV).astype(f32)
    rates_full = jnp.pad(
        small_full[:, rates_at:].reshape(width, 2 * heads), ((0, 0), (0, PAD - 2 * heads))
    )

    def normed_rows(rows):
        rows = rows.astype(f32)
        return (rows * root_scale(rows) * attn_gain_f).astype(bf16)

    normed_in = normed_rows(x)
    rates = matmul(normed_in, rates_full)
    projected = pltpu.with_memory_space_constraint(matmul(normed_in, in_full), pltpu.HBM)
    halo = matmul(normed_rows(before), in_full).reshape(seqs, HALO, conv_cols)
    qkv, inv, n, qe, tot, trans, states, mixed = forward_rule(
        starts, decay_par, projected, halo, rates, conv_full, seqs, heads
    )
    og, normed, nm, turned_in, hidden = mixer(
        normed_in, mixed, gate_full, x, ffn_gain_f, o_gain_full
    )
    late_grads, ffn_part, normed_grad, hidden_grad, ffn_gain_part, down_own = feed_forward_block(
        nm, ffn_full, ct, normed, gate_full, hidden, ffn_gain_f, cells
    )
    result, input_grad, gains, in_main, in_small, late_own = backward_rule(
        starts, decay_par, normed_grad, mixed, og, projected, rates, o_gain_full, n, qe, tot, trans, qkv,
        inv, states, halo, conv_full, hidden, hidden_grad, attn_gain_f, ffn_gain_part, ffn_part,
        in_full, gate_full, rates_full, turned_in, x, late_grads, heads,
    )
    grad_cells, grad_down, grad_out, grad_in, grad_rates, grad_conv, grad_decay, out, input_grad = (
        results(
            late_own, down_own, in_main, in_small, result, input_grad, units, cells, heads,
            QKV // shards,
        )
    )
    at = lax.axis_index(ALL)
    gains = gains.reshape(3, width)
    own_gains = lax.dynamic_slice(gains, (0, at * shard), (2, shard))
    onorm_own = lax.dynamic_slice(gains, (2, at * (DV // shards)), (1, DV // shards))
    return (
        out.reshape(tokens.shape),
        input_grad.reshape(tokens.shape),
        own_gains[0],
        grad_in,
        grad_rates.reshape(heads, 2, shard).transpose(2, 0, 1),
        grad_conv,
        grad_decay,
        onorm_own[0],
        grad_out.reshape(heads, DV, -1),
        own_gains[1],
        grad_cells.transpose(2, 0, 1),
        grad_down,
    )


def solution(mesh):
    weights = P(ALL)
    in_specs = (
        P("batch", "seq", None),
        P("batch"),
        weights,
        P(ALL, "head", None),
        P(ALL, "head", None),
        P(None, "head", ALL),
        P(None, "head"),
        weights,
        P("head", None, ALL),
        weights,
        P(ALL, None, "head"),
        P("head", ALL),
        P("batch", "seq", None),
    )
    out_specs = (
        P("batch", "seq", None),
        P("batch", "seq", None),
        weights,
        P(ALL, "head", None),
        P(ALL, "head", None),
        P(None, "head", ALL),
        P(None, "head"),
        weights,
        P("head", None, ALL),
        weights,
        P(ALL, None, "head"),
        P("head", ALL),
    )
    return jax.shard_map(
        per_device, mesh=mesh, in_specs=in_specs, out_specs=out_specs, check_vma=False
    )
```
